32 devices in a mesh: groups: 2 (over y), wide: 4 (over z), narrow: 2 (over x), pair: 2 (over core).
Axes of the slice: x: 2, y: 2, z: 4, core: 2. Of those that a mesh axis runs over, the one named last changes fastest.
Arguments:
- offsets: float32 [3, 32768], P(None, ('groups', 'wide', 'narrow')), parts along dimension 1, may hold values from -0.5 to 0.5
- charges: float32 [32768], P(('groups', 'wide', 'narrow')), parts along dimension 0, may hold values from -1.5 to 1.5
- stress: float32 [32768], P(('groups', 'wide', 'narrow', 'pair')), parts along dimension 0, may hold values from -6 to 6
- decay_rate: float32 [512], P(('groups', 'wide', 'narrow', 'pair')), parts along dimension 0, may hold values from 0.3 to 0.9
- morton_keys: int32 [512], P(('groups', 'wide', 'narrow')), parts along dimension 0, may hold values from 0 to 2047, as said below
- levels: int32 [512], P(('groups', 'wide', 'narrow')), parts along dimension 0, may hold values from 8 to 10
- bead_counts: int32 [512], P(('groups', 'wide', 'narrow')), parts along dimension 0, may hold values from 32 to 64
- send_boxes: int32 [16, 16], P(('groups', 'wide', 'narrow')), parts along dimension 0, may hold values from 0 to 31
- m2l_source: int32 [512, 32], P(('groups', 'wide', 'narrow')), parts along dimension 0, may hold values from 0 to 47
- m2l_type: int32 [512, 32], P(('groups', 'wide', 'narrow')), parts along dimension 0, may hold values from 0 to 315
- m2l_count: int32 [512], P(('groups', 'wide', 'narrow')), parts along dimension 0, may hold values from 16 to 32
- near_source: int32 [512, 16], P(('groups', 'wide', 'narrow')), parts along dimension 0, may hold values from 0 to 95, as said below
- up_inverse: float32 [152, 152], replicated, may hold values from -0.5 to 0.5
- down_inverse: float32 [152, 152], replicated, may hold values from -0.5 to 0.5
- translations: float32 [316, 2, 1728], P(None, None, 'pair'), may hold values from -6 to 6
Outputs:
- potential: float32 [32768], P(('groups', 'wide', 'narrow', 'pair')), parts along dimension 0
- new_stress: float32 [32768], P(('groups', 'wide', 'narrow', 'pair')), parts along dimension 0
The draws below stay inside these ranges and needn't reach their ends.
There are 2 independent parts, one for each index of `groups`. The reference program is written for one: setup_inputs(seed, part) draws one part's arguments, and reference() takes and returns one part's arrays. A program takes and returns all parts, laid end to end along the dimension named above; an argument that names none is the same for every part. Nothing has to cross between parts.
Inputs may be any that keep to these rules, and one draw needn't show every extreme that they name: `morton_keys`: leaf i has a key from 8 i to 8 i + 7. `near_source`: entry 0 of a leaf's list is the leaf itself (32 plus its position on its device); every entry lies within 32 of that.
All inputs are finite; a program needn't handle non-finite values.
Results may differ from the reference program's by a relative error of at most 0.0003.
Values sent between devices are 32-bit elements; how exact they have to be, the bound alone decides.
No kernel may reach another device: no remote copies, remote signals or barrier semaphores. Data moves between devices by JAX's collectives and lax.ppermute only.
A program may use at most 64 MiB of HBM per device.

```python
import jax
import jax.numpy as jnp
import numpy as np
from jax import lax

Q = 152
PGRID = 12
G = 1728
KTYPES = 316
MAXL = 10
BCAP = 64
LIST = 32
NEAR = 16
CAP = 2
LEAF_DEV = 32
NDEV = 8
LEAVES = 256
BEADS = 16384
SRC = 48


def ragged_counts(key, most):
    key_cap, key_draw, key_spot, key_low = jax.random.split(key, 4)
    ceiling = jax.random.randint(key_cap, (NDEV, 1), 3 * most // 4 + 1, most + 1)
    counts = jax.random.randint(key_draw, (NDEV, LEAF_DEV), most // 2, ceiling + 1).reshape(-1)
    position = jax.random.randint(key_spot, (), 0, LEAVES)
    lowest = jax.random.randint(key_low, (), 0, LEAVES)
    counts = counts.at[lowest].set(most // 2)
    return counts.at[position].set(most).astype(jnp.int32)


def draw_morton_keys(key, part):
    key = jax.random.fold_in(key, 11)
    jitter = jax.random.randint(key, (LEAVES,), 0, 8)
    jitter = jitter.at[0].set(0).at[LEAVES - 1].set(7)
    return (jnp.arange(LEAVES, dtype=jnp.int32) * 8 + jitter).astype(jnp.int32)


def draw_bead_counts(key, part):
    key = jax.random.fold_in(key, 12)
    return ragged_counts(key, BCAP)


def draw_m2l_count(key, part):
    key = jax.random.fold_in(key, 13)
    return ragged_counts(key, LIST)


def draw_near_source(key, part):
    key = jax.random.fold_in(key, 14)
    targets = jnp.arange(LEAVES, dtype=jnp.int32) % LEAF_DEV
    entries = targets[:, None] + jax.random.randint(key, (LEAVES, NEAR), 0, 2 * LEAF_DEV + 1)
    entries = entries.at[:, 0].set(targets + LEAF_DEV)
    entries = entries.at[0, 1].set(0).at[LEAVES - 1, 1].set(3 * LEAF_DEV - 1)
    return entries.astype(jnp.int32)


def place_ends(array, key, low, high):
    extent = array.shape
    index_at = [jax.random.randint(jax.random.fold_in(key, axis), (), 0, extent[axis]) for axis in range(len(extent))]
    array = array.at[tuple(index_at)].set(low)
    longest = extent.index(max(extent))
    index_at[longest] = (index_at[longest] + 1) % extent[longest]
    return array.at[tuple(index_at)].set(high)


def level_of(stream_key, shape, shards, low, high):
    level = 1.0
    for dim, blocks in shards:
        heights = jax.random.uniform(jax.random.fold_in(jax.random.fold_in(stream_key, 6), dim), (blocks,), jnp.float32, low / len(shards), high / len(shards))
        level = level * jnp.repeat(jnp.exp(heights), shape[dim] // blocks).reshape((-1,) + (1,) * (len(shape) - 1 - dim))
    return level


def gaussian(own_key, extent, width, limit, pieces=(), kind=jnp.bfloat16):
    level = level_of(own_key, extent, pieces, -0.22, 0.18) if pieces else 1.0
    values = jax.random.normal(own_key, extent, jnp.float32) * width * level
    return jnp.minimum(jnp.maximum(values, -limit), limit).astype(kind)


def setup_inputs(seed: int = 0, part: int = 0) -> dict:
    seeds = jax.random.split(jax.random.key(seed), 16)
    own_keys = jax.random.split(jax.random.fold_in(seeds[15], part), 16)
    return {
        "offsets": jnp.clip(jax.random.uniform(own_keys[0], (3, BEADS), jnp.float32, -0.5, 0.5) * level_of(own_keys[0], (3, BEADS), ((1, 8),), -0.4, 0.0), -0.5, 0.5),
        "charges": gaussian(own_keys[1], (BEADS,), 0.25, 1.5, ((0, 8),), jnp.float32),
        "stress": gaussian(own_keys[2], (BEADS,), 1.0, 6.0, ((0, 16),), jnp.float32),
        "decay_rate": jnp.clip(0.3 + 0.59999996 * jax.random.uniform(own_keys[3], (LEAVES,), jnp.float32) ** level_of(own_keys[3], (LEAVES,), ((0, 16),), -0.2, 0.2), 0.3, 0.9),
        "morton_keys": draw_morton_keys(jax.random.fold_in(jax.random.fold_in(seeds[15], part), 71), part),
        "levels": place_ends(jax.random.randint(own_keys[5], (LEAVES,), MAXL - 2, MAXL + 1), jax.random.fold_in(own_keys[5], 1), MAXL - 2, MAXL).astype(jnp.int32),
        "bead_counts": draw_bead_counts(jax.random.fold_in(jax.random.fold_in(seeds[15], part), 71), part),
        "send_boxes": place_ends(jax.random.randint(own_keys[7], (NDEV, NDEV * CAP), 0, LEAF_DEV), jax.random.fold_in(own_keys[7], 1), 0, LEAF_DEV - 1).astype(jnp.int32),
        "m2l_source": place_ends(jax.random.randint(own_keys[8], (LEAVES, LIST), 0, SRC), jax.random.fold_in(own_keys[8], 1), 0, SRC - 1).astype(jnp.int32),
        "m2l_type": place_ends(jax.random.randint(own_keys[9], (LEAVES, LIST), 0, KTYPES), jax.random.fold_in(own_keys[9], 1), 0, KTYPES - 1).astype(jnp.int32),
        "m2l_count": draw_m2l_count(jax.random.fold_in(jax.random.fold_in(seeds[15], part), 71), part),
        "near_source": draw_near_source(jax.random.fold_in(jax.random.fold_in(seeds[15], part), 71), part),
        "up_inverse": gaussian(seeds[12], (Q, Q), Q ** -0.5, 0.5, (), jnp.float32),
        "down_inverse": gaussian(seeds[13], (Q, Q), Q ** -0.5, 0.5, (), jnp.float32),
        "translations": gaussian(seeds[14], (KTYPES, 2, G), 1.0, 6.0, ((2, 2),), jnp.float32),
    }


precise = lax.Precision.HIGHEST
softening = 0.04
surface_reach = 1.25

def surface_cells():
    lattice = np.stack(np.meshgrid(np.arange(6), np.arange(6), np.arange(6), indexing='ij'), 0).reshape(3, -1)
    on_face = np.any((lattice == 0) | (lattice == 5), axis=0)
    return lattice[:, on_face]

def surface_points():
    return jnp.asarray((surface_cells().astype(np.float32) - 2.5) / 2.5)

def box_geometry(morton_keys, levels):
    coords = []
    for axis_id in range(3):
        summed = jnp.zeros_like(morton_keys)
        for bit_id in range(MAXL):
            summed = summed + (jnp.right_shift(morton_keys, 3 * bit_id + axis_id) & 1) * (1 << bit_id)
        coords.append(summed)
    corner = jnp.stack(coords, 0).astype(jnp.float32)
    widths = jnp.left_shift(jnp.ones_like(levels), MAXL - levels).astype(jnp.float32)
    return (corner + 0.5 * widths[None, :], widths)

def outer_layer(centers, widths, surface):
    return centers[:, :, None] + (surface_reach * (0.5 * widths))[None, :, None] * surface[:, None, :]

def pair_sum(targets, sources, weights):
    squared = jnp.zeros((targets.shape[1], targets.shape[2], sources.shape[2]), jnp.float32)
    for axis_id in range(3):
        gap = targets[axis_id][:, :, None] - sources[axis_id][:, None, :]
        squared = squared + gap * gap
    return jnp.einsum('bms,bs->bm', lax.rsqrt(squared + softening), weights, precision=precise)

def reference(offsets, charges, stress, decay_rate, morton_keys, levels, bead_counts, send_boxes, m2l_source, m2l_type, m2l_count, near_source, up_inverse, down_inverse, translations):
    surface = surface_points()
    cells = surface_cells()
    centers, widths = box_geometry(morton_keys, levels)
    slot_ids = jnp.arange(BCAP, dtype=jnp.int32)
    occupied = slot_ids[None, :] < bead_counts[:, None]
    places = centers[:, :, None] + widths[None, :, None] * offsets.reshape(3, LEAVES, BCAP)
    weights = jnp.where(occupied, charges.reshape(LEAVES, BCAP), 0.0)
    outer_points = outer_layer(centers, widths, surface)
    up_check = pair_sum(outer_points, places, weights)
    up_density = jnp.dot(up_check, up_inverse, precision=precise)
    grid = jnp.zeros((LEAVES, PGRID, PGRID, PGRID), jnp.float32).at[:, cells[0], cells[1], cells[2]].set(up_density)
    spectrum = jnp.fft.fftn(grid, axes=(1, 2, 3)).reshape(LEAVES, G)
    spec_re = jnp.real(spectrum).astype(jnp.float32)
    spec_im = jnp.imag(spectrum).astype(jnp.float32)
    owners = jnp.arange(LEAVES, dtype=jnp.int32) // LEAF_DEV
    remote = jnp.maximum(m2l_source - LEAF_DEV, 0)
    peer_ids = remote // CAP
    column = owners[:, None] * CAP + remote % CAP
    far_source = jnp.where(m2l_source < LEAF_DEV, owners[:, None] * LEAF_DEV + m2l_source, peer_ids * LEAF_DEV + send_boxes[peer_ids, column])
    local_re = jnp.zeros((LEAVES, G), jnp.float32)
    local_im = jnp.zeros((LEAVES, G), jnp.float32)
    for slot_id in range(LIST):
        live_share = (slot_id < m2l_count).astype(jnp.float32)[:, None]
        src_re = spec_re[far_source[:, slot_id]]
        src_im = spec_im[far_source[:, slot_id]]
        kernels = translations[m2l_type[:, slot_id]]
        local_re = local_re + live_share * (kernels[:, 0] * src_re - kernels[:, 1] * src_im)
        local_im = local_im + live_share * (kernels[:, 0] * src_im + kernels[:, 1] * src_re)
    back = jnp.fft.ifftn((local_re + 1j * local_im).reshape(LEAVES, PGRID, PGRID, PGRID), axes=(1, 2, 3))
    down_check = jnp.real(back[:, cells[0], cells[1], cells[2]]).astype(jnp.float32)
    down_density = jnp.dot(down_check, down_inverse, precision=precise)
    far_part = pair_sum(places, outer_points, down_density)
    near_part = jnp.zeros((LEAVES, BCAP), jnp.float32)
    for slot_id in range(NEAR):
        entries = near_source[:, slot_id]
        source_dev = owners - 1 + entries // LEAF_DEV
        exists = (source_dev >= 0) & (source_dev < NDEV)
        leaf_ids = jnp.clip(source_dev, 0, NDEV - 1) * LEAF_DEV + entries % LEAF_DEV
        near_part = near_part + pair_sum(places, places[:, leaf_ids], jnp.where(exists[:, None], weights[leaf_ids], 0.0))
    combined = far_part + near_part
    potential = jnp.where(occupied, combined, 0.0).reshape(-1)
    new_stress = jnp.where(occupied, decay_rate[:, None] * stress.reshape(LEAVES, BCAP) + combined, 0.0).reshape(-1)
    return (potential, new_stress)
```

```python
import functools

import jax
import jax.numpy as jnp
import ml_dtypes
import numpy as np
from jax import lax
from jax.experimental import pallas as pl
from jax.experimental.pallas import tpu as pltpu
from jax.sharding import PartitionSpec as P

PGRID = 12
G = 1728
MAXL = 10
BCAP = 64
Q = 152
LANES = 128
BINS = 864
TILES = 7
ROWS = 16
precise = lax.Precision.HIGHEST
softening = 0.04
surface_reach = 1.25
CELLS = [
    (i, j, k)
    for i in range(6)
    for j in range(6)
    for k in range(6)
    if 0 in (i, j, k) or 5 in (i, j, k)
]
PARTS = ("wide", "narrow")


def transform_table():
    cells = np.array(CELLS)
    bins = np.arange(BINS)
    freq = np.stack([bins // 144, bins // 12 % 12, bins % 12])
    angle = (cells @ freq % PGRID) * (2.0 * np.pi / PGRID)
    table = np.zeros((Q, 2 * TILES * LANES))
    table[:, :BINS] = np.cos(angle)
    table[:, TILES * LANES : TILES * LANES + BINS] = -np.sin(angle)
    table[np.abs(table) < 1e-9] = 0.0
    high = table.astype(ml_dtypes.bfloat16)
    low = (table - high.astype(np.float64)).astype(ml_dtypes.bfloat16)
    return high, low


def sign_rows():
    rows = np.ones((8, Q), np.float32)
    rows[1] = [(-1.0) ** i for i, _, _ in CELLS]
    return rows


def iota(shape, dim):
    return lax.broadcasted_iota(jnp.int32, shape, dim)


def per_leaf(row, count):
    lane, pair_row = iota((count, LANES), 1), iota((count, LANES), 0)
    even = jnp.sum(jnp.where(lane == 2 * pair_row, row, 0.0), axis=1, keepdims=True)
    odd = jnp.sum(jnp.where(lane == 2 * pair_row + 1, row, 0.0), axis=1, keepdims=True)
    return jnp.where(lane < BCAP, even, odd)


def block_transpose(x):
    lane, row = iota(x.shape, 1), iota(x.shape, 0)
    for k in (1, 2, 4):
        row_bit, lane_bit = (row & k) != 0, (lane & k) != 0
        below = pltpu.roll(pltpu.roll(x, 8 - k, 0), k, 1)
        above = pltpu.roll(pltpu.roll(x, k, 0), LANES - k, 1)
        x = jnp.where(row_bit == lane_bit, x, jnp.where(lane_bit, below, above))
    return x


def split(x):
    high = x.astype(jnp.bfloat16)
    return high, (x - high.astype(jnp.float32)).astype(jnp.bfloat16)


def axis_squares(offset, width):
    area = width * width
    planes = [surface_reach * 0.5 * (i - 2.5) / 2.5 for i in range(6)]
    return [(plane - offset) * (plane - offset) * area for plane in planes]


def surface_kernels(offsets, width):
    gx, gy, gz = [axis_squares(offset, width) for offset in offsets]
    gz = [g + softening for g in gz]
    last, gxy = None, None
    for q, (i, j, k) in enumerate(CELLS):
        if last != (i, j):
            last, gxy = (i, j), gx[i] + gy[j]
        yield q, lax.rsqrt(gxy + gz[k])


def upward(offsets, weights, width, up_inverse, checks):
    offsets = [block_transpose(x) for x in offsets]
    weights, width = block_transpose(weights), block_transpose(width)
    for q, kernel in surface_kernels(offsets, width):
        checks[pl.ds(8 * q, 8), :] = kernel * weights
    check = checks[pl.ds(0, Q, stride=8), :]
    for s in range(1, 8):
        check = check + checks[pl.ds(s, Q, stride=8), :]
    density = lax.dot_general(
        check, up_inverse, (((0,), (0,)), ((), ())), precision=precise,
        preferred_element_type=jnp.float32,
    )
    density = density.reshape(2, 8, 8, Q)
    total = density[:, 0]
    for g in range(1, 8):
        total = total + density[:, g]
    return total.reshape(16, Q)


def transform(density, table_high, table_low):
    count = density.shape[0]
    high, low = split(density)
    both = jnp.dot(
        jnp.concatenate([high, low], 0), table_high, preferred_element_type=jnp.float32
    )
    return both[:count] + both[count:] + jnp.dot(high, table_low, preferred_element_type=jnp.float32)


def store_spectra(spectra, target, first_leaf):
    for block in range(spectra.shape[0] // 16):
        for h in range(2):
            rows = spectra[block * 16 + h * 8 : block * 16 + h * 8 + 8]
            for c in range(2):
                for t in range(TILES):
                    column = (c * TILES + t) * LANES
                    start = (first_leaf + block * 16 + h) * ROWS + c * 8 + t
                    target[pl.ds(start, 8, stride=2 * ROWS), :] = rows[:, column : column + LANES]


def pack_kernel(offsets, charges, keys, levels, counts, send_boxes, out):
    leaves = keys.shape[1]
    half = leaves // 2
    out[4 * half :, :] = jnp.zeros((8, LANES), jnp.float32)
    width = jnp.left_shift(jnp.ones_like(levels[...]), MAXL - levels[...]).astype(jnp.float32)
    for a in range(3):
        summed = jnp.zeros_like(keys[...])
        for bit in range(MAXL):
            summed = summed + (jnp.right_shift(keys[...], 3 * bit + a) & 1) * (1 << bit)
        out[4 * half + a : 4 * half + a + 1, :leaves] = summed.astype(jnp.float32) + 0.5 * width
    out[4 * half + 3 : 4 * half + 4, :leaves] = width
    sends = send_boxes.shape[1]
    for row, first in enumerate(range(0, sends, LANES)):
        many = min(LANES, sends - first)
        out[4 * half + 4 + row : 4 * half + 5 + row, :many] = send_boxes[
            :, first : first + many
        ].astype(jnp.float32)
    for r in range(half):
        out[pl.ds(r, 3, stride=half), :] = offsets[:, r * LANES : (r + 1) * LANES]
    lane, pair_row = iota((half, leaves), 1), iota((half, leaves), 0)
    held = counts[...].astype(jnp.float32)
    even = jnp.sum(jnp.where(lane == 2 * pair_row, held, 0.0), axis=1, keepdims=True)
    odd = jnp.sum(jnp.where(lane == 2 * pair_row + 1, held, 0.0), axis=1, keepdims=True)
    slot = iota((half, LANES), 1)
    beads = jnp.where(slot < BCAP, even, odd)
    occupied = (slot & (BCAP - 1)).astype(jnp.float32) < beads
    out[3 * half : 4 * half, :] = jnp.where(occupied, charges[...], 0.0)


def own_kernel(packed, up_inverse, table_high, table_low, signs, pair, spectra, checks):
    half = (packed.shape[0] - 8) // 4
    width = per_leaf(packed[4 * half + 3 : 4 * half + 4, :], half)
    sign = jnp.where(pair[0] == 1, signs[1:2, :], signs[0:1, :])
    densities = []
    for block in range(half // 8):
        rows = [packed[c * half + block * 8 : c * half + block * 8 + 8, :] for c in range(4)]
        densities.append(
            upward(rows[:3], rows[3], width[block * 8 : block * 8 + 8], up_inverse[...], checks)
        )
    density = jnp.concatenate(densities, 0) * sign
    store_spectra(transform(density, table_high[...], table_low[...]), spectra, 0)


def far_kernel(
    sources, kinds, counts, place, gathered, up_inverse, table_high, table_low, signs,
    own_spectra, translations, kept, sent, spectra, kernels, totals, checks, result, sems,
):
    leaves, entries = sources.shape
    half = leaves // 2
    stride = 4 * half + 8
    parts = gathered.shape[0] // stride
    kind_count = translations.shape[0]
    device, pair = place[0], place[1]

    own_copy = pltpu.make_async_copy(
        own_spectra, spectra.at[pl.ds(0, leaves * ROWS), :], sems.at[TILES - 1]
    )
    own_copy.start()
    copies = []
    for t in range(TILES - 1):
        copies.append(pltpu.make_async_copy(
            translations.at[:, :, pl.ds(t * LANES, LANES)],
            kernels.at[pl.ds(0, kind_count), pl.ds(2 * t, 2), :],
            sems.at[t],
        ))
        copies[-1].start()
    tail = BINS - (TILES - 1) * LANES
    kernels[:kind_count, 2 * TILES - 2 : 2 * TILES, :tail] = translations[:, :, BINS - tail :]
    kernels[kind_count] = jnp.zeros((ROWS, LANES), jnp.float32)

    sign = jnp.where(pair == 1, signs[1:2, :], signs[0:1, :])
    lane = iota((8, LANES), 1)

    def arrive(block, carry):
        base = block * 8 * stride
        column = 2 * device
        boxes = gathered[pl.ds(base + 4 * half + 4 + column // LANES, 8, stride=stride), :]
        widths = gathered[pl.ds(base + 4 * half + 3, 8, stride=stride), :]
        picked = []
        for c in range(2):
            box = jnp.sum(
                jnp.where(lane == column % LANES + c, boxes, 0.0), axis=1, keepdims=True
            ).astype(jnp.int32)
            width = jnp.sum(jnp.where(lane == box, widths, 0.0), axis=1, keepdims=True)
            row_of = jnp.broadcast_to(box >> 1, (8, LANES))
            found = [jnp.zeros((8, LANES), jnp.float32)] * 4
            for r in range(half):
                here = row_of == r
                for ch in range(4):
                    rows = gathered[pl.ds(base + ch * half + r, 8, stride=stride), :]
                    found[ch] = jnp.where(here, rows, found[ch])
            aligned = jnp.broadcast_to((box & 1) == c, (8, LANES))
            found = [jnp.where(aligned, x, pltpu.roll(x, BCAP, 1)) for x in found]
            picked.append(found + [jnp.broadcast_to(width, (8, LANES))])
        rows = [jnp.where(lane < BCAP, a, b) for a, b in zip(*picked)]
        density = upward(rows[:3], rows[3], rows[4], up_inverse[...], checks) * sign
        store_spectra(
            transform(density, table_high[...], table_low[...]), spectra, leaves + block * 16
        )
        return carry

    if parts // 8 == 1:
        arrive(0, 0)
    else:
        lax.fori_loop(0, parts // 8, arrive, 0)
    own_copy.wait()
    for copy in copies:
        copy.wait()

    def translate(leaf, carry):
        live = counts[leaf]
        sums = [[None] * 4, [None] * 4]
        for entry in range(entries):
            source = sources[leaf, entry]
            kind = kinds[leaf, entry]
            if entry >= entries // 2:
                kind = jnp.where(entry < live, kind, kind_count)
            k_re = kernels[kind, pl.ds(0, 8, stride=2), :]
            k_im = kernels[kind, pl.ds(1, 8, stride=2), :]
            start = pl.multiple_of(source * ROWS, ROWS)
            s_re = spectra[pl.ds(start, 8), :]
            s_im = spectra[pl.ds(start + 8, 8), :]
            terms = (k_re * s_re, k_im * s_im, k_re * s_im, k_im * s_re)
            side = sums[entry % 2]
            for n, term in enumerate(terms):
                side[n] = term if side[n] is None else side[n] + term
        rr, ii, ri, ir = [a + b for a, b in zip(*sums)]
        start = pl.multiple_of(leaf * ROWS, ROWS)
        totals[pl.ds(start, 8), :] = rr - ii
        totals[pl.ds(start + 8, 8), :] = ri + ir
        return carry

    lax.fori_loop(0, leaves, translate, 0)

    wide_lane = iota((leaves, LANES), 1)
    columns = []
    for c in range(2):
        for t in range(TILES):
            rows = totals[pl.ds(c * 8 + t, leaves, stride=ROWS), :]
            if t == TILES - 1:
                rows = jnp.where(wide_lane < BINS - t * LANES, rows, 0.0)
            columns.append(rows)
    high, low = split(jnp.concatenate(columns, 1))
    across = (((1,), (1,)), ((), ()))
    both = lax.dot_general(
        jnp.concatenate([high, low], 0), table_high[...], across,
        preferred_element_type=jnp.float32,
    )
    check = both[:leaves] + both[leaves:] + lax.dot_general(
        high, table_low[...], across, preferred_element_type=jnp.float32
    )
    result[...] = check * (sign * (1.0 / G))
    kept[...] = result[pl.ds(pl.multiple_of(pair * half, 8), half), :]
    sent[...] = result[pl.ds(pl.multiple_of((1 - pair) * half, 8), half), :]


def near_kernel(near_source, place, gathered, out, table, targets, sums, own):
    leaves, entries = near_source.shape
    half = leaves // 2
    stride = 4 * half + 8
    parts = gathered.shape[0] // stride
    device, pair = place[0], place[1]
    lane = iota((half, LANES), 1)
    low = lane < BCAP
    for n in range(3):
        there = device - 1 + n
        live = jnp.where((there >= 0) & (there < parts), 1.0, 0.0)
        base = pl.multiple_of(jnp.clip(there, 0, parts - 1) * stride, 8)
        shape = gathered[pl.ds(base + 4 * half, 8), :]
        width = per_leaf(shape[3:4], half)
        for ch in range(4):
            rows = gathered[pl.ds(base + ch * half, half), :]
            if ch < 3:
                rows = per_leaf(shape[ch : ch + 1], half) + width * rows
                if n == 1:
                    own[ch] = rows
            else:
                rows = rows * live
            turned = pltpu.roll(rows, BCAP, 1)
            first = n * leaves * 8 + ch
            table[pl.ds(first, half, stride=16), :] = jnp.where(low, rows, turned)
            table[pl.ds(first + 8, half, stride=16), :] = jnp.where(low, turned, rows)
    for ch in range(3):
        mine = own[ch, pl.ds(pl.multiple_of(pair * (half // 2), 8), half // 2), :]
        flipped = mine.T
        for r in range(half // 2):
            for h in range(2):
                start = ((2 * r + h) * 3 + ch) * BCAP
                targets[pl.ds(start, BCAP), :] = jnp.broadcast_to(
                    flipped[h * BCAP : (h + 1) * BCAP, r : r + 1], (BCAP, LANES)
                )
    low = iota((8, LANES), 1) < BCAP

    def one_leaf(t, carry):
        leaf = pair * half + t
        start = pl.multiple_of(t * 3 * BCAP, 8)
        tx, ty, tz = [targets[pl.ds(start + ch * BCAP, BCAP), :] for ch in range(3)]
        total = jnp.zeros((BCAP, LANES), jnp.float32)
        for n in range(entries // 2):
            left = pl.multiple_of(near_source[leaf, 2 * n] * 8, 8)
            right = pl.multiple_of(near_source[leaf, 2 * n + 1] * 8, 8)
            both = jnp.where(low, table[pl.ds(left, 8), :], table[pl.ds(right, 8), :])
            gx, gy, gz = tx - both[0:1], ty - both[1:2], tz - both[2:3]
            squared = gx * gx + gy * gy + (gz * gz + softening)
            total = total + lax.rsqrt(squared) * both[3:4]
        sums[pl.ds(pl.multiple_of(t * BCAP, 8), BCAP), :] = total
        return carry

    lax.fori_loop(0, half, one_leaf, 0)
    for r in range(half // 2):
        block = sums[r * LANES : (r + 1) * LANES, :].T
        out[r : r + 1, :] = jnp.sum(block, axis=0, keepdims=True)


def final_kernel(
    place, packed, kept, received, down_inverse, near, counts, decay_rate, stress,
    potential, new_stress, densities,
):
    half = (packed.shape[0] - 8) // 4
    rows = half // 2
    start = pl.multiple_of(place[1] * rows, 8)
    lane = iota((rows, LANES), 1)
    row = iota((rows, LANES), 0)
    leaf_of = 2 * (iota((half, LANES), 1) & 7) + (iota((half, LANES), 1) >> 6)
    spread = jnp.where(iota((half, LANES), 0) == leaf_of, 1.0, 0.0)
    check = kept[...] + received[...]
    density = jnp.dot(
        check, down_inverse[...], precision=precise, preferred_element_type=jnp.float32
    )
    densities[...] = lax.dot_general(
        density, spread, (((0,), (0,)), ((), ())), precision=precise,
        preferred_element_type=jnp.float32,
    )

    def mine(values):
        even = jnp.sum(jnp.where(lane == 2 * row, values, 0.0), axis=1, keepdims=True)
        odd = jnp.sum(jnp.where(lane == 2 * row + 1, values, 0.0), axis=1, keepdims=True)
        return jnp.where(lane < BCAP, even, odd)

    first = place[1] * half
    def widen(values, shift):
        line = values
        even = jnp.sum(jnp.where(lane == 2 * row + shift, line, 0.0), axis=1, keepdims=True)
        odd = jnp.sum(jnp.where(lane == 2 * row + 1 + shift, line, 0.0), axis=1, keepdims=True)
        return jnp.where(lane < BCAP, even, odd)

    width = block_transpose(widen(packed[4 * half + 3 : 4 * half + 4, :], first))
    offsets = [
        block_transpose(packed[pl.ds(pl.multiple_of(c * half + start, 8), rows), :])
        for c in range(3)
    ]
    total = None
    for q, kernel in surface_kernels(offsets, width):
        term = kernel * densities[q : q + 1, :]
        total = term if total is None else total + term
    combined = block_transpose(total) + near[...]
    beads = widen(counts[...], first)
    occupied = (lane & (BCAP - 1)).astype(jnp.float32) < beads
    decay = widen(decay_rate[...], 0)
    potential[...] = jnp.where(occupied, combined, 0.0)
    new_stress[...] = jnp.where(occupied, decay * stress[...] + combined, 0.0)


VMEM = pl.BlockSpec(memory_space=pltpu.VMEM)
SMEM = pl.BlockSpec(memory_space=pltpu.SMEM)
ANY = pl.BlockSpec(memory_space=pl.ANY)
LIMIT = 40 * 1024 * 1024


def call(kernel, outs, in_specs, scratch=(), flops=0, bytes_accessed=0):
    return pl.pallas_call(
        kernel,
        out_shape=outs,
        in_specs=in_specs,
        out_specs=jax.tree.map(lambda _: VMEM, outs),
        scratch_shapes=list(scratch),
        compiler_params=pltpu.CompilerParams(vmem_limit_bytes=LIMIT),
        cost_estimate=pl.CostEstimate(
            flops=flops, bytes_accessed=bytes_accessed, transcendentals=0
        ),
    )


def body(
    offsets,
    charges,
    stress,
    decay_rate,
    morton_keys,
    levels,
    bead_counts,
    send_boxes,
    m2l_source,
    m2l_type,
    m2l_count,
    near_source,
    up_inverse,
    down_inverse,
    translations,
):
    f32 = jnp.float32
    leaves = morton_keys.shape[0]
    half = leaves // 2
    parts = lax.axis_size("wide") * lax.axis_size("narrow")
    high, low = [jnp.asarray(x) for x in transform_table()]
    signs = jnp.asarray(sign_rows())
    pair = lax.axis_index("pair")
    device = lax.axis_index("wide") * lax.axis_size("narrow") + lax.axis_index("narrow")
    place = jnp.stack([device, pair]).astype(jnp.int32)
    rows = 4 * half + 8

    packed = call(
        pack_kernel, jax.ShapeDtypeStruct((rows, LANES), f32), [VMEM] * 6
    )(
        offsets, charges.reshape(half, LANES), morton_keys.reshape(1, leaves),
        levels.reshape(1, leaves), bead_counts.reshape(1, leaves), send_boxes,
    )
    gathered = lax.all_gather(packed, PARTS, axis=0, tiled=True)
    own_spectra = call(
        own_kernel,
        jax.ShapeDtypeStruct((leaves * ROWS, LANES), f32),
        [VMEM] * 5 + [SMEM],
        [pltpu.VMEM((Q * 8, LANES), f32)],
        flops=10**9,
        bytes_accessed=4 * 10**6,
    )(packed, up_inverse, high, low, signs, pair.reshape(1))

    kept, sent = call(
        far_kernel,
        [jax.ShapeDtypeStruct((half, Q), f32)] * 2,
        [SMEM] * 4 + [VMEM] * 5 + [ANY, VMEM],
        [
            pltpu.VMEM(((leaves + 2 * parts) * ROWS, LANES), f32),
            pltpu.VMEM((translations.shape[0] + 1, ROWS, LANES), f32),
            pltpu.VMEM((leaves * ROWS, LANES), f32),
            pltpu.VMEM((Q * 8, LANES), f32),
            pltpu.VMEM((leaves, Q), f32),
            pltpu.SemaphoreType.DMA((TILES,)),
        ],
    )(
        m2l_source, m2l_type, m2l_count, place, gathered, up_inverse, high, low, signs,
        own_spectra, translations,
    )
    received = lax.ppermute(sent, "pair", [(0, 1), (1, 0)])
    near = call(
        near_kernel,
        jax.ShapeDtypeStruct((half // 2, LANES), f32),
        [SMEM] * 2 + [VMEM],
        [
            pltpu.VMEM((3 * leaves * 8, LANES), f32),
            pltpu.VMEM((half * 3 * BCAP, LANES), f32),
            pltpu.VMEM((half * BCAP, LANES), f32),
            pltpu.VMEM((3, half, LANES), f32),
        ],
        flops=10**9,
        bytes_accessed=4 * 10**6,
    )(near_source, place, gathered)

    def lanes(values):
        return jnp.zeros((1, LANES), f32).at[0, : values.shape[0]].set(values.astype(f32))

    out = jax.ShapeDtypeStruct((half // 2, LANES), f32)
    potential, new_stress = call(
        final_kernel,
        [out, out],
        [SMEM] + [VMEM] * 8,
        [pltpu.VMEM((Q, LANES), f32)],
    )(
        place, packed, kept, received, down_inverse, near, lanes(bead_counts),
        lanes(decay_rate), stress.reshape(half // 2, LANES),
    )
    return potential.reshape(-1), new_stress.reshape(-1)


def solution(mesh):
    return jax.shard_map(
        body,
        mesh=mesh,
        in_specs=(
            P(None, ("groups", "wide", "narrow")),
            P(("groups", "wide", "narrow")),
            P(("groups", "wide", "narrow", "pair")),
            P(("groups", "wide", "narrow", "pair")),
            P(("groups", "wide", "narrow")),
            P(("groups", "wide", "narrow")),
            P(("groups", "wide", "narrow")),
            P(("groups", "wide", "narrow"), None),
            P(("groups", "wide", "narrow"), None),
            P(("groups", "wide", "narrow"), None),
            P(("groups", "wide", "narrow")),
            P(("groups", "wide", "narrow"), None),
            P(),
            P(),
            P(None, None, "pair"),
        ),
        out_specs=(
            P(("groups", "wide", "narrow", "pair")),
            P(("groups", "wide", "narrow", "pair")),
        ),
        check_vma=False,
    )
```

```python
import functools

import jax
import jax.numpy as jnp
import ml_dtypes
import numpy as np
from jax import lax
from jax.experimental import pallas as pl
from jax.experimental.pallas import tpu as pltpu
from jax.sharding import PartitionSpec as P

PGRID = 12
G = 1728
MAXL = 10
BCAP = 64
Q = 152
LANES = 128
BINS = 864
TILES = 7
ROWS = 16
precise = lax.Precision.HIGHEST
softening = 0.04
surface_reach = 1.25
CELLS = [
    (i, j, k)
    for i in range(6)
    for j in range(6)
    for k in range(6)
    if 0 in (i, j, k) or 5 in (i, j, k)
]
PARTS = ("wide", "narrow")


def transform_table():
    cells = np.array(CELLS)
    bins = np.arange(BINS)
    freq = np.stack([bins // 144, bins // 12 % 12, bins % 12])
    angle = (cells @ freq % PGRID) * (2.0 * np.pi / PGRID)
    table = np.zeros((Q, 2 * TILES * LANES))
    table[:, :BINS] = np.cos(angle)
    table[:, TILES * LANES : TILES * LANES + BINS] = -np.sin(angle)
    table[np.abs(table) < 1e-9] = 0.0
    high = table.astype(ml_dtypes.bfloat16)
    low = (table - high.astype(np.float64)).astype(ml_dtypes.bfloat16)
    return high, low


def sign_rows():
    rows = np.ones((8, Q), np.float32)
    rows[1] = [(-1.0) ** i for i, _, _ in CELLS]
    return rows


def iota(shape, dim):
    return lax.broadcasted_iota(jnp.int32, shape, dim)


def per_leaf(values, count, first=0):
    shape = (count, values.shape[1])
    leaf, lane = first + 2 * iota(shape, 0), iota(shape, 1)
    even = jnp.sum(jnp.where(lane == leaf, values, 0.0), axis=1, keepdims=True)
    odd = jnp.sum(jnp.where(lane == leaf + 1, values, 0.0), axis=1, keepdims=True)
    return jnp.where(iota((count, LANES), 1) < BCAP, even, odd)


def block_transpose(x):
    lane, row = iota(x.shape, 1), iota(x.shape, 0)
    for k in (1, 2, 4):
        row_bit, lane_bit = (row & k) != 0, (lane & k) != 0
        below = pltpu.roll(pltpu.roll(x, 8 - k, 0), k, 1)
        above = pltpu.roll(pltpu.roll(x, k, 0), LANES - k, 1)
        x = jnp.where(row_bit == lane_bit, x, jnp.where(lane_bit, below, above))
    return x


def split(x):
    high = x.astype(jnp.bfloat16)
    return high, (x - high.astype(jnp.float32)).astype(jnp.bfloat16)


def axis_squares(offset, width):
    area = width * width
    planes = [surface_reach * 0.5 * (i - 2.5) / 2.5 for i in range(6)]
    return [(plane - offset) * (plane - offset) * area for plane in planes]


def surface_kernels(offsets, width):
    gx, gy, gz = [axis_squares(offset, width) for offset in offsets]
    gz = [g + softening for g in gz]
    last, gxy = None, None
    for q, (i, j, k) in enumerate(CELLS):
        if last != (i, j):
            last, gxy = (i, j), gx[i] + gy[j]
        yield q, lax.rsqrt(gxy + gz[k])


def upward(offsets, weights, width, up_inverse, checks):
    offsets = [block_transpose(x) for x in offsets]
    weights, width = block_transpose(weights), block_transpose(width)
    for q, kernel in surface_kernels(offsets, width):
        checks[pl.ds(8 * q, 8), :] = kernel * weights
    check = checks[pl.ds(0, Q, stride=8), :]
    for s in range(1, 8):
        check = check + checks[pl.ds(s, Q, stride=8), :]
    density = lax.dot_general(
        check, up_inverse, (((0,), (0,)), ((), ())), precision=precise,
        preferred_element_type=jnp.float32,
    )
    density = density.reshape(2, 8, 8, Q)
    total = density[:, 0]
    for g in range(1, 8):
        total = total + density[:, g]
    return total.reshape(16, Q)


def transform(density, table_high, table_low):
    count = density.shape[0]
    high, low = split(density)
    both = jnp.dot(
        jnp.concatenate([high, low], 0), table_high, preferred_element_type=jnp.float32
    )
    return both[:count] + both[count:] + jnp.dot(high, table_low, preferred_element_type=jnp.float32)


def store_spectra(spectra, target, first_leaf):
    for block in range(spectra.shape[0] // 16):
        for h in range(2):
            rows = spectra[block * 16 + h * 8 : block * 16 + h * 8 + 8]
            for c in range(2):
                for t in range(TILES):
                    column = (c * TILES + t) * LANES
                    start = (first_leaf + block * 16 + h) * ROWS + c * 8 + t
                    target[pl.ds(start, 8, stride=2 * ROWS), :] = rows[:, column : column + LANES]


def pack_kernel(offsets, charges, keys, levels, counts, send_boxes, out, blocks):
    leaves = keys.shape[1]
    half = leaves // 2
    out[4 * half :, :] = jnp.zeros((8, LANES), jnp.float32)
    width = jnp.left_shift(jnp.ones_like(levels[...]), MAXL - levels[...]).astype(jnp.float32)
    for a in range(3):
        summed = jnp.zeros_like(keys[...])
        for bit in range(MAXL):
            summed = summed + (jnp.right_shift(keys[...], 3 * bit + a) & 1) * (1 << bit)
        out[4 * half + a : 4 * half + a + 1, :leaves] = summed.astype(jnp.float32) + 0.5 * width
    out[4 * half + 3 : 4 * half + 4, :leaves] = width
    for r in range(half):
        out[pl.ds(r, 3, stride=half), :] = offsets[:, r * LANES : (r + 1) * LANES]
    beads = per_leaf(counts[...].astype(jnp.float32), half)
    slot = iota((half, LANES), 1) & (BCAP - 1)
    out[3 * half : 4 * half, :] = jnp.where(slot.astype(jnp.float32) < beads, charges[...], 0.0)

    sends = send_boxes.shape[1]
    lane = iota((8, LANES), 1)
    for block in range(sends // 16):
        picked = []
        for c in range(2):
            column = block * 16 + 2 * iota((8, sends), 0) + c
            box = jnp.sum(
                jnp.where(iota((8, sends), 1) == column, send_boxes[...].astype(jnp.float32), 0.0),
                axis=1, keepdims=True,
            ).astype(jnp.int32)
            width_here = jnp.sum(
                jnp.where(iota((8, leaves), 1) == box, width, 0.0), axis=1, keepdims=True
            )
            row_of = jnp.broadcast_to(box >> 1, (8, LANES))
            found = [jnp.zeros((8, LANES), jnp.float32)] * 4
            for r in range(half):
                here = row_of == r
                for ch in range(4):
                    found[ch] = jnp.where(here, out[ch * half + r : ch * half + r + 1, :], found[ch])
            aligned = jnp.broadcast_to((box & 1) == c, (8, LANES))
            found = [jnp.where(aligned, x, pltpu.roll(x, BCAP, 1)) for x in found]
            picked.append(found + [jnp.broadcast_to(width_here, (8, LANES))])
        for ch in range(5):
            blocks[pl.ds(block * 64 + ch, 8, stride=8), :] = jnp.where(
                lane < BCAP, picked[0][ch], picked[1][ch]
            )
        for ch in range(5, 8):
            blocks[pl.ds(block * 64 + ch, 8, stride=8), :] = jnp.zeros((8, LANES), jnp.float32)


def own_kernel(
    packed, up_inverse, table_high, table_low, signs, pair, translations,
    spectra, kernels, checks, sems,
):
    half = (packed.shape[0] - 8) // 4
    kind_count = translations.shape[0]
    copies = []
    for t in range(TILES - 1):
        copies.append(pltpu.make_async_copy(
            translations.at[:, :, pl.ds(t * LANES, LANES)],
            kernels.at[pl.ds(0, kind_count), pl.ds(2 * t, 2), :],
            sems.at[t],
        ))
        copies[-1].start()
    tail = BINS - (TILES - 1) * LANES
    kernels[:kind_count, 2 * TILES - 2 : 2 * TILES, :tail] = translations[:, :, BINS - tail :]
    kernels[kind_count] = jnp.zeros((ROWS, LANES), jnp.float32)
    width = per_leaf(packed[4 * half + 3 : 4 * half + 4, :], half)
    sign = jnp.where(pair[0] == 1, signs[1:2, :], signs[0:1, :])
    densities = []
    for block in range(half // 8):
        rows = [packed[c * half + block * 8 : c * half + block * 8 + 8, :] for c in range(4)]
        densities.append(
            upward(rows[:3], rows[3], width[block * 8 : block * 8 + 8], up_inverse[...], checks)
        )
    density = jnp.concatenate(densities, 0) * sign
    store_spectra(transform(density, table_high[...], table_low[...]), spectra, 0)
    for copy in copies:
        copy.wait()


def far_kernel(
    sources, kinds, counts, pair_ref, arrived, up_inverse, table_high, table_low, signs,
    kernels, own_spectra, kept, sent, spectra, totals, checks, result, sem,
):
    leaves, entries = sources.shape
    half = leaves // 2
    blocks = arrived.shape[0] // 64
    kind_count = kernels.shape[0] - 1
    pair = pair_ref[0]

    own_copy = pltpu.make_async_copy(own_spectra, spectra.at[pl.ds(0, leaves * ROWS), :], sem)
    own_copy.start()
    sign = jnp.where(pair == 1, signs[1:2, :], signs[0:1, :])

    def arrive(block, carry):
        rows = [arrived[pl.ds(block * 64 + ch, 8, stride=8), :] for ch in range(5)]
        density = upward(rows[:3], rows[3], rows[4], up_inverse[...], checks) * sign
        store_spectra(
            transform(density, table_high[...], table_low[...]), spectra, leaves + block * 16
        )
        return carry

    if blocks == 1:
        arrive(0, 0)
    else:
        lax.fori_loop(0, blocks, arrive, 0)
    own_copy.wait()

    def translate(leaf, carry):
        live = counts[leaf]
        sums = [[None] * 4, [None] * 4]
        for entry in range(entries):
            source = sources[leaf, entry]
            kind = kinds[leaf, entry]
            if entry >= entries // 2:
                kind = jnp.where(entry < live, kind, kind_count)
            k_re = kernels[kind, pl.ds(0, 8, stride=2), :]
            k_im = kernels[kind, pl.ds(1, 8, stride=2), :]
            start = pl.multiple_of(source * ROWS, ROWS)
            s_re = spectra[pl.ds(start, 8), :]
            s_im = spectra[pl.ds(start + 8, 8), :]
            terms = (k_re * s_re, k_im * s_im, k_re * s_im, k_im * s_re)
            side = sums[entry % 2]
            for n, term in enumerate(terms):
                side[n] = term if side[n] is None else side[n] + term
        rr, ii, ri, ir = [a + b for a, b in zip(*sums)]
        start = pl.multiple_of(leaf * ROWS, ROWS)
        totals[pl.ds(start, 8), :] = rr - ii
        totals[pl.ds(start + 8, 8), :] = ri + ir
        return carry

    lax.fori_loop(0, leaves, translate, 0)

    wide_lane = iota((leaves, LANES), 1)
    columns = []
    for c in range(2):
        for t in range(TILES):
            rows = totals[pl.ds(c * 8 + t, leaves, stride=ROWS), :]
            if t == TILES - 1:
                rows = jnp.where(wide_lane < BINS - t * LANES, rows, 0.0)
            columns.append(rows)
    high, low = split(jnp.concatenate(columns, 1))
    across = (((1,), (1,)), ((), ()))
    both = lax.dot_general(
        jnp.concatenate([high, low], 0), table_high[...], across,
        preferred_element_type=jnp.float32,
    )
    check = both[:leaves] + both[leaves:] + lax.dot_general(
        high, table_low[...], across, preferred_element_type=jnp.float32
    )
    result[...] = check * (sign * (1.0 / G))
    kept[...] = result[pl.ds(pl.multiple_of(pair * half, 8), half), :]
    sent[...] = result[pl.ds(pl.multiple_of((1 - pair) * half, 8), half), :]


def near_kernel(near_source, pair_ref, before, packed, after, out, table, targets, sums, own):
    leaves, entries = near_source.shape
    half = leaves // 2
    pair = pair_ref[0]
    lane = iota((half, LANES), 1)
    low = lane < BCAP
    for n, rows_of in enumerate((before, packed, after)):
        shape = rows_of[4 * half :, :]
        width = per_leaf(shape[3:4], half)
        for ch in range(4):
            rows = rows_of[ch * half : (ch + 1) * half, :]
            if ch < 3:
                rows = per_leaf(shape[ch : ch + 1], half) + width * rows
                if n == 1:
                    own[ch] = rows
            turned = pltpu.roll(rows, BCAP, 1)
            first = n * leaves * 8 + ch
            table[pl.ds(first, half, stride=16), :] = jnp.where(low, rows, turned)
            table[pl.ds(first + 8, half, stride=16), :] = jnp.where(low, turned, rows)
    for ch in range(3):
        mine = own[ch, pl.ds(pl.multiple_of(pair * (half // 2), 8), half // 2), :]
        flipped = mine.T
        for r in range(half // 2):
            for h in range(2):
                start = ((2 * r + h) * 3 + ch) * BCAP
                targets[pl.ds(start, BCAP), :] = jnp.broadcast_to(
                    flipped[h * BCAP : (h + 1) * BCAP, r : r + 1], (BCAP, LANES)
                )
    low = iota((8, LANES), 1) < BCAP

    def one_leaf(t, carry):
        leaf = pair * half + t
        start = pl.multiple_of(t * 3 * BCAP, 8)
        tx, ty, tz = [targets[pl.ds(start + ch * BCAP, BCAP), :] for ch in range(3)]
        total = jnp.zeros((BCAP, LANES), jnp.float32)
        for n in range(entries // 2):
            left = pl.multiple_of(near_source[leaf, 2 * n] * 8, 8)
            right = pl.multiple_of(near_source[leaf, 2 * n + 1] * 8, 8)
            both = jnp.where(low, table[pl.ds(left, 8), :], table[pl.ds(right, 8), :])
            gx, gy, gz = tx - both[0:1], ty - both[1:2], tz - both[2:3]
            squared = gx * gx + gy * gy + (gz * gz + softening)
            total = total + lax.rsqrt(squared) * both[3:4]
        sums[pl.ds(pl.multiple_of(t * BCAP, 8), BCAP), :] = total
        return carry

    lax.fori_loop(0, half, one_leaf, 0)
    for r in range(half // 2):
        block = sums[r * LANES : (r + 1) * LANES, :].T
        out[r : r + 1, :] = jnp.sum(block, axis=0, keepdims=True)


def final_kernel(
    pair_ref, packed, kept, received, down_inverse, near, counts, decay_rate, stress,
    potential, new_stress, densities,
):
    half = (packed.shape[0] - 8) // 4
    rows = half // 2
    start = pl.multiple_of(pair_ref[0] * rows, 8)
    first = pair_ref[0] * half
    leaf_of = 2 * (iota((half, LANES), 1) & 7) + (iota((half, LANES), 1) >> 6)
    spread = jnp.where(iota((half, LANES), 0) == leaf_of, 1.0, 0.0)
    check = kept[...] + received[...]
    density = jnp.dot(
        check, down_inverse[...], precision=precise, preferred_element_type=jnp.float32
    )
    densities[...] = lax.dot_general(
        density, spread, (((0,), (0,)), ((), ())), precision=precise,
        preferred_element_type=jnp.float32,
    )
    width = block_transpose(per_leaf(packed[4 * half + 3 : 4 * half + 4, :], rows, first))
    offsets = [
        block_transpose(packed[pl.ds(pl.multiple_of(c * half + start, 8), rows), :])
        for c in range(3)
    ]
    total = None
    for q, kernel in surface_kernels(offsets, width):
        term = kernel * densities[q : q + 1, :]
        total = term if total is None else total + term
    combined = block_transpose(total) + near[...]
    beads = per_leaf(counts[...].astype(jnp.float32), rows, first)
    slot = iota((rows, LANES), 1) & (BCAP - 1)
    occupied = slot.astype(jnp.float32) < beads
    decay = per_leaf(decay_rate[...], rows)
    potential[...] = jnp.where(occupied, combined, 0.0)
    new_stress[...] = jnp.where(occupied, decay * stress[...] + combined, 0.0)


VMEM = pl.BlockSpec(memory_space=pltpu.VMEM)
SMEM = pl.BlockSpec(memory_space=pltpu.SMEM)
ANY = pl.BlockSpec(memory_space=pl.ANY)
MIB = 1024 * 1024


def call(kernel, outs, in_specs, scratch=(), limit=40, flops=0, bytes_accessed=0):
    return pl.pallas_call(
        kernel,
        out_shape=outs,
        in_specs=in_specs,
        out_specs=jax.tree.map(lambda _: VMEM, outs),
        scratch_shapes=list(scratch),
        compiler_params=pltpu.CompilerParams(vmem_limit_bytes=limit * MIB),
        cost_estimate=pl.CostEstimate(
            flops=flops, bytes_accessed=bytes_accessed, transcendentals=0
        ),
    )


def body(
    offsets,
    charges,
    stress,
    decay_rate,
    morton_keys,
    levels,
    bead_counts,
    send_boxes,
    m2l_source,
    m2l_type,
    m2l_count,
    near_source,
    up_inverse,
    down_inverse,
    translations,
):
    f32 = jnp.float32
    leaves = morton_keys.shape[0]
    half = leaves // 2
    parts = lax.axis_size("wide") * lax.axis_size("narrow")
    high, low = [jnp.asarray(x) for x in transform_table()]
    signs = jnp.asarray(sign_rows())
    pair = lax.axis_index("pair").reshape(1)
    kind_count = translations.shape[0]

    packed, blocks = call(
        pack_kernel,
        [
            jax.ShapeDtypeStruct((4 * half + 8, LANES), f32),
            jax.ShapeDtypeStruct((8 * parts, LANES), f32),
        ],
        [VMEM] * 6,
        limit=62,
    )(
        offsets, charges.reshape(half, LANES), morton_keys.reshape(1, leaves),
        levels.reshape(1, leaves), bead_counts.reshape(1, leaves), send_boxes,
    )
    arrived = lax.all_to_all(
        blocks.reshape(parts, 8, LANES), PARTS, split_axis=0, concat_axis=0, tiled=True
    ).reshape(8 * parts, LANES)
    up = [(i, i + 1) for i in range(parts - 1)]
    before = lax.ppermute(packed, PARTS, up)
    after = lax.ppermute(packed, PARTS, [(j, i) for i, j in up])
    own_spectra, kernels = call(
        own_kernel,
        [
            jax.ShapeDtypeStruct((leaves * ROWS, LANES), f32),
            jax.ShapeDtypeStruct((kind_count + 1, ROWS, LANES), f32),
        ],
        [VMEM] * 5 + [SMEM, VMEM],
        [pltpu.VMEM((Q * 8, LANES), f32), pltpu.SemaphoreType.DMA((TILES - 1,))],
        flops=10**9,
        bytes_accessed=4 * 10**6,
    )(packed, up_inverse, high, low, signs, pair, translations)

    kept, sent = call(
        far_kernel,
        [jax.ShapeDtypeStruct((half, Q), f32)] * 2,
        [SMEM] * 4 + [VMEM] * 6 + [ANY],
        [
            pltpu.VMEM(((leaves + 2 * parts) * ROWS, LANES), f32),
            pltpu.VMEM((leaves * ROWS, LANES), f32),
            pltpu.VMEM((Q * 8, LANES), f32),
            pltpu.VMEM((leaves, Q), f32),
            pltpu.SemaphoreType.DMA,
        ],
    )(
        m2l_source, m2l_type, m2l_count, pair, arrived, up_inverse, high, low, signs,
        kernels, own_spectra,
    )
    received = lax.ppermute(sent, "pair", [(0, 1), (1, 0)])
    near = call(
        near_kernel,
        jax.ShapeDtypeStruct((half // 2, LANES), f32),
        [SMEM] * 2 + [VMEM] * 3,
        [
            pltpu.VMEM((3 * leaves * 8, LANES), f32),
            pltpu.VMEM((half * 3 * BCAP, LANES), f32),
            pltpu.VMEM((half * BCAP, LANES), f32),
            pltpu.VMEM((3, half, LANES), f32),
        ],
        flops=10**9,
        bytes_accessed=4 * 10**6,
    )(near_source, pair, before, packed, after)

    out = jax.ShapeDtypeStruct((half // 2, LANES), f32)
    potential, new_stress = call(
        final_kernel,
        [out, out],
        [SMEM] + [VMEM] * 8,
        [pltpu.VMEM((Q, LANES), f32)],
    )(
        pair, packed, kept, received, down_inverse, near, bead_counts.reshape(1, leaves),
        decay_rate.reshape(1, half), stress.reshape(half // 2, LANES),
    )
    return potential.reshape(-1), new_stress.reshape(-1)


def solution(mesh):
    return jax.shard_map(
        body,
        mesh=mesh,
        in_specs=(
            P(None, ("groups", "wide", "narrow")),
            P(("groups", "wide", "narrow")),
            P(("groups", "wide", "narrow", "pair")),
            P(("groups", "wide", "narrow", "pair")),
            P(("groups", "wide", "narrow")),
            P(("groups", "wide", "narrow")),
            P(("groups", "wide", "narrow")),
            P(("groups", "wide", "narrow"), None),
            P(("groups", "wide", "narrow"), None),
            P(("groups", "wide", "narrow"), None),
            P(("groups", "wide", "narrow")),
            P(("groups", "wide", "narrow"), None),
            P(),
            P(),
            P(None, None, "pair"),
        ),
        out_specs=(
            P(("groups", "wide", "narrow", "pair")),
            P(("groups", "wide", "narrow", "pair")),
        ),
        check_vma=False,
    )
```

```python
import functools

import jax
import jax.numpy as jnp
import ml_dtypes
import numpy as np
from jax import lax
from jax.experimental import pallas as pl
from jax.experimental.pallas import tpu as pltpu
from jax.sharding import PartitionSpec as P

PGRID = 12
G = 1728
MAXL = 10
BCAP = 64
Q = 152
QPAD = 160
LANES = 128
BINS = 864
TILES = 7
ROWS = 16
precise = lax.Precision.HIGHEST
softening = 0.04
surface_reach = 1.25
CELLS = [
    (i, j, k)
    for i in range(6)
    for j in range(6)
    for k in range(6)
    if 0 in (i, j, k) or 5 in (i, j, k)
]
PARTS = ("wide", "narrow")


def transform_table():
    cells = np.array(CELLS)
    bins = np.arange(BINS)
    freq = np.stack([bins // 144, bins // 12 % 12, bins % 12])
    angle = (cells @ freq % PGRID) * (2.0 * np.pi / PGRID)
    table = np.zeros((QPAD, 2 * TILES * LANES))
    table[:Q, :BINS] = np.cos(angle)
    table[:Q, TILES * LANES : TILES * LANES + BINS] = -np.sin(angle)
    table[np.abs(table) < 1e-9] = 0.0
    high = table.astype(ml_dtypes.bfloat16)
    low = (table - high.astype(np.float64)).astype(ml_dtypes.bfloat16)
    return high, low


def sign_rows():
    rows = np.zeros((8, QPAD), np.float32)
    rows[0, :Q] = 1.0
    rows[1, :Q] = [(-1.0) ** i for i, _, _ in CELLS]
    return rows


def iota(shape, dim):
    return lax.broadcasted_iota(jnp.int32, shape, dim)


def per_leaf(values, count, first=0):
    shape = (count, values.shape[1])
    leaf, lane = first + 2 * iota(shape, 0), iota(shape, 1)
    even = jnp.sum(jnp.where(lane == leaf, values, 0.0), axis=1, keepdims=True)
    odd = jnp.sum(jnp.where(lane == leaf + 1, values, 0.0), axis=1, keepdims=True)
    return jnp.where(iota((count, LANES), 1) < BCAP, even, odd)


def block_transpose(x):
    lane, row = iota(x.shape, 1), iota(x.shape, 0)
    for k in (1, 2, 4):
        row_bit, lane_bit = (row & k) != 0, (lane & k) != 0
        below = pltpu.roll(pltpu.roll(x, 8 - k, 0), k, 1)
        above = pltpu.roll(pltpu.roll(x, k, 0), LANES - k, 1)
        x = jnp.where(row_bit == lane_bit, x, jnp.where(lane_bit, below, above))
    return x


def split(x):
    high = x.astype(jnp.bfloat16)
    return high, (x - high.astype(jnp.float32)).astype(jnp.bfloat16)


def axis_squares(offset, width):
    area = width * width
    planes = [surface_reach * 0.5 * (i - 2.5) / 2.5 for i in range(6)]
    return [(plane - offset) * (plane - offset) * area for plane in planes]


def surface_kernels(offsets, width):
    gx, gy, gz = [axis_squares(offset, width) for offset in offsets]
    gz = [g + softening for g in gz]
    last, gxy = None, None
    for q, (i, j, k) in enumerate(CELLS):
        if last != (i, j):
            last, gxy = (i, j), gx[i] + gy[j]
        yield q, lax.rsqrt(gxy + gz[k])


def upward(offsets, weights, width, up_inverse, checks):
    offsets = [block_transpose(x) for x in offsets]
    weights, width = block_transpose(weights), block_transpose(width)
    for q, kernel in surface_kernels(offsets, width):
        checks[pl.ds(8 * q, 8), :] = kernel * weights
    check = checks[pl.ds(0, Q, stride=8), :]
    for s in range(1, 8):
        check = check + checks[pl.ds(s, Q, stride=8), :]
    density = lax.dot_general(
        check, up_inverse, (((0,), (0,)), ((), ())), precision=precise,
        preferred_element_type=jnp.float32,
    )
    density = density.reshape(2, 8, 8, Q)
    total = density[:, 0]
    for g in range(1, 8):
        total = total + density[:, g]
    return total.reshape(16, Q)


def transform(density, table_high, table_low):
    count = density.shape[0]
    high, low = split(density)
    both = jnp.dot(
        jnp.concatenate([high, low], 0), table_high, preferred_element_type=jnp.float32
    )
    return both[:count] + both[count:] + jnp.dot(high, table_low, preferred_element_type=jnp.float32)


def store_spectra(spectra, target, first_leaf):
    for block in range(spectra.shape[0] // 16):
        for h in range(2):
            rows = spectra[block * 16 + h * 8 : block * 16 + h * 8 + 8]
            for c in range(2):
                for t in range(TILES):
                    column = (c * TILES + t) * LANES
                    start = (first_leaf + block * 16 + h) * ROWS + c * 8 + t
                    target[pl.ds(start, 8, stride=2 * ROWS), :] = rows[:, column : column + LANES]


def pack_kernel(offsets, charges, keys, levels, counts, send_boxes, out, blocks):
    leaves = keys.shape[1]
    half = leaves // 2
    out[4 * half :, :] = jnp.zeros((8, LANES), jnp.float32)
    width = jnp.left_shift(jnp.ones_like(levels[...]), MAXL - levels[...]).astype(jnp.float32)
    for a in range(3):
        summed = jnp.zeros_like(keys[...])
        for bit in range(MAXL):
            summed = summed + (jnp.right_shift(keys[...], 3 * bit + a) & 1) * (1 << bit)
        out[4 * half + a : 4 * half + a + 1, :leaves] = summed.astype(jnp.float32) + 0.5 * width
    out[4 * half + 3 : 4 * half + 4, :leaves] = width
    for r in range(half):
        out[pl.ds(r, 3, stride=half), :] = offsets[:, r * LANES : (r + 1) * LANES]
    beads = per_leaf(counts[...].astype(jnp.float32), half)
    slot = iota((half, LANES), 1) & (BCAP - 1)
    out[3 * half : 4 * half, :] = jnp.where(slot.astype(jnp.float32) < beads, charges[...], 0.0)

    sends = send_boxes.shape[1]
    lane = iota((8, LANES), 1)
    for block in range(sends // 16):
        picked = []
        for c in range(2):
            column = block * 16 + 2 * iota((8, sends), 0) + c
            box = jnp.sum(
                jnp.where(iota((8, sends), 1) == column, send_boxes[...].astype(jnp.float32), 0.0),
                axis=1, keepdims=True,
            ).astype(jnp.int32)
            width_here = jnp.sum(
                jnp.where(iota((8, leaves), 1) == box, width, 0.0), axis=1, keepdims=True
            )
            row_of = jnp.broadcast_to(box >> 1, (8, LANES))
            found = [jnp.zeros((8, LANES), jnp.float32)] * 4
            for r in range(half):
                here = row_of == r
                for ch in range(4):
                    found[ch] = jnp.where(here, out[ch * half + r : ch * half + r + 1, :], found[ch])
            aligned = jnp.broadcast_to((box & 1) == c, (8, LANES))
            found = [jnp.where(aligned, x, pltpu.roll(x, BCAP, 1)) for x in found]
            picked.append(found + [jnp.broadcast_to(width_here, (8, LANES))])
        for ch in range(5):
            blocks[pl.ds(block * 64 + ch, 8, stride=8), :] = jnp.where(
                lane < BCAP, picked[0][ch], picked[1][ch]
            )
        for ch in range(5, 8):
            blocks[pl.ds(block * 64 + ch, 8, stride=8), :] = jnp.zeros((8, LANES), jnp.float32)


def far_kernel(
    sources, kinds, counts, pair_ref, packed, arrived, up_inverse, signs, last_bins,
    table_high, table_low, translations, kept, sent,
    spectra, kernels, high_table, low_table, density, totals, checks, result, sems,
):
    leaves, entries = sources.shape
    half = leaves // 2
    blocks = arrived.shape[0] // 64
    kind_count = translations.shape[0]
    pair = pair_ref[0]

    table_copies = [
        pltpu.make_async_copy(table_high, high_table, sems.at[TILES - 1]),
        pltpu.make_async_copy(table_low, low_table, sems.at[TILES]),
    ]
    kernel_copies = [
        pltpu.make_async_copy(
            translations.at[:, :, pl.ds(t * LANES, LANES)],
            kernels.at[pl.ds(0, kind_count), pl.ds(2 * t, 2), :],
            sems.at[t],
        )
        for t in range(TILES - 1)
    ]
    for copy in table_copies + kernel_copies:
        copy.start()
    kernels[:kind_count, 2 * TILES - 2 : 2 * TILES, :] = last_bins[...]
    kernels[kind_count] = jnp.zeros((ROWS, LANES), jnp.float32)

    density[...] = jnp.zeros(density.shape, jnp.float32)
    width = per_leaf(packed[4 * half + 3 : 4 * half + 4, :], half)
    for block in range(half // 8):
        rows = [packed[c * half + block * 8 : c * half + block * 8 + 8, :] for c in range(4)]
        density[block * 16 : block * 16 + 16, :Q] = upward(
            rows[:3], rows[3], width[block * 8 : block * 8 + 8], up_inverse[...], checks
        )

    def arrive(block, carry):
        rows = [
            arrived[pl.ds(pl.multiple_of(block * 64, 64) + ch, 8, stride=8), :] for ch in range(5)
        ]
        density[pl.ds(pl.multiple_of(leaves + block * 16, 16), 16), :Q] = upward(
            rows[:3], rows[3], rows[4], up_inverse[...], checks
        )
        return carry

    if blocks == 1:
        arrive(0, 0)
    else:
        lax.fori_loop(0, blocks, arrive, 0)
    sign = jnp.where(pair == 1, signs[1:2, :], signs[0:1, :])
    for copy in table_copies:
        copy.wait()
    store_spectra(transform(density[...] * sign, high_table[...], low_table[...]), spectra, 0)
    for copy in kernel_copies:
        copy.wait()

    def translate(leaf, carry):
        live = counts[leaf]
        sums = [[None] * 4, [None] * 4]
        for entry in range(entries):
            source = sources[leaf, entry]
            kind = kinds[leaf, entry]
            if entry >= entries // 2:
                kind = jnp.where(entry < live, kind, kind_count)
            k_re = kernels[kind, pl.ds(0, 8, stride=2), :]
            k_im = kernels[kind, pl.ds(1, 8, stride=2), :]
            start = pl.multiple_of(source * ROWS, ROWS)
            s_re = spectra[pl.ds(start, 8), :]
            s_im = spectra[pl.ds(start + 8, 8), :]
            terms = (k_re * s_re, k_im * s_im, k_re * s_im, k_im * s_re)
            side = sums[entry % 2]
            for n, term in enumerate(terms):
                side[n] = term if side[n] is None else side[n] + term
        rr, ii, ri, ir = [a + b for a, b in zip(*sums)]
        start = pl.multiple_of(leaf * ROWS, ROWS)
        totals[pl.ds(start, 8), :] = rr - ii
        totals[pl.ds(start + 8, 8), :] = ri + ir
        return carry

    lax.fori_loop(0, leaves, translate, 0, unroll=4)

    wide_lane = iota((leaves, LANES), 1)
    columns = []
    for c in range(2):
        for t in range(TILES):
            rows = totals[pl.ds(c * 8 + t, leaves, stride=ROWS), :]
            if t == TILES - 1:
                rows = jnp.where(wide_lane < BINS - t * LANES, rows, 0.0)
            columns.append(rows)
    high, low = split(jnp.concatenate(columns, 1))
    across = (((1,), (1,)), ((), ()))
    both = lax.dot_general(
        jnp.concatenate([high, low], 0), high_table[...], across,
        preferred_element_type=jnp.float32,
    )
    check = both[:leaves] + both[leaves:] + lax.dot_general(
        high, low_table[...], across, preferred_element_type=jnp.float32
    )
    result[...] = (check * (sign * (1.0 / G)))[:, :Q]
    kept[...] = result[pl.ds(pl.multiple_of(pair * half, 8), half), :]
    sent[...] = result[pl.ds(pl.multiple_of((1 - pair) * half, 8), half), :]


def near_kernel(near_source, pair_ref, swapped, packed, passed, out, table, targets, sums, own):
    leaves, entries = near_source.shape
    half = leaves // 2
    pair = pair_ref[0]
    lane = iota((half, LANES), 1)
    low = lane < BCAP
    odd = pair_ref[1] & 1
    swapped_from = jnp.where((odd ^ pair) == 1, 0, 2)
    for n, place, rows_of in ((0, swapped_from, swapped), (1, 1, packed), (2, 2 - swapped_from, passed)):
        shape = rows_of[4 * half :, :]
        width = per_leaf(shape[3:4], half)
        for ch in range(4):
            rows = rows_of[ch * half : (ch + 1) * half, :]
            if ch < 3:
                rows = per_leaf(shape[ch : ch + 1], half) + width * rows
                if n == 1:
                    own[ch] = rows
            turned = pltpu.roll(rows, BCAP, 1)
            first = place * (leaves * 8)
            if n != 1:
                first = pl.multiple_of(first, 8)
            table[pl.ds(first + ch, half, stride=16), :] = jnp.where(low, rows, turned)
            table[pl.ds(first + 8 + ch, half, stride=16), :] = jnp.where(low, turned, rows)
    for ch in range(3):
        mine = own[ch, pl.ds(pl.multiple_of(pair * (half // 2), 8), half // 2), :]
        flipped = mine.T
        for r in range(half // 2):
            for h in range(2):
                start = ((2 * r + h) * 3 + ch) * BCAP
                targets[pl.ds(start, BCAP), :] = jnp.broadcast_to(
                    flipped[h * BCAP : (h + 1) * BCAP, r : r + 1], (BCAP, LANES)
                )
    low = iota((8, LANES), 1) < BCAP

    def one_leaf(t, carry):
        leaf = pair * half + t
        start = pl.multiple_of(t * 3 * BCAP, 8)
        tx, ty, tz = [targets[pl.ds(start + ch * BCAP, BCAP), :] for ch in range(3)]
        total = jnp.zeros((BCAP, LANES), jnp.float32)
        for n in range(entries // 2):
            left = pl.multiple_of(near_source[leaf, 2 * n] * 8, 8)
            right = pl.multiple_of(near_source[leaf, 2 * n + 1] * 8, 8)
            both = jnp.where(low, table[pl.ds(left, 8), :], table[pl.ds(right, 8), :])
            gx, gy, gz = tx - both[0:1], ty - both[1:2], tz - both[2:3]
            squared = gx * gx + gy * gy + (gz * gz + softening)
            total = total + lax.rsqrt(squared) * both[3:4]
        sums[pl.ds(pl.multiple_of(t * BCAP, 8), BCAP), :] = total
        return carry

    lax.fori_loop(0, half, one_leaf, 0)
    for r in range(half // 2):
        block = sums[r * LANES : (r + 1) * LANES, :].T
        out[r : r + 1, :] = jnp.sum(block, axis=0, keepdims=True)


def final_kernel(
    pair_ref, packed, kept, received, down_inverse, near, counts, decay_rate, stress,
    potential, new_stress, densities,
):
    half = (packed.shape[0] - 8) // 4
    rows = half // 2
    start = pl.multiple_of(pair_ref[0] * rows, 8)
    first = pair_ref[0] * half
    leaf_of = 2 * (iota((half, LANES), 1) & 7) + (iota((half, LANES), 1) >> 6)
    spread = jnp.where(iota((half, LANES), 0) == leaf_of, 1.0, 0.0)
    check = kept[...] + received[...]
    density = jnp.dot(
        check, down_inverse[...], precision=precise, preferred_element_type=jnp.float32
    )
    densities[...] = lax.dot_general(
        density, spread, (((0,), (0,)), ((), ())), precision=precise,
        preferred_element_type=jnp.float32,
    )
    width = block_transpose(per_leaf(packed[4 * half + 3 : 4 * half + 4, :], rows, first))
    offsets = [
        block_transpose(packed[pl.ds(pl.multiple_of(c * half + start, 8), rows), :])
        for c in range(3)
    ]
    total = None
    for q, kernel in surface_kernels(offsets, width):
        term = kernel * densities[q : q + 1, :]
        total = term if total is None else total + term
    combined = block_transpose(total) + near[...]
    beads = per_leaf(counts[...].astype(jnp.float32), rows, first)
    slot = iota((rows, LANES), 1) & (BCAP - 1)
    occupied = slot.astype(jnp.float32) < beads
    decay = per_leaf(decay_rate[...], rows)
    potential[...] = jnp.where(occupied, combined, 0.0)
    new_stress[...] = jnp.where(occupied, decay * stress[...] + combined, 0.0)


VMEM = pl.BlockSpec(memory_space=pltpu.VMEM)
SMEM = pl.BlockSpec(memory_space=pltpu.SMEM)
ANY = pl.BlockSpec(memory_space=pl.ANY)
MIB = 1024 * 1024


def call(kernel, outs, in_specs, scratch=(), limit=40, grid=(), flops=0, bytes_accessed=0):
    return pl.pallas_call(
        kernel,
        out_shape=outs,
        grid=grid,
        in_specs=in_specs,
        out_specs=jax.tree.map(lambda _: VMEM, outs),
        scratch_shapes=list(scratch),
        compiler_params=pltpu.CompilerParams(vmem_limit_bytes=limit * MIB),
        cost_estimate=pl.CostEstimate(
            flops=flops, bytes_accessed=bytes_accessed, transcendentals=0
        ),
    )


def body(
    offsets,
    charges,
    stress,
    decay_rate,
    morton_keys,
    levels,
    bead_counts,
    send_boxes,
    m2l_source,
    m2l_type,
    m2l_count,
    near_source,
    up_inverse,
    down_inverse,
    translations,
):
    f32 = jnp.float32
    leaves = morton_keys.shape[0]
    half = leaves // 2
    parts = lax.axis_size("wide") * lax.axis_size("narrow")
    high, low = [jnp.asarray(x) for x in transform_table()]
    signs = jnp.asarray(sign_rows())
    owner = lax.axis_index("wide") * lax.axis_size("narrow") + lax.axis_index("narrow")
    place = jnp.stack([lax.axis_index("pair"), owner])
    kind_count = translations.shape[0]

    packed, blocks = call(
        pack_kernel,
        [
            jax.ShapeDtypeStruct((4 * half + 8, LANES), f32),
            jax.ShapeDtypeStruct((8 * parts, LANES), f32),
        ],
        [VMEM] * 6,
        limit=62,
    )(
        offsets, charges.reshape(half, LANES), morton_keys.reshape(1, leaves),
        levels.reshape(1, leaves), bead_counts.reshape(1, leaves), send_boxes,
    )
    arrived = lax.all_to_all(
        blocks.reshape(parts, 8, LANES), PARTS, split_axis=0, concat_axis=0, tiled=True
    ).reshape(8 * parts, LANES)
    swaps = [(2 * d, 2 * (d ^ 1)) for d in range(parts)]
    for d in range(1, parts - 1, 2):
        swaps += [(2 * d + 1, 2 * d + 3), (2 * d + 3, 2 * d + 1)]
    swapped = lax.ppermute(packed, PARTS + ("pair",), swaps)
    passed = lax.ppermute(swapped, "pair", [(0, 1), (1, 0)])

    kept, sent = call(
        far_kernel,
        [jax.ShapeDtypeStruct((half, Q), f32)] * 2,
        [SMEM] * 4 + [VMEM] * 4
        + [pl.BlockSpec((kind_count, 2, LANES), lambda i: (0, 0, TILES - 1))]
        + [ANY] * 3,
        [
            pltpu.VMEM(((leaves + 2 * parts) * ROWS, LANES), f32),
            pltpu.VMEM((kind_count + 1, ROWS, LANES), f32),
            pltpu.VMEM(high.shape, jnp.bfloat16),
            pltpu.VMEM(low.shape, jnp.bfloat16),
            pltpu.VMEM((leaves + 2 * parts, QPAD), f32),
            pltpu.VMEM((leaves * ROWS, LANES), f32),
            pltpu.VMEM((Q * 8, LANES), f32),
            pltpu.VMEM((leaves, Q), f32),
            pltpu.SemaphoreType.DMA((TILES + 1,)),
        ],
        limit=62,
        grid=(1,),
    )(
        m2l_source, m2l_type, m2l_count, place, packed, arrived, up_inverse, signs, translations,
        high, low, translations,
    )
    received = lax.ppermute(sent, "pair", [(0, 1), (1, 0)])
    near = call(
        near_kernel,
        jax.ShapeDtypeStruct((half // 2, LANES), f32),
        [SMEM] * 2 + [VMEM] * 3,
        [
            pltpu.VMEM((3 * leaves * 8, LANES), f32),
            pltpu.VMEM((half * 3 * BCAP, LANES), f32),
            pltpu.VMEM((half * BCAP, LANES), f32),
            pltpu.VMEM((3, half, LANES), f32),
        ],
        flops=10**9,
        bytes_accessed=4 * 10**6,
    )(near_source, place, swapped, packed, passed)

    out = jax.ShapeDtypeStruct((half // 2, LANES), f32)
    potential, new_stress = call(
        final_kernel,
        [out, out],
        [SMEM] + [VMEM] * 8,
        [pltpu.VMEM((Q, LANES), f32)],
    )(
        place, packed, kept, received, down_inverse, near, bead_counts.reshape(1, leaves),
        decay_rate.reshape(1, half), stress.reshape(half // 2, LANES),
    )
    return potential.reshape(-1), new_stress.reshape(-1)


def solution(mesh):
    return jax.shard_map(
        body,
        mesh=mesh,
        in_specs=(
            P(None, ("groups", "wide", "narrow")),
            P(("groups", "wide", "narrow")),
            P(("groups", "wide", "narrow", "pair")),
            P(("groups", "wide", "narrow", "pair")),
            P(("groups", "wide", "narrow")),
            P(("groups", "wide", "narrow")),
            P(("groups", "wide", "narrow")),
            P(("groups", "wide", "narrow"), None),
            P(("groups", "wide", "narrow"), None),
            P(("groups", "wide", "narrow"), None),
            P(("groups", "wide", "narrow")),
            P(("groups", "wide", "narrow"), None),
            P(),
            P(),
            P(None, None, "pair"),
        ),
        out_specs=(
            P(("groups", "wide", "narrow", "pair")),
            P(("groups", "wide", "narrow", "pair")),
        ),
        check_vma=False,
    )
```

```python
import functools

import jax
import jax.numpy as jnp
import ml_dtypes
import numpy as np
from jax import lax
from jax.experimental import pallas as pl
from jax.experimental.pallas import tpu as pltpu
from jax.sharding import PartitionSpec as P

PGRID = 12
G = 1728
MAXL = 10
BCAP = 64
Q = 152
QPAD = 160
LANES = 128
BINS = 864
TILES = 7
ROWS = 16
precise = lax.Precision.HIGHEST
softening = 0.04
surface_reach = 1.25
CELLS = [
    (i, j, k)
    for i in range(6)
    for j in range(6)
    for k in range(6)
    if 0 in (i, j, k) or 5 in (i, j, k)
]
PARTS = ("wide", "narrow")


def transform_table():
    cells = np.array(CELLS)
    bins = np.arange(BINS)
    freq = np.stack([bins // 144, bins // 12 % 12, bins % 12])
    angle = (cells @ freq % PGRID) * (2.0 * np.pi / PGRID)
    table = np.zeros((QPAD, 2 * TILES * LANES))
    table[:Q, :BINS] = np.cos(angle)
    table[:Q, TILES * LANES : TILES * LANES + BINS] = -np.sin(angle)
    table[np.abs(table) < 1e-9] = 0.0
    high = table.astype(ml_dtypes.bfloat16)
    low = (table - high.astype(np.float64)).astype(ml_dtypes.bfloat16)
    return high, low


def sign_rows():
    rows = np.zeros((8, QPAD), np.float32)
    rows[0, :Q] = 1.0
    rows[1, :Q] = [(-1.0) ** i for i, _, _ in CELLS]
    return rows


def iota(shape, dim):
    return lax.broadcasted_iota(jnp.int32, shape, dim)


def per_leaf(values, count, first=0):
    shape = (count, values.shape[1])
    leaf, lane = first + 2 * iota(shape, 0), iota(shape, 1)
    even = jnp.sum(jnp.where(lane == leaf, values, 0.0), axis=1, keepdims=True)
    odd = jnp.sum(jnp.where(lane == leaf + 1, values, 0.0), axis=1, keepdims=True)
    return jnp.where(iota((count, LANES), 1) < BCAP, even, odd)


def block_transpose(x):
    lane, row = iota(x.shape, 1), iota(x.shape, 0)
    for k in (1, 2, 4):
        row_bit, lane_bit = (row & k) != 0, (lane & k) != 0
        below = pltpu.roll(pltpu.roll(x, 8 - k, 0), k, 1)
        above = pltpu.roll(pltpu.roll(x, k, 0), LANES - k, 1)
        x = jnp.where(row_bit == lane_bit, x, jnp.where(lane_bit, below, above))
    return x


def split(x):
    high = x.astype(jnp.bfloat16)
    return high, (x - high.astype(jnp.float32)).astype(jnp.bfloat16)


def axis_squares(offset, width):
    area = width * width
    planes = [surface_reach * 0.5 * (i - 2.5) / 2.5 for i in range(6)]
    return [(plane - offset) * (plane - offset) * area for plane in planes]


def surface_kernels(offsets, width):
    gx, gy, gz = [axis_squares(offset, width) for offset in offsets]
    gz = [g + softening for g in gz]
    last, gxy = None, None
    for q, (i, j, k) in enumerate(CELLS):
        if last != (i, j):
            last, gxy = (i, j), gx[i] + gy[j]
        yield q, lax.rsqrt(gxy + gz[k])


def upward(offsets, weights, width, up_inverse, checks):
    offsets = [block_transpose(x) for x in offsets]
    weights, width = block_transpose(weights), block_transpose(width)
    for q, kernel in surface_kernels(offsets, width):
        checks[pl.ds(8 * q, 8), :] = kernel * weights
    check = checks[pl.ds(0, Q, stride=8), :]
    for s in range(1, 8):
        check = check + checks[pl.ds(s, Q, stride=8), :]
    density = lax.dot_general(
        check, up_inverse, (((0,), (0,)), ((), ())), precision=precise,
        preferred_element_type=jnp.float32,
    )
    density = density.reshape(2, 8, 8, Q)
    total = density[:, 0]
    for g in range(1, 8):
        total = total + density[:, g]
    return total.reshape(16, Q)


def transform(density, table_high, table_low):
    count = density.shape[0]
    high, low = split(density)
    both = jnp.dot(
        jnp.concatenate([high, low], 0), table_high, preferred_element_type=jnp.float32
    )
    return both[:count] + both[count:] + jnp.dot(high, table_low, preferred_element_type=jnp.float32)


def store_spectra(spectra, target, first_leaf):
    for block in range(spectra.shape[0] // 16):
        for h in range(2):
            rows = spectra[block * 16 + h * 8 : block * 16 + h * 8 + 8]
            for c in range(2):
                for t in range(TILES):
                    column = (c * TILES + t) * LANES
                    start = (first_leaf + block * 16 + h) * ROWS + c * 8 + t
                    target[pl.ds(start, 8, stride=2 * ROWS), :] = rows[:, column : column + LANES]


def pack_kernel(offsets, charges, keys, levels, counts, send_boxes, out, blocks):
    leaves = keys.shape[1]
    half = leaves // 2
    out[4 * half :, :] = jnp.zeros((8, LANES), jnp.float32)
    width = jnp.left_shift(jnp.ones_like(levels[...]), MAXL - levels[...]).astype(jnp.float32)
    for a in range(3):
        summed = jnp.zeros_like(keys[...])
        for bit in range(MAXL):
            summed = summed + (jnp.right_shift(keys[...], 3 * bit + a) & 1) * (1 << bit)
        out[4 * half + a : 4 * half + a + 1, :leaves] = summed.astype(jnp.float32) + 0.5 * width
    out[4 * half + 3 : 4 * half + 4, :leaves] = width
    for r in range(half):
        out[pl.ds(r, 3, stride=half), :] = offsets[:, r * LANES : (r + 1) * LANES]
    beads = per_leaf(counts[...].astype(jnp.float32), half)
    slot = iota((half, LANES), 1) & (BCAP - 1)
    out[3 * half : 4 * half, :] = jnp.where(slot.astype(jnp.float32) < beads, charges[...], 0.0)

    sends = send_boxes.shape[1]
    lane = iota((8, LANES), 1)
    for block in range(sends // 16):
        picked = []
        for c in range(2):
            column = block * 16 + 2 * iota((8, sends), 0) + c
            box = jnp.sum(
                jnp.where(iota((8, sends), 1) == column, send_boxes[...].astype(jnp.float32), 0.0),
                axis=1, keepdims=True,
            ).astype(jnp.int32)
            width_here = jnp.sum(
                jnp.where(iota((8, leaves), 1) == box, width, 0.0), axis=1, keepdims=True
            )
            row_of = jnp.broadcast_to(box >> 1, (8, LANES))
            found = [jnp.zeros((8, LANES), jnp.float32)] * 4
            for r in range(half):
                here = row_of == r
                for ch in range(4):
                    found[ch] = jnp.where(here, out[ch * half + r : ch * half + r + 1, :], found[ch])
            aligned = jnp.broadcast_to((box & 1) == c, (8, LANES))
            found = [jnp.where(aligned, x, pltpu.roll(x, BCAP, 1)) for x in found]
            picked.append(found + [jnp.broadcast_to(width_here, (8, LANES))])
        for ch in range(5):
            blocks[pl.ds(block * 64 + ch, 8, stride=8), :] = jnp.where(
                lane < BCAP, picked[0][ch], picked[1][ch]
            )
        for ch in range(5, 8):
            blocks[pl.ds(block * 64 + ch, 8, stride=8), :] = jnp.zeros((8, LANES), jnp.float32)


def place_kernel(packed, out):
    half = out.shape[0] // 4
    width = per_leaf(packed[4 * half + 3 : 4 * half + 4, :], half)
    for ch in range(3):
        center = per_leaf(packed[4 * half + ch : 4 * half + ch + 1, :], half)
        out[ch * half : (ch + 1) * half, :] = center + width * packed[ch * half : (ch + 1) * half, :]
    out[3 * half :, :] = packed[3 * half : 4 * half, :]


def own_kernel(
    pair, packed, up_inverse, signs, table_high, table_low, spectra,
    high_table, low_table, density, checks, sems,
):
    half = (packed.shape[0] - 8) // 4
    copies = [
        pltpu.make_async_copy(table_high, high_table, sems.at[0]),
        pltpu.make_async_copy(table_low, low_table, sems.at[1]),
    ]
    for copy in copies:
        copy.start()
    density[...] = jnp.zeros(density.shape, jnp.float32)
    width = per_leaf(packed[4 * half + 3 : 4 * half + 4, :], half)
    for block in range(half // 8):
        rows = [packed[c * half + block * 8 : c * half + block * 8 + 8, :] for c in range(4)]
        density[block * 16 : block * 16 + 16, :Q] = upward(
            rows[:3], rows[3], width[block * 8 : block * 8 + 8], up_inverse[...], checks
        )
    sign = jnp.where(pair[0] == 1, signs[1:2, :], signs[0:1, :])
    for copy in copies:
        copy.wait()
    store_spectra(transform(density[...] * sign, high_table[...], low_table[...]), spectra, 0)


def far_kernel(
    sources, kinds, counts, pair_ref, arrived, up_inverse, signs, last_bins,
    table_high, table_low, translations, own_spectra, kept, sent,
    spectra, kernels, high_table, low_table, density, totals, checks, result, sems,
):
    leaves, entries = sources.shape
    half = leaves // 2
    blocks = arrived.shape[0] // 64
    kind_count = translations.shape[0]
    pair = pair_ref[0]

    table_copies = [
        pltpu.make_async_copy(table_high, high_table, sems.at[TILES - 1]),
        pltpu.make_async_copy(table_low, low_table, sems.at[TILES]),
    ]
    kernel_copies = [
        pltpu.make_async_copy(
            translations.at[:, :, pl.ds(t * LANES, LANES)],
            kernels.at[pl.ds(0, kind_count), pl.ds(2 * t, 2), :],
            sems.at[t],
        )
        for t in range(TILES - 1)
    ]
    own_copy = pltpu.make_async_copy(
        own_spectra, spectra.at[pl.ds(0, leaves * ROWS), :], sems.at[TILES + 1]
    )
    for copy in table_copies + kernel_copies + [own_copy]:
        copy.start()
    kernels[:kind_count, 2 * TILES - 2 : 2 * TILES, :] = last_bins[...]
    kernels[kind_count] = jnp.zeros((ROWS, LANES), jnp.float32)

    density[...] = jnp.zeros(density.shape, jnp.float32)

    def arrive(block, carry):
        rows = [
            arrived[pl.ds(pl.multiple_of(block * 64, 64) + ch, 8, stride=8), :] for ch in range(5)
        ]
        density[pl.ds(pl.multiple_of(block * 16, 16), 16), :Q] = upward(
            rows[:3], rows[3], rows[4], up_inverse[...], checks
        )
        return carry

    if blocks == 1:
        arrive(0, 0)
    else:
        lax.fori_loop(0, blocks, arrive, 0)
    sign = jnp.where(pair == 1, signs[1:2, :], signs[0:1, :])
    for copy in table_copies:
        copy.wait()
    store_spectra(transform(density[...] * sign, high_table[...], low_table[...]), spectra, leaves)
    for copy in kernel_copies + [own_copy]:
        copy.wait()

    def translate(leaf, carry):
        live = counts[leaf]
        sums = [[None] * 4, [None] * 4]
        for entry in range(entries):
            source = sources[leaf, entry]
            kind = kinds[leaf, entry]
            if entry >= entries // 2:
                kind = jnp.where(entry < live, kind, kind_count)
            k_re = kernels[kind, pl.ds(0, 8, stride=2), :]
            k_im = kernels[kind, pl.ds(1, 8, stride=2), :]
            start = pl.multiple_of(source * ROWS, ROWS)
            s_re = spectra[pl.ds(start, 8), :]
            s_im = spectra[pl.ds(start + 8, 8), :]
            terms = (k_re * s_re, k_im * s_im, k_re * s_im, k_im * s_re)
            side = sums[entry % 2]
            for n, term in enumerate(terms):
                side[n] = term if side[n] is None else side[n] + term
        rr, ii, ri, ir = [a + b for a, b in zip(*sums)]
        start = pl.multiple_of(leaf * ROWS, ROWS)
        totals[pl.ds(start, 8), :] = rr - ii
        totals[pl.ds(start + 8, 8), :] = ri + ir
        return carry

    lax.fori_loop(0, leaves, translate, 0, unroll=4)

    wide_lane = iota((leaves, LANES), 1)
    columns = []
    for c in range(2):
        for t in range(TILES):
            rows = totals[pl.ds(c * 8 + t, leaves, stride=ROWS), :]
            if t == TILES - 1:
                rows = jnp.where(wide_lane < BINS - t * LANES, rows, 0.0)
            columns.append(rows)
    high, low = split(jnp.concatenate(columns, 1))
    across = (((1,), (1,)), ((), ()))
    both = lax.dot_general(
        jnp.concatenate([high, low], 0), high_table[...], across,
        preferred_element_type=jnp.float32,
    )
    check = both[:leaves] + both[leaves:] + lax.dot_general(
        high, low_table[...], across, preferred_element_type=jnp.float32
    )
    result[...] = (check * (sign * (1.0 / G)))[:, :Q]
    kept[...] = result[pl.ds(pl.multiple_of(pair * half, 8), half), :]
    sent[...] = result[pl.ds(pl.multiple_of((1 - pair) * half, 8), half), :]


def near_kernel(
    near_source, pair_ref, owner_ref, swapped, placed, passed, out, table, targets, sums
):
    entries, leaves = near_source.shape
    half = leaves // 2
    pair = pair_ref[0]
    low = iota((half, LANES), 1) < BCAP
    swapped_from = jnp.where(((owner_ref[0] & 1) ^ pair) == 1, 0, 2)
    for n, rows_of in ((swapped_from, swapped), (1, placed), (2 - swapped_from, passed)):
        first = n * (leaves * 8)
        for ch in range(4):
            rows = rows_of[ch * half : (ch + 1) * half, :]
            turned = pltpu.roll(rows, BCAP, 1)
            table[pl.ds(first + ch, half, stride=16), :] = jnp.where(low, rows, turned)
            table[pl.ds(first + 8 + ch, half, stride=16), :] = jnp.where(low, turned, rows)
    for ch in range(3):
        mine = placed[pl.ds(pl.multiple_of(ch * half + pair * (half // 2), 8), half // 2), :]
        flipped = mine.T
        for r in range(half // 2):
            for h in range(2):
                start = ((2 * r + h) * 3 + ch) * BCAP
                targets[pl.ds(start, BCAP), :] = jnp.broadcast_to(
                    flipped[h * BCAP : (h + 1) * BCAP, r : r + 1], (BCAP, LANES)
                )
    low = iota((8, LANES), 1) < BCAP

    def one_leaf(t, carry):
        leaf = pair * half + t
        start = pl.multiple_of(t * 3 * BCAP, 8)
        tx, ty, tz = [targets[pl.ds(start + ch * BCAP, BCAP), :] for ch in range(3)]
        total = jnp.zeros((BCAP, LANES), jnp.float32)
        for n in range(entries // 2):
            left = pl.multiple_of(near_source[2 * n, leaf] * 8, 8)
            right = pl.multiple_of(near_source[2 * n + 1, leaf] * 8, 8)
            both = jnp.where(low, table[pl.ds(left, 8), :], table[pl.ds(right, 8), :])
            gx, gy, gz = tx - both[0:1], ty - both[1:2], tz - both[2:3]
            squared = gx * gx + gy * gy + (gz * gz + softening)
            total = total + lax.rsqrt(squared) * both[3:4]
        sums[pl.ds(pl.multiple_of(t * BCAP, 8), BCAP), :] = total
        return carry

    lax.fori_loop(0, half, one_leaf, 0)
    for r in range(half // 2):
        block = sums[r * LANES : (r + 1) * LANES, :].T
        out[r : r + 1, :] = jnp.sum(block, axis=0, keepdims=True)


def final_kernel(
    pair_ref, packed, kept, received, down_inverse, near, counts, decay_rate, stress,
    potential, new_stress, densities,
):
    half = (packed.shape[0] - 8) // 4
    rows = half // 2
    start = pl.multiple_of(pair_ref[0] * rows, 8)
    first = pair_ref[0] * half
    leaf_of = 2 * (iota((half, LANES), 1) & 7) + (iota((half, LANES), 1) >> 6)
    spread = jnp.where(iota((half, LANES), 0) == leaf_of, 1.0, 0.0)
    check = kept[...] + received[...]
    density = jnp.dot(
        check, down_inverse[...], precision=precise, preferred_element_type=jnp.float32
    )
    densities[...] = lax.dot_general(
        density, spread, (((0,), (0,)), ((), ())), precision=precise,
        preferred_element_type=jnp.float32,
    )
    width = block_transpose(per_leaf(packed[4 * half + 3 : 4 * half + 4, :], rows, first))
    offsets = [
        block_transpose(packed[pl.ds(pl.multiple_of(c * half + start, 8), rows), :])
        for c in range(3)
    ]
    total = None
    for q, kernel in surface_kernels(offsets, width):
        term = kernel * densities[q : q + 1, :]
        total = term if total is None else total + term
    combined = block_transpose(total) + near[...]
    beads = per_leaf(counts[...].astype(jnp.float32), rows, first)
    slot = iota((rows, LANES), 1) & (BCAP - 1)
    occupied = slot.astype(jnp.float32) < beads
    decay = per_leaf(decay_rate[...], rows)
    potential[...] = jnp.where(occupied, combined, 0.0)
    new_stress[...] = jnp.where(occupied, decay * stress[...] + combined, 0.0)


VMEM = pl.BlockSpec(memory_space=pltpu.VMEM)
SMEM = pl.BlockSpec(memory_space=pltpu.SMEM)
ANY = pl.BlockSpec(memory_space=pl.ANY)
MIB = 1024 * 1024


def call(kernel, outs, in_specs, scratch=(), limit=40, grid=(), flops=0, bytes_accessed=0):
    return pl.pallas_call(
        kernel,
        out_shape=outs,
        grid=grid,
        in_specs=in_specs,
        out_specs=jax.tree.map(lambda _: VMEM, outs),
        scratch_shapes=list(scratch),
        compiler_params=pltpu.CompilerParams(vmem_limit_bytes=limit * MIB),
        cost_estimate=pl.CostEstimate(
            flops=flops, bytes_accessed=bytes_accessed, transcendentals=0
        ),
    )


def body(
    offsets,
    charges,
    stress,
    decay_rate,
    morton_keys,
    levels,
    bead_counts,
    send_boxes,
    m2l_source,
    m2l_type,
    m2l_count,
    near_source,
    up_inverse,
    down_inverse,
    translations,
):
    f32 = jnp.float32
    leaves = morton_keys.shape[0]
    half = leaves // 2
    parts = lax.axis_size("wide") * lax.axis_size("narrow")
    high, low = [jnp.asarray(x) for x in transform_table()]
    signs = jnp.asarray(sign_rows())
    pair = lax.axis_index("pair").reshape(1)
    owner = (
        lax.axis_index("wide") * lax.axis_size("narrow") + lax.axis_index("narrow")
    ).reshape(1)
    kind_count = translations.shape[0]
    bf16 = jnp.bfloat16

    packed, blocks = call(
        pack_kernel,
        [
            jax.ShapeDtypeStruct((4 * half + 8, LANES), f32),
            jax.ShapeDtypeStruct((8 * parts, LANES), f32),
        ],
        [VMEM] * 6,
        limit=62,
    )(
        offsets, charges.reshape(half, LANES), morton_keys.reshape(1, leaves),
        levels.reshape(1, leaves), bead_counts.reshape(1, leaves), send_boxes,
    )
    arrived = lax.all_to_all(
        blocks.reshape(parts, 8, LANES), PARTS, split_axis=0, concat_axis=0, tiled=True
    ).reshape(8 * parts, LANES)
    swaps = [(2 * d, 2 * (d ^ 1)) for d in range(parts)]
    for d in range(1, parts - 1, 2):
        swaps += [(2 * d + 1, 2 * d + 3), (2 * d + 3, 2 * d + 1)]
    placed = call(
        place_kernel, jax.ShapeDtypeStruct((4 * half, LANES), f32), [VMEM], limit=62,
        flops=10**10, bytes_accessed=4 * 10**6,
    )(packed)
    swapped = lax.ppermute(placed, PARTS + ("pair",), swaps)
    own_spectra = call(
        own_kernel,
        jax.ShapeDtypeStruct((leaves * ROWS, LANES), f32),
        [SMEM] + [VMEM] * 3 + [ANY] * 2,
        [
            pltpu.VMEM(high.shape, bf16),
            pltpu.VMEM(low.shape, bf16),
            pltpu.VMEM((leaves, QPAD), f32),
            pltpu.VMEM((Q * 8, LANES), f32),
            pltpu.SemaphoreType.DMA((2,)),
        ],
        limit=62,
        flops=10**9,
        bytes_accessed=4 * 10**6,
    )(pair, packed, up_inverse, signs, high, low)
    passed = lax.ppermute(swapped, "pair", [(0, 1), (1, 0)])

    kept, sent = call(
        far_kernel,
        [jax.ShapeDtypeStruct((half, Q), f32)] * 2,
        [SMEM] * 4 + [VMEM] * 3
        + [pl.BlockSpec((kind_count, 2, LANES), lambda i: (0, 0, TILES - 1))]
        + [ANY] * 4,
        [
            pltpu.VMEM(((leaves + 2 * parts) * ROWS, LANES), f32),
            pltpu.VMEM((kind_count + 1, ROWS, LANES), f32),
            pltpu.VMEM(high.shape, bf16),
            pltpu.VMEM(low.shape, bf16),
            pltpu.VMEM((2 * parts, QPAD), f32),
            pltpu.VMEM((leaves * ROWS, LANES), f32),
            pltpu.VMEM((Q * 8, LANES), f32),
            pltpu.VMEM((leaves, Q), f32),
            pltpu.SemaphoreType.DMA((TILES + 2,)),
        ],
        limit=62,
        grid=(1,),
        flops=2 * 10**9,
        bytes_accessed=8 * 10**6,
    )(
        m2l_source, m2l_type, m2l_count, pair, arrived, up_inverse, signs, translations,
        high, low, translations, own_spectra,
    )
    received = lax.ppermute(sent, "pair", [(0, 1), (1, 0)])
    near = call(
        near_kernel,
        jax.ShapeDtypeStruct((half // 2, LANES), f32),
        [SMEM] * 3 + [VMEM] * 3,
        [
            pltpu.VMEM((3 * leaves * 8, LANES), f32),
            pltpu.VMEM((half * 3 * BCAP, LANES), f32),
            pltpu.VMEM((half * BCAP, LANES), f32),
        ],
        flops=10**9,
        bytes_accessed=4 * 10**6,
    )(near_source.T, pair, owner, swapped, placed, passed)

    out = jax.ShapeDtypeStruct((half // 2, LANES), f32)
    potential, new_stress = call(
        final_kernel,
        [out, out],
        [SMEM] + [VMEM] * 8,
        [pltpu.VMEM((Q, LANES), f32)],
    )(
        pair, packed, kept, received, down_inverse, near, bead_counts.reshape(1, leaves),
        decay_rate.reshape(1, half), stress.reshape(half // 2, LANES),
    )
    return potential.reshape(-1), new_stress.reshape(-1)


def solution(mesh):
    return jax.shard_map(
        body,
        mesh=mesh,
        in_specs=(
            P(None, ("groups", "wide", "narrow")),
            P(("groups", "wide", "narrow")),
            P(("groups", "wide", "narrow", "pair")),
            P(("groups", "wide", "narrow", "pair")),
            P(("groups", "wide", "narrow")),
            P(("groups", "wide", "narrow")),
            P(("groups", "wide", "narrow")),
            P(("groups", "wide", "narrow"), None),
            P(("groups", "wide", "narrow"), None),
            P(("groups", "wide", "narrow"), None),
            P(("groups", "wide", "narrow")),
            P(("groups", "wide", "narrow"), None),
            P(),
            P(),
            P(None, None, "pair"),
        ),
        out_specs=(
            P(("groups", "wide", "narrow", "pair")),
            P(("groups", "wide", "narrow", "pair")),
        ),
        check_vma=False,
    )
```

```python
import functools

import jax
import jax.numpy as jnp
import ml_dtypes
import numpy as np
from jax import lax
from jax.experimental import pallas as pl
from jax.experimental.pallas import tpu as pltpu
from jax.sharding import PartitionSpec as P

PGRID = 12
G = 1728
MAXL = 10
BCAP = 64
Q = 152
QPAD = 160
LANES = 128
BINS = 864
TILES = 7
ROWS = 16
precise = lax.Precision.HIGHEST
softening = 0.04
surface_reach = 1.25
CELLS = [
    (i, j, k)
    for i in range(6)
    for j in range(6)
    for k in range(6)
    if 0 in (i, j, k) or 5 in (i, j, k)
]
PARTS = ("wide", "narrow")


def transform_table(back=False):
    cells = np.array(CELLS)
    bins = np.arange(BINS)
    freq = np.stack([bins // 144, bins // 12 % 12, bins % 12])
    angle = (cells @ freq % PGRID) * (2.0 * np.pi / PGRID)
    table = np.zeros((QPAD, 2 * TILES * LANES))
    table[:Q, :BINS] = np.cos(angle)
    table[:Q, TILES * LANES : TILES * LANES + BINS] = -np.sin(angle)
    table[np.abs(table) < 1e-9] = 0.0
    table = np.ascontiguousarray(table.T) if back else table
    high = table.astype(ml_dtypes.bfloat16)
    low = (table - high.astype(np.float64)).astype(ml_dtypes.bfloat16)
    return high, low


def sign_rows():
    rows = np.zeros((8, QPAD), np.float32)
    rows[0, :Q] = 1.0
    rows[1, :Q] = [(-1.0) ** i for i, _, _ in CELLS]
    return rows


def iota(shape, dim):
    return lax.broadcasted_iota(jnp.int32, shape, dim)


def per_leaf(values, count, first=0):
    shape = (count, values.shape[1])
    leaf, lane = first + 2 * iota(shape, 0), iota(shape, 1)
    even = jnp.sum(jnp.where(lane == leaf, values, 0.0), axis=1, keepdims=True)
    odd = jnp.sum(jnp.where(lane == leaf + 1, values, 0.0), axis=1, keepdims=True)
    return jnp.where(iota((count, LANES), 1) < BCAP, even, odd)


def block_transpose(x):
    lane, row = iota(x.shape, 1), iota(x.shape, 0)
    for k in (1, 2, 4):
        row_bit, lane_bit = (row & k) != 0, (lane & k) != 0
        below = pltpu.roll(pltpu.roll(x, 8 - k, 0), k, 1)
        above = pltpu.roll(pltpu.roll(x, k, 0), LANES - k, 1)
        x = jnp.where(row_bit == lane_bit, x, jnp.where(lane_bit, below, above))
    return x


def split(x):
    high = x.astype(jnp.bfloat16)
    return high, (x - high.astype(jnp.float32)).astype(jnp.bfloat16)


def axis_squares(offset, width):
    area = width * width
    planes = [surface_reach * 0.5 * (i - 2.5) / 2.5 for i in range(6)]
    return [(plane - offset) * (plane - offset) * area for plane in planes]


def surface_kernels(offsets, width):
    gx, gy, gz = [axis_squares(offset, width) for offset in offsets]
    gz = [g + softening for g in gz]
    last, gxy = None, None
    for q, (i, j, k) in enumerate(CELLS):
        if last != (i, j):
            last, gxy = (i, j), gx[i] + gy[j]
        yield q, lax.rsqrt(gxy + gz[k])


def upward(offsets, weights, width, up_inverse, checks):
    offsets = [block_transpose(x) for x in offsets]
    weights, width = block_transpose(weights), block_transpose(width)
    for q, kernel in surface_kernels(offsets, width):
        checks[pl.ds(8 * q, 8), :] = kernel * weights
    check = checks[pl.ds(0, Q, stride=8), :]
    for s in range(1, 8):
        check = check + checks[pl.ds(s, Q, stride=8), :]
    density = lax.dot_general(
        check, up_inverse, (((0,), (0,)), ((), ())), precision=precise,
        preferred_element_type=jnp.float32,
    )
    density = density.reshape(2, 8, 8, Q)
    total = density[:, 0]
    for g in range(1, 8):
        total = total + density[:, g]
    return total.reshape(16, Q)


def transform(density, table_high, table_low):
    count = density.shape[0]
    high, low = split(density)
    both = jnp.dot(
        jnp.concatenate([high, low], 0), table_high, preferred_element_type=jnp.float32
    )
    return both[:count] + both[count:] + jnp.dot(high, table_low, preferred_element_type=jnp.float32)


def store_spectra(spectra, target, first_leaf):
    for block in range(spectra.shape[0] // 16):
        for h in range(2):
            rows = spectra[block * 16 + h * 8 : block * 16 + h * 8 + 8]
            for c in range(2):
                for t in range(TILES):
                    column = (c * TILES + t) * LANES
                    start = (first_leaf + block * 16 + h) * ROWS + c * 8 + t
                    target[pl.ds(start, 8, stride=2 * ROWS), :] = rows[:, column : column + LANES]


def pack_kernel(offsets, charges, keys, levels, counts, send_boxes, out, blocks, placed):
    leaves = keys.shape[1]
    half = leaves // 2
    out[4 * half :, :] = jnp.zeros((8, LANES), jnp.float32)
    width = jnp.left_shift(jnp.ones_like(levels[...]), MAXL - levels[...]).astype(jnp.float32)
    for a in range(3):
        summed = jnp.zeros_like(keys[...])
        for bit in range(MAXL):
            summed = summed + (jnp.right_shift(keys[...], 3 * bit + a) & 1) * (1 << bit)
        out[4 * half + a : 4 * half + a + 1, :leaves] = summed.astype(jnp.float32) + 0.5 * width
    out[4 * half + 3 : 4 * half + 4, :leaves] = width
    for r in range(half):
        out[pl.ds(r, 3, stride=half), :] = offsets[:, r * LANES : (r + 1) * LANES]
    beads = per_leaf(counts[...].astype(jnp.float32), half)
    slot = iota((half, LANES), 1) & (BCAP - 1)
    out[3 * half : 4 * half, :] = jnp.where(slot.astype(jnp.float32) < beads, charges[...], 0.0)

    spread = per_leaf(width, half)
    for ch in range(3):
        center = per_leaf(out[4 * half + ch : 4 * half + ch + 1, :leaves], half)
        placed[ch * half : (ch + 1) * half, :] = center + spread * out[ch * half : (ch + 1) * half, :]
    placed[3 * half :, :] = out[3 * half : 4 * half, :]

    sends = send_boxes.shape[1]
    lane = iota((8, LANES), 1)
    for block in range(sends // 16):
        picked = []
        for c in range(2):
            column = block * 16 + 2 * iota((8, sends), 0) + c
            box = jnp.sum(
                jnp.where(iota((8, sends), 1) == column, send_boxes[...].astype(jnp.float32), 0.0),
                axis=1, keepdims=True,
            ).astype(jnp.int32)
            width_here = jnp.sum(
                jnp.where(iota((8, leaves), 1) == box, width, 0.0), axis=1, keepdims=True
            )
            row_of = jnp.broadcast_to(box >> 1, (8, LANES))
            found = [jnp.zeros((8, LANES), jnp.float32)] * 4
            for r in range(half):
                here = row_of == r
                for ch in range(4):
                    found[ch] = jnp.where(here, out[ch * half + r : ch * half + r + 1, :], found[ch])
            aligned = jnp.broadcast_to((box & 1) == c, (8, LANES))
            found = [jnp.where(aligned, x, pltpu.roll(x, BCAP, 1)) for x in found]
            picked.append(found + [jnp.broadcast_to(width_here, (8, LANES))])
        for ch in range(5):
            blocks[pl.ds(block * 64 + ch, 8, stride=8), :] = jnp.where(
                lane < BCAP, picked[0][ch], picked[1][ch]
            )
        for ch in range(5, 8):
            blocks[pl.ds(block * 64 + ch, 8, stride=8), :] = jnp.zeros((8, LANES), jnp.float32)


def far_kernel(
    sources, kinds, counts, pair_ref, packed, arrived, up_inverse, signs, last_bins,
    table_high, table_low, back_high, back_low, translations, near, kept, sent,
    spectra, kernels, high_table, low_table, high_back, low_back, density, totals, checks,
    result, sems,
):
    leaves, entries = sources.shape
    half = leaves // 2
    blocks = arrived.shape[0] // 64
    kind_count = translations.shape[0]
    pair = pair_ref[0]

    table_copies = [
        pltpu.make_async_copy(table_high, high_table, sems.at[0]),
        pltpu.make_async_copy(table_low, low_table, sems.at[1]),
    ]
    back_copies = [
        pltpu.make_async_copy(back_high, high_back, sems.at[2]),
        pltpu.make_async_copy(back_low, low_back, sems.at[3]),
    ]
    kernel_copies = [
        pltpu.make_async_copy(
            translations.at[:, :, pl.ds(t * LANES, LANES)],
            kernels.at[pl.ds(0, kind_count), pl.ds(2 * t, 2), :],
            sems.at[4 + t],
        )
        for t in range(TILES - 1)
    ]
    for copy in table_copies + kernel_copies + back_copies:
        copy.start()
    kernels[:kind_count, 2 * TILES - 2 : 2 * TILES, :] = last_bins[...]
    kernels[kind_count] = jnp.zeros((ROWS, LANES), jnp.float32)

    density[...] = jnp.zeros(density.shape, jnp.float32)
    width = per_leaf(packed[4 * half + 3 : 4 * half + 4, :], half)
    for block in range(half // 8):
        rows = [packed[c * half + block * 8 : c * half + block * 8 + 8, :] for c in range(4)]
        density[block * 16 : block * 16 + 16, :Q] = upward(
            rows[:3], rows[3], width[block * 8 : block * 8 + 8], up_inverse[...], checks
        )

    def arrive(block, carry):
        rows = [
            arrived[pl.ds(pl.multiple_of(block * 64, 64) + ch, 8, stride=8), :] for ch in range(5)
        ]
        density[pl.ds(pl.multiple_of(leaves + block * 16, 16), 16), :Q] = upward(
            rows[:3], rows[3], rows[4], up_inverse[...], checks
        )
        return carry

    if blocks == 1:
        arrive(0, 0)
    else:
        lax.fori_loop(0, blocks, arrive, 0)
    sign = jnp.where(pair == 1, signs[1:2, :], signs[0:1, :])
    for copy in table_copies:
        copy.wait()
    store_spectra(transform(density[...] * sign, high_table[...], low_table[...]), spectra, 0)
    for copy in kernel_copies:
        copy.wait()

    def translate(leaf, carry):
        live = counts[leaf]
        sums = [[None] * 4, [None] * 4]
        for entry in range(entries):
            source = sources[leaf, entry]
            kind = kinds[leaf, entry]
            if entry >= entries // 2:
                kind = jnp.where(entry < live, kind, kind_count)
            k_re = kernels[kind, pl.ds(0, 8, stride=2), :]
            k_im = kernels[kind, pl.ds(1, 8, stride=2), :]
            start = pl.multiple_of(source * ROWS, ROWS)
            s_re = spectra[pl.ds(start, 8), :]
            s_im = spectra[pl.ds(start + 8, 8), :]
            terms = (k_re * s_re, k_im * s_im, k_re * s_im, k_im * s_re)
            side = sums[entry % 2]
            for n, term in enumerate(terms):
                side[n] = term if side[n] is None else side[n] + term
        rr, ii, ri, ir = [a + b for a, b in zip(*sums)]
        start = pl.multiple_of(leaf * ROWS, ROWS)
        totals[pl.ds(start, 8), :] = rr - ii
        totals[pl.ds(start + 8, 8), :] = ri + ir
        return carry

    lax.fori_loop(0, leaves, translate, 0, unroll=4)

    wide_lane = iota((leaves, LANES), 1)
    columns = []
    for c in range(2):
        for t in range(TILES):
            rows = totals[pl.ds(c * 8 + t, leaves, stride=ROWS), :]
            if t == TILES - 1:
                rows = jnp.where(wide_lane < BINS - t * LANES, rows, 0.0)
            columns.append(rows)
    for copy in back_copies:
        copy.wait()
    check = transform(jnp.concatenate(columns, 1), high_back[...], low_back[...])
    result[...] = (check * (sign * (1.0 / G)))[:, :Q]
    kept[...] = result[pl.ds(pl.multiple_of(pair * half, 8), half), :]
    sent[...] = result[pl.ds(pl.multiple_of((1 - pair) * half, 8), half), :]


def near_kernel(
    near_source, pair_ref, owner_ref, swapped, placed, passed, out, table, targets, sums
):
    entries, leaves = near_source.shape
    half = leaves // 2
    pair = pair_ref[0]
    low = iota((half, LANES), 1) < BCAP
    swapped_from = jnp.where(((owner_ref[0] & 1) ^ pair) == 1, 0, 2)
    for n, rows_of in ((swapped_from, swapped), (1, placed), (2 - swapped_from, passed)):
        first = n * (leaves * 8)
        for ch in range(4):
            rows = rows_of[ch * half : (ch + 1) * half, :]
            turned = pltpu.roll(rows, BCAP, 1)
            table[pl.ds(first + ch, half, stride=16), :] = jnp.where(low, rows, turned)
            table[pl.ds(first + 8 + ch, half, stride=16), :] = jnp.where(low, turned, rows)
    for ch in range(3):
        mine = placed[pl.ds(pl.multiple_of(ch * half + pair * (half // 2), 8), half // 2), :]
        flipped = mine.T
        for r in range(half // 2):
            for h in range(2):
                start = ((2 * r + h) * 3 + ch) * BCAP
                targets[pl.ds(start, BCAP), :] = jnp.broadcast_to(
                    flipped[h * BCAP : (h + 1) * BCAP, r : r + 1], (BCAP, LANES)
                )
    low = iota((8, LANES), 1) < BCAP

    def one_leaf(t, carry):
        leaf = pair * half + t
        start = pl.multiple_of(t * 3 * BCAP, 8)
        tx, ty, tz = [targets[pl.ds(start + ch * BCAP, BCAP), :] for ch in range(3)]
        total = jnp.zeros((BCAP, LANES), jnp.float32)
        for n in range(entries // 2):
            left = pl.multiple_of(near_source[2 * n, leaf] * 8, 8)
            right = pl.multiple_of(near_source[2 * n + 1, leaf] * 8, 8)
            both = jnp.where(low, table[pl.ds(left, 8), :], table[pl.ds(right, 8), :])
            gx, gy, gz = tx - both[0:1], ty - both[1:2], tz - both[2:3]
            squared = gx * gx + gy * gy + (gz * gz + softening)
            total = total + lax.rsqrt(squared) * both[3:4]
        sums[pl.ds(pl.multiple_of(t * BCAP, 8), BCAP), :] = total
        return carry

    lax.fori_loop(0, half, one_leaf, 0)
    for r in range(half // 2):
        block = sums[r * LANES : (r + 1) * LANES, :].T
        out[r : r + 1, :] = jnp.sum(block, axis=0, keepdims=True)


def final_kernel(
    pair_ref, packed, kept, received, down_inverse, near, counts, decay_rate, stress,
    potential, new_stress, densities,
):
    half = (packed.shape[0] - 8) // 4
    rows = half // 2
    start = pl.multiple_of(pair_ref[0] * rows, 8)
    first = pair_ref[0] * half
    leaf_of = 2 * (iota((half, LANES), 1) & 7) + (iota((half, LANES), 1) >> 6)
    spread = jnp.where(iota((half, LANES), 0) == leaf_of, 1.0, 0.0)
    check = kept[...] + received[...]
    density = jnp.dot(
        check, down_inverse[...], precision=precise, preferred_element_type=jnp.float32
    )
    densities[...] = lax.dot_general(
        density, spread, (((0,), (0,)), ((), ())), precision=precise,
        preferred_element_type=jnp.float32,
    )
    width = block_transpose(per_leaf(packed[4 * half + 3 : 4 * half + 4, :], rows, first))
    offsets = [
        block_transpose(packed[pl.ds(pl.multiple_of(c * half + start, 8), rows), :])
        for c in range(3)
    ]
    total = None
    for q, kernel in surface_kernels(offsets, width):
        term = kernel * densities[q : q + 1, :]
        total = term if total is None else total + term
    combined = block_transpose(total) + near[...]
    beads = per_leaf(counts[...].astype(jnp.float32), rows, first)
    slot = iota((rows, LANES), 1) & (BCAP - 1)
    occupied = slot.astype(jnp.float32) < beads
    decay = per_leaf(decay_rate[...], rows)
    potential[...] = jnp.where(occupied, combined, 0.0)
    new_stress[...] = jnp.where(occupied, decay * stress[...] + combined, 0.0)


VMEM = pl.BlockSpec(memory_space=pltpu.VMEM)
SMEM = pl.BlockSpec(memory_space=pltpu.SMEM)
ANY = pl.BlockSpec(memory_space=pl.ANY)
MIB = 1024 * 1024


def call(kernel, outs, in_specs, scratch=(), limit=40, grid=(), flops=0, bytes_accessed=0):
    return pl.pallas_call(
        kernel,
        out_shape=outs,
        grid=grid,
        in_specs=in_specs,
        out_specs=jax.tree.map(lambda _: VMEM, outs),
        scratch_shapes=list(scratch),
        compiler_params=pltpu.CompilerParams(vmem_limit_bytes=limit * MIB),
        cost_estimate=pl.CostEstimate(
            flops=flops, bytes_accessed=bytes_accessed, transcendentals=0
        ),
    )


def body(
    offsets,
    charges,
    stress,
    decay_rate,
    morton_keys,
    levels,
    bead_counts,
    send_boxes,
    m2l_source,
    m2l_type,
    m2l_count,
    near_source,
    up_inverse,
    down_inverse,
    translations,
):
    f32 = jnp.float32
    leaves = morton_keys.shape[0]
    half = leaves // 2
    parts = lax.axis_size("wide") * lax.axis_size("narrow")
    high, low = [jnp.asarray(x) for x in transform_table()]
    signs = jnp.asarray(sign_rows())
    pair = lax.axis_index("pair").reshape(1)
    owner = (
        lax.axis_index("wide") * lax.axis_size("narrow") + lax.axis_index("narrow")
    ).reshape(1)
    kind_count = translations.shape[0]
    bf16 = jnp.bfloat16

    back = [jnp.asarray(x) for x in transform_table(back=True)]
    packed, blocks, placed = call(
        pack_kernel,
        [
            jax.ShapeDtypeStruct((4 * half + 8, LANES), f32),
            jax.ShapeDtypeStruct((8 * parts, LANES), f32),
            jax.ShapeDtypeStruct((4 * half, LANES), f32),
        ],
        [VMEM] * 6,
        limit=62,
    )(
        offsets, charges.reshape(half, LANES), morton_keys.reshape(1, leaves),
        levels.reshape(1, leaves), bead_counts.reshape(1, leaves), send_boxes,
    )
    arrived = lax.all_to_all(
        blocks.reshape(parts, 8, LANES), PARTS, split_axis=0, concat_axis=0, tiled=True
    ).reshape(8 * parts, LANES)
    swaps = [(2 * d, 2 * (d ^ 1)) for d in range(parts)]
    for d in range(1, parts - 1, 2):
        swaps += [(2 * d + 1, 2 * d + 3), (2 * d + 3, 2 * d + 1)]
    swapped = lax.ppermute(placed, PARTS + ("pair",), swaps)
    passed = lax.ppermute(swapped, "pair", [(0, 1), (1, 0)])

    near = call(
        near_kernel,
        jax.ShapeDtypeStruct((half // 2, LANES), f32),
        [SMEM] * 3 + [VMEM] * 3,
        [
            pltpu.VMEM((3 * leaves * 8, LANES), f32),
            pltpu.VMEM((half * 3 * BCAP, LANES), f32),
            pltpu.VMEM((half * BCAP, LANES), f32),
        ],
        flops=10**9,
        bytes_accessed=4 * 10**6,
    )(near_source.T, pair, owner, swapped, placed, passed)

    kept, sent = call(
        far_kernel,
        [jax.ShapeDtypeStruct((half, Q), f32)] * 2,
        [SMEM] * 4 + [VMEM] * 4
        + [pl.BlockSpec((kind_count, 2, LANES), lambda i: (0, 0, TILES - 1))]
        + [ANY] * 6,
        [
            pltpu.VMEM(((leaves + 2 * parts) * ROWS, LANES), f32),
            pltpu.VMEM((kind_count + 1, ROWS, LANES), f32),
            pltpu.VMEM(high.shape, bf16),
            pltpu.VMEM(low.shape, bf16),
            pltpu.VMEM(back[0].shape, bf16),
            pltpu.VMEM(back[1].shape, bf16),
            pltpu.VMEM((leaves + 2 * parts, QPAD), f32),
            pltpu.VMEM((leaves * ROWS, LANES), f32),
            pltpu.VMEM((Q * 8, LANES), f32),
            pltpu.VMEM((leaves, Q), f32),
            pltpu.SemaphoreType.DMA((TILES + 3,)),
        ],
        limit=62,
        grid=(1,),
        flops=2 * 10**9,
        bytes_accessed=8 * 10**6,
    )(
        m2l_source, m2l_type, m2l_count, pair, packed, arrived, up_inverse, signs, translations,
        high, low, back[0], back[1], translations, near,
    )
    received = lax.ppermute(sent, "pair", [(0, 1), (1, 0)])
    out = jax.ShapeDtypeStruct((half // 2, LANES), f32)
    potential, new_stress = call(
        final_kernel,
        [out, out],
        [SMEM] + [VMEM] * 8,
        [pltpu.VMEM((Q, LANES), f32)],
    )(
        pair, packed, kept, received, down_inverse, near, bead_counts.reshape(1, leaves),
        decay_rate.reshape(1, half), stress.reshape(half // 2, LANES),
    )
    return potential.reshape(-1), new_stress.reshape(-1)


def solution(mesh):
    return jax.shard_map(
        body,
        mesh=mesh,
        in_specs=(
            P(None, ("groups", "wide", "narrow")),
            P(("groups", "wide", "narrow")),
            P(("groups", "wide", "narrow", "pair")),
            P(("groups", "wide", "narrow", "pair")),
            P(("groups", "wide", "narrow")),
            P(("groups", "wide", "narrow")),
            P(("groups", "wide", "narrow")),
            P(("groups", "wide", "narrow"), None),
            P(("groups", "wide", "narrow"), None),
            P(("groups", "wide", "narrow"), None),
            P(("groups", "wide", "narrow")),
            P(("groups", "wide", "narrow"), None),
            P(),
            P(),
            P(None, None, "pair"),
        ),
        out_specs=(
            P(("groups", "wide", "narrow", "pair")),
            P(("groups", "wide", "narrow", "pair")),
        ),
        check_vma=False,
    )
```

```python
import functools

import jax
import jax.numpy as jnp
import ml_dtypes
import numpy as np
from jax import lax
from jax.experimental import pallas as pl
from jax.experimental.pallas import tpu as pltpu
from jax.sharding import PartitionSpec as P

PGRID = 12
G = 1728
MAXL = 10
BCAP = 64
Q = 152
QPAD = 160
LANES = 128
BINS = 864
TILES = 7
ROWS = 16
precise = lax.Precision.HIGHEST
softening = 0.04
surface_reach = 1.25
CELLS = [
    (i, j, k)
    for i in range(6)
    for j in range(6)
    for k in range(6)
    if 0 in (i, j, k) or 5 in (i, j, k)
]
PARTS = ("wide", "narrow")


def transform_table():
    cells = np.array(CELLS)
    bins = np.arange(BINS)
    freq = np.stack([bins // 144, bins // 12 % 12, bins % 12])
    angle = (cells @ freq % PGRID) * (2.0 * np.pi / PGRID)
    table = np.zeros((QPAD, 2 * TILES * LANES))
    table[:Q, :BINS] = np.cos(angle)
    table[:Q, TILES * LANES : TILES * LANES + BINS] = -np.sin(angle)
    table[np.abs(table) < 1e-9] = 0.0
    high = table.astype(ml_dtypes.bfloat16)
    low = (table - high.astype(np.float64)).astype(ml_dtypes.bfloat16)
    return high, low


def sign_rows():
    rows = np.zeros((8, QPAD), np.float32)
    rows[0, :Q] = 1.0
    rows[1, :Q] = [(-1.0) ** i for i, _, _ in CELLS]
    return rows


def iota(shape, dim):
    return lax.broadcasted_iota(jnp.int32, shape, dim)


def per_leaf(values, count, first=0):
    shape = (count, values.shape[1])
    leaf, lane = first + 2 * iota(shape, 0), iota(shape, 1)
    even = jnp.sum(jnp.where(lane == leaf, values, 0.0), axis=1, keepdims=True)
    odd = jnp.sum(jnp.where(lane == leaf + 1, values, 0.0), axis=1, keepdims=True)
    return jnp.where(iota((count, LANES), 1) < BCAP, even, odd)


def block_transpose(x):
    lane, row = iota(x.shape, 1), iota(x.shape, 0)
    for k in (1, 2, 4):
        row_bit, lane_bit = (row & k) != 0, (lane & k) != 0
        below = pltpu.roll(pltpu.roll(x, 8 - k, 0), k, 1)
        above = pltpu.roll(pltpu.roll(x, k, 0), LANES - k, 1)
        x = jnp.where(row_bit == lane_bit, x, jnp.where(lane_bit, below, above))
    return x


def split(x):
    high = x.astype(jnp.bfloat16)
    return high, (x - high.astype(jnp.float32)).astype(jnp.bfloat16)


def axis_squares(offset, width):
    area = width * width
    planes = [surface_reach * 0.5 * (i - 2.5) / 2.5 for i in range(6)]
    return [(plane - offset) * (plane - offset) * area for plane in planes]


def surface_kernels(offsets, width):
    gx, gy, gz = [axis_squares(offset, width) for offset in offsets]
    gz = [g + softening for g in gz]
    last, gxy = None, None
    for q, (i, j, k) in enumerate(CELLS):
        if last != (i, j):
            last, gxy = (i, j), gx[i] + gy[j]
        yield q, lax.rsqrt(gxy + gz[k])


def upward(offsets, weights, width, up_inverse, checks):
    offsets = [block_transpose(x) for x in offsets]
    weights, width = block_transpose(weights), block_transpose(width)
    for q, kernel in surface_kernels(offsets, width):
        checks[pl.ds(8 * q, 8), :] = kernel * weights
    check = checks[pl.ds(0, Q, stride=8), :]
    for s in range(1, 8):
        check = check + checks[pl.ds(s, Q, stride=8), :]
    density = lax.dot_general(
        check, up_inverse, (((0,), (0,)), ((), ())), precision=precise,
        preferred_element_type=jnp.float32,
    )
    density = density.reshape(2, 8, 8, Q)
    total = density[:, 0]
    for g in range(1, 8):
        total = total + density[:, g]
    return total.reshape(16, Q)


def transform(density, table_high, table_low):
    count = density.shape[0]
    high, low = split(density)
    both = jnp.dot(
        jnp.concatenate([high, low], 0), table_high, preferred_element_type=jnp.float32
    )
    return both[:count] + both[count:] + jnp.dot(high, table_low, preferred_element_type=jnp.float32)


def store_spectra(spectra, target, first_leaf):
    for block in range(spectra.shape[0] // 16):
        for h in range(2):
            rows = spectra[block * 16 + h * 8 : block * 16 + h * 8 + 8]
            for c in range(2):
                for t in range(TILES):
                    column = (c * TILES + t) * LANES
                    start = (first_leaf + block * 16 + h) * ROWS + c * 8 + t
                    target[pl.ds(start, 8, stride=2 * ROWS), :] = rows[:, column : column + LANES]


def pack_kernel(offsets, charges, keys, levels, counts, send_boxes, out, blocks, placed):
    leaves = keys.shape[1]
    half = leaves // 2
    out[4 * half :, :] = jnp.zeros((8, LANES), jnp.float32)
    width = jnp.left_shift(jnp.ones_like(levels[...]), MAXL - levels[...]).astype(jnp.float32)
    for a in range(3):
        summed = jnp.zeros_like(keys[...])
        for bit in range(MAXL):
            summed = summed + (jnp.right_shift(keys[...], 3 * bit + a) & 1) * (1 << bit)
        out[4 * half + a : 4 * half + a + 1, :leaves] = summed.astype(jnp.float32) + 0.5 * width
    out[4 * half + 3 : 4 * half + 4, :leaves] = width
    for r in range(half):
        out[pl.ds(r, 3, stride=half), :] = offsets[:, r * LANES : (r + 1) * LANES]
    beads = per_leaf(counts[...].astype(jnp.float32), half)
    slot = iota((half, LANES), 1) & (BCAP - 1)
    out[3 * half : 4 * half, :] = jnp.where(slot.astype(jnp.float32) < beads, charges[...], 0.0)

    spread = per_leaf(width, half)
    for ch in range(3):
        center = per_leaf(out[4 * half + ch : 4 * half + ch + 1, :leaves], half)
        placed[ch * half : (ch + 1) * half, :] = center + spread * out[ch * half : (ch + 1) * half, :]
    placed[3 * half :, :] = out[3 * half : 4 * half, :]

    sends = send_boxes.shape[1]
    lane = iota((8, LANES), 1)
    for block in range(sends // 16):
        picked = []
        for c in range(2):
            column = block * 16 + 2 * iota((8, sends), 0) + c
            box = jnp.sum(
                jnp.where(iota((8, sends), 1) == column, send_boxes[...].astype(jnp.float32), 0.0),
                axis=1, keepdims=True,
            ).astype(jnp.int32)
            width_here = jnp.sum(
                jnp.where(iota((8, leaves), 1) == box, width, 0.0), axis=1, keepdims=True
            )
            row_of = jnp.broadcast_to(box >> 1, (8, LANES))
            found = [jnp.zeros((8, LANES), jnp.float32)] * 4
            for r in range(half):
                here = row_of == r
                for ch in range(4):
                    found[ch] = jnp.where(here, out[ch * half + r : ch * half + r + 1, :], found[ch])
            aligned = jnp.broadcast_to((box & 1) == c, (8, LANES))
            found = [jnp.where(aligned, x, pltpu.roll(x, BCAP, 1)) for x in found]
            picked.append(found + [jnp.broadcast_to(width_here, (8, LANES))])
        for ch in range(5):
            blocks[pl.ds(block * 64 + ch, 8, stride=8), :] = jnp.where(
                lane < BCAP, picked[0][ch], picked[1][ch]
            )
        for ch in range(5, 8):
            blocks[pl.ds(block * 64 + ch, 8, stride=8), :] = jnp.zeros((8, LANES), jnp.float32)


def own_kernel(
    pair, packed, up_inverse, signs, table_high, table_low, spectra,
    high_table, low_table, density, checks, sems,
):
    half = (packed.shape[0] - 8) // 4
    copies = [
        pltpu.make_async_copy(table_high, high_table, sems.at[0]),
        pltpu.make_async_copy(table_low, low_table, sems.at[1]),
    ]
    for copy in copies:
        copy.start()
    density[...] = jnp.zeros(density.shape, jnp.float32)
    width = per_leaf(packed[4 * half + 3 : 4 * half + 4, :], half)
    for block in range(half // 8):
        rows = [packed[c * half + block * 8 : c * half + block * 8 + 8, :] for c in range(4)]
        density[block * 16 : block * 16 + 16, :Q] = upward(
            rows[:3], rows[3], width[block * 8 : block * 8 + 8], up_inverse[...], checks
        )
    sign = jnp.where(pair[0] == 1, signs[1:2, :], signs[0:1, :])
    for copy in copies:
        copy.wait()
    store_spectra(transform(density[...] * sign, high_table[...], low_table[...]), spectra, 0)


def far_kernel(
    sources, kinds, counts, pair_ref, arrived, up_inverse, signs, last_bins,
    table_high, table_low, translations, own_spectra, kept, sent,
    spectra, kernels, high_table, low_table, density, totals, checks, result, sems,
):
    leaves, entries = sources.shape
    half = leaves // 2
    blocks = arrived.shape[0] // 64
    kind_count = translations.shape[0]
    pair = pair_ref[0]

    table_copies = [
        pltpu.make_async_copy(table_high, high_table, sems.at[2 * TILES - 2]),
        pltpu.make_async_copy(table_low, low_table, sems.at[2 * TILES - 1]),
    ]
    kernel_copies = [
        pltpu.make_async_copy(
            translations.at[:, pl.ds(c, 1), pl.ds(t * LANES, LANES)],
            kernels.at[pl.ds(0, kind_count), pl.ds(8 * c + t, 1), :],
            sems.at[c * (TILES - 1) + t],
        )
        for c in range(2)
        for t in range(TILES - 1)
    ]
    own_copy = pltpu.make_async_copy(
        own_spectra, spectra.at[pl.ds(0, leaves * ROWS), :], sems.at[2 * TILES]
    )
    for copy in table_copies + kernel_copies + [own_copy]:
        copy.start()
    for c in range(2):
        row = 8 * c + TILES - 1
        kernels[:kind_count, row : row + 1, :] = last_bins[:, c : c + 1, :]
    kernels[kind_count] = jnp.zeros((ROWS, LANES), jnp.float32)

    density[...] = jnp.zeros(density.shape, jnp.float32)

    def arrive(block, carry):
        rows = [
            arrived[pl.ds(pl.multiple_of(block * 64, 64) + ch, 8, stride=8), :] for ch in range(5)
        ]
        density[pl.ds(pl.multiple_of(block * 16, 16), 16), :Q] = upward(
            rows[:3], rows[3], rows[4], up_inverse[...], checks
        )
        return carry

    if blocks == 1:
        arrive(0, 0)
    else:
        lax.fori_loop(0, blocks, arrive, 0)
    sign = jnp.where(pair == 1, signs[1:2, :], signs[0:1, :])
    for copy in table_copies:
        copy.wait()
    store_spectra(transform(density[...] * sign, high_table[...], low_table[...]), spectra, leaves)
    for copy in kernel_copies + [own_copy]:
        copy.wait()

    def translate(leaf, carry):
        live = counts[leaf]
        sums = [[None] * 4, [None] * 4]
        for entry in range(entries):
            source = sources[leaf, entry]
            kind = kinds[leaf, entry]
            if entry >= entries // 2:
                kind = jnp.where(entry < live, kind, kind_count)
            k_re = kernels[kind, :8, :]
            k_im = kernels[kind, 8:, :]
            start = pl.multiple_of(source * ROWS, ROWS)
            s_re = spectra[pl.ds(start, 8), :]
            s_im = spectra[pl.ds(start + 8, 8), :]
            terms = (k_re * s_re, k_im * s_im, k_re * s_im, k_im * s_re)
            side = sums[entry % 2]
            for n, term in enumerate(terms):
                side[n] = term if side[n] is None else side[n] + term
        rr, ii, ri, ir = [a + b for a, b in zip(*sums)]
        start = pl.multiple_of(leaf * ROWS, ROWS)
        totals[pl.ds(start, 8), :] = rr - ii
        totals[pl.ds(start + 8, 8), :] = ri + ir
        return carry

    lax.fori_loop(0, leaves, translate, 0, unroll=4)

    wide_lane = iota((leaves, LANES), 1)
    columns = []
    for c in range(2):
        for t in range(TILES):
            rows = totals[pl.ds(c * 8 + t, leaves, stride=ROWS), :]
            if t == TILES - 1:
                rows = jnp.where(wide_lane < BINS - t * LANES, rows, 0.0)
            columns.append(rows)
    high, low = split(jnp.concatenate(columns, 1))
    across = (((1,), (1,)), ((), ()))
    both = lax.dot_general(
        jnp.concatenate([high, low], 0), high_table[...], across,
        preferred_element_type=jnp.float32,
    )
    check = both[:leaves] + both[leaves:] + lax.dot_general(
        high, low_table[...], across, preferred_element_type=jnp.float32
    )
    result[...] = (check * (sign * (1.0 / G)))[:, :Q]
    kept[...] = result[pl.ds(pl.multiple_of(pair * half, 8), half), :]
    sent[...] = result[pl.ds(pl.multiple_of((1 - pair) * half, 8), half), :]


def near_kernel(
    near_source, pair_ref, owner_ref, swapped, placed, passed, out, table, targets, sums
):
    entries, leaves = near_source.shape
    half = leaves // 2
    pair = pair_ref[0]
    low = iota((half, LANES), 1) < BCAP
    swapped_from = jnp.where(((owner_ref[0] & 1) ^ pair) == 1, 0, 2)
    for n, rows_of in ((swapped_from, swapped), (1, placed), (2 - swapped_from, passed)):
        first = n * (leaves * 8)
        for ch in range(4):
            rows = rows_of[ch * half : (ch + 1) * half, :]
            turned = pltpu.roll(rows, BCAP, 1)
            table[pl.ds(first + ch, half, stride=16), :] = jnp.where(low, rows, turned)
            table[pl.ds(first + 8 + ch, half, stride=16), :] = jnp.where(low, turned, rows)
    for ch in range(3):
        mine = placed[pl.ds(pl.multiple_of(ch * half + pair * (half // 2), 8), half // 2), :]
        flipped = mine.T
        for r in range(half // 2):
            for h in range(2):
                start = ((2 * r + h) * 3 + ch) * BCAP
                targets[pl.ds(start, BCAP), :] = jnp.broadcast_to(
                    flipped[h * BCAP : (h + 1) * BCAP, r : r + 1], (BCAP, LANES)
                )
    low = iota((8, LANES), 1) < BCAP

    def one_leaf(t, carry):
        leaf = pair * half + t
        start = pl.multiple_of(t * 3 * BCAP, 8)
        tx, ty, tz = [targets[pl.ds(start + ch * BCAP, BCAP), :] for ch in range(3)]
        total = jnp.zeros((BCAP, LANES), jnp.float32)
        for n in range(entries // 2):
            left = pl.multiple_of(near_source[2 * n, leaf] * 8, 8)
            right = pl.multiple_of(near_source[2 * n + 1, leaf] * 8, 8)
            both = jnp.where(low, table[pl.ds(left, 8), :], table[pl.ds(right, 8), :])
            gx, gy, gz = tx - both[0:1], ty - both[1:2], tz - both[2:3]
            squared = gx * gx + gy * gy + (gz * gz + softening)
            total = total + lax.rsqrt(squared) * both[3:4]
        sums[pl.ds(pl.multiple_of(t * BCAP, 8), BCAP), :] = total
        return carry

    lax.fori_loop(0, half, one_leaf, 0, unroll=2)
    for r in range(half // 2):
        block = sums[r * LANES : (r + 1) * LANES, :].T
        out[r : r + 1, :] = jnp.sum(block, axis=0, keepdims=True)


def final_kernel(
    pair_ref, packed, kept, received, down_inverse, near, counts, decay_rate, stress,
    potential, new_stress, densities,
):
    half = (packed.shape[0] - 8) // 4
    rows = half // 2
    start = pl.multiple_of(pair_ref[0] * rows, 8)
    first = pair_ref[0] * half
    leaf_of = 2 * (iota((half, LANES), 1) & 7) + (iota((half, LANES), 1) >> 6)
    spread = jnp.where(iota((half, LANES), 0) == leaf_of, 1.0, 0.0)
    check = kept[...] + received[...]
    density = jnp.dot(
        check, down_inverse[...], precision=precise, preferred_element_type=jnp.float32
    )
    densities[...] = lax.dot_general(
        density, spread, (((0,), (0,)), ((), ())), precision=precise,
        preferred_element_type=jnp.float32,
    )
    width = block_transpose(per_leaf(packed[4 * half + 3 : 4 * half + 4, :], rows, first))
    offsets = [
        block_transpose(packed[pl.ds(pl.multiple_of(c * half + start, 8), rows), :])
        for c in range(3)
    ]
    total = None
    for q, kernel in surface_kernels(offsets, width):
        term = kernel * densities[q : q + 1, :]
        total = term if total is None else total + term
    combined = block_transpose(total) + near[...]
    beads = per_leaf(counts[...].astype(jnp.float32), rows, first)
    slot = iota((rows, LANES), 1) & (BCAP - 1)
    occupied = slot.astype(jnp.float32) < beads
    decay = per_leaf(decay_rate[...], rows)
    potential[...] = jnp.where(occupied, combined, 0.0)
    new_stress[...] = jnp.where(occupied, decay * stress[...] + combined, 0.0)


VMEM = pl.BlockSpec(memory_space=pltpu.VMEM)
SMEM = pl.BlockSpec(memory_space=pltpu.SMEM)
ANY = pl.BlockSpec(memory_space=pl.ANY)
MIB = 1024 * 1024


def call(kernel, outs, in_specs, scratch=(), limit=40, grid=(), flops=0, bytes_accessed=0):
    return pl.pallas_call(
        kernel,
        out_shape=outs,
        grid=grid,
        in_specs=in_specs,
        out_specs=jax.tree.map(lambda _: VMEM, outs),
        scratch_shapes=list(scratch),
        compiler_params=pltpu.CompilerParams(vmem_limit_bytes=limit * MIB),
        cost_estimate=pl.CostEstimate(
            flops=flops, bytes_accessed=bytes_accessed, transcendentals=0
        ),
    )


def body(
    offsets,
    charges,
    stress,
    decay_rate,
    morton_keys,
    levels,
    bead_counts,
    send_boxes,
    m2l_source,
    m2l_type,
    m2l_count,
    near_source,
    up_inverse,
    down_inverse,
    translations,
):
    f32 = jnp.float32
    leaves = morton_keys.shape[0]
    half = leaves // 2
    parts = lax.axis_size("wide") * lax.axis_size("narrow")
    high, low = [jnp.asarray(x) for x in transform_table()]
    signs = jnp.asarray(sign_rows())
    pair = lax.axis_index("pair").reshape(1)
    owner = (
        lax.axis_index("wide") * lax.axis_size("narrow") + lax.axis_index("narrow")
    ).reshape(1)
    kind_count = translations.shape[0]
    bf16 = jnp.bfloat16

    packed, blocks, placed = call(
        pack_kernel,
        [
            jax.ShapeDtypeStruct((4 * half + 8, LANES), f32),
            jax.ShapeDtypeStruct((8 * parts, LANES), f32),
            jax.ShapeDtypeStruct((4 * half, LANES), f32),
        ],
        [VMEM] * 6,
        limit=62,
    )(
        offsets, charges.reshape(half, LANES), morton_keys.reshape(1, leaves),
        levels.reshape(1, leaves), bead_counts.reshape(1, leaves), send_boxes,
    )
    arrived = lax.all_to_all(
        blocks.reshape(parts, 8, LANES), PARTS, split_axis=0, concat_axis=0, tiled=True
    ).reshape(8 * parts, LANES)
    swaps = [(2 * d, 2 * (d ^ 1)) for d in range(parts)]
    for d in range(1, parts - 1, 2):
        swaps += [(2 * d + 1, 2 * d + 3), (2 * d + 3, 2 * d + 1)]
    swapped = lax.ppermute(placed, PARTS + ("pair",), swaps)
    own_spectra = call(
        own_kernel,
        jax.ShapeDtypeStruct((leaves * ROWS, LANES), f32),
        [SMEM] + [VMEM] * 3 + [ANY] * 2,
        [
            pltpu.VMEM(high.shape, bf16),
            pltpu.VMEM(low.shape, bf16),
            pltpu.VMEM((leaves, QPAD), f32),
            pltpu.VMEM((Q * 8, LANES), f32),
            pltpu.SemaphoreType.DMA((2,)),
        ],
        limit=62,
        flops=10**10,
        bytes_accessed=4 * 10**6,
    )(pair, packed, up_inverse, signs, high, low)
    passed = lax.ppermute(swapped, "pair", [(0, 1), (1, 0)])

    kept, sent = call(
        far_kernel,
        [jax.ShapeDtypeStruct((half, Q), f32)] * 2,
        [SMEM] * 4 + [VMEM] * 3
        + [pl.BlockSpec((kind_count, 2, LANES), lambda i: (0, 0, TILES - 1))]
        + [ANY] * 4,
        [
            pltpu.VMEM(((leaves + 2 * parts) * ROWS, LANES), f32),
            pltpu.VMEM((kind_count + 1, ROWS, LANES), f32),
            pltpu.VMEM(high.shape, bf16),
            pltpu.VMEM(low.shape, bf16),
            pltpu.VMEM((2 * parts, QPAD), f32),
            pltpu.VMEM((leaves * ROWS, LANES), f32),
            pltpu.VMEM((Q * 8, LANES), f32),
            pltpu.VMEM((leaves, Q), f32),
            pltpu.SemaphoreType.DMA((2 * TILES + 1,)),
        ],
        limit=62,
        grid=(1,),
        flops=2 * 10**9,
        bytes_accessed=8 * 10**6,
    )(
        m2l_source, m2l_type, m2l_count, pair, arrived, up_inverse, signs, translations,
        high, low, translations, own_spectra,
    )
    received = lax.ppermute(sent, "pair", [(0, 1), (1, 0)])
    near = call(
        near_kernel,
        jax.ShapeDtypeStruct((half // 2, LANES), f32),
        [SMEM] * 3 + [VMEM] * 3,
        [
            pltpu.VMEM((3 * leaves * 8, LANES), f32),
            pltpu.VMEM((half * 3 * BCAP, LANES), f32),
            pltpu.VMEM((half * BCAP, LANES), f32),
        ],
        flops=10**9,
        bytes_accessed=4 * 10**6,
    )(near_source.T, pair, owner, swapped, placed, passed)

    out = jax.ShapeDtypeStruct((half // 2, LANES), f32)
    potential, new_stress = call(
        final_kernel,
        [out, out],
        [SMEM] + [VMEM] * 8,
        [pltpu.VMEM((Q, LANES), f32)],
    )(
        pair, packed, kept, received, down_inverse, near, bead_counts.reshape(1, leaves),
        decay_rate.reshape(1, half), stress.reshape(half // 2, LANES),
    )
    return potential.reshape(-1), new_stress.reshape(-1)


def solution(mesh):
    return jax.shard_map(
        body,
        mesh=mesh,
        in_specs=(
            P(None, ("groups", "wide", "narrow")),
            P(("groups", "wide", "narrow")),
            P(("groups", "wide", "narrow", "pair")),
            P(("groups", "wide", "narrow", "pair")),
            P(("groups", "wide", "narrow")),
            P(("groups", "wide", "narrow")),
            P(("groups", "wide", "narrow")),
            P(("groups", "wide", "narrow"), None),
            P(("groups", "wide", "narrow"), None),
            P(("groups", "wide", "narrow"), None),
            P(("groups", "wide", "narrow")),
            P(("groups", "wide", "narrow"), None),
            P(),
            P(),
            P(None, None, "pair"),
        ),
        out_specs=(
            P(("groups", "wide", "narrow", "pair")),
            P(("groups", "wide", "narrow", "pair")),
        ),
        check_vma=False,
    )
```

```python
import functools

import jax
import jax.numpy as jnp
import ml_dtypes
import numpy as np
from jax import lax
from jax.experimental import pallas as pl
from jax.experimental.pallas import tpu as pltpu
from jax.sharding import PartitionSpec as P

PGRID = 12
G = 1728
MAXL = 10
BCAP = 64
Q = 152
QPAD = 160
LANES = 128
BINS = 864
TILES = 7
ROWS = 32
precise = lax.Precision.HIGHEST
softening = 0.04
surface_reach = 1.25
CELLS = [
    (i, j, k)
    for i in range(6)
    for j in range(6)
    for k in range(6)
    if 0 in (i, j, k) or 5 in (i, j, k)
]
PARTS = ("wide", "narrow")


def transform_table():
    cells = np.array(CELLS)
    bins = np.arange(BINS)
    freq = np.stack([bins // 144, bins // 12 % 12, bins % 12])
    angle = (cells @ freq % PGRID) * (2.0 * np.pi / PGRID)
    table = np.zeros((QPAD, 2 * TILES * LANES))
    table[:Q, :BINS] = np.cos(angle)
    table[:Q, TILES * LANES : TILES * LANES + BINS] = -np.sin(angle)
    table[np.abs(table) < 1e-9] = 0.0
    high = table.astype(ml_dtypes.bfloat16)
    low = (table - high.astype(np.float64)).astype(ml_dtypes.bfloat16)
    return high, low


def sign_rows():
    rows = np.zeros((8, QPAD), np.float32)
    rows[0, :Q] = 1.0
    rows[1, :Q] = [(-1.0) ** i for i, _, _ in CELLS]
    return rows


def iota(shape, dim):
    return lax.broadcasted_iota(jnp.int32, shape, dim)


def per_leaf(values, count, first=0):
    shape = (count, values.shape[1])
    leaf, lane = first + 2 * iota(shape, 0), iota(shape, 1)
    even = jnp.sum(jnp.where(lane == leaf, values, 0.0), axis=1, keepdims=True)
    odd = jnp.sum(jnp.where(lane == leaf + 1, values, 0.0), axis=1, keepdims=True)
    return jnp.where(iota((count, LANES), 1) < BCAP, even, odd)


def block_transpose(x):
    lane, row = iota(x.shape, 1), iota(x.shape, 0)
    for k in (1, 2, 4):
        row_bit, lane_bit = (row & k) != 0, (lane & k) != 0
        below = pltpu.roll(pltpu.roll(x, 8 - k, 0), k, 1)
        above = pltpu.roll(pltpu.roll(x, k, 0), LANES - k, 1)
        x = jnp.where(row_bit == lane_bit, x, jnp.where(lane_bit, below, above))
    return x


def split(x):
    high = x.astype(jnp.bfloat16)
    return high, (x - high.astype(jnp.float32)).astype(jnp.bfloat16)


def axis_squares(offset, width):
    area = width * width
    planes = [surface_reach * 0.5 * (i - 2.5) / 2.5 for i in range(6)]
    return [(plane - offset) * (plane - offset) * area for plane in planes]


def surface_kernels(offsets, width):
    gx, gy, gz = [axis_squares(offset, width) for offset in offsets]
    gz = [g + softening for g in gz]
    last, gxy = None, None
    for q, (i, j, k) in enumerate(CELLS):
        if last != (i, j):
            last, gxy = (i, j), gx[i] + gy[j]
        yield q, lax.rsqrt(gxy + gz[k])


def upward(offsets, weights, width, up_inverse, checks):
    offsets = [block_transpose(x) for x in offsets]
    weights, width = block_transpose(weights), block_transpose(width)
    for q, kernel in surface_kernels(offsets, width):
        checks[pl.ds(8 * q, 8), :] = kernel * weights
    check = checks[pl.ds(0, Q, stride=8), :]
    for s in range(1, 8):
        check = check + checks[pl.ds(s, Q, stride=8), :]
    density = lax.dot_general(
        check, up_inverse, (((0,), (0,)), ((), ())), precision=precise,
        preferred_element_type=jnp.float32,
    )
    density = density.reshape(2, 8, 8, Q)
    total = density[:, 0]
    for g in range(1, 8):
        total = total + density[:, g]
    return total.reshape(16, Q)


def store_spectra(density, table_high, table_low, target):
    count = density.shape[0] // 2
    high, low = split(density)
    both = jnp.concatenate([high, low], 0)
    for first in range(0, 2 * TILES, 2):
        columns = pl.ds(first * LANES, 2 * LANES)
        part = jnp.dot(both, table_high[:, columns], preferred_element_type=jnp.float32)
        spectra = part[: 2 * count] + part[2 * count :] + jnp.dot(
            high, table_low[:, columns], preferred_element_type=jnp.float32
        )
        for tile in range(first, first + 2):
            for side in range(2):
                for block in range(count // 16):
                    for h in range(2):
                        row = side * count + block * 16 + h * 8
                        start = (block * 16 + h) * ROWS + 16 * side + 8 * (tile // TILES) + tile % TILES
                        target[pl.ds(start, 8, stride=2 * ROWS), :] = spectra[
                            row : row + 8, (tile - first) * LANES : (tile - first + 1) * LANES
                        ]


def pack_kernel(
    kind_count, offsets, charges, keys, levels, counts, send_boxes, m2l_source, m2l_type, m2l_count,
    out, blocks, placed, sources, kinds,
):
    leaves = keys.shape[1]
    half = leaves // 2
    out[4 * half :, :] = jnp.zeros((8, LANES), jnp.float32)
    width = jnp.left_shift(jnp.ones_like(levels[...]), MAXL - levels[...]).astype(jnp.float32)
    for a in range(3):
        summed = jnp.zeros_like(keys[...])
        for bit in range(MAXL):
            summed = summed + (jnp.right_shift(keys[...], 3 * bit + a) & 1) * (1 << bit)
        out[4 * half + a : 4 * half + a + 1, :leaves] = summed.astype(jnp.float32) + 0.5 * width
    out[4 * half + 3 : 4 * half + 4, :leaves] = width
    for r in range(half):
        out[pl.ds(r, 3, stride=half), :] = offsets[:, r * LANES : (r + 1) * LANES]
    beads = per_leaf(counts[...].astype(jnp.float32), half)
    slot = iota((half, LANES), 1) & (BCAP - 1)
    out[3 * half : 4 * half, :] = jnp.where(slot.astype(jnp.float32) < beads, charges[...], 0.0)

    entry = iota(m2l_type.shape, 1)
    square = (leaves, leaves)
    live = jnp.sum(
        jnp.where(iota(square, 0) == iota(square, 1), m2l_count[...].astype(jnp.float32), 0.0),
        axis=1, keepdims=True,
    )
    kinds[...] = jnp.where(entry.astype(jnp.float32) < live, m2l_type[...], kind_count)
    sources[...] = m2l_source[...] * ROWS

    spread = per_leaf(width, half)
    for ch in range(3):
        center = per_leaf(out[4 * half + ch : 4 * half + ch + 1, :leaves], half)
        placed[ch * half : (ch + 1) * half, :] = center + spread * out[ch * half : (ch + 1) * half, :]
    placed[3 * half :, :] = out[3 * half : 4 * half, :]

    sends = send_boxes.shape[1]
    lane = iota((8, LANES), 1)
    for block in range(sends // 16):
        picked = []
        for c in range(2):
            column = block * 16 + 2 * iota((8, sends), 0) + c
            box = jnp.sum(
                jnp.where(iota((8, sends), 1) == column, send_boxes[...].astype(jnp.float32), 0.0),
                axis=1, keepdims=True,
            ).astype(jnp.int32)
            width_here = jnp.sum(
                jnp.where(iota((8, leaves), 1) == box, width, 0.0), axis=1, keepdims=True
            )
            row_of = jnp.broadcast_to(box >> 1, (8, LANES))
            found = [jnp.zeros((8, LANES), jnp.float32)] * 4
            for r in range(half):
                here = row_of == r
                for ch in range(4):
                    found[ch] = jnp.where(here, out[ch * half + r : ch * half + r + 1, :], found[ch])
            aligned = jnp.broadcast_to((box & 1) == c, (8, LANES))
            found = [jnp.where(aligned, x, pltpu.roll(x, BCAP, 1)) for x in found]
            picked.append(found + [jnp.broadcast_to(width_here, (8, LANES))])
        for ch in range(5):
            blocks[pl.ds(block * 64 + ch, 8, stride=8), :] = jnp.where(
                lane < BCAP, picked[0][ch], picked[1][ch]
            )
        for ch in range(5, 8):
            blocks[pl.ds(block * 64 + ch, 8, stride=8), :] = jnp.zeros((8, LANES), jnp.float32)


def own_kernel(packed, up_inverse, density, checks):
    half = (packed.shape[0] - 8) // 4
    density[...] = jnp.zeros(density.shape, jnp.float32)
    width = per_leaf(packed[4 * half + 3 : 4 * half + 4, :], half)
    for block in range(half // 8):
        rows = [packed[c * half + block * 8 : c * half + block * 8 + 8, :] for c in range(4)]
        density[block * 16 : block * 16 + 16, :Q] = upward(
            rows[:3], rows[3], width[block * 8 : block * 8 + 8], up_inverse[...], checks
        )


def far_kernel(
    sources, kinds, pair_ref, packed, arrived, own_density, up_inverse, down_inverse, signs,
    last_bins, other_last_bins, table_high, table_low, translations, other_translations, out,
    spectra, kernels, high_table, low_table, density, totals, checks, densities, sems,
):
    leaves, entries = sources.shape
    half = leaves // 2
    rows = half // 2
    blocks = arrived.shape[0] // 64
    kind_count = translations.shape[0]
    pair = pair_ref[0]

    table_copies = [
        pltpu.make_async_copy(table_high, high_table, sems.at[0]),
        pltpu.make_async_copy(table_low, low_table, sems.at[1]),
    ]
    kernel_copies = []
    for side, (bins, last) in enumerate(
        ((translations, last_bins), (other_translations, other_last_bins))
    ):
        for c in range(2):
            for t in range(TILES - 1):
                kernel_copies.append(pltpu.make_async_copy(
                    bins.at[:, pl.ds(c, 1), pl.ds(t * LANES, LANES)],
                    kernels.at[pl.ds(0, kind_count), pl.ds(16 * side + 8 * c + t, 1), :],
                    sems.at[2 + len(kernel_copies)],
                ))
    for copy in table_copies + kernel_copies:
        copy.start()
    for side, last in enumerate((last_bins, other_last_bins)):
        for c in range(2):
            row = 16 * side + 8 * c + TILES - 1
            kernels[:kind_count, row : row + 1, :] = last[:, c : c + 1, :]
    kernels[kind_count] = jnp.zeros((ROWS, LANES), jnp.float32)

    density[:leaves, :] = own_density[...]
    density[leaves:, :] = jnp.zeros((density.shape[0] - leaves, QPAD), jnp.float32)

    def arrive(block, carry):
        beads = [
            arrived[pl.ds(pl.multiple_of(block * 64, 64) + ch, 8, stride=8), :] for ch in range(5)
        ]
        density[pl.ds(pl.multiple_of(leaves + block * 16, 16), 16), :Q] = upward(
            beads[:3], beads[3], beads[4], up_inverse[...], checks
        )
        return carry

    if blocks == 1:
        arrive(0, 0)
    else:
        lax.fori_loop(0, blocks, arrive, 0)
    sign = jnp.where(pair == 1, signs[1:2, :], signs[0:1, :])
    other_sign = jnp.where(pair == 1, signs[0:1, :], signs[1:2, :])
    for copy in table_copies:
        copy.wait()
    store_spectra(
        jnp.concatenate([density[...] * sign, density[...] * other_sign], 0),
        high_table, low_table, spectra,
    )
    for copy in kernel_copies:
        copy.wait()

    def translate(t, carry):
        leaf = pair * half + t
        sums = [[None] * 4, [None] * 4]
        for entry in range(entries):
            kind = kinds[leaf, entry]
            start = pl.multiple_of(sources[leaf, entry], ROWS)
            for side in range(2):
                k_re = kernels[kind, 16 * side : 16 * side + 8, :]
                k_im = kernels[kind, 16 * side + 8 : 16 * side + 16, :]
                s_re = spectra[pl.ds(start + 16 * side, 8), :]
                s_im = spectra[pl.ds(start + 16 * side + 8, 8), :]
                terms = (k_re * s_re, k_im * s_im, k_re * s_im, k_im * s_re)
                for n, term in enumerate(terms):
                    sums[side][n] = term if sums[side][n] is None else sums[side][n] + term
        start = pl.multiple_of(t * ROWS, ROWS)
        for side in range(2):
            rr, ii, ri, ir = sums[side]
            totals[pl.ds(start + 16 * side, 8), :] = rr - ii
            totals[pl.ds(start + 16 * side + 8, 8), :] = ri + ir
        return carry

    lax.fori_loop(0, half, translate, 0, unroll=2)

    lane = iota((half, LANES), 1)
    sides = []
    for side in range(2):
        columns = []
        for c in range(2):
            for t in range(TILES):
                line = totals[pl.ds(16 * side + c * 8 + t, half, stride=ROWS), :]
                if t == TILES - 1:
                    line = jnp.where(lane < BINS - t * LANES, line, 0.0)
                columns.append(line)
        sides.append(jnp.concatenate(columns, 1))
    high, low = split(jnp.concatenate(sides, 0))
    across = (((1,), (1,)), ((), ()))
    both = lax.dot_general(
        jnp.concatenate([high, low], 0), high_table[...], across,
        preferred_element_type=jnp.float32,
    )
    check = both[:leaves] + both[leaves:] + lax.dot_general(
        high, low_table[...], across, preferred_element_type=jnp.float32
    )
    check = (check[:half] * sign + check[half:] * other_sign)[:, :Q] * (1.0 / G)

    leaf_of = 2 * (lane & 7) + (lane >> 6)
    spread = jnp.where(iota((half, LANES), 0) == leaf_of, 1.0, 0.0)
    down = jnp.dot(
        check, down_inverse[...], precision=precise, preferred_element_type=jnp.float32
    )
    densities[...] = lax.dot_general(
        down, spread, (((0,), (0,)), ((), ())), precision=precise,
        preferred_element_type=jnp.float32,
    )
    width = block_transpose(
        per_leaf(packed[4 * half + 3 : 4 * half + 4, :], rows, pair * half)
    )
    offsets = [
        block_transpose(packed[pl.ds(pl.multiple_of(c * half + pair * rows, 8), rows), :])
        for c in range(3)
    ]
    total = None
    for q, kernel in surface_kernels(offsets, width):
        term = kernel * densities[q : q + 1, :]
        total = term if total is None else total + term
    out[...] = block_transpose(total)


def near_kernel(
    near_source, pair_ref, owner_ref, swapped, placed, passed, far, counts, decay_rate, stress,
    potential, new_stress, table, targets, sums,
):
    entries, leaves = near_source.shape
    half = leaves // 2
    pair = pair_ref[0]
    low = iota((half, LANES), 1) < BCAP
    swapped_from = jnp.where(((owner_ref[0] & 1) ^ pair) == 1, 0, 2)
    for n, rows_of in ((swapped_from, swapped), (1, placed), (2 - swapped_from, passed)):
        first = n * (leaves * 8)
        for ch in range(4):
            rows = rows_of[ch * half : (ch + 1) * half, :]
            turned = pltpu.roll(rows, BCAP, 1)
            table[pl.ds(first + ch, half, stride=16), :] = jnp.where(low, rows, turned)
            table[pl.ds(first + 8 + ch, half, stride=16), :] = jnp.where(low, turned, rows)
    for ch in range(3):
        mine = placed[pl.ds(pl.multiple_of(ch * half + pair * (half // 2), 8), half // 2), :]
        flipped = mine.T
        for r in range(half // 2):
            for h in range(2):
                start = ((2 * r + h) * 3 + ch) * BCAP
                targets[pl.ds(start, BCAP), :] = jnp.broadcast_to(
                    flipped[h * BCAP : (h + 1) * BCAP, r : r + 1], (BCAP, LANES)
                )
    low = iota((8, LANES), 1) < BCAP

    def one_leaf(t, carry):
        leaf = pair * half + t
        start = pl.multiple_of(t * 3 * BCAP, 8)
        tx, ty, tz = [targets[pl.ds(start + ch * BCAP, BCAP), :] for ch in range(3)]
        total = jnp.zeros((BCAP, LANES), jnp.float32)
        for n in range(entries // 2):
            left = pl.multiple_of(near_source[2 * n, leaf] * 8, 8)
            right = pl.multiple_of(near_source[2 * n + 1, leaf] * 8, 8)
            both = jnp.where(low, table[pl.ds(left, 8), :], table[pl.ds(right, 8), :])
            gx, gy, gz = tx - both[0:1], ty - both[1:2], tz - both[2:3]
            squared = gx * gx + gy * gy + (gz * gz + softening)
            total = total + lax.rsqrt(squared) * both[3:4]
        sums[pl.ds(pl.multiple_of(t * BCAP, 8), BCAP), :] = total
        return carry

    lax.fori_loop(0, half, one_leaf, 0, unroll=2)
    rows = half // 2
    for r in range(rows):
        block = sums[r * LANES : (r + 1) * LANES, :].T
        potential[r : r + 1, :] = jnp.sum(block, axis=0, keepdims=True)
    combined = potential[...] + far[...]
    beads = per_leaf(counts[...].astype(jnp.float32), rows, pair * half)
    slot = iota((rows, LANES), 1) & (BCAP - 1)
    occupied = slot.astype(jnp.float32) < beads
    decay = per_leaf(decay_rate[...], rows)
    potential[...] = jnp.where(occupied, combined, 0.0)
    new_stress[...] = jnp.where(occupied, decay * stress[...] + combined, 0.0)


VMEM = pl.BlockSpec(memory_space=pltpu.VMEM)
SMEM = pl.BlockSpec(memory_space=pltpu.SMEM)
ANY = pl.BlockSpec(memory_space=pl.ANY)
MIB = 1024 * 1024


def call(kernel, outs, in_specs, scratch=(), limit=40, grid=(), flops=0, bytes_accessed=0):
    return pl.pallas_call(
        kernel,
        out_shape=outs,
        grid=grid,
        in_specs=in_specs,
        out_specs=jax.tree.map(lambda _: VMEM, outs),
        scratch_shapes=list(scratch),
        compiler_params=pltpu.CompilerParams(vmem_limit_bytes=limit * MIB),
        cost_estimate=pl.CostEstimate(
            flops=flops, bytes_accessed=bytes_accessed, transcendentals=0
        ),
    )


def body(
    offsets,
    charges,
    stress,
    decay_rate,
    morton_keys,
    levels,
    bead_counts,
    send_boxes,
    m2l_source,
    m2l_type,
    m2l_count,
    near_source,
    up_inverse,
    down_inverse,
    translations,
):
    f32 = jnp.float32
    leaves = morton_keys.shape[0]
    half = leaves // 2
    parts = lax.axis_size("wide") * lax.axis_size("narrow")
    high, low = [jnp.asarray(x) for x in transform_table()]
    signs = jnp.asarray(sign_rows())
    pair = lax.axis_index("pair").reshape(1)
    owner = (
        lax.axis_index("wide") * lax.axis_size("narrow") + lax.axis_index("narrow")
    ).reshape(1)
    kind_count = translations.shape[0]
    bf16 = jnp.bfloat16

    other_translations = lax.ppermute(translations, "pair", [(0, 1), (1, 0)])
    packed, blocks, placed, sources, kinds = call(
        functools.partial(pack_kernel, kind_count),
        [
            jax.ShapeDtypeStruct((4 * half + 8, LANES), f32),
            jax.ShapeDtypeStruct((8 * parts, LANES), f32),
            jax.ShapeDtypeStruct((4 * half, LANES), f32),
            jax.ShapeDtypeStruct(m2l_source.shape, jnp.int32),
            jax.ShapeDtypeStruct(m2l_type.shape, jnp.int32),
        ],
        [VMEM] * 9,
        limit=62,
    )(
        offsets, charges.reshape(half, LANES), morton_keys.reshape(1, leaves),
        levels.reshape(1, leaves), bead_counts.reshape(1, leaves), send_boxes,
        m2l_source, m2l_type, m2l_count.reshape(1, leaves),
    )
    arrived = lax.all_to_all(
        blocks.reshape(parts, 8, LANES), PARTS, split_axis=0, concat_axis=0, tiled=True
    ).reshape(8 * parts, LANES)
    swaps = [(2 * d, 2 * (d ^ 1)) for d in range(parts)]
    for d in range(1, parts - 1, 2):
        swaps += [(2 * d + 1, 2 * d + 3), (2 * d + 3, 2 * d + 1)]
    swapped = lax.ppermute(placed, PARTS + ("pair",), swaps)
    own_density = call(
        own_kernel,
        jax.ShapeDtypeStruct((leaves, QPAD), f32),
        [VMEM] * 2,
        [pltpu.VMEM((Q * 8, LANES), f32)],
        limit=62,
        flops=10**10,
        bytes_accessed=4 * 10**6,
    )(packed, up_inverse)
    passed = lax.ppermute(swapped, "pair", [(0, 1), (1, 0)])

    last = pl.BlockSpec((kind_count, 2, LANES), lambda i: (0, 0, TILES - 1))
    far = call(
        far_kernel,
        jax.ShapeDtypeStruct((half // 2, LANES), f32),
        [SMEM] * 3 + [VMEM] * 6 + [last] * 2 + [ANY] * 4,
        [
            pltpu.VMEM(((leaves + 2 * parts) * ROWS, LANES), f32),
            pltpu.VMEM((kind_count + 1, ROWS, LANES), f32),
            pltpu.VMEM(high.shape, bf16),
            pltpu.VMEM(low.shape, bf16),
            pltpu.VMEM((leaves + 2 * parts, QPAD), f32),
            pltpu.VMEM((half * ROWS, LANES), f32),
            pltpu.VMEM((Q * 8, LANES), f32),
            pltpu.VMEM((Q, LANES), f32),
            pltpu.SemaphoreType.DMA((4 * TILES - 2,)),
        ],
        limit=62,
        grid=(1,),
        flops=2 * 10**9,
        bytes_accessed=8 * 10**6,
    )(
        sources, kinds, pair, packed, arrived, own_density, up_inverse, down_inverse, signs,
        translations, other_translations, high, low, translations, other_translations,
    )

    out = jax.ShapeDtypeStruct((half // 2, LANES), f32)
    potential, new_stress = call(
        near_kernel,
        [out, out],
        [SMEM] * 3 + [VMEM] * 7,
        [
            pltpu.VMEM((3 * leaves * 8, LANES), f32),
            pltpu.VMEM((half * 3 * BCAP, LANES), f32),
            pltpu.VMEM((half * BCAP, LANES), f32),
        ],
    )(
        near_source.T, pair, owner, swapped, placed, passed, far, bead_counts.reshape(1, leaves),
        decay_rate.reshape(1, half), stress.reshape(half // 2, LANES),
    )
    return potential.reshape(-1), new_stress.reshape(-1)


def solution(mesh):
    return jax.shard_map(
        body,
        mesh=mesh,
        in_specs=(
            P(None, ("groups", "wide", "narrow")),
            P(("groups", "wide", "narrow")),
            P(("groups", "wide", "narrow", "pair")),
            P(("groups", "wide", "narrow", "pair")),
            P(("groups", "wide", "narrow")),
            P(("groups", "wide", "narrow")),
            P(("groups", "wide", "narrow")),
            P(("groups", "wide", "narrow"), None),
            P(("groups", "wide", "narrow"), None),
            P(("groups", "wide", "narrow"), None),
            P(("groups", "wide", "narrow")),
            P(("groups", "wide", "narrow"), None),
            P(),
            P(),
            P(None, None, "pair"),
        ),
        out_specs=(
            P(("groups", "wide", "narrow", "pair")),
            P(("groups", "wide", "narrow", "pair")),
        ),
        check_vma=False,
    )
```

```python
import functools

import jax
import jax.numpy as jnp
import ml_dtypes
import numpy as np
from jax import lax
from jax.experimental import pallas as pl
from jax.experimental.pallas import tpu as pltpu
from jax.sharding import PartitionSpec as P

PGRID = 12
G = 1728
MAXL = 10
BCAP = 64
Q = 152
QPAD = 160
LANES = 128
BINS = 864
TILES = 7
ROWS = 32
precise = lax.Precision.HIGHEST
softening = 0.04
surface_reach = 1.25
CELLS = [
    (i, j, k)
    for i in range(6)
    for j in range(6)
    for k in range(6)
    if 0 in (i, j, k) or 5 in (i, j, k)
]
PARTS = ("wide", "narrow")


def transform_table():
    cells = np.array(CELLS)
    bins = np.arange(BINS)
    freq = np.stack([bins // 144, bins // 12 % 12, bins % 12])
    angle = (cells @ freq % PGRID) * (2.0 * np.pi / PGRID)
    table = np.zeros((QPAD, 2 * TILES * LANES))
    table[:Q, :BINS] = np.cos(angle)
    table[:Q, TILES * LANES : TILES * LANES + BINS] = -np.sin(angle)
    table[np.abs(table) < 1e-9] = 0.0
    high = table.astype(ml_dtypes.bfloat16)
    low = (table - high.astype(np.float64)).astype(ml_dtypes.bfloat16)
    return high, low


def sign_rows():
    rows = np.zeros((8, QPAD), np.float32)
    rows[0, :Q] = 1.0
    rows[1, :Q] = [(-1.0) ** i for i, _, _ in CELLS]
    return rows


def iota(shape, dim):
    return lax.broadcasted_iota(jnp.int32, shape, dim)


def per_leaf(values, count, first=0):
    shape = (count, values.shape[1])
    leaf, lane = first + 2 * iota(shape, 0), iota(shape, 1)
    even = jnp.sum(jnp.where(lane == leaf, values, 0.0), axis=1, keepdims=True)
    odd = jnp.sum(jnp.where(lane == leaf + 1, values, 0.0), axis=1, keepdims=True)
    return jnp.where(iota((count, LANES), 1) < BCAP, even, odd)


def block_transpose(x):
    lane, row = iota(x.shape, 1), iota(x.shape, 0)
    for k in (1, 2, 4):
        row_bit, lane_bit = (row & k) != 0, (lane & k) != 0
        below = pltpu.roll(pltpu.roll(x, 8 - k, 0), k, 1)
        above = pltpu.roll(pltpu.roll(x, k, 0), LANES - k, 1)
        x = jnp.where(row_bit == lane_bit, x, jnp.where(lane_bit, below, above))
    return x


def split(x):
    high = x.astype(jnp.bfloat16)
    return high, (x - high.astype(jnp.float32)).astype(jnp.bfloat16)


def axis_squares(offset, width):
    area = width * width
    planes = [surface_reach * 0.5 * (i - 2.5) / 2.5 for i in range(6)]
    return [(plane - offset) * (plane - offset) * area for plane in planes]


def surface_kernels(offsets, width):
    gx, gy, gz = [axis_squares(offset, width) for offset in offsets]
    gz = [g + softening for g in gz]
    last, gxy = None, None
    for q, (i, j, k) in enumerate(CELLS):
        if last != (i, j):
            last, gxy = (i, j), gx[i] + gy[j]
        yield q, lax.rsqrt(gxy + gz[k])


def upward(offsets, weights, width, up_inverse, checks):
    offsets = [block_transpose(x) for x in offsets]
    weights, width = block_transpose(weights), block_transpose(width)
    for q, kernel in surface_kernels(offsets, width):
        checks[pl.ds(8 * q, 8), :] = kernel * weights
    check = checks[pl.ds(0, Q, stride=8), :]
    for s in range(1, 8):
        check = check + checks[pl.ds(s, Q, stride=8), :]
    density = lax.dot_general(
        check, up_inverse, (((0,), (0,)), ((), ())), precision=precise,
        preferred_element_type=jnp.float32,
    )
    density = density.reshape(2, 8, 8, Q)
    total = density[:, 0]
    for g in range(1, 8):
        total = total + density[:, g]
    return total.reshape(16, Q)


def store_spectra(density, table_high, table_low, target):
    count = density.shape[0] // 2
    high, low = split(density)
    both = jnp.concatenate([high, low], 0)
    for first in range(0, 2 * TILES, 2):
        columns = pl.ds(first * LANES, 2 * LANES)
        part = jnp.dot(both, table_high[:, columns], preferred_element_type=jnp.float32)
        spectra = part[: 2 * count] + part[2 * count :] + jnp.dot(
            high, table_low[:, columns], preferred_element_type=jnp.float32
        )
        for tile in range(first, first + 2):
            for side in range(2):
                for block in range(count // 16):
                    for h in range(2):
                        row = side * count + block * 16 + h * 8
                        start = (block * 16 + h) * ROWS + 16 * side + 8 * (tile // TILES) + tile % TILES
                        target[pl.ds(start, 8, stride=2 * ROWS), :] = spectra[
                            row : row + 8, (tile - first) * LANES : (tile - first + 1) * LANES
                        ]


def pack_kernel(
    kind_count, offsets, charges, keys, levels, counts, send_boxes, m2l_source, m2l_type, m2l_count,
    out, blocks, placed, sources, kinds,
):
    leaves = keys.shape[1]
    half = leaves // 2
    out[4 * half :, :] = jnp.zeros((8, LANES), jnp.float32)
    width = jnp.left_shift(jnp.ones_like(levels[...]), MAXL - levels[...]).astype(jnp.float32)
    for a in range(3):
        summed = jnp.zeros_like(keys[...])
        for bit in range(MAXL):
            summed = summed + (jnp.right_shift(keys[...], 3 * bit + a) & 1) * (1 << bit)
        out[4 * half + a : 4 * half + a + 1, :leaves] = summed.astype(jnp.float32) + 0.5 * width
    out[4 * half + 3 : 4 * half + 4, :leaves] = width
    for r in range(half):
        out[pl.ds(r, 3, stride=half), :] = offsets[:, r * LANES : (r + 1) * LANES]
    beads = per_leaf(counts[...].astype(jnp.float32), half)
    slot = iota((half, LANES), 1) & (BCAP - 1)
    out[3 * half : 4 * half, :] = jnp.where(slot.astype(jnp.float32) < beads, charges[...], 0.0)

    entry = iota(m2l_type.shape, 1)
    square = (leaves, leaves)
    live = jnp.sum(
        jnp.where(iota(square, 0) == iota(square, 1), m2l_count[...].astype(jnp.float32), 0.0),
        axis=1, keepdims=True,
    )
    kinds[...] = jnp.where(entry.astype(jnp.float32) < live, m2l_type[...], kind_count)
    sources[...] = m2l_source[...] * ROWS

    spread = per_leaf(width, half)
    for ch in range(3):
        center = per_leaf(out[4 * half + ch : 4 * half + ch + 1, :leaves], half)
        placed[ch * half : (ch + 1) * half, :] = center + spread * out[ch * half : (ch + 1) * half, :]
    placed[3 * half :, :] = out[3 * half : 4 * half, :]

    sends = send_boxes.shape[1]
    lane = iota((8, LANES), 1)
    for block in range(sends // 16):
        picked = []
        for c in range(2):
            column = block * 16 + 2 * iota((8, sends), 0) + c
            box = jnp.sum(
                jnp.where(iota((8, sends), 1) == column, send_boxes[...].astype(jnp.float32), 0.0),
                axis=1, keepdims=True,
            ).astype(jnp.int32)
            width_here = jnp.sum(
                jnp.where(iota((8, leaves), 1) == box, width, 0.0), axis=1, keepdims=True
            )
            row_of = jnp.broadcast_to(box >> 1, (8, LANES))
            found = [jnp.zeros((8, LANES), jnp.float32)] * 4
            for r in range(half):
                here = row_of == r
                for ch in range(4):
                    found[ch] = jnp.where(here, out[ch * half + r : ch * half + r + 1, :], found[ch])
            aligned = jnp.broadcast_to((box & 1) == c, (8, LANES))
            found = [jnp.where(aligned, x, pltpu.roll(x, BCAP, 1)) for x in found]
            picked.append(found + [jnp.broadcast_to(width_here, (8, LANES))])
        for ch in range(5):
            blocks[pl.ds(block * 64 + ch, 8, stride=8), :] = jnp.where(
                lane < BCAP, picked[0][ch], picked[1][ch]
            )
        for ch in range(5, 8):
            blocks[pl.ds(block * 64 + ch, 8, stride=8), :] = jnp.zeros((8, LANES), jnp.float32)


def own_kernel(packed, up_inverse, density, checks):
    half = (packed.shape[0] - 8) // 4
    density[...] = jnp.zeros(density.shape, jnp.float32)
    width = per_leaf(packed[4 * half + 3 : 4 * half + 4, :], half)
    for block in range(half // 8):
        rows = [packed[c * half + block * 8 : c * half + block * 8 + 8, :] for c in range(4)]
        density[block * 16 : block * 16 + 16, :Q] = upward(
            rows[:3], rows[3], width[block * 8 : block * 8 + 8], up_inverse[...], checks
        )


def far_kernel(
    sources, kinds, pair_ref, packed, arrived, own_density, up_inverse, down_inverse, signs,
    last_bins, other_last_bins, table_high, table_low, translations, other_translations, out,
    spectra, kernels, high_table, low_table, density, totals, checks, densities, sems,
):
    leaves, entries = sources.shape
    half = leaves // 2
    rows = half // 2
    blocks = arrived.shape[0] // 64
    kind_count = translations.shape[0]
    pair = pair_ref[0]

    table_copies = [
        pltpu.make_async_copy(table_high, high_table, sems.at[0]),
        pltpu.make_async_copy(table_low, low_table, sems.at[1]),
    ]
    kernel_copies = []
    for side, bins in enumerate((translations, other_translations)):
        for t in range(TILES - 1):
            kernel_copies.append(pltpu.make_async_copy(
                bins.at[:, :, pl.ds(t * LANES, LANES)],
                kernels.at[pl.ds(0, kind_count), pl.ds(16 * side + 2 * t, 2), :],
                sems.at[2 + len(kernel_copies)],
            ))
    for copy in table_copies + kernel_copies:
        copy.start()
    for side, last in enumerate((last_bins, other_last_bins)):
        row = 16 * side + 2 * TILES - 2
        kernels[:kind_count, row : row + 2, :] = last[...]
    kernels[kind_count] = jnp.zeros((ROWS, LANES), jnp.float32)

    density[:leaves, :] = own_density[...]
    density[leaves:, :] = jnp.zeros((density.shape[0] - leaves, QPAD), jnp.float32)

    def arrive(block, carry):
        beads = [
            arrived[pl.ds(pl.multiple_of(block * 64, 64) + ch, 8, stride=8), :] for ch in range(5)
        ]
        density[pl.ds(pl.multiple_of(leaves + block * 16, 16), 16), :Q] = upward(
            beads[:3], beads[3], beads[4], up_inverse[...], checks
        )
        return carry

    if blocks == 1:
        arrive(0, 0)
    else:
        lax.fori_loop(0, blocks, arrive, 0)
    sign = jnp.where(pair == 1, signs[1:2, :], signs[0:1, :])
    other_sign = jnp.where(pair == 1, signs[0:1, :], signs[1:2, :])
    for copy in table_copies:
        copy.wait()
    store_spectra(
        jnp.concatenate([density[...] * sign, density[...] * other_sign], 0),
        high_table, low_table, spectra,
    )
    for copy in kernel_copies:
        copy.wait()

    def translate(t, carry):
        leaf = pair * half + t
        sums = [[None] * 4, [None] * 4]
        for entry in range(entries):
            kind = kinds[leaf, entry]
            start = pl.multiple_of(sources[leaf, entry], ROWS)
            for side in range(2):
                k_re = kernels[kind, pl.ds(16 * side, 8, stride=2), :]
                k_im = kernels[kind, pl.ds(16 * side + 1, 8, stride=2), :]
                s_re = spectra[pl.ds(start + 16 * side, 8), :]
                s_im = spectra[pl.ds(start + 16 * side + 8, 8), :]
                terms = (k_re * s_re, k_im * s_im, k_re * s_im, k_im * s_re)
                for n, term in enumerate(terms):
                    sums[side][n] = term if sums[side][n] is None else sums[side][n] + term
        start = pl.multiple_of(t * ROWS, ROWS)
        for side in range(2):
            rr, ii, ri, ir = sums[side]
            totals[pl.ds(start + 16 * side, 8), :] = rr - ii
            totals[pl.ds(start + 16 * side + 8, 8), :] = ri + ir
        return carry

    lax.fori_loop(0, half, translate, 0, unroll=2)

    lane = iota((half, LANES), 1)
    sides = []
    for side in range(2):
        columns = []
        for c in range(2):
            for t in range(TILES):
                line = totals[pl.ds(16 * side + c * 8 + t, half, stride=ROWS), :]
                if t == TILES - 1:
                    line = jnp.where(lane < BINS - t * LANES, line, 0.0)
                columns.append(line)
        sides.append(jnp.concatenate(columns, 1))
    high, low = split(jnp.concatenate(sides, 0))
    across = (((1,), (1,)), ((), ()))
    both = lax.dot_general(
        jnp.concatenate([high, low], 0), high_table[...], across,
        preferred_element_type=jnp.float32,
    )
    check = both[:leaves] + both[leaves:] + lax.dot_general(
        high, low_table[...], across, preferred_element_type=jnp.float32
    )
    check = (check[:half] * sign + check[half:] * other_sign)[:, :Q] * (1.0 / G)

    leaf_of = 2 * (lane & 7) + (lane >> 6)
    spread = jnp.where(iota((half, LANES), 0) == leaf_of, 1.0, 0.0)
    down = jnp.dot(
        check, down_inverse[...], precision=precise, preferred_element_type=jnp.float32
    )
    densities[...] = lax.dot_general(
        down, spread, (((0,), (0,)), ((), ())), precision=precise,
        preferred_element_type=jnp.float32,
    )
    width = block_transpose(
        per_leaf(packed[4 * half + 3 : 4 * half + 4, :], rows, pair * half)
    )
    offsets = [
        block_transpose(packed[pl.ds(pl.multiple_of(c * half + pair * rows, 8), rows), :])
        for c in range(3)
    ]
    total = None
    for q, kernel in surface_kernels(offsets, width):
        term = kernel * densities[q : q + 1, :]
        total = term if total is None else total + term
    out[...] = block_transpose(total)


def near_kernel(
    near_source, pair_ref, owner_ref, swapped, placed, passed, far, counts, decay_rate, stress,
    potential, new_stress, table, targets, sums,
):
    entries, leaves = near_source.shape
    half = leaves // 2
    pair = pair_ref[0]
    low = iota((half, LANES), 1) < BCAP
    swapped_from = jnp.where(((owner_ref[0] & 1) ^ pair) == 1, 0, 2)
    for n, rows_of in ((swapped_from, swapped), (1, placed), (2 - swapped_from, passed)):
        first = n * (leaves * 8)
        for ch in range(4):
            rows = rows_of[ch * half : (ch + 1) * half, :]
            turned = pltpu.roll(rows, BCAP, 1)
            table[pl.ds(first + ch, half, stride=16), :] = jnp.where(low, rows, turned)
            table[pl.ds(first + 8 + ch, half, stride=16), :] = jnp.where(low, turned, rows)
    for ch in range(3):
        mine = placed[pl.ds(pl.multiple_of(ch * half + pair * (half // 2), 8), half // 2), :]
        flipped = mine.T
        for r in range(half // 2):
            for h in range(2):
                start = ((2 * r + h) * 3 + ch) * BCAP
                targets[pl.ds(start, BCAP), :] = jnp.broadcast_to(
                    flipped[h * BCAP : (h + 1) * BCAP, r : r + 1], (BCAP, LANES)
                )
    low = iota((8, LANES), 1) < BCAP

    def one_leaf(t, carry):
        leaf = pair * half + t
        start = pl.multiple_of(t * 3 * BCAP, 8)
        tx, ty, tz = [targets[pl.ds(start + ch * BCAP, BCAP), :] for ch in range(3)]
        total = jnp.zeros((BCAP, LANES), jnp.float32)
        for n in range(entries // 2):
            left = pl.multiple_of(near_source[2 * n, leaf] * 8, 8)
            right = pl.multiple_of(near_source[2 * n + 1, leaf] * 8, 8)
            both = jnp.where(low, table[pl.ds(left, 8), :], table[pl.ds(right, 8), :])
            gx, gy, gz = tx - both[0:1], ty - both[1:2], tz - both[2:3]
            squared = gx * gx + gy * gy + (gz * gz + softening)
            total = total + lax.rsqrt(squared) * both[3:4]
        sums[pl.ds(pl.multiple_of(t * BCAP, 8), BCAP), :] = total
        return carry

    lax.fori_loop(0, half, one_leaf, 0, unroll=2)
    rows = half // 2
    for r in range(rows):
        block = sums[r * LANES : (r + 1) * LANES, :].T
        potential[r : r + 1, :] = jnp.sum(block, axis=0, keepdims=True)
    combined = potential[...] + far[...]
    beads = per_leaf(counts[...].astype(jnp.float32), rows, pair * half)
    slot = iota((rows, LANES), 1) & (BCAP - 1)
    occupied = slot.astype(jnp.float32) < beads
    decay = per_leaf(decay_rate[...], rows)
    potential[...] = jnp.where(occupied, combined, 0.0)
    new_stress[...] = jnp.where(occupied, decay * stress[...] + combined, 0.0)


VMEM = pl.BlockSpec(memory_space=pltpu.VMEM)
SMEM = pl.BlockSpec(memory_space=pltpu.SMEM)
ANY = pl.BlockSpec(memory_space=pl.ANY)
MIB = 1024 * 1024


def call(kernel, outs, in_specs, scratch=(), limit=40, grid=(), flops=0, bytes_accessed=0):
    return pl.pallas_call(
        kernel,
        out_shape=outs,
        grid=grid,
        in_specs=in_specs,
        out_specs=jax.tree.map(lambda _: VMEM, outs),
        scratch_shapes=list(scratch),
        compiler_params=pltpu.CompilerParams(vmem_limit_bytes=int(limit * MIB)),
        cost_estimate=pl.CostEstimate(
            flops=flops, bytes_accessed=bytes_accessed, transcendentals=0
        ),
    )


def body(
    offsets,
    charges,
    stress,
    decay_rate,
    morton_keys,
    levels,
    bead_counts,
    send_boxes,
    m2l_source,
    m2l_type,
    m2l_count,
    near_source,
    up_inverse,
    down_inverse,
    translations,
):
    f32 = jnp.float32
    leaves = morton_keys.shape[0]
    half = leaves // 2
    parts = lax.axis_size("wide") * lax.axis_size("narrow")
    high, low = [jnp.asarray(x) for x in transform_table()]
    signs = jnp.asarray(sign_rows())
    pair = lax.axis_index("pair").reshape(1)
    owner = (
        lax.axis_index("wide") * lax.axis_size("narrow") + lax.axis_index("narrow")
    ).reshape(1)
    kind_count = translations.shape[0]
    bf16 = jnp.bfloat16

    other_translations = lax.ppermute(translations, "pair", [(0, 1), (1, 0)])
    packed, blocks, placed, sources, kinds = call(
        functools.partial(pack_kernel, kind_count),
        [
            jax.ShapeDtypeStruct((4 * half + 8, LANES), f32),
            jax.ShapeDtypeStruct((8 * parts, LANES), f32),
            jax.ShapeDtypeStruct((4 * half, LANES), f32),
            jax.ShapeDtypeStruct(m2l_source.shape, jnp.int32),
            jax.ShapeDtypeStruct(m2l_type.shape, jnp.int32),
        ],
        [VMEM] * 9,
        limit=62,
    )(
        offsets, charges.reshape(half, LANES), morton_keys.reshape(1, leaves),
        levels.reshape(1, leaves), bead_counts.reshape(1, leaves), send_boxes,
        m2l_source, m2l_type, m2l_count.reshape(1, leaves),
    )
    arrived = lax.all_to_all(
        blocks.reshape(parts, 8, LANES), PARTS, split_axis=0, concat_axis=0, tiled=True
    ).reshape(8 * parts, LANES)
    swaps = [(2 * d, 2 * (d ^ 1)) for d in range(parts)]
    for d in range(1, parts - 1, 2):
        swaps += [(2 * d + 1, 2 * d + 3), (2 * d + 3, 2 * d + 1)]
    swapped = lax.ppermute(placed, PARTS + ("pair",), swaps)
    own_density = call(
        own_kernel,
        jax.ShapeDtypeStruct((leaves, QPAD), f32),
        [VMEM] * 2,
        [pltpu.VMEM((Q * 8, LANES), f32)],
        limit=62,
        flops=10**10,
        bytes_accessed=4 * 10**6,
    )(packed, up_inverse)
    passed = lax.ppermute(swapped, "pair", [(0, 1), (1, 0)])

    last = pl.BlockSpec((kind_count, 2, LANES), lambda i: (0, 0, TILES - 1))
    far = call(
        far_kernel,
        jax.ShapeDtypeStruct((half // 2, LANES), f32),
        [SMEM] * 3 + [VMEM] * 6 + [last] * 2 + [ANY] * 4,
        [
            pltpu.VMEM(((leaves + 2 * parts) * ROWS, LANES), f32),
            pltpu.VMEM((kind_count + 1, ROWS, LANES), f32),
            pltpu.VMEM(high.shape, bf16),
            pltpu.VMEM(low.shape, bf16),
            pltpu.VMEM((leaves + 2 * parts, QPAD), f32),
            pltpu.VMEM((half * ROWS, LANES), f32),
            pltpu.VMEM((Q * 8, LANES), f32),
            pltpu.VMEM((Q, LANES), f32),
            pltpu.SemaphoreType.DMA((2 * TILES,)),
        ],
        limit=63.75,
        grid=(1,),
        flops=2 * 10**9,
        bytes_accessed=8 * 10**6,
    )(
        sources, kinds, pair, packed, arrived, own_density, up_inverse, down_inverse, signs,
        translations, other_translations, high, low, translations, other_translations,
    )

    out = jax.ShapeDtypeStruct((half // 2, LANES), f32)
    potential, new_stress = call(
        near_kernel,
        [out, out],
        [SMEM] * 3 + [VMEM] * 7,
        [
            pltpu.VMEM((3 * leaves * 8, LANES), f32),
            pltpu.VMEM((half * 3 * BCAP, LANES), f32),
            pltpu.VMEM((half * BCAP, LANES), f32),
        ],
        limit=62,
    )(
        near_source.T, pair, owner, swapped, placed, passed, far, bead_counts.reshape(1, leaves),
        decay_rate.reshape(1, half), stress.reshape(half // 2, LANES),
    )
    return potential.reshape(-1), new_stress.reshape(-1)


def solution(mesh):
    return jax.shard_map(
        body,
        mesh=mesh,
        in_specs=(
            P(None, ("groups", "wide", "narrow")),
            P(("groups", "wide", "narrow")),
            P(("groups", "wide", "narrow", "pair")),
            P(("groups", "wide", "narrow", "pair")),
            P(("groups", "wide", "narrow")),
            P(("groups", "wide", "narrow")),
            P(("groups", "wide", "narrow")),
            P(("groups", "wide", "narrow"), None),
            P(("groups", "wide", "narrow"), None),
            P(("groups", "wide", "narrow"), None),
            P(("groups", "wide", "narrow")),
            P(("groups", "wide", "narrow"), None),
            P(),
            P(),
            P(None, None, "pair"),
        ),
        out_specs=(
            P(("groups", "wide", "narrow", "pair")),
            P(("groups", "wide", "narrow", "pair")),
        ),
        check_vma=False,
    )
```

```python
import functools

import jax
import jax.numpy as jnp
import ml_dtypes
import numpy as np
from jax import lax
from jax.experimental import pallas as pl
from jax.experimental.pallas import tpu as pltpu
from jax.sharding import PartitionSpec as P

PGRID = 12
G = 1728
MAXL = 10
BCAP = 64
Q = 152
QPAD = 160
LANES = 128
BINS = 864
TILES = 7
ROWS = 32
precise = lax.Precision.HIGHEST
softening = 0.04
surface_reach = 1.25
CELLS = [
    (i, j, k)
    for i in range(6)
    for j in range(6)
    for k in range(6)
    if 0 in (i, j, k) or 5 in (i, j, k)
]
PARTS = ("wide", "narrow")


def transform_table():
    cells = np.array(CELLS)
    bins = np.arange(BINS)
    freq = np.stack([bins // 144, bins // 12 % 12, bins % 12])
    angle = (cells @ freq % PGRID) * (2.0 * np.pi / PGRID)
    table = np.zeros((QPAD, 2 * TILES * LANES))
    table[:Q, :BINS] = np.cos(angle)
    table[:Q, TILES * LANES : TILES * LANES + BINS] = -np.sin(angle)
    table[np.abs(table) < 1e-9] = 0.0
    high = table.astype(ml_dtypes.bfloat16)
    low = (table - high.astype(np.float64)).astype(ml_dtypes.bfloat16)
    return high, low


def sign_rows():
    rows = np.zeros((8, QPAD), np.float32)
    rows[0, :Q] = 1.0
    rows[1, :Q] = [(-1.0) ** i for i, _, _ in CELLS]
    return rows


def iota(shape, dim):
    return lax.broadcasted_iota(jnp.int32, shape, dim)


def per_leaf(values, count, first=0):
    shape = (count, values.shape[1])
    leaf, lane = first + 2 * iota(shape, 0), iota(shape, 1)
    even = jnp.sum(jnp.where(lane == leaf, values, 0.0), axis=1, keepdims=True)
    odd = jnp.sum(jnp.where(lane == leaf + 1, values, 0.0), axis=1, keepdims=True)
    return jnp.where(iota((count, LANES), 1) < BCAP, even, odd)


def block_transpose(x):
    lane, row = iota(x.shape, 1), iota(x.shape, 0)
    for k in (1, 2, 4):
        row_bit, lane_bit = (row & k) != 0, (lane & k) != 0
        below = pltpu.roll(pltpu.roll(x, 8 - k, 0), k, 1)
        above = pltpu.roll(pltpu.roll(x, k, 0), LANES - k, 1)
        x = jnp.where(row_bit == lane_bit, x, jnp.where(lane_bit, below, above))
    return x


def split(x):
    high = x.astype(jnp.bfloat16)
    return high, (x - high.astype(jnp.float32)).astype(jnp.bfloat16)


def axis_squares(offset, width):
    area = width * width
    planes = [surface_reach * 0.5 * (i - 2.5) / 2.5 for i in range(6)]
    return [(plane - offset) * (plane - offset) * area for plane in planes]


def surface_kernels(offsets, width):
    gx, gy, gz = [axis_squares(offset, width) for offset in offsets]
    gz = [g + softening for g in gz]
    last, gxy = None, None
    for q, (i, j, k) in enumerate(CELLS):
        if last != (i, j):
            last, gxy = (i, j), gx[i] + gy[j]
        yield q, lax.rsqrt(gxy + gz[k])


def upward(offsets, weights, width, up_inverse, checks):
    offsets = [block_transpose(x) for x in offsets]
    weights, width = block_transpose(weights), block_transpose(width)
    for q, kernel in surface_kernels(offsets, width):
        checks[pl.ds(8 * q, 8), :] = kernel * weights
    check = checks[pl.ds(0, Q, stride=8), :]
    for s in range(1, 8):
        check = check + checks[pl.ds(s, Q, stride=8), :]
    density = lax.dot_general(
        check, up_inverse, (((0,), (0,)), ((), ())), precision=precise,
        preferred_element_type=jnp.float32,
    )
    density = density.reshape(2, 8, 8, Q)
    total = density[:, 0]
    for g in range(1, 8):
        total = total + density[:, g]
    return total.reshape(16, Q)


def store_spectra(density, table_high, table_low, target):
    count = density.shape[0] // 2
    high, low = split(density)
    both = jnp.concatenate([high, low], 0)
    for first in range(0, 2 * TILES, 2):
        columns = pl.ds(first * LANES, 2 * LANES)
        part = jnp.dot(both, table_high[:, columns], preferred_element_type=jnp.float32)
        spectra = part[: 2 * count] + part[2 * count :] + jnp.dot(
            high, table_low[:, columns], preferred_element_type=jnp.float32
        )
        for tile in range(first, first + 2):
            for side in range(2):
                for block in range(count // 16):
                    for h in range(2):
                        row = side * count + block * 16 + h * 8
                        start = (block * 16 + h) * ROWS + 16 * side + 8 * (tile // TILES) + tile % TILES
                        target[pl.ds(start, 8, stride=2 * ROWS), :] = spectra[
                            row : row + 8, (tile - first) * LANES : (tile - first + 1) * LANES
                        ]


def pack_kernel(
    kind_count, offsets, charges, keys, levels, counts, send_boxes, m2l_source, m2l_type, m2l_count,
    out, blocks, placed, sources, kinds,
):
    leaves = keys.shape[1]
    half = leaves // 2
    out[4 * half :, :] = jnp.zeros((8, LANES), jnp.float32)
    width = jnp.left_shift(jnp.ones_like(levels[...]), MAXL - levels[...]).astype(jnp.float32)
    for a in range(3):
        summed = jnp.zeros_like(keys[...])
        for bit in range(MAXL):
            summed = summed + (jnp.right_shift(keys[...], 3 * bit + a) & 1) * (1 << bit)
        out[4 * half + a : 4 * half + a + 1, :leaves] = summed.astype(jnp.float32) + 0.5 * width
    out[4 * half + 3 : 4 * half + 4, :leaves] = width
    for r in range(half):
        out[pl.ds(r, 3, stride=half), :] = offsets[:, r * LANES : (r + 1) * LANES]
    beads = per_leaf(counts[...].astype(jnp.float32), half)
    slot = iota((half, LANES), 1) & (BCAP - 1)
    out[3 * half : 4 * half, :] = jnp.where(slot.astype(jnp.float32) < beads, charges[...], 0.0)

    entry = iota(m2l_type.shape, 1)
    square = (leaves, leaves)
    live = jnp.sum(
        jnp.where(iota(square, 0) == iota(square, 1), m2l_count[...].astype(jnp.float32), 0.0),
        axis=1, keepdims=True,
    )
    kinds[...] = jnp.where(entry.astype(jnp.float32) < live, m2l_type[...], kind_count)
    sources[...] = m2l_source[...] * ROWS

    spread = per_leaf(width, half)
    for ch in range(3):
        center = per_leaf(out[4 * half + ch : 4 * half + ch + 1, :leaves], half)
        placed[ch * half : (ch + 1) * half, :] = center + spread * out[ch * half : (ch + 1) * half, :]
    placed[3 * half :, :] = out[3 * half : 4 * half, :]

    sends = send_boxes.shape[1]
    lane = iota((8, LANES), 1)
    for block in range(sends // 16):
        picked = []
        for c in range(2):
            column = block * 16 + 2 * iota((8, sends), 0) + c
            box = jnp.sum(
                jnp.where(iota((8, sends), 1) == column, send_boxes[...].astype(jnp.float32), 0.0),
                axis=1, keepdims=True,
            ).astype(jnp.int32)
            width_here = jnp.sum(
                jnp.where(iota((8, leaves), 1) == box, width, 0.0), axis=1, keepdims=True
            )
            row_of = jnp.broadcast_to(box >> 1, (8, LANES))
            found = [jnp.zeros((8, LANES), jnp.float32)] * 4
            for r in range(half):
                here = row_of == r
                for ch in range(4):
                    found[ch] = jnp.where(here, out[ch * half + r : ch * half + r + 1, :], found[ch])
            aligned = jnp.broadcast_to((box & 1) == c, (8, LANES))
            found = [jnp.where(aligned, x, pltpu.roll(x, BCAP, 1)) for x in found]
            picked.append(found + [jnp.broadcast_to(width_here, (8, LANES))])
        for ch in range(5):
            blocks[pl.ds(block * 64 + ch, 8, stride=8), :] = jnp.where(
                lane < BCAP, picked[0][ch], picked[1][ch]
            )
        for ch in range(5, 8):
            blocks[pl.ds(block * 64 + ch, 8, stride=8), :] = jnp.zeros((8, LANES), jnp.float32)


def own_kernel(packed, up_inverse, density, checks):
    half = (packed.shape[0] - 8) // 4
    density[...] = jnp.zeros(density.shape, jnp.float32)
    width = per_leaf(packed[4 * half + 3 : 4 * half + 4, :], half)
    for block in range(half // 8):
        rows = [packed[c * half + block * 8 : c * half + block * 8 + 8, :] for c in range(4)]
        density[block * 16 : block * 16 + 16, :Q] = upward(
            rows[:3], rows[3], width[block * 8 : block * 8 + 8], up_inverse[...], checks
        )


def far_kernel(
    sources, kinds, pair_ref, packed, arrived, own_density, up_inverse, down_inverse, signs,
    last_bins, other_last_bins, table_high, table_low, translations, other_translations, out,
    spectra, kernels, high_table, low_table, density, totals, checks, densities, sems,
):
    leaves, entries = sources.shape
    half = leaves // 2
    rows = half // 2
    blocks = arrived.shape[0] // 64
    kind_count = translations.shape[0]
    pair = pair_ref[0]

    table_copies = [
        pltpu.make_async_copy(table_high, high_table, sems.at[0]),
        pltpu.make_async_copy(table_low, low_table, sems.at[1]),
    ]
    kernel_copies = []
    for side, bins in enumerate((translations, other_translations)):
        for t in range(TILES - 1):
            kernel_copies.append(pltpu.make_async_copy(
                bins.at[:, :, pl.ds(t * LANES, LANES)],
                kernels.at[pl.ds(0, kind_count), pl.ds(16 * side + 2 * t, 2), :],
                sems.at[2 + len(kernel_copies)],
            ))
    for copy in table_copies + kernel_copies:
        copy.start()
    for side, last in enumerate((last_bins, other_last_bins)):
        row = 16 * side + 2 * TILES - 2
        kernels[:kind_count, row : row + 2, :] = last[...]
    kernels[kind_count] = jnp.zeros((ROWS, LANES), jnp.float32)

    density[:leaves, :] = own_density[...]
    density[leaves:, :] = jnp.zeros((density.shape[0] - leaves, QPAD), jnp.float32)

    def arrive(block, carry):
        beads = [
            arrived[pl.ds(pl.multiple_of(block * 64, 64) + ch, 8, stride=8), :] for ch in range(5)
        ]
        density[pl.ds(pl.multiple_of(leaves + block * 16, 16), 16), :Q] = upward(
            beads[:3], beads[3], beads[4], up_inverse[...], checks
        )
        return carry

    if blocks == 1:
        arrive(0, 0)
    else:
        lax.fori_loop(0, blocks, arrive, 0)
    sign = jnp.where(pair == 1, signs[1:2, :], signs[0:1, :])
    other_sign = jnp.where(pair == 1, signs[0:1, :], signs[1:2, :])
    for copy in table_copies:
        copy.wait()
    store_spectra(
        jnp.concatenate([density[...] * sign, density[...] * other_sign], 0),
        high_table, low_table, spectra,
    )
    for copy in kernel_copies:
        copy.wait()

    def translate(t, carry):
        leaf = pair * half + t
        sums = [[None] * 4, [None] * 4]
        for entry in range(entries):
            kind = kinds[leaf, entry]
            start = pl.multiple_of(sources[leaf, entry], ROWS)
            for side in range(2):
                k_re = kernels[kind, pl.ds(16 * side, 8, stride=2), :]
                k_im = kernels[kind, pl.ds(16 * side + 1, 8, stride=2), :]
                s_re = spectra[pl.ds(start + 16 * side, 8), :]
                s_im = spectra[pl.ds(start + 16 * side + 8, 8), :]
                terms = (k_re * s_re, k_im * s_im, k_re * s_im, k_im * s_re)
                for n, term in enumerate(terms):
                    sums[side][n] = term if sums[side][n] is None else sums[side][n] + term
        start = pl.multiple_of(t * ROWS, ROWS)
        for side in range(2):
            rr, ii, ri, ir = sums[side]
            totals[pl.ds(start + 16 * side, 8), :] = rr - ii
            totals[pl.ds(start + 16 * side + 8, 8), :] = ri + ir
        return carry

    lax.fori_loop(0, half, translate, 0, unroll=2)

    lane = iota((half, LANES), 1)
    sides = []
    for side in range(2):
        columns = []
        for c in range(2):
            for t in range(TILES):
                line = totals[pl.ds(16 * side + c * 8 + t, half, stride=ROWS), :]
                if t == TILES - 1:
                    line = jnp.where(lane < BINS - t * LANES, line, 0.0)
                columns.append(line)
        sides.append(jnp.concatenate(columns, 1))
    high, low = split(jnp.concatenate(sides, 0))
    across = (((1,), (1,)), ((), ()))
    both = lax.dot_general(
        jnp.concatenate([high, low], 0), high_table[...], across,
        preferred_element_type=jnp.float32,
    )
    check = both[:leaves] + both[leaves:] + lax.dot_general(
        high, low_table[...], across, preferred_element_type=jnp.float32
    )
    check = (check[:half] * sign + check[half:] * other_sign)[:, :Q] * (1.0 / G)

    leaf_of = 2 * (lane & 7) + (lane >> 6)
    spread = jnp.where(iota((half, LANES), 0) == leaf_of, 1.0, 0.0)
    down = jnp.dot(
        check, down_inverse[...], precision=precise, preferred_element_type=jnp.float32
    )
    densities[...] = lax.dot_general(
        down, spread, (((0,), (0,)), ((), ())), precision=precise,
        preferred_element_type=jnp.float32,
    )
    width = block_transpose(
        per_leaf(packed[4 * half + 3 : 4 * half + 4, :], rows, pair * half)
    )
    offsets = [
        block_transpose(packed[pl.ds(pl.multiple_of(c * half + pair * rows, 8), rows), :])
        for c in range(3)
    ]
    total = None
    for q, kernel in surface_kernels(offsets, width):
        term = kernel * densities[q : q + 1, :]
        total = term if total is None else total + term
    out[...] = block_transpose(total)


def near_kernel(
    near_source, pair_ref, owner_ref, swapped, placed, passed, far, counts, decay_rate, stress,
    potential, new_stress, table, targets, sums,
):
    entries, leaves = near_source.shape
    half = leaves // 2
    pair = pair_ref[0]
    low = iota((half, LANES), 1) < BCAP
    swapped_from = jnp.where(((owner_ref[0] & 1) ^ pair) == 1, 0, 2)
    for n, rows_of in ((swapped_from, swapped), (1, placed), (2 - swapped_from, passed)):
        first = n * (leaves * 8)
        for ch in range(4):
            rows = rows_of[ch * half : (ch + 1) * half, :]
            turned = pltpu.roll(rows, BCAP, 1)
            table[pl.ds(first + ch, half, stride=16), :] = jnp.where(low, rows, turned)
            table[pl.ds(first + 8 + ch, half, stride=16), :] = jnp.where(low, turned, rows)
    for ch in range(3):
        mine = placed[pl.ds(pl.multiple_of(ch * half + pair * (half // 2), 8), half // 2), :]
        flipped = mine.T
        for r in range(half // 2):
            for h in range(2):
                start = ((2 * r + h) * 3 + ch) * BCAP
                targets[pl.ds(start, BCAP), :] = jnp.broadcast_to(
                    flipped[h * BCAP : (h + 1) * BCAP, r : r + 1], (BCAP, LANES)
                )
    low = iota((8, LANES), 1) < BCAP

    def one_leaf(t, carry):
        leaf = pair * half + t
        start = pl.multiple_of(t * 3 * BCAP, 8)
        tx, ty, tz = [targets[pl.ds(start + ch * BCAP, BCAP), :] for ch in range(3)]
        total = jnp.zeros((BCAP, LANES), jnp.float32)
        for n in range(entries // 2):
            left = pl.multiple_of(near_source[2 * n, leaf] * 8, 8)
            right = pl.multiple_of(near_source[2 * n + 1, leaf] * 8, 8)
            both = jnp.where(low, table[pl.ds(left, 8), :], table[pl.ds(right, 8), :])
            gx, gy, gz = tx - both[0:1], ty - both[1:2], tz - both[2:3]
            squared = gx * gx + gy * gy + (gz * gz + softening)
            total = total + lax.rsqrt(squared) * both[3:4]
        sums[pl.ds(pl.multiple_of(t * BCAP, 8), BCAP), :] = total
        return carry

    lax.fori_loop(0, half, one_leaf, 0, unroll=2)
    rows = half // 2
    for r in range(rows):
        block = sums[r * LANES : (r + 1) * LANES, :].T
        potential[r : r + 1, :] = jnp.sum(block, axis=0, keepdims=True)
    combined = potential[...] + far[...]
    beads = per_leaf(counts[...].astype(jnp.float32), rows, pair * half)
    slot = iota((rows, LANES), 1) & (BCAP - 1)
    occupied = slot.astype(jnp.float32) < beads
    decay = per_leaf(decay_rate[...], rows)
    potential[...] = jnp.where(occupied, combined, 0.0)
    new_stress[...] = jnp.where(occupied, decay * stress[...] + combined, 0.0)


VMEM = pl.BlockSpec(memory_space=pltpu.VMEM)
SMEM = pl.BlockSpec(memory_space=pltpu.SMEM)
ANY = pl.BlockSpec(memory_space=pl.ANY)
MIB = 1024 * 1024


def call(kernel, outs, in_specs, scratch=(), limit=40, grid=(), flops=0, bytes_accessed=0):
    return pl.pallas_call(
        kernel,
        out_shape=outs,
        grid=grid,
        in_specs=in_specs,
        out_specs=jax.tree.map(lambda _: VMEM, outs),
        scratch_shapes=list(scratch),
        compiler_params=pltpu.CompilerParams(vmem_limit_bytes=limit * MIB),
        cost_estimate=pl.CostEstimate(
            flops=flops, bytes_accessed=bytes_accessed, transcendentals=0
        ),
    )


def body(
    offsets,
    charges,
    stress,
    decay_rate,
    morton_keys,
    levels,
    bead_counts,
    send_boxes,
    m2l_source,
    m2l_type,
    m2l_count,
    near_source,
    up_inverse,
    down_inverse,
    translations,
):
    f32 = jnp.float32
    leaves = morton_keys.shape[0]
    half = leaves // 2
    parts = lax.axis_size("wide") * lax.axis_size("narrow")
    high, low = [jnp.asarray(x) for x in transform_table()]
    signs = jnp.asarray(sign_rows())
    pair = lax.axis_index("pair").reshape(1)
    owner = (
        lax.axis_index("wide") * lax.axis_size("narrow") + lax.axis_index("narrow")
    ).reshape(1)
    kind_count = translations.shape[0]
    bf16 = jnp.bfloat16

    other_translations = lax.ppermute(translations, "pair", [(0, 1), (1, 0)])
    packed, blocks, placed, sources, kinds = call(
        functools.partial(pack_kernel, kind_count),
        [
            jax.ShapeDtypeStruct((4 * half + 8, LANES), f32),
            jax.ShapeDtypeStruct((8 * parts, LANES), f32),
            jax.ShapeDtypeStruct((4 * half, LANES), f32),
            jax.ShapeDtypeStruct(m2l_source.shape, jnp.int32),
            jax.ShapeDtypeStruct(m2l_type.shape, jnp.int32),
        ],
        [VMEM] * 9,
        limit=62,
    )(
        offsets, charges.reshape(half, LANES), morton_keys.reshape(1, leaves),
        levels.reshape(1, leaves), bead_counts.reshape(1, leaves), send_boxes,
        m2l_source, m2l_type, m2l_count.reshape(1, leaves),
    )
    arrived = lax.all_to_all(
        blocks.reshape(parts, 8, LANES), PARTS, split_axis=0, concat_axis=0, tiled=True
    ).reshape(8 * parts, LANES)
    swaps = [(2 * d, 2 * (d ^ 1)) for d in range(parts)]
    for d in range(1, parts - 1, 2):
        swaps += [(2 * d + 1, 2 * d + 3), (2 * d + 3, 2 * d + 1)]
    swapped = lax.ppermute(placed, PARTS + ("pair",), swaps)
    own_density = call(
        own_kernel,
        jax.ShapeDtypeStruct((leaves, QPAD), f32),
        [VMEM] * 2,
        [pltpu.VMEM((Q * 8, LANES), f32)],
        flops=10**10,
    )(packed, up_inverse)
    passed = lax.ppermute(swapped, "pair", [(0, 1), (1, 0)])

    last = pl.BlockSpec((kind_count, 2, LANES), lambda i: (0, 0, TILES - 1))
    far = call(
        far_kernel,
        jax.ShapeDtypeStruct((half // 2, LANES), f32),
        [SMEM] * 3 + [VMEM] * 6 + [last] * 2 + [ANY] * 4,
        [
            pltpu.VMEM(((leaves + 2 * parts) * ROWS, LANES), f32),
            pltpu.VMEM((kind_count + 1, ROWS, LANES), f32),
            pltpu.VMEM(high.shape, bf16),
            pltpu.VMEM(low.shape, bf16),
            pltpu.VMEM((leaves + 2 * parts, QPAD), f32),
            pltpu.VMEM((half * ROWS, LANES), f32),
            pltpu.VMEM((Q * 8, LANES), f32),
            pltpu.VMEM((Q, LANES), f32),
            pltpu.SemaphoreType.DMA((2 * TILES,)),
        ],
        grid=(1,),
        flops=10**10,
        bytes_accessed=4 * 10**6,
    )(
        sources, kinds, pair, packed, arrived, own_density, up_inverse, down_inverse, signs,
        translations, other_translations, high, low, translations, other_translations,
    )

    out = jax.ShapeDtypeStruct((half // 2, LANES), f32)
    potential, new_stress = call(
        near_kernel,
        [out, out],
        [SMEM] * 3 + [VMEM] * 7,
        [
            pltpu.VMEM((3 * leaves * 8, LANES), f32),
            pltpu.VMEM((half * 3 * BCAP, LANES), f32),
            pltpu.VMEM((half * BCAP, LANES), f32),
        ],
    )(
        near_source.T, pair, owner, swapped, placed, passed, far, bead_counts.reshape(1, leaves),
        decay_rate.reshape(1, half), stress.reshape(half // 2, LANES),
    )
    return potential.reshape(-1), new_stress.reshape(-1)


def solution(mesh):
    return jax.shard_map(
        body,
        mesh=mesh,
        in_specs=(
            P(None, ("groups", "wide", "narrow")),
            P(("groups", "wide", "narrow")),
            P(("groups", "wide", "narrow", "pair")),
            P(("groups", "wide", "narrow", "pair")),
            P(("groups", "wide", "narrow")),
            P(("groups", "wide", "narrow")),
            P(("groups", "wide", "narrow")),
            P(("groups", "wide", "narrow"), None),
            P(("groups", "wide", "narrow"), None),
            P(("groups", "wide", "narrow"), None),
            P(("groups", "wide", "narrow")),
            P(("groups", "wide", "narrow"), None),
            P(),
            P(),
            P(None, None, "pair"),
        ),
        out_specs=(
            P(("groups", "wide", "narrow", "pair")),
            P(("groups", "wide", "narrow", "pair")),
        ),
        check_vma=False,
    )
```

```python
import functools

import jax
import jax.numpy as jnp
import ml_dtypes
import numpy as np
from jax import lax
from jax.experimental import pallas as pl
from jax.experimental.pallas import tpu as pltpu
from jax.sharding import PartitionSpec as P

PGRID = 12
G = 1728
MAXL = 10
BCAP = 64
Q = 152
QPAD = 160
LANES = 128
BINS = 864
TILES = 7
ROWS = 32
precise = lax.Precision.HIGHEST
softening = 0.04
surface_reach = 1.25
CELLS = [
    (i, j, k)
    for i in range(6)
    for j in range(6)
    for k in range(6)
    if 0 in (i, j, k) or 5 in (i, j, k)
]
PARTS = ("wide", "narrow")


def transform_table():
    cells = np.array(CELLS)
    bins = np.arange(BINS)
    freq = np.stack([bins // 144, bins // 12 % 12, bins % 12])
    angle = (cells @ freq % PGRID) * (2.0 * np.pi / PGRID)
    table = np.zeros((QPAD, 2 * TILES * LANES))
    table[:Q, :BINS] = np.cos(angle)
    table[:Q, TILES * LANES : TILES * LANES + BINS] = -np.sin(angle)
    table[np.abs(table) < 1e-9] = 0.0
    high = table.astype(ml_dtypes.bfloat16)
    low = (table - high.astype(np.float64)).astype(ml_dtypes.bfloat16)
    return high, low


def sign_rows():
    rows = np.zeros((8, QPAD), np.float32)
    rows[0, :Q] = 1.0
    rows[1, :Q] = [(-1.0) ** i for i, _, _ in CELLS]
    return rows


def iota(shape, dim):
    return lax.broadcasted_iota(jnp.int32, shape, dim)


def per_leaf(values, count, first=0):
    shape = (count, values.shape[1])
    leaf, lane = first + 2 * iota(shape, 0), iota(shape, 1)
    even = jnp.sum(jnp.where(lane == leaf, values, 0.0), axis=1, keepdims=True)
    odd = jnp.sum(jnp.where(lane == leaf + 1, values, 0.0), axis=1, keepdims=True)
    return jnp.where(iota((count, LANES), 1) < BCAP, even, odd)


def block_transpose(x):
    lane, row = iota(x.shape, 1), iota(x.shape, 0)
    for k in (1, 2, 4):
        row_bit, lane_bit = (row & k) != 0, (lane & k) != 0
        below = pltpu.roll(pltpu.roll(x, 8 - k, 0), k, 1)
        above = pltpu.roll(pltpu.roll(x, k, 0), LANES - k, 1)
        x = jnp.where(row_bit == lane_bit, x, jnp.where(lane_bit, below, above))
    return x


def split(x):
    high = x.astype(jnp.bfloat16)
    return high, (x - high.astype(jnp.float32)).astype(jnp.bfloat16)


def axis_squares(offset, width):
    area = width * width
    planes = [surface_reach * 0.5 * (i - 2.5) / 2.5 for i in range(6)]
    return [(plane - offset) * (plane - offset) * area for plane in planes]


def surface_kernels(offsets, width):
    gx, gy, gz = [axis_squares(offset, width) for offset in offsets]
    gz = [g + softening for g in gz]
    last, gxy = None, None
    for q, (i, j, k) in enumerate(CELLS):
        if last != (i, j):
            last, gxy = (i, j), gx[i] + gy[j]
        yield q, lax.rsqrt(gxy + gz[k])


def fetch(sources, targets, sems):
    copies = [
        pltpu.make_async_copy(source, target, sems.at[n])
        for n, (source, target) in enumerate(zip(sources, targets))
    ]
    for copy in copies:
        copy.start()
    return copies


def upward(offsets, weights, width, up_inverse, checks):
    offsets = [block_transpose(x) for x in offsets]
    weights, width = block_transpose(weights), block_transpose(width)
    for q, kernel in surface_kernels(offsets, width):
        checks[pl.ds(8 * q, 8), :] = kernel * weights
    check = checks[pl.ds(0, Q, stride=8), :]
    for s in range(1, 8):
        check = check + checks[pl.ds(s, Q, stride=8), :]
    density = lax.dot_general(
        check, up_inverse, (((0,), (0,)), ((), ())), precision=precise,
        preferred_element_type=jnp.float32,
    )
    density = density.reshape(2, 8, 8, Q)
    total = density[:, 0]
    for g in range(1, 8):
        total = total + density[:, g]
    return total.reshape(16, Q)


def store_spectra(density, table_high, table_low, target):
    count = density.shape[0] // 2
    high, low = split(density)
    both = jnp.concatenate([high, low], 0)
    for first in range(0, 2 * TILES, 2):
        columns = pl.ds(first * LANES, 2 * LANES)
        part = jnp.dot(both, table_high[:, columns], preferred_element_type=jnp.float32)
        spectra = part[: 2 * count] + part[2 * count :] + jnp.dot(
            high, table_low[:, columns], preferred_element_type=jnp.float32
        )
        for tile in range(first, first + 2):
            for side in range(2):
                for block in range(count // 16):
                    for h in range(2):
                        row = side * count + block * 16 + h * 8
                        start = (block * 16 + h) * ROWS + 16 * side + 8 * (tile // TILES) + tile % TILES
                        target[pl.ds(start, 8, stride=2 * ROWS), :] = spectra[
                            row : row + 8, (tile - first) * LANES : (tile - first + 1) * LANES
                        ]


def pack_kernel(
    kind_count, *refs
):
    inputs, (out, blocks, placed, sources, kinds), held, sems = refs[:9], refs[9:14], refs[14:-1], refs[-1]
    for copy in fetch(inputs, held, sems):
        copy.wait()
    offsets, charges, keys, levels, counts, send_boxes, m2l_source, m2l_type, m2l_count = held
    leaves = keys.shape[1]
    half = leaves // 2
    out[4 * half :, :] = jnp.zeros((8, LANES), jnp.float32)
    width = jnp.left_shift(jnp.ones_like(levels[...]), MAXL - levels[...]).astype(jnp.float32)
    for a in range(3):
        summed = jnp.zeros_like(keys[...])
        for bit in range(MAXL):
            summed = summed + (jnp.right_shift(keys[...], 3 * bit + a) & 1) * (1 << bit)
        out[4 * half + a : 4 * half + a + 1, :leaves] = summed.astype(jnp.float32) + 0.5 * width
    out[4 * half + 3 : 4 * half + 4, :leaves] = width
    for r in range(half):
        out[pl.ds(r, 3, stride=half), :] = offsets[:, r * LANES : (r + 1) * LANES]
    beads = per_leaf(counts[...].astype(jnp.float32), half)
    slot = iota((half, LANES), 1) & (BCAP - 1)
    out[3 * half : 4 * half, :] = jnp.where(slot.astype(jnp.float32) < beads, charges[...], 0.0)

    entry = iota(m2l_type.shape, 1)
    square = (leaves, leaves)
    live = jnp.sum(
        jnp.where(iota(square, 0) == iota(square, 1), m2l_count[...].astype(jnp.float32), 0.0),
        axis=1, keepdims=True,
    )
    kinds[...] = jnp.where(entry.astype(jnp.float32) < live, m2l_type[...], kind_count)
    sources[...] = m2l_source[...] * ROWS

    spread = per_leaf(width, half)
    for ch in range(3):
        center = per_leaf(out[4 * half + ch : 4 * half + ch + 1, :leaves], half)
        placed[ch * half : (ch + 1) * half, :] = center + spread * out[ch * half : (ch + 1) * half, :]
    placed[3 * half :, :] = out[3 * half : 4 * half, :]

    sends = send_boxes.shape[1]
    lane = iota((8, LANES), 1)
    for block in range(sends // 16):
        picked = []
        for c in range(2):
            column = block * 16 + 2 * iota((8, sends), 0) + c
            box = jnp.sum(
                jnp.where(iota((8, sends), 1) == column, send_boxes[...].astype(jnp.float32), 0.0),
                axis=1, keepdims=True,
            ).astype(jnp.int32)
            width_here = jnp.sum(
                jnp.where(iota((8, leaves), 1) == box, width, 0.0), axis=1, keepdims=True
            )
            row_of = jnp.broadcast_to(box >> 1, (8, LANES))
            found = [jnp.zeros((8, LANES), jnp.float32)] * 4
            for r in range(half):
                here = row_of == r
                for ch in range(4):
                    found[ch] = jnp.where(here, out[ch * half + r : ch * half + r + 1, :], found[ch])
            aligned = jnp.broadcast_to((box & 1) == c, (8, LANES))
            found = [jnp.where(aligned, x, pltpu.roll(x, BCAP, 1)) for x in found]
            picked.append(found + [jnp.broadcast_to(width_here, (8, LANES))])
        for ch in range(5):
            blocks[pl.ds(block * 64 + ch, 8, stride=8), :] = jnp.where(
                lane < BCAP, picked[0][ch], picked[1][ch]
            )
        for ch in range(5, 8):
            blocks[pl.ds(block * 64 + ch, 8, stride=8), :] = jnp.zeros((8, LANES), jnp.float32)


def own_kernel(packed, up_inverse_in, density, up_inverse, checks, sems):
    half = (packed.shape[0] - 8) // 4
    copy = fetch([up_inverse_in], [up_inverse], sems)[0]
    density[...] = jnp.zeros(density.shape, jnp.float32)
    width = per_leaf(packed[4 * half + 3 : 4 * half + 4, :], half)
    copy.wait()
    for block in range(half // 8):
        rows = [packed[c * half + block * 8 : c * half + block * 8 + 8, :] for c in range(4)]
        density[block * 16 : block * 16 + 16, :Q] = upward(
            rows[:3], rows[3], width[block * 8 : block * 8 + 8], up_inverse[...], checks
        )


def far_kernel(
    sources, kinds, pair_ref, packed, arrived, own_density, last_bins, other_last_bins,
    up_inverse_in, down_inverse_in, signs_in, table_high, table_low, translations,
    other_translations, out,
    up_inverse, down_inverse, signs, high_table, low_table,
    spectra, kernels, density, totals, checks, densities, copy_sems, sems,
):
    leaves, entries = sources.shape
    half = leaves // 2
    rows = half // 2
    blocks = arrived.shape[0] // 64
    kind_count = translations.shape[0]
    pair = pair_ref[0]

    copies = fetch(
        (up_inverse_in, down_inverse_in, signs_in, table_high, table_low),
        (up_inverse, down_inverse, signs, high_table, low_table),
        copy_sems,
    )
    kernel_copies = []
    for side, bins in enumerate((translations, other_translations)):
        for c in range(2):
            for t in range(TILES - 1):
                kernel_copies.append(pltpu.make_async_copy(
                    bins.at[:, pl.ds(c, 1), pl.ds(t * LANES, LANES)],
                    kernels.at[pl.ds(0, kind_count), pl.ds(16 * side + 8 * c + t, 1), :],
                    sems.at[len(kernel_copies)],
                ))
    for copy in kernel_copies:
        copy.start()
    for side, last in enumerate((last_bins, other_last_bins)):
        for c in range(2):
            row = 16 * side + 8 * c + TILES - 1
            kernels[:kind_count, row : row + 1, :] = last[:, c : c + 1, :]
    kernels[kind_count] = jnp.zeros((ROWS, LANES), jnp.float32)

    density[:leaves, :] = own_density[...]
    density[leaves:, :] = jnp.zeros((density.shape[0] - leaves, QPAD), jnp.float32)
    copies[0].wait()

    def arrive(block, carry):
        beads = [
            arrived[pl.ds(pl.multiple_of(block * 64, 64) + ch, 8, stride=8), :] for ch in range(5)
        ]
        density[pl.ds(pl.multiple_of(leaves + block * 16, 16), 16), :Q] = upward(
            beads[:3], beads[3], beads[4], up_inverse[...], checks
        )
        return carry

    if blocks == 1:
        arrive(0, 0)
    else:
        lax.fori_loop(0, blocks, arrive, 0)
    for copy in copies[1:]:
        copy.wait()
    sign = jnp.where(pair == 1, signs[1:2, :], signs[0:1, :])
    other_sign = jnp.where(pair == 1, signs[0:1, :], signs[1:2, :])
    store_spectra(
        jnp.concatenate([density[...] * sign, density[...] * other_sign], 0),
        high_table, low_table, spectra,
    )
    for copy in kernel_copies:
        copy.wait()

    def translate(t, carry):
        leaf = pair * half + t
        sums = [[None] * 4, [None] * 4]
        for entry in range(entries):
            kernel = kernels[kinds[leaf, entry]]
            source = spectra[pl.ds(pl.multiple_of(sources[leaf, entry], ROWS), ROWS), :]
            for side in range(2):
                k_re, k_im = kernel[16 * side : 16 * side + 8], kernel[16 * side + 8 : 16 * side + 16]
                s_re, s_im = source[16 * side : 16 * side + 8], source[16 * side + 8 : 16 * side + 16]
                terms = (k_re * s_re, k_im * s_im, k_re * s_im, k_im * s_re)
                for n, term in enumerate(terms):
                    sums[side][n] = term if sums[side][n] is None else sums[side][n] + term
        start = pl.multiple_of(t * ROWS, ROWS)
        for side in range(2):
            rr, ii, ri, ir = sums[side]
            totals[pl.ds(start + 16 * side, 8), :] = rr - ii
            totals[pl.ds(start + 16 * side + 8, 8), :] = ri + ir
        return carry

    lax.fori_loop(0, half, translate, 0, unroll=2)

    lane = iota((half, LANES), 1)
    sides = []
    for side in range(2):
        columns = []
        for c in range(2):
            for t in range(TILES):
                line = totals[pl.ds(16 * side + c * 8 + t, half, stride=ROWS), :]
                if t == TILES - 1:
                    line = jnp.where(lane < BINS - t * LANES, line, 0.0)
                columns.append(line)
        sides.append(jnp.concatenate(columns, 1))
    high, low = split(jnp.concatenate(sides, 0))
    across = (((1,), (1,)), ((), ()))
    both = lax.dot_general(
        jnp.concatenate([high, low], 0), high_table[...], across,
        preferred_element_type=jnp.float32,
    )
    check = both[:leaves] + both[leaves:] + lax.dot_general(
        high, low_table[...], across, preferred_element_type=jnp.float32
    )
    check = (check[:half] * sign + check[half:] * other_sign)[:, :Q] * (1.0 / G)

    leaf_of = 2 * (lane & 7) + (lane >> 6)
    spread = jnp.where(iota((half, LANES), 0) == leaf_of, 1.0, 0.0)
    down = jnp.dot(
        check, down_inverse[...], precision=precise, preferred_element_type=jnp.float32
    )
    densities[...] = lax.dot_general(
        down, spread, (((0,), (0,)), ((), ())), precision=precise,
        preferred_element_type=jnp.float32,
    )
    width = block_transpose(
        per_leaf(packed[4 * half + 3 : 4 * half + 4, :], rows, pair * half)
    )
    offsets = [
        block_transpose(packed[pl.ds(pl.multiple_of(c * half + pair * rows, 8), rows), :])
        for c in range(3)
    ]
    parts = [jnp.zeros((rows, LANES), jnp.float32)] * 4
    for q, kernel in surface_kernels(offsets, width):
        parts[q % 4] = parts[q % 4] + kernel * densities[q : q + 1, :]
    out[...] = block_transpose((parts[0] + parts[1]) + (parts[2] + parts[3]))


def near_kernel(
    near_source, pair_ref, owner_ref, swapped, placed, passed, packed, far, counts, decay_rate,
    stress, potential, new_stress, table, targets, centers, sums,
):
    entries, leaves = near_source.shape
    half = leaves // 2
    pair = pair_ref[0]
    low = iota((half, LANES), 1) < BCAP
    swapped_from = jnp.where(((owner_ref[0] & 1) ^ pair) == 1, 0, 2)
    for n, rows_of in ((swapped_from, swapped), (1, placed), (2 - swapped_from, passed)):
        first = n * (leaves * 8)
        for ch in range(4):
            rows = rows_of[ch * half : (ch + 1) * half, :]
            turned = pltpu.roll(rows, BCAP, 1)
            table[pl.ds(first + ch, half, stride=16), :] = jnp.where(low, rows, turned)
            table[pl.ds(first + 8 + ch, half, stride=16), :] = jnp.where(low, turned, rows)
    rows = half // 2
    low = iota((rows, LANES), 1) < BCAP
    centers[...] = jnp.zeros(centers.shape, jnp.float32)
    squares = jnp.zeros((rows, LANES), jnp.float32)
    for ch in range(4):
        if ch < 3:
            center = per_leaf(packed[4 * half + ch : 4 * half + ch + 1, :], rows, pair * half)
            turned = pltpu.roll(center, BCAP, 1)
            centers[pl.ds(ch, rows, stride=16), :] = jnp.where(low, center, turned)
            centers[pl.ds(8 + ch, rows, stride=16), :] = jnp.where(low, turned, center)
            mine = placed[pl.ds(pl.multiple_of(ch * half + pair * rows, 8), rows), :] - center
            squares = squares + mine * mine
        else:
            mine = squares
        flipped = mine.T
        for r in range(rows):
            for h in range(2):
                start = ((2 * r + h) * 4 + ch) * BCAP
                targets[pl.ds(start, BCAP), :] = jnp.broadcast_to(
                    flipped[h * BCAP : (h + 1) * BCAP, r : r + 1], (BCAP, LANES)
                )
    low = iota((8, LANES), 1) < BCAP

    def one_leaf(t, carry):
        leaf = pair * half + t
        start = pl.multiple_of(t * 4 * BCAP, 8)
        tx, ty, tz, norm = [targets[pl.ds(start + ch * BCAP, BCAP), :] for ch in range(4)]
        center = centers[pl.ds(pl.multiple_of(t * 8, 8), 8), :]
        total = jnp.zeros((BCAP, LANES), jnp.float32)
        for n in range(entries // 2):
            left = pl.multiple_of(near_source[2 * n, leaf] * 8, 8)
            right = pl.multiple_of(near_source[2 * n + 1, leaf] * 8, 8)
            both = jnp.where(low, table[pl.ds(left, 8), :], table[pl.ds(right, 8), :]) - center
            twice = both * -2.0
            square = both * both
            source_norm = (square[0:1] + square[1:2]) + (square[2:3] + softening)
            squared = (norm + source_norm) + tx * twice[0:1] + ty * twice[1:2] + tz * twice[2:3]
            total = total + lax.rsqrt(squared) * both[3:4]
        sums[pl.ds(pl.multiple_of(t * BCAP, 8), BCAP), :] = total
        return carry

    lax.fori_loop(0, half, one_leaf, 0, unroll=2)
    for r in range(rows):
        block = sums[r * LANES : (r + 1) * LANES, :].T
        potential[r : r + 1, :] = jnp.sum(block, axis=0, keepdims=True)
    combined = potential[...] + far[...]
    beads = per_leaf(counts[...].astype(jnp.float32), rows, pair * half)
    slot = iota((rows, LANES), 1) & (BCAP - 1)
    occupied = slot.astype(jnp.float32) < beads
    decay = per_leaf(decay_rate[...], rows)
    potential[...] = jnp.where(occupied, combined, 0.0)
    new_stress[...] = jnp.where(occupied, decay * stress[...] + combined, 0.0)


VMEM = pl.BlockSpec(memory_space=pltpu.VMEM)
SMEM = pl.BlockSpec(memory_space=pltpu.SMEM)
HBM = pl.BlockSpec(memory_space=pltpu.HBM)
ANY = pl.BlockSpec(memory_space=pl.ANY)
MIB = 1024 * 1024


def call(kernel, outs, in_specs, scratch=(), limit=40, grid=(), flops=0, bytes_accessed=0):
    return pl.pallas_call(
        kernel,
        out_shape=outs,
        grid=grid,
        in_specs=in_specs,
        out_specs=jax.tree.map(lambda _: VMEM, outs),
        scratch_shapes=list(scratch),
        compiler_params=pltpu.CompilerParams(vmem_limit_bytes=limit * MIB),
        cost_estimate=pl.CostEstimate(
            flops=flops, bytes_accessed=bytes_accessed, transcendentals=0
        ),
    )


def body(
    offsets,
    charges,
    stress,
    decay_rate,
    morton_keys,
    levels,
    bead_counts,
    send_boxes,
    m2l_source,
    m2l_type,
    m2l_count,
    near_source,
    up_inverse,
    down_inverse,
    translations,
):
    f32 = jnp.float32
    leaves = morton_keys.shape[0]
    half = leaves // 2
    parts = lax.axis_size("wide") * lax.axis_size("narrow")
    high, low = [jnp.asarray(x) for x in transform_table()]
    signs = jnp.asarray(sign_rows())
    pair = lax.axis_index("pair").reshape(1)
    owner = (
        lax.axis_index("wide") * lax.axis_size("narrow") + lax.axis_index("narrow")
    ).reshape(1)
    kind_count = translations.shape[0]
    bf16 = jnp.bfloat16

    other_translations = lax.ppermute(translations, "pair", [(0, 1), (1, 0)])
    raw = [
        offsets, charges.reshape(half, LANES), morton_keys.reshape(1, leaves),
        levels.reshape(1, leaves), bead_counts.reshape(1, leaves), send_boxes,
        m2l_source, m2l_type, m2l_count.reshape(1, leaves),
    ]
    packed, blocks, placed, sources, kinds = call(
        functools.partial(pack_kernel, kind_count),
        [
            jax.ShapeDtypeStruct((4 * half + 8, LANES), f32),
            jax.ShapeDtypeStruct((8 * parts, LANES), f32),
            jax.ShapeDtypeStruct((4 * half, LANES), f32),
            jax.ShapeDtypeStruct(m2l_source.shape, jnp.int32),
            jax.ShapeDtypeStruct(m2l_type.shape, jnp.int32),
        ],
        [HBM] * 9,
        [pltpu.VMEM(x.shape, x.dtype) for x in raw] + [pltpu.SemaphoreType.DMA((9,))],
    )(*raw)
    arrived = lax.all_to_all(
        blocks.reshape(parts, 8, LANES), PARTS, split_axis=0, concat_axis=0, tiled=True
    ).reshape(8 * parts, LANES)
    swaps = [(2 * d, 2 * (d ^ 1)) for d in range(parts)]
    for d in range(1, parts - 1, 2):
        swaps += [(2 * d + 1, 2 * d + 3), (2 * d + 3, 2 * d + 1)]
    swapped = lax.ppermute(placed, PARTS + ("pair",), swaps)
    own_density = call(
        own_kernel,
        jax.ShapeDtypeStruct((leaves, QPAD), f32),
        [VMEM, HBM],
        [
            pltpu.VMEM((Q, Q), f32),
            pltpu.VMEM((Q * 8, LANES), f32),
            pltpu.SemaphoreType.DMA((1,)),
        ],
        flops=10**10,
    )(packed, up_inverse)
    passed = lax.ppermute(swapped, "pair", [(0, 1), (1, 0)])

    last = pl.BlockSpec((kind_count, 2, LANES), lambda i: (0, 0, TILES - 1))
    far = call(
        far_kernel,
        jax.ShapeDtypeStruct((half // 2, LANES), f32),
        [SMEM] * 3 + [VMEM] * 3 + [last] * 2 + [HBM] * 5 + [ANY] * 2,
        [
            pltpu.VMEM((Q, Q), f32),
            pltpu.VMEM((Q, Q), f32),
            pltpu.VMEM(signs.shape, f32),
            pltpu.VMEM(high.shape, bf16),
            pltpu.VMEM(low.shape, bf16),
            pltpu.VMEM(((leaves + 2 * parts) * ROWS, LANES), f32),
            pltpu.VMEM((kind_count + 1, ROWS, LANES), f32),
            pltpu.VMEM((leaves + 2 * parts, QPAD), f32),
            pltpu.VMEM((half * ROWS, LANES), f32),
            pltpu.VMEM((Q * 8, LANES), f32),
            pltpu.VMEM((Q, LANES), f32),
            pltpu.SemaphoreType.DMA((5,)),
            pltpu.SemaphoreType.DMA((4 * TILES - 4,)),
        ],
        grid=(1,),
        flops=10**10,
        bytes_accessed=4 * 10**6,
    )(
        sources, kinds, pair, packed, arrived, own_density, translations, other_translations,
        up_inverse, down_inverse, signs, high, low, translations, other_translations,
    )

    out = jax.ShapeDtypeStruct((half // 2, LANES), f32)
    potential, new_stress = call(
        near_kernel,
        [out, out],
        [SMEM] * 3 + [VMEM] * 8,
        [
            pltpu.VMEM((3 * leaves * 8, LANES), f32),
            pltpu.VMEM((half * 4 * BCAP, LANES), f32),
            pltpu.VMEM((half * 8, LANES), f32),
            pltpu.VMEM((half * BCAP, LANES), f32),
        ],
    )(
        near_source.T, pair, owner, swapped, placed, passed, packed, far, bead_counts.reshape(1, leaves),
        decay_rate.reshape(1, half), stress.reshape(half // 2, LANES),
    )
    return potential.reshape(-1), new_stress.reshape(-1)


def solution(mesh):
    return jax.shard_map(
        body,
        mesh=mesh,
        in_specs=(
            P(None, ("groups", "wide", "narrow")),
            P(("groups", "wide", "narrow")),
            P(("groups", "wide", "narrow", "pair")),
            P(("groups", "wide", "narrow", "pair")),
            P(("groups", "wide", "narrow")),
            P(("groups", "wide", "narrow")),
            P(("groups", "wide", "narrow")),
            P(("groups", "wide", "narrow"), None),
            P(("groups", "wide", "narrow"), None),
            P(("groups", "wide", "narrow"), None),
            P(("groups", "wide", "narrow")),
            P(("groups", "wide", "narrow"), None),
            P(),
            P(),
            P(None, None, "pair"),
        ),
        out_specs=(
            P(("groups", "wide", "narrow", "pair")),
            P(("groups", "wide", "narrow", "pair")),
        ),
        check_vma=False,
    )
```

```python
import functools

import jax
import jax.numpy as jnp
import ml_dtypes
import numpy as np
from jax import lax
from jax.experimental import pallas as pl
from jax.experimental.pallas import tpu as pltpu
from jax.sharding import PartitionSpec as P

PGRID = 12
G = 1728
MAXL = 10
BCAP = 64
Q = 152
QPAD = 160
LANES = 128
BINS = 864
TILES = 7
ROWS = 32
precise = lax.Precision.HIGHEST
softening = 0.04
surface_reach = 1.25
CELLS = [
    (i, j, k)
    for i in range(6)
    for j in range(6)
    for k in range(6)
    if 0 in (i, j, k) or 5 in (i, j, k)
]
PARTS = ("wide", "narrow")


def transform_table():
    cells = np.array(CELLS)
    bins = np.arange(BINS)
    freq = np.stack([bins // 144, bins // 12 % 12, bins % 12])
    angle = (cells @ freq % PGRID) * (2.0 * np.pi / PGRID)
    table = np.zeros((QPAD, 2 * TILES * LANES))
    table[:Q, :BINS] = np.cos(angle)
    table[:Q, TILES * LANES : TILES * LANES + BINS] = -np.sin(angle)
    table[np.abs(table) < 1e-9] = 0.0
    return table.astype(ml_dtypes.bfloat16)


def low_part(high):
    root = np.sqrt(0.75)
    held = float(np.asarray(root).astype(ml_dtypes.bfloat16))
    scale = (root - held) / (held * (held * held - 1.0) * (held * held - 0.25))
    value = high.astype(jnp.float32)
    square = value * value
    return (value * (square - 1.0) * (square - 0.25) * scale).astype(jnp.bfloat16)


def sign_rows():
    rows = np.zeros((8, QPAD), np.float32)
    rows[0, :Q] = 1.0
    rows[1, :Q] = [(-1.0) ** i for i, _, _ in CELLS]
    return rows


def iota(shape, dim):
    return lax.broadcasted_iota(jnp.int32, shape, dim)


def per_leaf(values, count, first=0):
    shape = (count, values.shape[1])
    leaf, lane = first + 2 * iota(shape, 0), iota(shape, 1)
    even = jnp.sum(jnp.where(lane == leaf, values, 0.0), axis=1, keepdims=True)
    odd = jnp.sum(jnp.where(lane == leaf + 1, values, 0.0), axis=1, keepdims=True)
    return jnp.where(iota((count, LANES), 1) < BCAP, even, odd)


def block_transpose(x):
    lane, row = iota(x.shape, 1), iota(x.shape, 0)
    for k in (1, 2, 4):
        row_bit, lane_bit = (row & k) != 0, (lane & k) != 0
        below = pltpu.roll(pltpu.roll(x, 8 - k, 0), k, 1)
        above = pltpu.roll(pltpu.roll(x, k, 0), LANES - k, 1)
        x = jnp.where(row_bit == lane_bit, x, jnp.where(lane_bit, below, above))
    return x


def split(x):
    high = x.astype(jnp.bfloat16)
    return high, (x - high.astype(jnp.float32)).astype(jnp.bfloat16)


def axis_squares(offset, width):
    area = width * width
    planes = [surface_reach * 0.5 * (i - 2.5) / 2.5 for i in range(6)]
    return [(plane - offset) * (plane - offset) * area for plane in planes]


def surface_kernels(offsets, width):
    gx, gy, gz = [axis_squares(offset, width) for offset in offsets]
    gz = [g + softening for g in gz]
    last, gxy = None, None
    for q, (i, j, k) in enumerate(CELLS):
        if last != (i, j):
            last, gxy = (i, j), gx[i] + gy[j]
        yield q, lax.rsqrt(gxy + gz[k])


def check_sums(offsets, weights, width, checks):
    offsets = [block_transpose(x) for x in offsets]
    weights, width = block_transpose(weights), block_transpose(width)
    for q, kernel in surface_kernels(offsets, width):
        checks[pl.ds(8 * q, 8), :] = kernel * weights
    check = checks[pl.ds(0, Q, stride=8), :]
    for s in range(1, 8):
        check = check + checks[pl.ds(s, Q, stride=8), :]
    return check


def upward(check, up_inverse):
    density = lax.dot_general(
        check, up_inverse, (((0,), (0,)), ((), ())), precision=precise,
        preferred_element_type=jnp.float32,
    )
    blocks = check.shape[1] // LANES
    density = density.reshape(2 * blocks, 8, 8, Q)
    total = density[:, 0]
    for g in range(1, 8):
        total = total + density[:, g]
    return total.reshape(16 * blocks, Q)


def store_spectra(density, table_high, table_low, target):
    count = density.shape[0] // 2
    high, low = split(density)
    both = jnp.concatenate([high, low], 0)
    for first in range(0, 2 * TILES, 2):
        columns = pl.ds(first * LANES, 2 * LANES)
        part = jnp.dot(both, table_high[:, columns], preferred_element_type=jnp.float32)
        spectra = part[: 2 * count] + part[2 * count :] + jnp.dot(
            high, table_low[:, columns], preferred_element_type=jnp.float32
        )
        for tile in range(first, first + 2):
            for side in range(2):
                for block in range(count // 16):
                    for h in range(2):
                        row = side * count + block * 16 + h * 8
                        start = (block * 16 + h) * ROWS + 16 * side + 8 * (tile // TILES) + tile % TILES
                        target[pl.ds(start, 8, stride=2 * ROWS), :] = spectra[
                            row : row + 8, (tile - first) * LANES : (tile - first + 1) * LANES
                        ]


def pack_kernel(
    kind_count, offsets, charges, keys, levels, counts, send_boxes, m2l_source, m2l_type, m2l_count,
    out, blocks, placed, sources, kinds,
):
    leaves = keys.shape[1]
    half = leaves // 2
    out[4 * half :, :] = jnp.zeros((8, LANES), jnp.float32)
    width = jnp.left_shift(jnp.ones_like(levels[...]), MAXL - levels[...]).astype(jnp.float32)
    for a in range(3):
        summed = jnp.zeros_like(keys[...])
        for bit in range(MAXL):
            summed = summed + (jnp.right_shift(keys[...], 3 * bit + a) & 1) * (1 << bit)
        out[4 * half + a : 4 * half + a + 1, :leaves] = summed.astype(jnp.float32) + 0.5 * width
    out[4 * half + 3 : 4 * half + 4, :leaves] = width
    for r in range(half):
        out[pl.ds(r, 3, stride=half), :] = offsets[:, r * LANES : (r + 1) * LANES]
    beads = per_leaf(counts[...].astype(jnp.float32), half)
    slot = iota((half, LANES), 1) & (BCAP - 1)
    out[3 * half : 4 * half, :] = jnp.where(slot.astype(jnp.float32) < beads, charges[...], 0.0)

    entry = iota(m2l_type.shape, 1)
    square = (leaves, leaves)
    live = jnp.sum(
        jnp.where(iota(square, 0) == iota(square, 1), m2l_count[...].astype(jnp.float32), 0.0),
        axis=1, keepdims=True,
    )
    kinds[...] = jnp.where(entry.astype(jnp.float32) < live, m2l_type[...], kind_count)
    sources[...] = m2l_source[...] * ROWS

    spread = per_leaf(width, half)
    for ch in range(3):
        center = per_leaf(out[4 * half + ch : 4 * half + ch + 1, :leaves], half)
        placed[ch * half : (ch + 1) * half, :] = center + spread * out[ch * half : (ch + 1) * half, :]
    placed[3 * half :, :] = out[3 * half : 4 * half, :]

    sends = send_boxes.shape[1]
    lane = iota((8, LANES), 1)
    for block in range(sends // 16):
        picked = []
        for c in range(2):
            column = block * 16 + 2 * iota((8, sends), 0) + c
            box = jnp.sum(
                jnp.where(iota((8, sends), 1) == column, send_boxes[...].astype(jnp.float32), 0.0),
                axis=1, keepdims=True,
            ).astype(jnp.int32)
            width_here = jnp.sum(
                jnp.where(iota((8, leaves), 1) == box, width, 0.0), axis=1, keepdims=True
            )
            row_of = jnp.broadcast_to(box >> 1, (8, LANES))
            found = [jnp.zeros((8, LANES), jnp.float32)] * 4
            for r in range(half):
                here = row_of == r
                for ch in range(4):
                    found[ch] = jnp.where(here, out[ch * half + r : ch * half + r + 1, :], found[ch])
            aligned = jnp.broadcast_to((box & 1) == c, (8, LANES))
            found = [jnp.where(aligned, x, pltpu.roll(x, BCAP, 1)) for x in found]
            picked.append(found + [jnp.broadcast_to(width_here, (8, LANES))])
        for ch in range(5):
            blocks[pl.ds(block * 64 + ch, 8, stride=8), :] = jnp.where(
                lane < BCAP, picked[0][ch], picked[1][ch]
            )
        for ch in range(5, 8):
            blocks[pl.ds(block * 64 + ch, 8, stride=8), :] = jnp.zeros((8, LANES), jnp.float32)


def own_kernel(packed, out, checks):
    half = (packed.shape[0] - 8) // 4
    width = per_leaf(packed[4 * half + 3 : 4 * half + 4, :], half)
    for block in range(half // 8):
        rows = [packed[c * half + block * 8 : c * half + block * 8 + 8, :] for c in range(4)]
        out[:, block * LANES : (block + 1) * LANES] = check_sums(
            rows[:3], rows[3], width[block * 8 : block * 8 + 8], checks.at[block]
        )


def far_kernel(
    sources, kinds, pair_ref, packed, arrived, own_check, up_inverse, down_inverse, signs,
    last_bins, other_last_bins, table, translations, other_translations, out,
    spectra, kernels, high_table, low_table, density, totals, check, checks, near_kernels,
    densities, sems,
):
    leaves, entries = sources.shape
    half = leaves // 2
    rows = half // 2
    blocks = arrived.shape[0] // 64
    kind_count = translations.shape[0]
    pair = pair_ref[0]

    table_copy = pltpu.make_async_copy(table, high_table, sems.at[0])
    table_copy.start()
    kernel_copies = []
    for side, bins in enumerate((translations, other_translations)):
        for t in range(TILES - 1):
            kernel_copies.append(pltpu.make_async_copy(
                bins.at[:, :, pl.ds(t * LANES, LANES)],
                kernels.at[pl.ds(0, kind_count), pl.ds(16 * side + 2 * t, 2), :],
                sems.at[1 + len(kernel_copies)],
            ))
    for copy in kernel_copies:
        copy.start()
    for side, last in enumerate((last_bins, other_last_bins)):
        row = 16 * side + 2 * TILES - 2
        kernels[:kind_count, row : row + 2, :] = last[...]
    kernels[kind_count] = jnp.zeros((ROWS, LANES), jnp.float32)

    width = block_transpose(
        per_leaf(packed[4 * half + 3 : 4 * half + 4, :], rows, pair * half)
    )
    offsets = [
        block_transpose(packed[pl.ds(pl.multiple_of(c * half + pair * rows, 8), rows), :])
        for c in range(3)
    ]
    for q, kernel in surface_kernels(offsets, width):
        near_kernels[pl.ds(8 * q, 8), :] = kernel

    density[...] = jnp.zeros(density.shape, jnp.float32)
    check[0, :, :] = own_check[:, :LANES]
    check[1, :, :] = own_check[:, LANES:]

    def arrive(block, carry):
        beads = [
            arrived[pl.ds(pl.multiple_of(block * 64, 64) + ch, 8, stride=8), :] for ch in range(5)
        ]
        check[leaves // 16 + block, :, :] = check_sums(beads[:3], beads[3], beads[4], checks)
        return carry

    if blocks == 1:
        arrive(0, 0)
    else:
        lax.fori_loop(0, blocks, arrive, 0)
    count = check.shape[0]
    for first in range(0, count, 3):
        some = range(first, min(first + 3, count))
        density[16 * first : 16 * first + 16 * len(some), :Q] = upward(
            jnp.concatenate([check[n] for n in some], 1), up_inverse[...]
        )
    table_copy.wait()
    low_table[...] = low_part(high_table[...])
    sign = jnp.where(pair == 1, signs[1:2, :], signs[0:1, :])
    other_sign = jnp.where(pair == 1, signs[0:1, :], signs[1:2, :])
    store_spectra(
        jnp.concatenate([density[...] * sign, density[...] * other_sign], 0),
        high_table, low_table, spectra,
    )
    for copy in kernel_copies:
        copy.wait()

    def translate(t, carry):
        leaf = pair * half + t
        sums = [[None] * 4, [None] * 4]
        for entry in range(entries):
            kind = kinds[leaf, entry]
            start = pl.multiple_of(sources[leaf, entry], ROWS)
            for side in range(2):
                k_re = kernels[kind, pl.ds(16 * side, 8, stride=2), :]
                k_im = kernels[kind, pl.ds(16 * side + 1, 8, stride=2), :]
                s_re = spectra[pl.ds(start + 16 * side, 8), :]
                s_im = spectra[pl.ds(start + 16 * side + 8, 8), :]
                terms = (k_re * s_re, k_im * s_im, k_re * s_im, k_im * s_re)
                for n, term in enumerate(terms):
                    sums[side][n] = term if sums[side][n] is None else sums[side][n] + term
        start = pl.multiple_of(t * ROWS, ROWS)
        for side in range(2):
            rr, ii, ri, ir = sums[side]
            totals[pl.ds(start + 16 * side, 8), :] = rr - ii
            totals[pl.ds(start + 16 * side + 8, 8), :] = ri + ir
        return carry

    lax.fori_loop(0, half, translate, 0, unroll=2)

    lane = iota((half, LANES), 1)
    sides = []
    for side in range(2):
        columns = []
        for c in range(2):
            for t in range(TILES):
                line = totals[pl.ds(16 * side + c * 8 + t, half, stride=ROWS), :]
                if t == TILES - 1:
                    line = jnp.where(lane < BINS - t * LANES, line, 0.0)
                columns.append(line)
        sides.append(jnp.concatenate(columns, 1))
    high, low = split(jnp.concatenate(sides, 0))
    across = (((1,), (1,)), ((), ()))
    both = lax.dot_general(
        jnp.concatenate([high, low], 0), high_table[...], across,
        preferred_element_type=jnp.float32,
    )
    check = both[:leaves] + both[leaves:] + lax.dot_general(
        high, low_table[...], across, preferred_element_type=jnp.float32
    )
    check = (check[:half] * sign + check[half:] * other_sign)[:, :Q] * (1.0 / G)

    leaf_of = 2 * (lane & 7) + (lane >> 6)
    spread = jnp.where(iota((half, LANES), 0) == leaf_of, 1.0, 0.0)
    down = jnp.dot(
        check, down_inverse[...], precision=precise, preferred_element_type=jnp.float32
    )
    densities[...] = lax.dot_general(
        down, spread, (((0,), (0,)), ((), ())), precision=precise,
        preferred_element_type=jnp.float32,
    )
    parts = [jnp.zeros((rows, LANES), jnp.float32)] * 4
    for q in range(Q):
        term = near_kernels[8 * q : 8 * q + 8, :] * densities[q : q + 1, :]
        parts[q % 4] = parts[q % 4] + term
    out[...] = block_transpose((parts[0] + parts[1]) + (parts[2] + parts[3]))


def near_kernel(
    near_source, pair_ref, owner_ref, swapped, placed, passed, far, counts, decay_rate, stress,
    potential, new_stress, table, targets, sums,
):
    entries, leaves = near_source.shape
    half = leaves // 2
    pair = pair_ref[0]
    low = iota((half, LANES), 1) < BCAP
    swapped_from = jnp.where(((owner_ref[0] & 1) ^ pair) == 1, 0, 2)
    for n, rows_of in ((swapped_from, swapped), (1, placed), (2 - swapped_from, passed)):
        first = n * (leaves * 8)
        for ch in range(4):
            rows = rows_of[ch * half : (ch + 1) * half, :]
            turned = pltpu.roll(rows, BCAP, 1)
            table[pl.ds(first + ch, half, stride=16), :] = jnp.where(low, rows, turned)
            table[pl.ds(first + 8 + ch, half, stride=16), :] = jnp.where(low, turned, rows)
    for ch in range(3):
        mine = placed[pl.ds(pl.multiple_of(ch * half + pair * (half // 2), 8), half // 2), :]
        flipped = mine.T
        for r in range(half // 2):
            for h in range(2):
                start = ((2 * r + h) * 3 + ch) * BCAP
                targets[pl.ds(start, BCAP), :] = jnp.broadcast_to(
                    flipped[h * BCAP : (h + 1) * BCAP, r : r + 1], (BCAP, LANES)
                )
    low = iota((8, LANES), 1) < BCAP

    part = BCAP // 2

    def half_leaf(step, carry):
        t, side = step // 2, step % 2
        leaf = pair * half + t
        start = pl.multiple_of(t * 3 * BCAP + side * part, 8)
        tx, ty, tz = [targets[pl.ds(start + ch * BCAP, part), :] for ch in range(3)]
        total = jnp.zeros((part, LANES), jnp.float32)
        for n in range(entries // 2):
            left = pl.multiple_of(near_source[2 * n, leaf] * 8, 8)
            right = pl.multiple_of(near_source[2 * n + 1, leaf] * 8, 8)
            both = jnp.where(low, table[pl.ds(left, 8), :], table[pl.ds(right, 8), :])
            gx, gy, gz = tx - both[0:1], ty - both[1:2], tz - both[2:3]
            squared = gx * gx + gy * gy + (gz * gz + softening)
            total = total + lax.rsqrt(squared) * both[3:4]
        sums[pl.ds(pl.multiple_of(step * part, 8), part), :] = total
        return carry

    lax.fori_loop(0, 2 * half, half_leaf, 0, unroll=2)
    rows = half // 2
    for r in range(rows):
        block = sums[r * LANES : (r + 1) * LANES, :].T
        potential[r : r + 1, :] = jnp.sum(block, axis=0, keepdims=True)
    combined = potential[...] + far[...]
    beads = per_leaf(counts[...].astype(jnp.float32), rows, pair * half)
    slot = iota((rows, LANES), 1) & (BCAP - 1)
    occupied = slot.astype(jnp.float32) < beads
    decay = per_leaf(decay_rate[...], rows)
    potential[...] = jnp.where(occupied, combined, 0.0)
    new_stress[...] = jnp.where(occupied, decay * stress[...] + combined, 0.0)


VMEM = pl.BlockSpec(memory_space=pltpu.VMEM)
SMEM = pl.BlockSpec(memory_space=pltpu.SMEM)
ANY = pl.BlockSpec(memory_space=pl.ANY)
MIB = 1024 * 1024


def call(kernel, outs, in_specs, scratch=(), limit=40, grid=(), flops=0, bytes_accessed=0):
    return pl.pallas_call(
        kernel,
        out_shape=outs,
        grid=grid,
        in_specs=in_specs,
        out_specs=jax.tree.map(lambda _: VMEM, outs),
        scratch_shapes=list(scratch),
        compiler_params=pltpu.CompilerParams(vmem_limit_bytes=limit * MIB),
        cost_estimate=pl.CostEstimate(
            flops=flops, bytes_accessed=bytes_accessed, transcendentals=0
        ),
    )


def body(
    offsets,
    charges,
    stress,
    decay_rate,
    morton_keys,
    levels,
    bead_counts,
    send_boxes,
    m2l_source,
    m2l_type,
    m2l_count,
    near_source,
    up_inverse,
    down_inverse,
    translations,
):
    f32 = jnp.float32
    leaves = morton_keys.shape[0]
    half = leaves // 2
    parts = lax.axis_size("wide") * lax.axis_size("narrow")
    table = jnp.asarray(transform_table())
    signs = jnp.asarray(sign_rows())
    pair = lax.axis_index("pair").reshape(1)
    owner = (
        lax.axis_index("wide") * lax.axis_size("narrow") + lax.axis_index("narrow")
    ).reshape(1)
    kind_count = translations.shape[0]

    other_translations = lax.ppermute(translations, "pair", [(0, 1), (1, 0)])
    packed, blocks, placed, sources, kinds = call(
        functools.partial(pack_kernel, kind_count),
        [
            jax.ShapeDtypeStruct((4 * half + 8, LANES), f32),
            jax.ShapeDtypeStruct((8 * parts, LANES), f32),
            jax.ShapeDtypeStruct((4 * half, LANES), f32),
            jax.ShapeDtypeStruct(m2l_source.shape, jnp.int32),
            jax.ShapeDtypeStruct(m2l_type.shape, jnp.int32),
        ],
        [VMEM] * 9,
        limit=62,
    )(
        offsets, charges.reshape(half, LANES), morton_keys.reshape(1, leaves),
        levels.reshape(1, leaves), bead_counts.reshape(1, leaves), send_boxes,
        m2l_source, m2l_type, m2l_count.reshape(1, leaves),
    )
    arrived = lax.all_to_all(
        blocks.reshape(parts, 8, LANES), PARTS, split_axis=0, concat_axis=0, tiled=True
    ).reshape(8 * parts, LANES)
    swaps = [(2 * d, 2 * (d ^ 1)) for d in range(parts)]
    for d in range(1, parts - 1, 2):
        swaps += [(2 * d + 1, 2 * d + 3), (2 * d + 3, 2 * d + 1)]
    swapped = lax.ppermute(placed, PARTS + ("pair",), swaps)
    own_check = call(
        own_kernel,
        jax.ShapeDtypeStruct((Q, leaves // 16 * LANES), f32),
        [VMEM],
        [pltpu.VMEM((leaves // 16, Q * 8, LANES), f32)],
        flops=4 * 10**10,
    )(packed)
    passed = lax.ppermute(swapped, "pair", [(0, 1), (1, 0)])

    last = pl.BlockSpec((kind_count, 2, LANES), lambda i: (0, 0, TILES - 1))
    far = call(
        far_kernel,
        jax.ShapeDtypeStruct((half // 2, LANES), f32),
        [SMEM] * 3 + [VMEM] * 6 + [last] * 2 + [ANY] * 3,
        [
            pltpu.VMEM(((leaves + 2 * parts) * ROWS, LANES), f32),
            pltpu.VMEM((kind_count + 1, ROWS, LANES), f32),
            pltpu.VMEM(table.shape, jnp.bfloat16),
            pltpu.VMEM(table.shape, jnp.bfloat16),
            pltpu.VMEM((leaves + 2 * parts, QPAD), f32),
            pltpu.VMEM((half * ROWS, LANES), f32),
            pltpu.VMEM(((leaves + 2 * parts) // 16, Q, LANES), f32),
            pltpu.VMEM((Q * 8, LANES), f32),
            pltpu.VMEM((Q * 8, LANES), f32),
            pltpu.VMEM((Q, LANES), f32),
            pltpu.SemaphoreType.DMA((2 * TILES - 1,)),
        ],
        grid=(1,),
        flops=10**10,
        bytes_accessed=4 * 10**6,
    )(
        sources, kinds, pair, packed, arrived, own_check, up_inverse, down_inverse, signs,
        translations, other_translations, table, translations, other_translations,
    )

    out = jax.ShapeDtypeStruct((half // 2, LANES), f32)
    potential, new_stress = call(
        near_kernel,
        [out, out],
        [SMEM] * 3 + [VMEM] * 7,
        [
            pltpu.VMEM((3 * leaves * 8, LANES), f32),
            pltpu.VMEM((half * 3 * BCAP, LANES), f32),
            pltpu.VMEM((half * BCAP, LANES), f32),
        ],
    )(
        near_source.T, pair, owner, swapped, placed, passed, far, bead_counts.reshape(1, leaves),
        decay_rate.reshape(1, half), stress.reshape(half // 2, LANES),
    )
    return potential.reshape(-1), new_stress.reshape(-1)


def solution(mesh):
    return jax.shard_map(
        body,
        mesh=mesh,
        in_specs=(
            P(None, ("groups", "wide", "narrow")),
            P(("groups", "wide", "narrow")),
            P(("groups", "wide", "narrow", "pair")),
            P(("groups", "wide", "narrow", "pair")),
            P(("groups", "wide", "narrow")),
            P(("groups", "wide", "narrow")),
            P(("groups", "wide", "narrow")),
            P(("groups", "wide", "narrow"), None),
            P(("groups", "wide", "narrow"), None),
            P(("groups", "wide", "narrow"), None),
            P(("groups", "wide", "narrow")),
            P(("groups", "wide", "narrow"), None),
            P(),
            P(),
            P(None, None, "pair"),
        ),
        out_specs=(
            P(("groups", "wide", "narrow", "pair")),
            P(("groups", "wide", "narrow", "pair")),
        ),
        check_vma=False,
    )
```

```python
import functools

import jax
import jax.numpy as jnp
import ml_dtypes
import numpy as np
from jax import lax
from jax.experimental import pallas as pl
from jax.experimental.pallas import tpu as pltpu
from jax.sharding import PartitionSpec as P

PGRID = 12
G = 1728
MAXL = 10
BCAP = 64
Q = 152
QPAD = 160
LANES = 128
BINS = 864
TILES = 7
ROWS = 32
precise = lax.Precision.HIGHEST
softening = 0.04
surface_reach = 1.25
CELLS = [
    (i, j, k)
    for i in range(6)
    for j in range(6)
    for k in range(6)
    if 0 in (i, j, k) or 5 in (i, j, k)
]
PARTS = ("wide", "narrow")


def transform_table():
    cells = np.array(CELLS)
    bins = np.arange(BINS)
    freq = np.stack([bins // 144, bins // 12 % 12, bins % 12])
    angle = (cells @ freq % PGRID) * (2.0 * np.pi / PGRID)
    table = np.zeros((QPAD, 2 * TILES * LANES))
    table[:Q, :BINS] = np.cos(angle)
    table[:Q, TILES * LANES : TILES * LANES + BINS] = -np.sin(angle)
    table[np.abs(table) < 1e-9] = 0.0
    return table.astype(ml_dtypes.bfloat16)


def low_part(high):
    root = np.sqrt(0.75)
    held = float(np.asarray(root).astype(ml_dtypes.bfloat16))
    scale = (root - held) / (held * (held * held - 1.0) * (held * held - 0.25))
    value = high.astype(jnp.float32)
    square = value * value
    return (value * (square - 1.0) * (square - 0.25) * scale).astype(jnp.bfloat16)


def sign_rows():
    rows = np.zeros((8, QPAD), np.float32)
    rows[0, :Q] = 1.0
    rows[1, :Q] = [(-1.0) ** i for i, _, _ in CELLS]
    return rows


def iota(shape, dim):
    return lax.broadcasted_iota(jnp.int32, shape, dim)


def per_leaf(values, count, first=0):
    shape = (count, values.shape[1])
    leaf, lane = first + 2 * iota(shape, 0), iota(shape, 1)
    even = jnp.sum(jnp.where(lane == leaf, values, 0.0), axis=1, keepdims=True)
    odd = jnp.sum(jnp.where(lane == leaf + 1, values, 0.0), axis=1, keepdims=True)
    return jnp.where(iota((count, LANES), 1) < BCAP, even, odd)


def block_transpose(x):
    lane, row = iota(x.shape, 1), iota(x.shape, 0)
    for k in (1, 2, 4):
        row_bit, lane_bit = (row & k) != 0, (lane & k) != 0
        below = pltpu.roll(pltpu.roll(x, 8 - k, 0), k, 1)
        above = pltpu.roll(pltpu.roll(x, k, 0), LANES - k, 1)
        x = jnp.where(row_bit == lane_bit, x, jnp.where(lane_bit, below, above))
    return x


def split(x):
    high = x.astype(jnp.bfloat16)
    return high, (x - high.astype(jnp.float32)).astype(jnp.bfloat16)


def axis_squares(offset, width):
    area = width * width
    planes = [surface_reach * 0.5 * (i - 2.5) / 2.5 for i in range(6)]
    return [(plane - offset) * (plane - offset) * area for plane in planes]


def surface_kernels(offsets, width):
    gx, gy, gz = [axis_squares(offset, width) for offset in offsets]
    gz = [g + softening for g in gz]
    last, gxy = None, None
    for q, (i, j, k) in enumerate(CELLS):
        if last != (i, j):
            last, gxy = (i, j), gx[i] + gy[j]
        yield q, lax.rsqrt(gxy + gz[k])


def check_sums(offsets, weights, width, checks):
    offsets = [block_transpose(x) for x in offsets]
    weights, width = block_transpose(weights), block_transpose(width)
    for q, kernel in surface_kernels(offsets, width):
        checks[pl.ds(8 * q, 8), :] = kernel * weights
    check = checks[pl.ds(0, Q, stride=8), :]
    for s in range(1, 8):
        check = check + checks[pl.ds(s, Q, stride=8), :]
    return check


def upward(check, up_inverse):
    density = lax.dot_general(
        check, up_inverse, (((0,), (0,)), ((), ())), precision=precise,
        preferred_element_type=jnp.float32,
    )
    blocks = check.shape[1] // LANES
    density = density.reshape(2 * blocks, 8, 8, Q)
    total = density[:, 0]
    for g in range(1, 8):
        total = total + density[:, g]
    return total.reshape(16 * blocks, Q)


def store_spectra(density, table_high, table_low, target):
    count = density.shape[0] // 2
    high, low = split(density)
    both = jnp.concatenate([high, low], 0)
    for first in range(0, 2 * TILES, 2):
        columns = pl.ds(first * LANES, 2 * LANES)
        part = jnp.dot(both, table_high[:, columns], preferred_element_type=jnp.float32)
        spectra = part[: 2 * count] + part[2 * count :] + jnp.dot(
            high, table_low[:, columns], preferred_element_type=jnp.float32
        )
        for tile in range(first, first + 2):
            for side in range(2):
                for block in range(count // 16):
                    for h in range(2):
                        row = side * count + block * 16 + h * 8
                        start = (block * 16 + h) * ROWS + 16 * side + 8 * (tile // TILES) + tile % TILES
                        target[pl.ds(start, 8, stride=2 * ROWS), :] = spectra[
                            row : row + 8, (tile - first) * LANES : (tile - first + 1) * LANES
                        ]


def pack_kernel(
    kind_count, offsets, charges, keys, levels, counts, send_boxes, m2l_source, m2l_type, m2l_count,
    out, blocks, placed, sources, kinds,
):
    leaves = keys.shape[1]
    half = leaves // 2
    out[4 * half :, :] = jnp.zeros((8, LANES), jnp.float32)
    width = jnp.left_shift(jnp.ones_like(levels[...]), MAXL - levels[...]).astype(jnp.float32)
    for a in range(3):
        summed = jnp.zeros_like(keys[...])
        for bit in range(MAXL):
            summed = summed + (jnp.right_shift(keys[...], 3 * bit + a) & 1) * (1 << bit)
        out[4 * half + a : 4 * half + a + 1, :leaves] = summed.astype(jnp.float32) + 0.5 * width
    out[4 * half + 3 : 4 * half + 4, :leaves] = width
    for r in range(half):
        out[pl.ds(r, 3, stride=half), :] = offsets[:, r * LANES : (r + 1) * LANES]
    beads = per_leaf(counts[...].astype(jnp.float32), half)
    slot = iota((half, LANES), 1) & (BCAP - 1)
    out[3 * half : 4 * half, :] = jnp.where(slot.astype(jnp.float32) < beads, charges[...], 0.0)

    entry = iota(m2l_type.shape, 1)
    square = (leaves, leaves)
    live = jnp.sum(
        jnp.where(iota(square, 0) == iota(square, 1), m2l_count[...].astype(jnp.float32), 0.0),
        axis=1, keepdims=True,
    )
    kinds[...] = jnp.where(entry.astype(jnp.float32) < live, m2l_type[...], kind_count)
    sources[...] = m2l_source[...] * ROWS

    spread = per_leaf(width, half)
    for ch in range(3):
        center = per_leaf(out[4 * half + ch : 4 * half + ch + 1, :leaves], half)
        placed[ch * half : (ch + 1) * half, :] = center + spread * out[ch * half : (ch + 1) * half, :]
    placed[3 * half :, :] = out[3 * half : 4 * half, :]

    sends = send_boxes.shape[1]
    lane = iota((8, LANES), 1)
    for block in range(sends // 16):
        picked = []
        for c in range(2):
            column = block * 16 + 2 * iota((8, sends), 0) + c
            box = jnp.sum(
                jnp.where(iota((8, sends), 1) == column, send_boxes[...].astype(jnp.float32), 0.0),
                axis=1, keepdims=True,
            ).astype(jnp.int32)
            width_here = jnp.sum(
                jnp.where(iota((8, leaves), 1) == box, width, 0.0), axis=1, keepdims=True
            )
            row_of = jnp.broadcast_to(box >> 1, (8, LANES))
            found = [jnp.zeros((8, LANES), jnp.float32)] * 4
            for r in range(half):
                here = row_of == r
                for ch in range(4):
                    found[ch] = jnp.where(here, out[ch * half + r : ch * half + r + 1, :], found[ch])
            aligned = jnp.broadcast_to((box & 1) == c, (8, LANES))
            found = [jnp.where(aligned, x, pltpu.roll(x, BCAP, 1)) for x in found]
            picked.append(found + [jnp.broadcast_to(width_here, (8, LANES))])
        for ch in range(5):
            blocks[pl.ds(block * 64 + ch, 8, stride=8), :] = jnp.where(
                lane < BCAP, picked[0][ch], picked[1][ch]
            )
        for ch in range(5, 8):
            blocks[pl.ds(block * 64 + ch, 8, stride=8), :] = jnp.zeros((8, LANES), jnp.float32)


def own_kernel(pair_ref, packed, placed, out, eval_kernels, targets, checks):
    half = (packed.shape[0] - 8) // 4
    rows = half // 2
    pair = pair_ref[0]
    width = per_leaf(packed[4 * half + 3 : 4 * half + 4, :], half)
    for block in range(half // 8):
        beads = [packed[c * half + block * 8 : c * half + block * 8 + 8, :] for c in range(4)]
        out[:, block * LANES : (block + 1) * LANES] = check_sums(
            beads[:3], beads[3], width[block * 8 : block * 8 + 8], checks.at[block]
        )
    width = block_transpose(
        per_leaf(packed[4 * half + 3 : 4 * half + 4, :], rows, pair * half)
    )
    offsets = [
        block_transpose(packed[pl.ds(pl.multiple_of(c * half + pair * rows, 8), rows), :])
        for c in range(3)
    ]
    for q, kernel in surface_kernels(offsets, width):
        eval_kernels[pl.ds(8 * q, 8), :] = kernel
    for ch in range(3):
        mine = placed[pl.ds(pl.multiple_of(ch * half + pair * rows, 8), rows), :]
        flipped = mine.T
        for r in range(rows):
            for h in range(2):
                start = ((2 * r + h) * 3 + ch) * BCAP
                targets[pl.ds(start, BCAP), :] = jnp.broadcast_to(
                    flipped[h * BCAP : (h + 1) * BCAP, r : r + 1], (BCAP, LANES)
                )


def far_kernel(
    sources, kinds, pair_ref, arrived, own_check, eval_kernels, up_inverse, down_inverse, signs,
    last_bins, other_last_bins, table, translations, other_translations, out,
    spectra, kernels, high_table, low_table, density, totals, check, checks, densities, sems,
):
    leaves, entries = sources.shape
    half = leaves // 2
    rows = half // 2
    blocks = arrived.shape[0] // 64
    kind_count = translations.shape[0]
    pair = pair_ref[0]

    table_copy = pltpu.make_async_copy(table, high_table, sems.at[0])
    table_copy.start()
    kernel_copies = []
    for side, bins in enumerate((translations, other_translations)):
        for t in range(TILES - 1):
            kernel_copies.append(pltpu.make_async_copy(
                bins.at[:, :, pl.ds(t * LANES, LANES)],
                kernels.at[pl.ds(0, kind_count), pl.ds(16 * side + 2 * t, 2), :],
                sems.at[1 + len(kernel_copies)],
            ))
    for copy in kernel_copies:
        copy.start()
    for side, last in enumerate((last_bins, other_last_bins)):
        row = 16 * side + 2 * TILES - 2
        kernels[:kind_count, row : row + 2, :] = last[...]
    kernels[kind_count] = jnp.zeros((ROWS, LANES), jnp.float32)

    density[...] = jnp.zeros(density.shape, jnp.float32)
    check[0, :, :] = own_check[:, :LANES]
    check[1, :, :] = own_check[:, LANES:]

    def arrive(block, carry):
        beads = [
            arrived[pl.ds(pl.multiple_of(block * 64, 64) + ch, 8, stride=8), :] for ch in range(5)
        ]
        check[leaves // 16 + block, :, :] = check_sums(beads[:3], beads[3], beads[4], checks)
        return carry

    if blocks == 1:
        arrive(0, 0)
    else:
        lax.fori_loop(0, blocks, arrive, 0)
    count = check.shape[0]
    for first in range(0, count, 3):
        some = range(first, min(first + 3, count))
        density[16 * first : 16 * first + 16 * len(some), :Q] = upward(
            jnp.concatenate([check[n] for n in some], 1), up_inverse[...]
        )
    table_copy.wait()
    low_table[...] = low_part(high_table[...])
    sign = jnp.where(pair == 1, signs[1:2, :], signs[0:1, :])
    other_sign = jnp.where(pair == 1, signs[0:1, :], signs[1:2, :])
    store_spectra(
        jnp.concatenate([density[...] * sign, density[...] * other_sign], 0),
        high_table, low_table, spectra,
    )
    def translate(side, t):
        leaf = pair * half + t
        sums = [[None] * 4, [None] * 4]
        for entry in range(entries):
            kind = kinds[leaf, entry]
            start = pl.multiple_of(sources[leaf, entry], ROWS)
            k_re = kernels[kind, pl.ds(16 * side, 8, stride=2), :]
            k_im = kernels[kind, pl.ds(16 * side + 1, 8, stride=2), :]
            s_re = spectra[pl.ds(start + 16 * side, 8), :]
            s_im = spectra[pl.ds(start + 16 * side + 8, 8), :]
            terms = (k_re * s_re, k_im * s_im, k_re * s_im, k_im * s_re)
            chain = sums[entry % 2]
            for n, term in enumerate(terms):
                chain[n] = term if chain[n] is None else chain[n] + term
        rr, ii, ri, ir = [x + y for x, y in zip(*sums)]
        start = pl.multiple_of(t * ROWS, ROWS)
        totals[pl.ds(start + 16 * side, 8), :] = rr - ii
        totals[pl.ds(start + 16 * side + 8, 8), :] = ri + ir

    for side in range(2):
        for copy in kernel_copies[side * (TILES - 1) : (side + 1) * (TILES - 1)]:
            copy.wait()
        lax.fori_loop(0, half, lambda t, c, side=side: (translate(side, t), c)[1], 0, unroll=4)

    lane = iota((half, LANES), 1)
    sides = []
    for side in range(2):
        columns = []
        for c in range(2):
            for t in range(TILES):
                line = totals[pl.ds(16 * side + c * 8 + t, half, stride=ROWS), :]
                if t == TILES - 1:
                    line = jnp.where(lane < BINS - t * LANES, line, 0.0)
                columns.append(line)
        sides.append(jnp.concatenate(columns, 1))
    high, low = split(jnp.concatenate(sides, 0))
    across = (((1,), (1,)), ((), ()))
    both = lax.dot_general(
        jnp.concatenate([high, low], 0), high_table[...], across,
        preferred_element_type=jnp.float32,
    )
    check = both[:leaves] + both[leaves:] + lax.dot_general(
        high, low_table[...], across, preferred_element_type=jnp.float32
    )
    check = (check[:half] * sign + check[half:] * other_sign)[:, :Q] * (1.0 / G)

    leaf_of = 2 * (lane & 7) + (lane >> 6)
    spread = jnp.where(iota((half, LANES), 0) == leaf_of, 1.0, 0.0)
    down = jnp.dot(
        check, down_inverse[...], precision=precise, preferred_element_type=jnp.float32
    )
    densities[...] = lax.dot_general(
        down, spread, (((0,), (0,)), ((), ())), precision=precise,
        preferred_element_type=jnp.float32,
    )
    parts = [jnp.zeros((rows, LANES), jnp.float32)] * 4
    for q in range(Q):
        term = eval_kernels[8 * q : 8 * q + 8, :] * densities[q : q + 1, :]
        parts[q % 4] = parts[q % 4] + term
    out[...] = block_transpose((parts[0] + parts[1]) + (parts[2] + parts[3]))


def near_kernel(
    near_source, pair_ref, owner_ref, swapped, placed, passed, targets, far, counts, decay_rate,
    stress, potential, new_stress, table, merged, sums,
):
    entries, leaves = near_source.shape
    half = leaves // 2
    pair = pair_ref[0]
    low = iota((half, LANES), 1) < BCAP
    swapped_from = jnp.where(((owner_ref[0] & 1) ^ pair) == 1, 0, 2)
    for n, rows_of in ((swapped_from, swapped), (1, placed), (2 - swapped_from, passed)):
        first = n * (leaves * 8)
        for ch in range(4):
            rows = rows_of[ch * half : (ch + 1) * half, :]
            turned = pltpu.roll(rows, BCAP, 1)
            table[pl.ds(first + ch, half, stride=16), :] = jnp.where(low, rows, turned)
            table[pl.ds(first + 8 + ch, half, stride=16), :] = jnp.where(low, turned, rows)
    low = iota((8, LANES), 1) < BCAP

    def merge(t, carry):
        leaf = pair * half + t
        for n in range(entries // 2):
            left = pl.multiple_of(near_source[2 * n, leaf] * 8, 8)
            right = pl.multiple_of(near_source[2 * n + 1, leaf] * 8, 8)
            start = pl.multiple_of((t * (entries // 2) + n) * 8, 8)
            merged[pl.ds(start, 8), :] = jnp.where(
                low, table[pl.ds(left, 8), :], table[pl.ds(right, 8), :]
            )
        return carry

    lax.fori_loop(0, half, merge, 0, unroll=4)

    def one_leaf(t, carry):
        start = pl.multiple_of(t * 3 * BCAP, 8)
        tx, ty, tz = [targets[pl.ds(start + ch * BCAP, BCAP), :] for ch in range(3)]
        total = jnp.zeros((BCAP, LANES), jnp.float32)
        for n in range(entries // 2):
            first = pl.multiple_of((t * (entries // 2) + n) * 8, 8)
            sx, sy, sz, weight = [merged[pl.ds(first + ch, 1), :] for ch in range(4)]
            gx, gy, gz = tx - sx, ty - sy, tz - sz
            squared = gx * gx + gy * gy + (gz * gz + softening)
            total = total + lax.rsqrt(squared) * weight
        sums[pl.ds(pl.multiple_of(t * BCAP, 8), BCAP), :] = total
        return carry

    lax.fori_loop(0, half, one_leaf, 0, unroll=2)
    rows = half // 2
    for r in range(rows):
        block = sums[r * LANES : (r + 1) * LANES, :].T
        potential[r : r + 1, :] = jnp.sum(block, axis=0, keepdims=True)
    combined = potential[...] + far[...]
    beads = per_leaf(counts[...].astype(jnp.float32), rows, pair * half)
    slot = iota((rows, LANES), 1) & (BCAP - 1)
    occupied = slot.astype(jnp.float32) < beads
    decay = per_leaf(decay_rate[...], rows)
    potential[...] = jnp.where(occupied, combined, 0.0)
    new_stress[...] = jnp.where(occupied, decay * stress[...] + combined, 0.0)


VMEM = pl.BlockSpec(memory_space=pltpu.VMEM)
SMEM = pl.BlockSpec(memory_space=pltpu.SMEM)
ANY = pl.BlockSpec(memory_space=pl.ANY)
MIB = 1024 * 1024


def call(kernel, outs, in_specs, scratch=(), limit=40, grid=(), flops=0, bytes_accessed=0):
    return pl.pallas_call(
        kernel,
        out_shape=outs,
        grid=grid,
        in_specs=in_specs,
        out_specs=jax.tree.map(lambda _: VMEM, outs),
        scratch_shapes=list(scratch),
        compiler_params=pltpu.CompilerParams(vmem_limit_bytes=limit * MIB),
        cost_estimate=pl.CostEstimate(
            flops=flops, bytes_accessed=bytes_accessed, transcendentals=0
        ),
    )


def body(
    offsets,
    charges,
    stress,
    decay_rate,
    morton_keys,
    levels,
    bead_counts,
    send_boxes,
    m2l_source,
    m2l_type,
    m2l_count,
    near_source,
    up_inverse,
    down_inverse,
    translations,
):
    f32 = jnp.float32
    leaves = morton_keys.shape[0]
    half = leaves // 2
    parts = lax.axis_size("wide") * lax.axis_size("narrow")
    table = jnp.asarray(transform_table())
    signs = jnp.asarray(sign_rows())
    pair = lax.axis_index("pair").reshape(1)
    owner = (
        lax.axis_index("wide") * lax.axis_size("narrow") + lax.axis_index("narrow")
    ).reshape(1)
    kind_count = translations.shape[0]

    other_translations = lax.ppermute(translations, "pair", [(0, 1), (1, 0)])
    packed, blocks, placed, sources, kinds = call(
        functools.partial(pack_kernel, kind_count),
        [
            jax.ShapeDtypeStruct((4 * half + 8, LANES), f32),
            jax.ShapeDtypeStruct((8 * parts, LANES), f32),
            jax.ShapeDtypeStruct((4 * half, LANES), f32),
            jax.ShapeDtypeStruct(m2l_source.shape, jnp.int32),
            jax.ShapeDtypeStruct(m2l_type.shape, jnp.int32),
        ],
        [VMEM] * 9,
        limit=62,
    )(
        offsets, charges.reshape(half, LANES), morton_keys.reshape(1, leaves),
        levels.reshape(1, leaves), bead_counts.reshape(1, leaves), send_boxes,
        m2l_source, m2l_type, m2l_count.reshape(1, leaves),
    )
    arrived = lax.all_to_all(
        blocks.reshape(parts, 8, LANES), PARTS, split_axis=0, concat_axis=0, tiled=True
    ).reshape(8 * parts, LANES)
    swaps = [(2 * d, 2 * (d ^ 1)) for d in range(parts)]
    for d in range(1, parts - 1, 2):
        swaps += [(2 * d + 1, 2 * d + 3), (2 * d + 3, 2 * d + 1)]
    swapped = lax.ppermute(placed, PARTS + ("pair",), swaps)
    own_check, eval_kernels, targets = call(
        own_kernel,
        [
            jax.ShapeDtypeStruct((Q, leaves // 16 * LANES), f32),
            jax.ShapeDtypeStruct((Q * 8, LANES), f32),
            jax.ShapeDtypeStruct((half * 3 * BCAP, LANES), f32),
        ],
        [SMEM] + [VMEM] * 2,
        [pltpu.VMEM((leaves // 16, Q * 8, LANES), f32)],
        flops=4 * 10**10,
    )(pair, packed, placed)
    passed = lax.ppermute(swapped, "pair", [(0, 1), (1, 0)])

    last = pl.BlockSpec((kind_count, 2, LANES), lambda i: (0, 0, TILES - 1))
    far = call(
        far_kernel,
        jax.ShapeDtypeStruct((half // 2, LANES), f32),
        [SMEM] * 3 + [VMEM] * 6 + [last] * 2 + [ANY] * 3,
        [
            pltpu.VMEM(((leaves + 2 * parts) * ROWS, LANES), f32),
            pltpu.VMEM((kind_count + 1, ROWS, LANES), f32),
            pltpu.VMEM(table.shape, jnp.bfloat16),
            pltpu.VMEM(table.shape, jnp.bfloat16),
            pltpu.VMEM((leaves + 2 * parts, QPAD), f32),
            pltpu.VMEM((half * ROWS, LANES), f32),
            pltpu.VMEM(((leaves + 2 * parts) // 16, Q, LANES), f32),
            pltpu.VMEM((Q * 8, LANES), f32),
            pltpu.VMEM((Q, LANES), f32),
            pltpu.SemaphoreType.DMA((2 * TILES - 1,)),
        ],
        grid=(1,),
        flops=10**10,
        bytes_accessed=4 * 10**6,
    )(
        sources, kinds, pair, arrived, own_check, eval_kernels, up_inverse, down_inverse, signs,
        translations, other_translations, table, translations, other_translations,
    )

    out = jax.ShapeDtypeStruct((half // 2, LANES), f32)
    potential, new_stress = call(
        near_kernel,
        [out, out],
        [SMEM] * 3 + [VMEM] * 8,
        [
            pltpu.VMEM((3 * leaves * 8, LANES), f32),
            pltpu.VMEM((half * near_source.shape[1] // 2 * 8, LANES), f32),
            pltpu.VMEM((half * BCAP, LANES), f32),
        ],
    )(
        near_source.T, pair, owner, swapped, placed, passed, targets, far, bead_counts.reshape(1, leaves),
        decay_rate.reshape(1, half), stress.reshape(half // 2, LANES),
    )
    return potential.reshape(-1), new_stress.reshape(-1)


def solution(mesh):
    return jax.shard_map(
        body,
        mesh=mesh,
        in_specs=(
            P(None, ("groups", "wide", "narrow")),
            P(("groups", "wide", "narrow")),
            P(("groups", "wide", "narrow", "pair")),
            P(("groups", "wide", "narrow", "pair")),
            P(("groups", "wide", "narrow")),
            P(("groups", "wide", "narrow")),
            P(("groups", "wide", "narrow")),
            P(("groups", "wide", "narrow"), None),
            P(("groups", "wide", "narrow"), None),
            P(("groups", "wide", "narrow"), None),
            P(("groups", "wide", "narrow")),
            P(("groups", "wide", "narrow"), None),
            P(),
            P(),
            P(None, None, "pair"),
        ),
        out_specs=(
            P(("groups", "wide", "narrow", "pair")),
            P(("groups", "wide", "narrow", "pair")),
        ),
        check_vma=False,
    )
```

```python
import functools

import jax
import jax.numpy as jnp
import ml_dtypes
import numpy as np
from jax import lax
from jax.experimental import pallas as pl
from jax.experimental.pallas import tpu as pltpu
from jax.sharding import PartitionSpec as P

PGRID = 12
G = 1728
MAXL = 10
BCAP = 64
Q = 152
QPAD = 160
LANES = 128
BINS = 864
TILES = 7
ROWS = 32
precise = lax.Precision.HIGHEST
softening = 0.04
surface_reach = 1.25
CELLS = [
    (i, j, k)
    for i in range(6)
    for j in range(6)
    for k in range(6)
    if 0 in (i, j, k) or 5 in (i, j, k)
]
PARTS = ("wide", "narrow")


def transform_table():
    cells = np.array(CELLS)
    bins = np.arange(BINS)
    freq = np.stack([bins // 144, bins // 12 % 12, bins % 12])
    angle = (cells @ freq % PGRID) * (2.0 * np.pi / PGRID)
    table = np.zeros((QPAD, 2 * TILES * LANES))
    table[:Q, :BINS] = np.cos(angle)
    table[:Q, TILES * LANES : TILES * LANES + BINS] = -np.sin(angle)
    table[np.abs(table) < 1e-9] = 0.0
    return table.astype(ml_dtypes.bfloat16)


def low_part(high):
    root = np.sqrt(0.75)
    held = float(np.asarray(root).astype(ml_dtypes.bfloat16))
    scale = (root - held) / (held * (held * held - 1.0) * (held * held - 0.25))
    value = high.astype(jnp.float32)
    square = value * value
    return (value * (square - 1.0) * (square - 0.25) * scale).astype(jnp.bfloat16)


def sign_rows():
    rows = np.zeros((8, QPAD), np.float32)
    rows[0, :Q] = 1.0
    rows[1, :Q] = [(-1.0) ** i for i, _, _ in CELLS]
    return rows


def iota(shape, dim):
    return lax.broadcasted_iota(jnp.int32, shape, dim)


def per_leaf(values, count, first=0):
    shape = (count, values.shape[1])
    leaf, lane = first + 2 * iota(shape, 0), iota(shape, 1)
    even = jnp.sum(jnp.where(lane == leaf, values, 0.0), axis=1, keepdims=True)
    odd = jnp.sum(jnp.where(lane == leaf + 1, values, 0.0), axis=1, keepdims=True)
    return jnp.where(iota((count, LANES), 1) < BCAP, even, odd)


def block_transpose(x):
    lane, row = iota(x.shape, 1), iota(x.shape, 0)
    for k in (1, 2, 4):
        row_bit, lane_bit = (row & k) != 0, (lane & k) != 0
        below = pltpu.roll(pltpu.roll(x, 8 - k, 0), k, 1)
        above = pltpu.roll(pltpu.roll(x, k, 0), LANES - k, 1)
        x = jnp.where(row_bit == lane_bit, x, jnp.where(lane_bit, below, above))
    return x


def split(x):
    high = x.astype(jnp.bfloat16)
    return high, (x - high.astype(jnp.float32)).astype(jnp.bfloat16)


def axis_squares(offset, width):
    area = width * width
    planes = [surface_reach * 0.5 * (i - 2.5) / 2.5 for i in range(6)]
    return [(plane - offset) * (plane - offset) * area for plane in planes]


def surface_kernels(offsets, width):
    gx, gy, gz = [axis_squares(offset, width) for offset in offsets]
    gz = [g + softening for g in gz]
    last, gxy = None, None
    for q, (i, j, k) in enumerate(CELLS):
        if last != (i, j):
            last, gxy = (i, j), gx[i] + gy[j]
        yield q, lax.rsqrt(gxy + gz[k])


def check_sums(offsets, weights, width, checks):
    offsets = [block_transpose(x) for x in offsets]
    weights, width = block_transpose(weights), block_transpose(width)
    for q, kernel in surface_kernels(offsets, width):
        checks[pl.ds(8 * q, 8), :] = kernel * weights
    check = checks[pl.ds(0, Q, stride=8), :]
    for s in range(1, 8):
        check = check + checks[pl.ds(s, Q, stride=8), :]
    return check


def upward(check, up_inverse):
    density = lax.dot_general(
        check, up_inverse, (((0,), (0,)), ((), ())), precision=precise,
        preferred_element_type=jnp.float32,
    )
    blocks = check.shape[1] // LANES
    density = density.reshape(2 * blocks, 8, 8, Q)
    total = density[:, 0]
    for g in range(1, 8):
        total = total + density[:, g]
    return total.reshape(16 * blocks, Q)


def store_spectra(density, table_high, table_low, target):
    count = density.shape[0] // 2
    high, low = split(density)
    both = jnp.concatenate([high, low], 0)
    for first in range(0, 2 * TILES, 2):
        columns = pl.ds(first * LANES, 2 * LANES)
        part = jnp.dot(both, table_high[:, columns], preferred_element_type=jnp.float32)
        spectra = part[: 2 * count] + part[2 * count :] + jnp.dot(
            high, table_low[:, columns], preferred_element_type=jnp.float32
        )
        for tile in range(first, first + 2):
            for side in range(2):
                for block in range(count // 16):
                    for h in range(2):
                        row = side * count + block * 16 + h * 8
                        start = (block * 16 + h) * ROWS + 16 * side + 8 * (tile // TILES) + tile % TILES
                        target[pl.ds(start, 8, stride=2 * ROWS), :] = spectra[
                            row : row + 8, (tile - first) * LANES : (tile - first + 1) * LANES
                        ]


def pack_kernel(
    kind_count, offsets, charges, keys, levels, counts, send_boxes, m2l_source, m2l_type, m2l_count,
    out, blocks, placed, sources, kinds,
):
    leaves = keys.shape[1]
    half = leaves // 2
    out[4 * half :, :] = jnp.zeros((8, LANES), jnp.float32)
    width = jnp.left_shift(jnp.ones_like(levels[...]), MAXL - levels[...]).astype(jnp.float32)
    for a in range(3):
        summed = jnp.zeros_like(keys[...])
        for bit in range(MAXL):
            summed = summed + (jnp.right_shift(keys[...], 3 * bit + a) & 1) * (1 << bit)
        out[4 * half + a : 4 * half + a + 1, :leaves] = summed.astype(jnp.float32) + 0.5 * width
    out[4 * half + 3 : 4 * half + 4, :leaves] = width
    for r in range(half):
        out[pl.ds(r, 3, stride=half), :] = offsets[:, r * LANES : (r + 1) * LANES]
    beads = per_leaf(counts[...].astype(jnp.float32), half)
    slot = iota((half, LANES), 1) & (BCAP - 1)
    out[3 * half : 4 * half, :] = jnp.where(slot.astype(jnp.float32) < beads, charges[...], 0.0)

    entry = iota(m2l_type.shape, 1)
    square = (leaves, leaves)
    live = jnp.sum(
        jnp.where(iota(square, 0) == iota(square, 1), m2l_count[...].astype(jnp.float32), 0.0),
        axis=1, keepdims=True,
    )
    kinds[...] = jnp.where(entry.astype(jnp.float32) < live, m2l_type[...], kind_count)
    sources[...] = m2l_source[...] * ROWS

    spread = per_leaf(width, half)
    for ch in range(3):
        center = per_leaf(out[4 * half + ch : 4 * half + ch + 1, :leaves], half)
        placed[ch * half : (ch + 1) * half, :] = center + spread * out[ch * half : (ch + 1) * half, :]
    placed[3 * half :, :] = out[3 * half : 4 * half, :]

    sends = send_boxes.shape[1]
    lane = iota((8, LANES), 1)
    for block in range(sends // 16):
        picked = []
        for c in range(2):
            column = block * 16 + 2 * iota((8, sends), 0) + c
            box = jnp.sum(
                jnp.where(iota((8, sends), 1) == column, send_boxes[...].astype(jnp.float32), 0.0),
                axis=1, keepdims=True,
            ).astype(jnp.int32)
            width_here = jnp.sum(
                jnp.where(iota((8, leaves), 1) == box, width, 0.0), axis=1, keepdims=True
            )
            row_of = jnp.broadcast_to(box >> 1, (8, LANES))
            found = [jnp.zeros((8, LANES), jnp.float32)] * 4
            for r in range(half):
                here = row_of == r
                for ch in range(4):
                    found[ch] = jnp.where(here, out[ch * half + r : ch * half + r + 1, :], found[ch])
            aligned = jnp.broadcast_to((box & 1) == c, (8, LANES))
            found = [jnp.where(aligned, x, pltpu.roll(x, BCAP, 1)) for x in found]
            picked.append(found + [jnp.broadcast_to(width_here, (8, LANES))])
        for ch in range(5):
            blocks[pl.ds(block * 64 + ch, 8, stride=8), :] = jnp.where(
                lane < BCAP, picked[0][ch], picked[1][ch]
            )
        for ch in range(5, 8):
            blocks[pl.ds(block * 64 + ch, 8, stride=8), :] = jnp.zeros((8, LANES), jnp.float32)


def own_kernel(packed, out, checks):
    half = (packed.shape[0] - 8) // 4
    width = per_leaf(packed[4 * half + 3 : 4 * half + 4, :], half)
    for block in range(half // 8):
        rows = [packed[c * half + block * 8 : c * half + block * 8 + 8, :] for c in range(4)]
        out[:, block * LANES : (block + 1) * LANES] = check_sums(
            rows[:3], rows[3], width[block * 8 : block * 8 + 8], checks.at[block]
        )


def far_kernel(
    sources, kinds, pair_ref, arrived, own_check, up_inverse, signs,
    last_bins, other_last_bins, table, translations, other_translations, totals,
    spectra, kernels, high_table, low_table, density, check, checks, sems,
):
    leaves, entries = sources.shape
    half = leaves // 2
    blocks = arrived.shape[0] // 64
    kind_count = translations.shape[0]
    pair = pair_ref[0]

    table_copy = pltpu.make_async_copy(table, high_table, sems.at[0])
    table_copy.start()
    kernel_copies = []
    for side, bins in enumerate((translations, other_translations)):
        for t in range(TILES - 1):
            kernel_copies.append(pltpu.make_async_copy(
                bins.at[:, :, pl.ds(t * LANES, LANES)],
                kernels.at[pl.ds(0, kind_count), pl.ds(16 * side + 2 * t, 2), :],
                sems.at[1 + len(kernel_copies)],
            ))
    for copy in kernel_copies:
        copy.start()
    for side, last in enumerate((last_bins, other_last_bins)):
        row = 16 * side + 2 * TILES - 2
        kernels[:kind_count, row : row + 2, :] = last[...]
    kernels[kind_count] = jnp.zeros((ROWS, LANES), jnp.float32)

    density[...] = jnp.zeros(density.shape, jnp.float32)
    check[0, :, :] = own_check[:, :LANES]
    check[1, :, :] = own_check[:, LANES:]

    def arrive(block, carry):
        beads = [
            arrived[pl.ds(pl.multiple_of(block * 64, 64) + ch, 8, stride=8), :] for ch in range(5)
        ]
        check[leaves // 16 + block, :, :] = check_sums(beads[:3], beads[3], beads[4], checks)
        return carry

    if blocks == 1:
        arrive(0, 0)
    else:
        lax.fori_loop(0, blocks, arrive, 0)
    count = check.shape[0]
    for first in range(0, count, 3):
        some = range(first, min(first + 3, count))
        density[16 * first : 16 * first + 16 * len(some), :Q] = upward(
            jnp.concatenate([check[n] for n in some], 1), up_inverse[...]
        )
    table_copy.wait()
    low_table[...] = low_part(high_table[...])
    sign = jnp.where(pair == 1, signs[1:2, :], signs[0:1, :])
    other_sign = jnp.where(pair == 1, signs[0:1, :], signs[1:2, :])
    store_spectra(
        jnp.concatenate([density[...] * sign, density[...] * other_sign], 0),
        high_table, low_table, spectra,
    )
    for copy in kernel_copies:
        copy.wait()

    def translate(t, carry):
        leaf = pair * half + t
        sums = [[None] * 4, [None] * 4]
        for entry in range(entries):
            kind = kinds[leaf, entry]
            start = pl.multiple_of(sources[leaf, entry], ROWS)
            for side in range(2):
                k_re = kernels[kind, pl.ds(16 * side, 8, stride=2), :]
                k_im = kernels[kind, pl.ds(16 * side + 1, 8, stride=2), :]
                s_re = spectra[pl.ds(start + 16 * side, 8), :]
                s_im = spectra[pl.ds(start + 16 * side + 8, 8), :]
                terms = (k_re * s_re, k_im * s_im, k_re * s_im, k_im * s_re)
                for n, term in enumerate(terms):
                    sums[side][n] = term if sums[side][n] is None else sums[side][n] + term
        start = pl.multiple_of(t * ROWS, ROWS)
        for side in range(2):
            rr, ii, ri, ir = sums[side]
            totals[pl.ds(start + 16 * side, 8), :] = rr - ii
            totals[pl.ds(start + 16 * side + 8, 8), :] = ri + ir
        return carry

    lax.fori_loop(0, half, translate, 0, unroll=2)


def evaluate(pair, packed, totals, table, signs, down_inverse, low_table, eval_kernels, densities):
    half = (packed.shape[0] - 8) // 4
    leaves = 2 * half
    rows = half // 2
    width = block_transpose(
        per_leaf(packed[4 * half + 3 : 4 * half + 4, :], rows, pair * half)
    )
    offsets = [
        block_transpose(packed[pl.ds(pl.multiple_of(c * half + pair * rows, 8), rows), :])
        for c in range(3)
    ]
    for q, kernel in surface_kernels(offsets, width):
        eval_kernels[pl.ds(8 * q, 8), :] = kernel
    sign = jnp.where(pair == 1, signs[1:2, :], signs[0:1, :])
    other_sign = jnp.where(pair == 1, signs[0:1, :], signs[1:2, :])
    low_table[...] = low_part(table[...])
    lane = iota((half, LANES), 1)
    sides = []
    for side in range(2):
        columns = []
        for c in range(2):
            for t in range(TILES):
                line = totals[pl.ds(16 * side + c * 8 + t, half, stride=ROWS), :]
                if t == TILES - 1:
                    line = jnp.where(lane < BINS - t * LANES, line, 0.0)
                columns.append(line)
        sides.append(jnp.concatenate(columns, 1))
    high, low = split(jnp.concatenate(sides, 0))
    across = (((1,), (1,)), ((), ()))
    both = lax.dot_general(
        jnp.concatenate([high, low], 0), table[...], across,
        preferred_element_type=jnp.float32,
    )
    check = both[:leaves] + both[leaves:] + lax.dot_general(
        high, low_table[...], across, preferred_element_type=jnp.float32
    )
    check = (check[:half] * sign + check[half:] * other_sign)[:, :Q] * (1.0 / G)

    leaf_of = 2 * (lane & 7) + (lane >> 6)
    spread = jnp.where(iota((half, LANES), 0) == leaf_of, 1.0, 0.0)
    down = jnp.dot(
        check, down_inverse[...], precision=precise, preferred_element_type=jnp.float32
    )
    densities[...] = lax.dot_general(
        down, spread, (((0,), (0,)), ((), ())), precision=precise,
        preferred_element_type=jnp.float32,
    )
    parts = [jnp.zeros((rows, LANES), jnp.float32)] * 4
    for q in range(Q):
        term = eval_kernels[8 * q : 8 * q + 8, :] * densities[q : q + 1, :]
        parts[q % 4] = parts[q % 4] + term
    return block_transpose((parts[0] + parts[1]) + (parts[2] + parts[3]))


def near_kernel(
    near_source, pair_ref, owner_ref, swapped, placed, passed, packed, totals, transform_table_ref,
    signs, down_inverse, counts, decay_rate, stress, potential, new_stress,
    table, targets, merged, sums, low_table, eval_kernels, densities,
):
    entries, leaves = near_source.shape
    half = leaves // 2
    pair = pair_ref[0]
    low = iota((half, LANES), 1) < BCAP
    far = evaluate(
        pair, packed, totals, transform_table_ref, signs, down_inverse, low_table, eval_kernels,
        densities,
    )
    swapped_from = jnp.where(((owner_ref[0] & 1) ^ pair) == 1, 0, 2)
    for n, rows_of in ((swapped_from, swapped), (1, placed), (2 - swapped_from, passed)):
        first = n * (leaves * 8)
        for ch in range(4):
            rows = rows_of[ch * half : (ch + 1) * half, :]
            turned = pltpu.roll(rows, BCAP, 1)
            table[pl.ds(first + ch, half, stride=16), :] = jnp.where(low, rows, turned)
            table[pl.ds(first + 8 + ch, half, stride=16), :] = jnp.where(low, turned, rows)
    for ch in range(3):
        mine = placed[pl.ds(pl.multiple_of(ch * half + pair * (half // 2), 8), half // 2), :]
        flipped = mine.T
        for r in range(half // 2):
            for h in range(2):
                start = ((2 * r + h) * 3 + ch) * BCAP
                targets[pl.ds(start, BCAP), :] = jnp.broadcast_to(
                    flipped[h * BCAP : (h + 1) * BCAP, r : r + 1], (BCAP, LANES)
                )
    low = iota((8, LANES), 1) < BCAP

    def merge(t, carry):
        leaf = pair * half + t
        for n in range(entries // 2):
            left = pl.multiple_of(near_source[2 * n, leaf] * 8, 8)
            right = pl.multiple_of(near_source[2 * n + 1, leaf] * 8, 8)
            start = pl.multiple_of((t * (entries // 2) + n) * 8, 8)
            merged[pl.ds(start, 8), :] = jnp.where(
                low, table[pl.ds(left, 8), :], table[pl.ds(right, 8), :]
            )
        return carry

    lax.fori_loop(0, half, merge, 0, unroll=4)

    def one_leaf(t, carry):
        start = pl.multiple_of(t * 3 * BCAP, 8)
        tx, ty, tz = [targets[pl.ds(start + ch * BCAP, BCAP), :] for ch in range(3)]
        total = jnp.zeros((BCAP, LANES), jnp.float32)
        for n in range(entries // 2):
            first = pl.multiple_of((t * (entries // 2) + n) * 8, 8)
            sx, sy, sz, weight = [merged[pl.ds(first + ch, 1), :] for ch in range(4)]
            gx, gy, gz = tx - sx, ty - sy, tz - sz
            squared = gx * gx + gy * gy + (gz * gz + softening)
            total = total + lax.rsqrt(squared) * weight
        sums[pl.ds(pl.multiple_of(t * BCAP, 8), BCAP), :] = total
        return carry

    lax.fori_loop(0, half, one_leaf, 0, unroll=2)
    rows = half // 2
    for r in range(rows):
        block = sums[r * LANES : (r + 1) * LANES, :].T
        potential[r : r + 1, :] = jnp.sum(block, axis=0, keepdims=True)
    combined = potential[...] + far
    beads = per_leaf(counts[...].astype(jnp.float32), rows, pair * half)
    slot = iota((rows, LANES), 1) & (BCAP - 1)
    occupied = slot.astype(jnp.float32) < beads
    decay = per_leaf(decay_rate[...], rows)
    potential[...] = jnp.where(occupied, combined, 0.0)
    new_stress[...] = jnp.where(occupied, decay * stress[...] + combined, 0.0)


VMEM = pl.BlockSpec(memory_space=pltpu.VMEM)
SMEM = pl.BlockSpec(memory_space=pltpu.SMEM)
ANY = pl.BlockSpec(memory_space=pl.ANY)
MIB = 1024 * 1024


def call(kernel, outs, in_specs, scratch=(), limit=40, grid=(), flops=0, bytes_accessed=0):
    return pl.pallas_call(
        kernel,
        out_shape=outs,
        grid=grid,
        in_specs=in_specs,
        out_specs=jax.tree.map(lambda _: VMEM, outs),
        scratch_shapes=list(scratch),
        compiler_params=pltpu.CompilerParams(vmem_limit_bytes=limit * MIB),
        cost_estimate=pl.CostEstimate(
            flops=flops, bytes_accessed=bytes_accessed, transcendentals=0
        ),
    )


def body(
    offsets,
    charges,
    stress,
    decay_rate,
    morton_keys,
    levels,
    bead_counts,
    send_boxes,
    m2l_source,
    m2l_type,
    m2l_count,
    near_source,
    up_inverse,
    down_inverse,
    translations,
):
    f32 = jnp.float32
    leaves = morton_keys.shape[0]
    half = leaves // 2
    parts = lax.axis_size("wide") * lax.axis_size("narrow")
    table = jnp.asarray(transform_table())
    signs = jnp.asarray(sign_rows())
    pair = lax.axis_index("pair").reshape(1)
    owner = (
        lax.axis_index("wide") * lax.axis_size("narrow") + lax.axis_index("narrow")
    ).reshape(1)
    kind_count = translations.shape[0]

    other_translations = lax.ppermute(translations, "pair", [(0, 1), (1, 0)])
    packed, blocks, placed, sources, kinds = call(
        functools.partial(pack_kernel, kind_count),
        [
            jax.ShapeDtypeStruct((4 * half + 8, LANES), f32),
            jax.ShapeDtypeStruct((8 * parts, LANES), f32),
            jax.ShapeDtypeStruct((4 * half, LANES), f32),
            jax.ShapeDtypeStruct(m2l_source.shape, jnp.int32),
            jax.ShapeDtypeStruct(m2l_type.shape, jnp.int32),
        ],
        [VMEM] * 9,
        limit=62,
    )(
        offsets, charges.reshape(half, LANES), morton_keys.reshape(1, leaves),
        levels.reshape(1, leaves), bead_counts.reshape(1, leaves), send_boxes,
        m2l_source, m2l_type, m2l_count.reshape(1, leaves),
    )
    arrived = lax.all_to_all(
        blocks.reshape(parts, 8, LANES), PARTS, split_axis=0, concat_axis=0, tiled=True
    ).reshape(8 * parts, LANES)
    swaps = [(2 * d, 2 * (d ^ 1)) for d in range(parts)]
    for d in range(1, parts - 1, 2):
        swaps += [(2 * d + 1, 2 * d + 3), (2 * d + 3, 2 * d + 1)]
    swapped = lax.ppermute(placed, PARTS + ("pair",), swaps)
    own_check = call(
        own_kernel,
        jax.ShapeDtypeStruct((Q, leaves // 16 * LANES), f32),
        [VMEM],
        [pltpu.VMEM((leaves // 16, Q * 8, LANES), f32)],
        flops=4 * 10**10,
    )(packed)
    passed = lax.ppermute(swapped, "pair", [(0, 1), (1, 0)])

    last = pl.BlockSpec((kind_count, 2, LANES), lambda i: (0, 0, TILES - 1))
    totals = call(
        far_kernel,
        jax.ShapeDtypeStruct((half * ROWS, LANES), f32),
        [SMEM] * 3 + [VMEM] * 4 + [last] * 2 + [ANY] * 3,
        [
            pltpu.VMEM(((leaves + 2 * parts) * ROWS, LANES), f32),
            pltpu.VMEM((kind_count + 1, ROWS, LANES), f32),
            pltpu.VMEM(table.shape, jnp.bfloat16),
            pltpu.VMEM(table.shape, jnp.bfloat16),
            pltpu.VMEM((leaves + 2 * parts, QPAD), f32),
            pltpu.VMEM(((leaves + 2 * parts) // 16, Q, LANES), f32),
            pltpu.VMEM((Q * 8, LANES), f32),
            pltpu.SemaphoreType.DMA((2 * TILES - 1,)),
        ],
        grid=(1,),
        flops=10**10,
        bytes_accessed=4 * 10**6,
    )(
        sources, kinds, pair, arrived, own_check, up_inverse, signs, translations,
        other_translations, table, translations, other_translations,
    )

    out = jax.ShapeDtypeStruct((half // 2, LANES), f32)
    potential, new_stress = call(
        near_kernel,
        [out, out],
        [SMEM] * 3 + [VMEM] * 11,
        [
            pltpu.VMEM((3 * leaves * 8, LANES), f32),
            pltpu.VMEM((half * 3 * BCAP, LANES), f32),
            pltpu.VMEM((half * near_source.shape[1] // 2 * 8, LANES), f32),
            pltpu.VMEM((half * BCAP, LANES), f32),
            pltpu.VMEM(table.shape, jnp.bfloat16),
            pltpu.VMEM((Q * 8, LANES), f32),
            pltpu.VMEM((Q, LANES), f32),
        ],
    )(
        near_source.T, pair, owner, swapped, placed, passed, packed, totals, table, signs, down_inverse,
        bead_counts.reshape(1, leaves),
        decay_rate.reshape(1, half), stress.reshape(half // 2, LANES),
    )
    return potential.reshape(-1), new_stress.reshape(-1)


def solution(mesh):
    return jax.shard_map(
        body,
        mesh=mesh,
        in_specs=(
            P(None, ("groups", "wide", "narrow")),
            P(("groups", "wide", "narrow")),
            P(("groups", "wide", "narrow", "pair")),
            P(("groups", "wide", "narrow", "pair")),
            P(("groups", "wide", "narrow")),
            P(("groups", "wide", "narrow")),
            P(("groups", "wide", "narrow")),
            P(("groups", "wide", "narrow"), None),
            P(("groups", "wide", "narrow"), None),
            P(("groups", "wide", "narrow"), None),
            P(("groups", "wide", "narrow")),
            P(("groups", "wide", "narrow"), None),
            P(),
            P(),
            P(None, None, "pair"),
        ),
        out_specs=(
            P(("groups", "wide", "narrow", "pair")),
            P(("groups", "wide", "narrow", "pair")),
        ),
        check_vma=False,
    )
```

```python
import functools

import jax
import jax.numpy as jnp
import ml_dtypes
import numpy as np
from jax import lax
from jax.experimental import pallas as pl
from jax.experimental.pallas import tpu as pltpu
from jax.sharding import PartitionSpec as P

PGRID = 12
G = 1728
MAXL = 10
BCAP = 64
Q = 152
QPAD = 160
LANES = 128
BINS = 864
TILES = 7
ROWS = 32
softening = 0.04
surface_reach = 1.25
CELLS = [
    (i, j, k)
    for i in range(6)
    for j in range(6)
    for k in range(6)
    if 0 in (i, j, k) or 5 in (i, j, k)
]
PARTS = ("wide", "narrow")


def transform_table():
    cells = np.array(CELLS)
    bins = np.arange(BINS)
    freq = np.stack([bins // 144, bins // 12 % 12, bins % 12])
    angle = (cells @ freq % PGRID) * (2.0 * np.pi / PGRID)
    table = np.zeros((QPAD, 2 * TILES * LANES))
    table[:Q, :BINS] = np.cos(angle)
    table[:Q, TILES * LANES : TILES * LANES + BINS] = -np.sin(angle)
    table[np.abs(table) < 1e-9] = 0.0
    return table.astype(ml_dtypes.bfloat16)


def low_part(high):
    root = np.sqrt(0.75)
    held = float(np.asarray(root).astype(ml_dtypes.bfloat16))
    scale = (root - held) / (held * (held * held - 1.0) * (held * held - 0.25))
    value = high.astype(jnp.float32)
    square = value * value
    return (value * (square - 1.0) * (square - 0.25) * scale).astype(jnp.bfloat16)


def sign_rows():
    rows = np.zeros((8, QPAD), np.float32)
    rows[0, :Q] = 1.0
    rows[1, :Q] = [(-1.0) ** i for i, _, _ in CELLS]
    return rows


def iota(shape, dim):
    return lax.broadcasted_iota(jnp.int32, shape, dim)


def per_leaf(values, count, first=0):
    shape = (count, values.shape[1])
    leaf, lane = first + 2 * iota(shape, 0), iota(shape, 1)
    even = jnp.sum(jnp.where(lane == leaf, values, 0.0), axis=1, keepdims=True)
    odd = jnp.sum(jnp.where(lane == leaf + 1, values, 0.0), axis=1, keepdims=True)
    return jnp.where(iota((count, LANES), 1) < BCAP, even, odd)


def block_transpose(x):
    lane, row = iota(x.shape, 1), iota(x.shape, 0)
    for k in (1, 2, 4):
        row_bit, lane_bit = (row & k) != 0, (lane & k) != 0
        below = pltpu.roll(pltpu.roll(x, 8 - k, 0), k, 1)
        above = pltpu.roll(pltpu.roll(x, k, 0), LANES - k, 1)
        x = jnp.where(row_bit == lane_bit, x, jnp.where(lane_bit, below, above))
    return x


def split(x):
    high = x.astype(jnp.bfloat16)
    return high, (x - high.astype(jnp.float32)).astype(jnp.bfloat16)


def product(a, b, contract):
    dims = (((contract[0],), (contract[1],)), ((), ()))
    (a_high, a_low), (b_high, b_low) = split(a), split(b)

    def dot(x, y):
        return lax.dot_general(x, y, dims, preferred_element_type=jnp.float32)

    return dot(a_high, b_high) + (dot(a_low, b_high) + dot(a_high, b_low))


def axis_squares(offset, width):
    area = width * width
    planes = [surface_reach * 0.5 * (i - 2.5) / 2.5 for i in range(6)]
    return [(plane - offset) * (plane - offset) * area for plane in planes]


def surface_kernels(offsets, width):
    gx, gy, gz = [axis_squares(offset, width) for offset in offsets]
    gz = [g + softening for g in gz]
    last, gxy = None, None
    for q, (i, j, k) in enumerate(CELLS):
        if last != (i, j):
            last, gxy = (i, j), gx[i] + gy[j]
        yield q, lax.rsqrt(gxy + gz[k])


def check_sums(offsets, weights, width, checks):
    offsets = [block_transpose(x) for x in offsets]
    weights, width = block_transpose(weights), block_transpose(width)
    for q, kernel in surface_kernels(offsets, width):
        checks[pl.ds(8 * q, 8), :] = kernel * weights
    check = checks[pl.ds(0, Q, stride=8), :]
    for s in range(1, 8):
        check = check + checks[pl.ds(s, Q, stride=8), :]
    return check


def upward(check, up_inverse):
    density = product(check, up_inverse, (0, 0))
    blocks = check.shape[1] // LANES
    density = density.reshape(2 * blocks, 8, 8, Q)
    total = density[:, 0]
    for g in range(1, 8):
        total = total + density[:, g]
    return total.reshape(16 * blocks, Q)


def store_spectra(density, table_high, table_low, target):
    count = density.shape[0] // 2
    high, low = split(density)
    both = jnp.concatenate([high, low], 0)
    for first in range(0, 2 * TILES, 2):
        columns = pl.ds(first * LANES, 2 * LANES)
        part = jnp.dot(both, table_high[:, columns], preferred_element_type=jnp.float32)
        spectra = part[: 2 * count] + part[2 * count :] + jnp.dot(
            high, table_low[:, columns], preferred_element_type=jnp.float32
        )
        for tile in range(first, first + 2):
            for side in range(2):
                for block in range(count // 16):
                    for h in range(2):
                        row = side * count + block * 16 + h * 8
                        start = (block * 16 + h) * ROWS + 16 * side + 8 * (tile // TILES) + tile % TILES
                        target[pl.ds(start, 8, stride=2 * ROWS), :] = spectra[
                            row : row + 8, (tile - first) * LANES : (tile - first + 1) * LANES
                        ]


def pack_kernel(
    kind_count, offsets, charges, keys, levels, counts, send_boxes, m2l_source, m2l_type, m2l_count,
    out, blocks, placed, sources, kinds,
):
    leaves = keys.shape[1]
    half = leaves // 2
    out[4 * half :, :] = jnp.zeros((8, LANES), jnp.float32)
    width = jnp.left_shift(jnp.ones_like(levels[...]), MAXL - levels[...]).astype(jnp.float32)
    for a in range(3):
        summed = jnp.zeros_like(keys[...])
        for bit in range(MAXL):
            summed = summed + (jnp.right_shift(keys[...], 3 * bit + a) & 1) * (1 << bit)
        out[4 * half + a : 4 * half + a + 1, :leaves] = summed.astype(jnp.float32) + 0.5 * width
    out[4 * half + 3 : 4 * half + 4, :leaves] = width
    for r in range(half):
        out[pl.ds(r, 3, stride=half), :] = offsets[:, r * LANES : (r + 1) * LANES]
    beads = per_leaf(counts[...].astype(jnp.float32), half)
    slot = iota((half, LANES), 1) & (BCAP - 1)
    out[3 * half : 4 * half, :] = jnp.where(slot.astype(jnp.float32) < beads, charges[...], 0.0)

    entry = iota(m2l_type.shape, 1)
    square = (leaves, leaves)
    live = jnp.sum(
        jnp.where(iota(square, 0) == iota(square, 1), m2l_count[...].astype(jnp.float32), 0.0),
        axis=1, keepdims=True,
    )
    kinds[...] = jnp.where(entry.astype(jnp.float32) < live, m2l_type[...], kind_count)
    sources[...] = m2l_source[...] * ROWS

    spread = per_leaf(width, half)
    for ch in range(3):
        center = per_leaf(out[4 * half + ch : 4 * half + ch + 1, :leaves], half)
        placed[ch * half : (ch + 1) * half, :] = center + spread * out[ch * half : (ch + 1) * half, :]
    placed[3 * half :, :] = out[3 * half : 4 * half, :]

    sends = send_boxes.shape[1]
    lane = iota((8, LANES), 1)
    for block in range(sends // 16):
        picked = []
        for c in range(2):
            column = block * 16 + 2 * iota((8, sends), 0) + c
            box = jnp.sum(
                jnp.where(iota((8, sends), 1) == column, send_boxes[...].astype(jnp.float32), 0.0),
                axis=1, keepdims=True,
            ).astype(jnp.int32)
            width_here = jnp.sum(
                jnp.where(iota((8, leaves), 1) == box, width, 0.0), axis=1, keepdims=True
            )
            row_of = jnp.broadcast_to(box >> 1, (8, LANES))
            found = [jnp.zeros((8, LANES), jnp.float32)] * 4
            for r in range(half):
                here = row_of == r
                for ch in range(4):
                    found[ch] = jnp.where(here, out[ch * half + r : ch * half + r + 1, :], found[ch])
            aligned = jnp.broadcast_to((box & 1) == c, (8, LANES))
            found = [jnp.where(aligned, x, pltpu.roll(x, BCAP, 1)) for x in found]
            picked.append(found + [jnp.broadcast_to(width_here, (8, LANES))])
        for ch in range(5):
            blocks[pl.ds(block * 64 + ch, 8, stride=8), :] = jnp.where(
                lane < BCAP, picked[0][ch], picked[1][ch]
            )
        for ch in range(5, 8):
            blocks[pl.ds(block * 64 + ch, 8, stride=8), :] = jnp.zeros((8, LANES), jnp.float32)


def own_kernel(packed, out, checks):
    half = (packed.shape[0] - 8) // 4
    width = per_leaf(packed[4 * half + 3 : 4 * half + 4, :], half)
    for block in range(half // 8):
        rows = [packed[c * half + block * 8 : c * half + block * 8 + 8, :] for c in range(4)]
        out[:, block * LANES : (block + 1) * LANES] = check_sums(
            rows[:3], rows[3], width[block * 8 : block * 8 + 8], checks.at[block]
        )


def far_kernel(
    sources, kinds, pair_ref, arrived, own_check, up_inverse, signs,
    last_bins, other_last_bins, table, translations, other_translations, totals, low_table,
    spectra, kernels, high_table, density, check, checks, sems,
):
    leaves, entries = sources.shape
    half = leaves // 2
    blocks = arrived.shape[0] // 64
    kind_count = translations.shape[0]
    pair = pair_ref[0]

    table_copy = pltpu.make_async_copy(table, high_table, sems.at[0])
    table_copy.start()
    kernel_copies = []
    for side, bins in enumerate((translations, other_translations)):
        for t in range(TILES - 1):
            kernel_copies.append(pltpu.make_async_copy(
                bins.at[:, :, pl.ds(t * LANES, LANES)],
                kernels.at[pl.ds(0, kind_count), pl.ds(16 * side + 2 * t, 2), :],
                sems.at[1 + len(kernel_copies)],
            ))
        kernel_copies.append(pltpu.make_async_copy(
            (last_bins, other_last_bins)[side],
            kernels.at[pl.ds(0, kind_count), pl.ds(16 * side + 2 * TILES - 2, 2), :],
            sems.at[1 + len(kernel_copies)],
        ))
    for copy in kernel_copies:
        copy.start()
    kernels[kind_count] = jnp.zeros((ROWS, LANES), jnp.float32)

    density[...] = jnp.zeros(density.shape, jnp.float32)
    check[0, :, :] = own_check[:, :LANES]
    check[1, :, :] = own_check[:, LANES:]

    def arrive(block, carry):
        beads = [
            arrived[pl.ds(pl.multiple_of(block * 64, 64) + ch, 8, stride=8), :] for ch in range(5)
        ]
        check[leaves // 16 + block, :, :] = check_sums(beads[:3], beads[3], beads[4], checks)
        return carry

    if blocks == 1:
        arrive(0, 0)
    else:
        lax.fori_loop(0, blocks, arrive, 0)
    count = check.shape[0]
    for first in range(0, count, 3):
        some = range(first, min(first + 3, count))
        density[16 * first : 16 * first + 16 * len(some), :Q] = upward(
            jnp.concatenate([check[n] for n in some], 1), up_inverse[...]
        )
    table_copy.wait()
    low_table[...] = low_part(high_table[...])
    sign = jnp.where(pair == 1, signs[1:2, :], signs[0:1, :])
    other_sign = jnp.where(pair == 1, signs[0:1, :], signs[1:2, :])
    store_spectra(
        jnp.concatenate([density[...] * sign, density[...] * other_sign], 0),
        high_table, low_table, spectra,
    )
    for copy in kernel_copies:
        copy.wait()

    def translate(t, carry):
        leaf = pair * half + t
        sums = [[None] * 4, [None] * 4]
        for entry in range(entries):
            kind = kinds[leaf, entry]
            start = pl.multiple_of(sources[leaf, entry], ROWS)
            for side in range(2):
                k_re = kernels[kind, pl.ds(16 * side, 8, stride=2), :]
                k_im = kernels[kind, pl.ds(16 * side + 1, 8, stride=2), :]
                s_re = spectra[pl.ds(start + 16 * side, 8), :]
                s_im = spectra[pl.ds(start + 16 * side + 8, 8), :]
                terms = (k_re * s_re, k_im * s_im, k_re * s_im, k_im * s_re)
                for n, term in enumerate(terms):
                    sums[side][n] = term if sums[side][n] is None else sums[side][n] + term
        start = pl.multiple_of(t * ROWS, ROWS)
        for side in range(2):
            rr, ii, ri, ir = sums[side]
            totals[pl.ds(start + 16 * side, 8), :] = rr - ii
            totals[pl.ds(start + 16 * side + 8, 8), :] = ri + ir
        return carry

    lax.fori_loop(0, half, translate, 0, unroll=4)


def evaluate(
    pair, packed, totals, table, low_table, signs, down_inverse, eval_kernels, densities
):
    half = (packed.shape[0] - 8) // 4
    leaves = 2 * half
    rows = half // 2
    width = block_transpose(
        per_leaf(packed[4 * half + 3 : 4 * half + 4, :], rows, pair * half)
    )
    offsets = [
        block_transpose(packed[pl.ds(pl.multiple_of(c * half + pair * rows, 8), rows), :])
        for c in range(3)
    ]
    for q, kernel in surface_kernels(offsets, width):
        eval_kernels[pl.ds(8 * q, 8), :] = kernel
    sign = jnp.where(pair == 1, signs[1:2, :], signs[0:1, :])
    other_sign = jnp.where(pair == 1, signs[0:1, :], signs[1:2, :])
    lane = iota((half, LANES), 1)
    sides = []
    for side in range(2):
        columns = []
        for c in range(2):
            for t in range(TILES):
                line = totals[pl.ds(16 * side + c * 8 + t, half, stride=ROWS), :]
                if t == TILES - 1:
                    line = jnp.where(lane < BINS - t * LANES, line, 0.0)
                columns.append(line)
        sides.append(jnp.concatenate(columns, 1))
    high, low = split(jnp.concatenate(sides, 0))
    across = (((1,), (1,)), ((), ()))
    both = lax.dot_general(
        jnp.concatenate([high, low], 0), table[...], across,
        preferred_element_type=jnp.float32,
    )
    check = both[:leaves] + both[leaves:] + lax.dot_general(
        high, low_table[...], across, preferred_element_type=jnp.float32
    )
    check = (check[:half] * sign + check[half:] * other_sign)[:, :Q] * (1.0 / G)

    leaf_of = 2 * (lane & 7) + (lane >> 6)
    spread = jnp.where(iota((half, LANES), 0) == leaf_of, 1.0, 0.0)
    densities[...] = product(product(check, down_inverse[...], (1, 0)), spread, (0, 0))
    parts = [jnp.zeros((rows, LANES), jnp.float32)] * 4
    for q in range(Q):
        term = eval_kernels[8 * q : 8 * q + 8, :] * densities[q : q + 1, :]
        parts[q % 4] = parts[q % 4] + term
    return block_transpose((parts[0] + parts[1]) + (parts[2] + parts[3]))


def near_kernel(
    near_source, pair_ref, owner_ref, swapped, placed, passed, packed, totals, high_table, low_table,
    signs, down_inverse, counts, decay_rate, stress, potential, new_stress,
    table, targets, merged, sums, eval_kernels, densities,
):
    entries, leaves = near_source.shape
    half = leaves // 2
    pair = pair_ref[0]
    low = iota((half, LANES), 1) < BCAP
    far = evaluate(
        pair, packed, totals, high_table, low_table, signs, down_inverse, eval_kernels, densities
    )
    swapped_from = jnp.where(((owner_ref[0] & 1) ^ pair) == 1, 0, 2)
    for n, rows_of in ((swapped_from, swapped), (1, placed), (2 - swapped_from, passed)):
        first = n * (leaves * 8)
        for ch in range(4):
            rows = rows_of[ch * half : (ch + 1) * half, :]
            turned = pltpu.roll(rows, BCAP, 1)
            table[pl.ds(first + ch, half, stride=16), :] = jnp.where(low, rows, turned)
            table[pl.ds(first + 8 + ch, half, stride=16), :] = jnp.where(low, turned, rows)
    for ch in range(3):
        mine = placed[pl.ds(pl.multiple_of(ch * half + pair * (half // 2), 8), half // 2), :]
        flipped = mine.T
        for r in range(half // 2):
            for h in range(2):
                start = ((2 * r + h) * 3 + ch) * BCAP
                targets[pl.ds(start, BCAP), :] = jnp.broadcast_to(
                    flipped[h * BCAP : (h + 1) * BCAP, r : r + 1], (BCAP, LANES)
                )
    low = iota((8, LANES), 1) < BCAP

    def merge(t, carry):
        leaf = pair * half + t
        for n in range(entries // 2):
            left = pl.multiple_of(near_source[2 * n, leaf] * 8, 8)
            right = pl.multiple_of(near_source[2 * n + 1, leaf] * 8, 8)
            start = pl.multiple_of((t * (entries // 2) + n) * 8, 8)
            merged[pl.ds(start, 8), :] = jnp.where(
                low, table[pl.ds(left, 8), :], table[pl.ds(right, 8), :]
            )
        return carry

    lax.fori_loop(0, half, merge, 0, unroll=4)

    def one_leaf(t, carry):
        start = pl.multiple_of(t * 3 * BCAP, 8)
        tx, ty, tz = [targets[pl.ds(start + ch * BCAP, BCAP), :] for ch in range(3)]
        total = jnp.zeros((BCAP, LANES), jnp.float32)
        for n in range(entries // 2):
            first = pl.multiple_of((t * (entries // 2) + n) * 8, 8)
            sx, sy, sz, weight = [merged[pl.ds(first + ch, 1), :] for ch in range(4)]
            gx, gy, gz = tx - sx, ty - sy, tz - sz
            squared = gx * gx + gy * gy + (gz * gz + softening)
            total = total + lax.rsqrt(squared) * weight
        sums[pl.ds(pl.multiple_of(t * BCAP, 8), BCAP), :] = total
        return carry

    lax.fori_loop(0, half, one_leaf, 0, unroll=4)
    rows = half // 2
    for r in range(rows):
        block = sums[r * LANES : (r + 1) * LANES, :].T
        potential[r : r + 1, :] = jnp.sum(block, axis=0, keepdims=True)
    combined = potential[...] + far
    beads = per_leaf(counts[...].astype(jnp.float32), rows, pair * half)
    slot = iota((rows, LANES), 1) & (BCAP - 1)
    occupied = slot.astype(jnp.float32) < beads
    decay = per_leaf(decay_rate[...], rows)
    potential[...] = jnp.where(occupied, combined, 0.0)
    new_stress[...] = jnp.where(occupied, decay * stress[...] + combined, 0.0)


VMEM = pl.BlockSpec(memory_space=pltpu.VMEM)
SMEM = pl.BlockSpec(memory_space=pltpu.SMEM)
ANY = pl.BlockSpec(memory_space=pl.ANY)
MIB = 1024 * 1024


def call(kernel, outs, in_specs, scratch=(), limit=40, grid=(), flops=0, bytes_accessed=0):
    return pl.pallas_call(
        kernel,
        out_shape=outs,
        grid=grid,
        in_specs=in_specs,
        out_specs=jax.tree.map(lambda _: VMEM, outs),
        scratch_shapes=list(scratch),
        compiler_params=pltpu.CompilerParams(vmem_limit_bytes=limit * MIB),
        cost_estimate=pl.CostEstimate(
            flops=flops, bytes_accessed=bytes_accessed, transcendentals=0
        ),
    )


def body(
    offsets,
    charges,
    stress,
    decay_rate,
    morton_keys,
    levels,
    bead_counts,
    send_boxes,
    m2l_source,
    m2l_type,
    m2l_count,
    near_source,
    up_inverse,
    down_inverse,
    translations,
):
    f32 = jnp.float32
    leaves = morton_keys.shape[0]
    half = leaves // 2
    parts = lax.axis_size("wide") * lax.axis_size("narrow")
    table = jnp.asarray(transform_table())
    signs = jnp.asarray(sign_rows())
    pair = lax.axis_index("pair").reshape(1)
    owner = (
        lax.axis_index("wide") * lax.axis_size("narrow") + lax.axis_index("narrow")
    ).reshape(1)
    kind_count = translations.shape[0]

    other_translations = lax.ppermute(translations, "pair", [(0, 1), (1, 0)])
    packed, blocks, placed, sources, kinds = call(
        functools.partial(pack_kernel, kind_count),
        [
            jax.ShapeDtypeStruct((4 * half + 8, LANES), f32),
            jax.ShapeDtypeStruct((8 * parts, LANES), f32),
            jax.ShapeDtypeStruct((4 * half, LANES), f32),
            jax.ShapeDtypeStruct(m2l_source.shape, jnp.int32),
            jax.ShapeDtypeStruct(m2l_type.shape, jnp.int32),
        ],
        [VMEM] * 9,
        limit=62,
    )(
        offsets, charges.reshape(half, LANES), morton_keys.reshape(1, leaves),
        levels.reshape(1, leaves), bead_counts.reshape(1, leaves), send_boxes,
        m2l_source, m2l_type, m2l_count.reshape(1, leaves),
    )
    arrived = lax.all_to_all(
        blocks.reshape(parts, 8, LANES), PARTS, split_axis=0, concat_axis=0, tiled=True
    ).reshape(8 * parts, LANES)
    swaps = [(2 * d, 2 * (d ^ 1)) for d in range(parts)]
    for d in range(1, parts - 1, 2):
        swaps += [(2 * d + 1, 2 * d + 3), (2 * d + 3, 2 * d + 1)]
    swapped = lax.ppermute(placed, PARTS + ("pair",), swaps)
    own_check = call(
        own_kernel,
        jax.ShapeDtypeStruct((Q, leaves // 16 * LANES), f32),
        [VMEM],
        [pltpu.VMEM((leaves // 16, Q * 8, LANES), f32)],
        flops=4 * 10**10,
    )(packed)
    passed = lax.ppermute(swapped, "pair", [(0, 1), (1, 0)])

    last = pl.BlockSpec((kind_count, 2, LANES), lambda i: (0, 0, TILES - 1))
    totals, low_table = call(
        far_kernel,
        [
            jax.ShapeDtypeStruct((half * ROWS, LANES), f32),
            jax.ShapeDtypeStruct(table.shape, table.dtype),
        ],
        [SMEM] * 3 + [VMEM] * 4 + [last] * 2 + [ANY] * 3,
        [
            pltpu.VMEM(((leaves + 2 * parts) * ROWS, LANES), f32),
            pltpu.VMEM((kind_count + 1, ROWS, LANES), f32),
            pltpu.VMEM(table.shape, jnp.bfloat16),
            pltpu.VMEM((leaves + 2 * parts, QPAD), f32),
            pltpu.VMEM(((leaves + 2 * parts) // 16, Q, LANES), f32),
            pltpu.VMEM((Q * 8, LANES), f32),
            pltpu.SemaphoreType.DMA((2 * TILES + 1,)),
        ],
        grid=(1,),
        flops=10**10,
        bytes_accessed=4 * 10**6,
    )(
        sources, kinds, pair, arrived, own_check, up_inverse, signs, translations,
        other_translations, table, translations, other_translations,
    )

    out = jax.ShapeDtypeStruct((half // 2, LANES), f32)
    potential, new_stress = call(
        near_kernel,
        [out, out],
        [SMEM] * 3 + [VMEM] * 12,
        [
            pltpu.VMEM((3 * leaves * 8, LANES), f32),
            pltpu.VMEM((half * 3 * BCAP, LANES), f32),
            pltpu.VMEM((half * near_source.shape[1] // 2 * 8, LANES), f32),
            pltpu.VMEM((half * BCAP, LANES), f32),
            pltpu.VMEM((Q * 8, LANES), f32),
            pltpu.VMEM((Q, LANES), f32),
        ],
    )(
        near_source.T, pair, owner, swapped, placed, passed, packed, totals, table, low_table, signs,
        down_inverse, bead_counts.reshape(1, leaves),
        decay_rate.reshape(1, half), stress.reshape(half // 2, LANES),
    )
    return potential.reshape(-1), new_stress.reshape(-1)


def solution(mesh):
    return jax.shard_map(
        body,
        mesh=mesh,
        in_specs=(
            P(None, ("groups", "wide", "narrow")),
            P(("groups", "wide", "narrow")),
            P(("groups", "wide", "narrow", "pair")),
            P(("groups", "wide", "narrow", "pair")),
            P(("groups", "wide", "narrow")),
            P(("groups", "wide", "narrow")),
            P(("groups", "wide", "narrow")),
            P(("groups", "wide", "narrow"), None),
            P(("groups", "wide", "narrow"), None),
            P(("groups", "wide", "narrow"), None),
            P(("groups", "wide", "narrow")),
            P(("groups", "wide", "narrow"), None),
            P(),
            P(),
            P(None, None, "pair"),
        ),
        out_specs=(
            P(("groups", "wide", "narrow", "pair")),
            P(("groups", "wide", "narrow", "pair")),
        ),
        check_vma=False,
    )
```

```python
import functools

import jax
import jax.numpy as jnp
import ml_dtypes
import numpy as np
from jax import lax
from jax.experimental import pallas as pl
from jax.experimental.pallas import tpu as pltpu
from jax.sharding import PartitionSpec as P

PGRID = 12
G = 1728
MAXL = 10
BCAP = 64
Q = 152
QPAD = 160
LANES = 128
BINS = 864
TILES = 7
ROWS = 32
softening = 0.04
surface_reach = 1.25
CELLS = [
    (i, j, k)
    for i in range(6)
    for j in range(6)
    for k in range(6)
    if 0 in (i, j, k) or 5 in (i, j, k)
]
PARTS = ("wide", "narrow")


def transform_table():
    cells = np.array(CELLS)
    bins = np.arange(BINS)
    freq = np.stack([bins // 144, bins // 12 % 12, bins % 12])
    angle = (cells @ freq % PGRID) * (2.0 * np.pi / PGRID)
    table = np.zeros((QPAD, 2 * TILES * LANES))
    table[:Q, :BINS] = np.cos(angle)
    table[:Q, TILES * LANES : TILES * LANES + BINS] = -np.sin(angle)
    table[np.abs(table) < 1e-9] = 0.0
    return table.astype(ml_dtypes.bfloat16)


def low_part(high):
    root = np.sqrt(0.75)
    held = float(np.asarray(root).astype(ml_dtypes.bfloat16))
    scale = (root - held) / (held * (held * held - 1.0) * (held * held - 0.25))
    value = high.astype(jnp.float32)
    square = value * value
    return (value * (square - 1.0) * (square - 0.25) * scale).astype(jnp.bfloat16)


def sign_rows():
    rows = np.zeros((8, QPAD), np.float32)
    rows[0, :Q] = 1.0
    rows[1, :Q] = [(-1.0) ** i for i, _, _ in CELLS]
    return rows


def iota(shape, dim):
    return lax.broadcasted_iota(jnp.int32, shape, dim)


def per_leaf(values, count, first=0):
    shape = (count, values.shape[1])
    leaf, lane = first + 2 * iota(shape, 0), iota(shape, 1)
    even = jnp.sum(jnp.where(lane == leaf, values, 0.0), axis=1, keepdims=True)
    odd = jnp.sum(jnp.where(lane == leaf + 1, values, 0.0), axis=1, keepdims=True)
    return jnp.where(iota((count, LANES), 1) < BCAP, even, odd)


def block_transpose(x):
    lane, row = iota(x.shape, 1), iota(x.shape, 0)
    for k in (1, 2, 4):
        row_bit, lane_bit = (row & k) != 0, (lane & k) != 0
        below = pltpu.roll(pltpu.roll(x, 8 - k, 0), k, 1)
        above = pltpu.roll(pltpu.roll(x, k, 0), LANES - k, 1)
        x = jnp.where(row_bit == lane_bit, x, jnp.where(lane_bit, below, above))
    return x


def split(x):
    high = x.astype(jnp.bfloat16)
    return high, (x - high.astype(jnp.float32)).astype(jnp.bfloat16)


def thirds(x):
    high = x.astype(jnp.bfloat16).astype(jnp.float32)
    rest = x - high
    middle = rest.astype(jnp.bfloat16).astype(jnp.float32)
    return high, middle, rest - middle


def product(a, b, contract):
    dims = (((contract[0],), (contract[1],)), ((), ()))
    (a_high, a_low), (b_high, b_low) = split(a), split(b)

    def dot(x, y):
        return lax.dot_general(x, y, dims, preferred_element_type=jnp.float32)

    return dot(a_high, b_high) + (dot(a_low, b_high) + dot(a_high, b_low))


def axis_squares(offset, width):
    area = width * width
    planes = [surface_reach * 0.5 * (i - 2.5) / 2.5 for i in range(6)]
    return [(plane - offset) * (plane - offset) * area for plane in planes]


def surface_kernels(offsets, width):
    gx, gy, gz = [axis_squares(offset, width) for offset in offsets]
    gz = [g + softening for g in gz]
    last, gxy = None, None
    for q, (i, j, k) in enumerate(CELLS):
        if last != (i, j):
            last, gxy = (i, j), gx[i] + gy[j]
        yield q, lax.rsqrt(gxy + gz[k])


def check_sums(offsets, weights, width, checks):
    offsets = [block_transpose(x) for x in offsets]
    weights, width = block_transpose(weights), block_transpose(width)
    for q, kernel in surface_kernels(offsets, width):
        checks[pl.ds(8 * q, 8), :] = kernel * weights
    check = checks[pl.ds(0, Q, stride=8), :]
    for s in range(1, 8):
        check = check + checks[pl.ds(s, Q, stride=8), :]
    return check


def upward(check, up_inverse):
    density = product(check, up_inverse, (0, 0))
    blocks = check.shape[1] // LANES
    density = density.reshape(2 * blocks, 8, 8, Q)
    total = density[:, 0]
    for g in range(1, 8):
        total = total + density[:, g]
    return total.reshape(16 * blocks, Q)


def store_spectra(density, table_high, table_low, target):
    count = density.shape[0] // 2
    high, low = split(density)
    both = jnp.concatenate([high, low], 0)
    for first in range(0, 2 * TILES, 2):
        columns = pl.ds(first * LANES, 2 * LANES)
        part = jnp.dot(both, table_high[:, columns], preferred_element_type=jnp.float32)
        spectra = part[: 2 * count] + part[2 * count :] + jnp.dot(
            high, table_low[:, columns], preferred_element_type=jnp.float32
        )
        for tile in range(first, first + 2):
            for side in range(2):
                for block in range(count // 16):
                    for h in range(2):
                        row = side * count + block * 16 + h * 8
                        start = (block * 16 + h) * ROWS + 16 * side + 8 * (tile // TILES) + tile % TILES
                        target[pl.ds(start, 8, stride=2 * ROWS), :] = spectra[
                            row : row + 8, (tile - first) * LANES : (tile - first + 1) * LANES
                        ]


def pack_kernel(
    kind_count, offsets, charges, keys, levels, counts, send_boxes, m2l_source, m2l_type, m2l_count,
    out, blocks, placed, sources, kinds,
):
    leaves = keys.shape[1]
    half = leaves // 2
    out[4 * half :, :] = jnp.zeros((8, LANES), jnp.float32)
    width = jnp.left_shift(jnp.ones_like(levels[...]), MAXL - levels[...]).astype(jnp.float32)
    for a in range(3):
        summed = jnp.zeros_like(keys[...])
        for bit in range(MAXL):
            summed = summed + (jnp.right_shift(keys[...], 3 * bit + a) & 1) * (1 << bit)
        out[4 * half + a : 4 * half + a + 1, :leaves] = summed.astype(jnp.float32) + 0.5 * width
    out[4 * half + 3 : 4 * half + 4, :leaves] = width
    for r in range(half):
        out[pl.ds(r, 3, stride=half), :] = offsets[:, r * LANES : (r + 1) * LANES]
    beads = per_leaf(counts[...].astype(jnp.float32), half)
    slot = iota((half, LANES), 1) & (BCAP - 1)
    out[3 * half : 4 * half, :] = jnp.where(slot.astype(jnp.float32) < beads, charges[...], 0.0)

    entry = iota(m2l_type.shape, 1)
    square = (leaves, leaves)
    live = jnp.sum(
        jnp.where(iota(square, 0) == iota(square, 1), m2l_count[...].astype(jnp.float32), 0.0),
        axis=1, keepdims=True,
    )
    kinds[...] = jnp.where(entry.astype(jnp.float32) < live, m2l_type[...], kind_count)
    sources[...] = m2l_source[...] * ROWS

    spread = per_leaf(width, half)
    for ch in range(3):
        center = per_leaf(out[4 * half + ch : 4 * half + ch + 1, :leaves], half)
        placed[ch * half : (ch + 1) * half, :] = center + spread * out[ch * half : (ch + 1) * half, :]
    placed[3 * half :, :] = out[3 * half : 4 * half, :]

    sends = send_boxes.shape[1]
    lane = iota((8, LANES), 1)
    for block in range(sends // 16):
        picked = []
        for c in range(2):
            column = block * 16 + 2 * iota((8, sends), 0) + c
            box = jnp.sum(
                jnp.where(iota((8, sends), 1) == column, send_boxes[...].astype(jnp.float32), 0.0),
                axis=1, keepdims=True,
            ).astype(jnp.int32)
            width_here = jnp.sum(
                jnp.where(iota((8, leaves), 1) == box, width, 0.0), axis=1, keepdims=True
            )
            row_of = jnp.broadcast_to(box >> 1, (8, LANES))
            found = [jnp.zeros((8, LANES), jnp.float32)] * 4
            for r in range(half):
                here = row_of == r
                for ch in range(4):
                    found[ch] = jnp.where(here, out[ch * half + r : ch * half + r + 1, :], found[ch])
            aligned = jnp.broadcast_to((box & 1) == c, (8, LANES))
            found = [jnp.where(aligned, x, pltpu.roll(x, BCAP, 1)) for x in found]
            picked.append(found + [jnp.broadcast_to(width_here, (8, LANES))])
        for ch in range(5):
            blocks[pl.ds(block * 64 + ch, 8, stride=8), :] = jnp.where(
                lane < BCAP, picked[0][ch], picked[1][ch]
            )
        for ch in range(5, 8):
            blocks[pl.ds(block * 64 + ch, 8, stride=8), :] = jnp.zeros((8, LANES), jnp.float32)


def own_kernel(pair_ref, packed, out, eval_kernels, terms, checks, stacked):
    half = (packed.shape[0] - 8) // 4
    rows = half // 2
    pair = pair_ref[0]
    all_widths = per_leaf(packed[4 * half + 3 : 4 * half + 4, :], half)
    for block in range(half // 8):
        beads = [packed[c * half + block * 8 : c * half + block * 8 + 8, :] for c in range(4)]
        out[:, block * LANES : (block + 1) * LANES] = check_sums(
            beads[:3], beads[3], all_widths[block * 8 : block * 8 + 8], checks.at[block]
        )
    width = per_leaf(packed[4 * half + 3 : 4 * half + 4, :], rows, pair * half)
    offsets = [packed[pl.ds(pl.multiple_of(c * half + pair * rows, 8), rows), :] for c in range(3)]
    flat = [block_transpose(x) for x in offsets]
    for q, kernel in surface_kernels(flat, block_transpose(width)):
        eval_kernels[pl.ds(8 * q, 8), :] = kernel

    places = [width * x for x in offsets]
    norm = places[0] * places[0] + places[1] * places[1] + (places[2] * places[2] + softening)
    pieces = [thirds(-2.0 * x) for x in places]
    norms = thirds(norm)
    one, zero = jnp.ones((rows, LANES), jnp.float32), jnp.zeros((rows, LANES), jnp.float32)
    for third in range(3):
        x, y, z = [piece[third] for piece in pieces]
        unit = one if third == 0 else zero
        first = [x, y, z, unit, norms[third]]
        second = [x, y, z, unit] if third < 2 else [zero] * 4
        last = [x, y, z, unit] if third < 1 else [zero] * 4
        for row, values in enumerate(first + second + last + [zero] * 3):
            stacked[pl.ds(16 * third + row, rows, stride=48), :] = values
    for r in range(rows):
        terms[r * LANES : (r + 1) * LANES, :48] = (
            stacked[48 * r : 48 * (r + 1), :].T.astype(jnp.bfloat16)
        )


def far_kernel(
    sources, kinds, pair_ref, arrived, own_check, up_inverse, signs,
    last_bins, other_last_bins, table, translations, other_translations, totals, low_table,
    spectra, kernels, high_table, density, check, checks, sems,
):
    leaves, entries = sources.shape
    half = leaves // 2
    blocks = arrived.shape[0] // 64
    kind_count = translations.shape[0]
    pair = pair_ref[0]

    table_copy = pltpu.make_async_copy(table, high_table, sems.at[0])
    table_copy.start()
    kernel_copies = []
    for side, bins in enumerate((translations, other_translations)):
        for t in range(TILES - 1):
            kernel_copies.append(pltpu.make_async_copy(
                bins.at[:, :, pl.ds(t * LANES, LANES)],
                kernels.at[pl.ds(0, kind_count), pl.ds(16 * side + 2 * t, 2), :],
                sems.at[1 + len(kernel_copies)],
            ))
        kernel_copies.append(pltpu.make_async_copy(
            (last_bins, other_last_bins)[side],
            kernels.at[pl.ds(0, kind_count), pl.ds(16 * side + 2 * TILES - 2, 2), :],
            sems.at[1 + len(kernel_copies)],
        ))
    for copy in kernel_copies:
        copy.start()
    kernels[kind_count] = jnp.zeros((ROWS, LANES), jnp.float32)

    density[...] = jnp.zeros(density.shape, jnp.float32)
    check[0, :, :] = own_check[:, :LANES]
    check[1, :, :] = own_check[:, LANES:]

    def arrive(block, carry):
        beads = [
            arrived[pl.ds(pl.multiple_of(block * 64, 64) + ch, 8, stride=8), :] for ch in range(5)
        ]
        check[leaves // 16 + block, :, :] = check_sums(beads[:3], beads[3], beads[4], checks)
        return carry

    if blocks == 1:
        arrive(0, 0)
    else:
        lax.fori_loop(0, blocks, arrive, 0)
    count = check.shape[0]
    for first in range(0, count, 3):
        some = range(first, min(first + 3, count))
        density[16 * first : 16 * first + 16 * len(some), :Q] = upward(
            jnp.concatenate([check[n] for n in some], 1), up_inverse[...]
        )
    table_copy.wait()
    low_table[...] = low_part(high_table[...])
    sign = jnp.where(pair == 1, signs[1:2, :], signs[0:1, :])
    other_sign = jnp.where(pair == 1, signs[0:1, :], signs[1:2, :])
    store_spectra(
        jnp.concatenate([density[...] * sign, density[...] * other_sign], 0),
        high_table, low_table, spectra,
    )
    for copy in kernel_copies:
        copy.wait()

    def translate(t, carry):
        leaf = pair * half + t
        sums = [[None] * 4, [None] * 4]
        for entry in range(entries):
            kind = kinds[leaf, entry]
            start = pl.multiple_of(sources[leaf, entry], ROWS)
            for side in range(2):
                k_re = kernels[kind, pl.ds(16 * side, 8, stride=2), :]
                k_im = kernels[kind, pl.ds(16 * side + 1, 8, stride=2), :]
                s_re = spectra[pl.ds(start + 16 * side, 8), :]
                s_im = spectra[pl.ds(start + 16 * side + 8, 8), :]
                terms = (k_re * s_re, k_im * s_im, k_re * s_im, k_im * s_re)
                for n, term in enumerate(terms):
                    sums[side][n] = term if sums[side][n] is None else sums[side][n] + term
        start = pl.multiple_of(t * ROWS, ROWS)
        for side in range(2):
            rr, ii, ri, ir = sums[side]
            totals[pl.ds(start + 16 * side, 8), :] = rr - ii
            totals[pl.ds(start + 16 * side + 8, 8), :] = ri + ir
        return carry

    lax.fori_loop(0, half, translate, 0, unroll=4)


def evaluate(pair, totals, table, low_table, signs, down_inverse, eval_kernels, densities):
    half = totals.shape[0] // ROWS
    leaves = 2 * half
    rows = half // 2
    sign = jnp.where(pair == 1, signs[1:2, :], signs[0:1, :])
    other_sign = jnp.where(pair == 1, signs[0:1, :], signs[1:2, :])
    lane = iota((half, LANES), 1)
    sides = []
    for side in range(2):
        columns = []
        for c in range(2):
            for t in range(TILES):
                line = totals[pl.ds(16 * side + c * 8 + t, half, stride=ROWS), :]
                if t == TILES - 1:
                    line = jnp.where(lane < BINS - t * LANES, line, 0.0)
                columns.append(line)
        sides.append(jnp.concatenate(columns, 1))
    high, low = split(jnp.concatenate(sides, 0))
    across = (((1,), (1,)), ((), ()))
    both = lax.dot_general(
        jnp.concatenate([high, low], 0), table[...], across,
        preferred_element_type=jnp.float32,
    )
    check = both[:leaves] + both[leaves:] + lax.dot_general(
        high, low_table[...], across, preferred_element_type=jnp.float32
    )
    check = (check[:half] * sign + check[half:] * other_sign)[:, :Q] * (1.0 / G)

    leaf_of = 2 * (lane & 7) + (lane >> 6)
    spread = jnp.where(iota((half, LANES), 0) == leaf_of, 1.0, 0.0)
    densities[...] = product(product(check, down_inverse[...], (1, 0)), spread, (0, 0))
    parts = [jnp.zeros((rows, LANES), jnp.float32)] * 4
    for q in range(Q):
        term = eval_kernels[8 * q : 8 * q + 8, :] * densities[q : q + 1, :]
        parts[q % 4] = parts[q % 4] + term
    return block_transpose((parts[0] + parts[1]) + (parts[2] + parts[3]))


def near_kernel(
    near_source, pair_ref, owner_ref, swapped, placed, passed, packed, terms, eval_kernels, totals,
    high_table, low_table, signs, down_inverse, counts, decay_rate, stress, potential, new_stress,
    table, merged, centers, factors, sums, densities,
):
    entries, leaves = near_source.shape
    half = leaves // 2
    rows = half // 2
    pair = pair_ref[0]
    low = iota((half, LANES), 1) < BCAP
    far = evaluate(
        pair, totals, high_table, low_table, signs, down_inverse, eval_kernels, densities
    )
    swapped_from = jnp.where(((owner_ref[0] & 1) ^ pair) == 1, 0, 2)
    for n, rows_of in ((swapped_from, swapped), (1, placed), (2 - swapped_from, passed)):
        first = n * (leaves * 8)
        for ch in range(4):
            beads = rows_of[ch * half : (ch + 1) * half, :]
            turned = pltpu.roll(beads, BCAP, 1)
            table[pl.ds(first + ch, half, stride=16), :] = jnp.where(low, beads, turned)
            table[pl.ds(first + 8 + ch, half, stride=16), :] = jnp.where(low, turned, beads)
    low = iota((rows, LANES), 1) < BCAP
    for ch in range(3):
        center = per_leaf(packed[4 * half + ch : 4 * half + ch + 1, :], rows, pair * half)
        turned = pltpu.roll(center, BCAP, 1)
        centers[pl.ds(ch, rows, stride=16), :] = jnp.where(low, center, turned)
        centers[pl.ds(8 + ch, rows, stride=16), :] = jnp.where(low, turned, center)
    pairs = entries // 2
    one, zero = jnp.ones((pairs, LANES), jnp.float32), jnp.zeros((pairs, LANES), jnp.float32)

    def prepare(t, carry):
        leaf = pair * half + t
        start = pl.multiple_of(t * pairs * 8, 8)
        for n in range(pairs):
            left = pl.multiple_of(near_source[2 * n, leaf] * 8, 8)
            right = pl.multiple_of(near_source[2 * n + 1, leaf] * 8, 8)
            merged[pl.ds(start + n * 8, 8), :] = jnp.where(
                low, table[pl.ds(left, 8), :], table[pl.ds(right, 8), :]
            )
        place = pl.multiple_of(t * 8, 8)
        x, y, z = [
            merged[pl.ds(start + ch, pairs, stride=8), :] - centers[pl.ds(place + ch, 1), :]
            for ch in range(3)
        ]
        pieces = [thirds(v) for v in (x, y, z, x * x + y * y + z * z)]
        lines = [piece[0] for piece in pieces] + [one]
        lines += [piece[1] for piece in pieces] + [piece[2] for piece in pieces] + [zero] * 3
        start = pl.multiple_of(t * pairs * 16, 16)
        for row, values in enumerate(lines):
            factors[pl.ds(start + row, pairs, stride=16), :] = values
        return carry

    lax.fori_loop(0, half, prepare, 0, unroll=2)

    def one_leaf(t, carry):
        mine = terms[pl.ds(pl.multiple_of(t * BCAP, BCAP), BCAP), :48]
        total = jnp.zeros((BCAP, LANES), jnp.float32)
        for n in range(0, pairs, 2):
            start = pl.multiple_of((t * pairs + n) * 16, 16)
            both = jnp.concatenate(
                [factors[pl.ds(start, 16), :], factors[pl.ds(start + 16, 16), :]], 1
            ).astype(jnp.bfloat16)
            squared = jnp.dot(
                mine, jnp.concatenate([both] * 3, 0), preferred_element_type=jnp.float32
            )
            for side in range(2):
                weight = merged[pl.ds((t * pairs + n + side) * 8 + 3, 1), :]
                total = total + lax.rsqrt(squared[:, side * LANES : (side + 1) * LANES]) * weight
        sums[pl.ds(pl.multiple_of(t * BCAP, 8), BCAP), :] = total
        return carry

    lax.fori_loop(0, half, one_leaf, 0, unroll=4)
    for r in range(rows):
        block = sums[r * LANES : (r + 1) * LANES, :].T
        potential[r : r + 1, :] = jnp.sum(block, axis=0, keepdims=True)
    combined = potential[...] + far
    beads = per_leaf(counts[...].astype(jnp.float32), rows, pair * half)
    slot = iota((rows, LANES), 1) & (BCAP - 1)
    occupied = slot.astype(jnp.float32) < beads
    decay = per_leaf(decay_rate[...], rows)
    potential[...] = jnp.where(occupied, combined, 0.0)
    new_stress[...] = jnp.where(occupied, decay * stress[...] + combined, 0.0)


VMEM = pl.BlockSpec(memory_space=pltpu.VMEM)
SMEM = pl.BlockSpec(memory_space=pltpu.SMEM)
ANY = pl.BlockSpec(memory_space=pl.ANY)
MIB = 1024 * 1024


def call(kernel, outs, in_specs, scratch=(), limit=40, grid=(), flops=0, bytes_accessed=0):
    return pl.pallas_call(
        kernel,
        out_shape=outs,
        grid=grid,
        in_specs=in_specs,
        out_specs=jax.tree.map(lambda _: VMEM, outs),
        scratch_shapes=list(scratch),
        compiler_params=pltpu.CompilerParams(vmem_limit_bytes=limit * MIB),
        cost_estimate=pl.CostEstimate(
            flops=flops, bytes_accessed=bytes_accessed, transcendentals=0
        ),
    )


def body(
    offsets,
    charges,
    stress,
    decay_rate,
    morton_keys,
    levels,
    bead_counts,
    send_boxes,
    m2l_source,
    m2l_type,
    m2l_count,
    near_source,
    up_inverse,
    down_inverse,
    translations,
):
    f32 = jnp.float32
    leaves = morton_keys.shape[0]
    half = leaves // 2
    parts = lax.axis_size("wide") * lax.axis_size("narrow")
    table = jnp.asarray(transform_table())
    signs = jnp.asarray(sign_rows())
    pair = lax.axis_index("pair").reshape(1)
    owner = (
        lax.axis_index("wide") * lax.axis_size("narrow") + lax.axis_index("narrow")
    ).reshape(1)
    kind_count = translations.shape[0]

    other_translations = lax.ppermute(translations, "pair", [(0, 1), (1, 0)])
    packed, blocks, placed, sources, kinds = call(
        functools.partial(pack_kernel, kind_count),
        [
            jax.ShapeDtypeStruct((4 * half + 8, LANES), f32),
            jax.ShapeDtypeStruct((8 * parts, LANES), f32),
            jax.ShapeDtypeStruct((4 * half, LANES), f32),
            jax.ShapeDtypeStruct(m2l_source.shape, jnp.int32),
            jax.ShapeDtypeStruct(m2l_type.shape, jnp.int32),
        ],
        [VMEM] * 9,
        limit=62,
    )(
        offsets, charges.reshape(half, LANES), morton_keys.reshape(1, leaves),
        levels.reshape(1, leaves), bead_counts.reshape(1, leaves), send_boxes,
        m2l_source, m2l_type, m2l_count.reshape(1, leaves),
    )
    arrived = lax.all_to_all(
        blocks.reshape(parts, 8, LANES), PARTS, split_axis=0, concat_axis=0, tiled=True
    ).reshape(8 * parts, LANES)
    swaps = [(2 * d, 2 * (d ^ 1)) for d in range(parts)]
    for d in range(1, parts - 1, 2):
        swaps += [(2 * d + 1, 2 * d + 3), (2 * d + 3, 2 * d + 1)]
    swapped = lax.ppermute(placed, PARTS + ("pair",), swaps)
    own_check, eval_kernels, terms = call(
        own_kernel,
        [
            jax.ShapeDtypeStruct((Q, leaves // 16 * LANES), f32),
            jax.ShapeDtypeStruct((Q * 8, LANES), f32),
            jax.ShapeDtypeStruct((half * BCAP, LANES), jnp.bfloat16),
        ],
        [SMEM, VMEM],
        [
            pltpu.VMEM((leaves // 16, Q * 8, LANES), f32),
            pltpu.VMEM((half // 2 * 48, LANES), f32),
        ],
        flops=4 * 10**10,
    )(pair, packed)
    passed = lax.ppermute(swapped, "pair", [(0, 1), (1, 0)])

    last = pl.BlockSpec((kind_count, 2, LANES), lambda i: (0, 0, TILES - 1))
    totals, low_table = call(
        far_kernel,
        [
            jax.ShapeDtypeStruct((half * ROWS, LANES), f32),
            jax.ShapeDtypeStruct(table.shape, table.dtype),
        ],
        [SMEM] * 3 + [VMEM] * 4 + [last] * 2 + [ANY] * 3,
        [
            pltpu.VMEM(((leaves + 2 * parts) * ROWS, LANES), f32),
            pltpu.VMEM((kind_count + 1, ROWS, LANES), f32),
            pltpu.VMEM(table.shape, jnp.bfloat16),
            pltpu.VMEM((leaves + 2 * parts, QPAD), f32),
            pltpu.VMEM(((leaves + 2 * parts) // 16, Q, LANES), f32),
            pltpu.VMEM((Q * 8, LANES), f32),
            pltpu.SemaphoreType.DMA((2 * TILES + 1,)),
        ],
        grid=(1,),
        flops=10**10,
        bytes_accessed=4 * 10**6,
    )(
        sources, kinds, pair, arrived, own_check, up_inverse, signs, translations,
        other_translations, table, translations, other_translations,
    )

    out = jax.ShapeDtypeStruct((half // 2, LANES), f32)
    potential, new_stress = call(
        near_kernel,
        [out, out],
        [SMEM] * 3 + [VMEM] * 14,
        [
            pltpu.VMEM((3 * leaves * 8, LANES), f32),
            pltpu.VMEM((half * near_source.shape[1] // 2 * 8, LANES), f32),
            pltpu.VMEM((half * 8, LANES), f32),
            pltpu.VMEM((half * near_source.shape[1] // 2 * 16, LANES), f32),
            pltpu.VMEM((half * BCAP, LANES), f32),
            pltpu.VMEM((Q, LANES), f32),
        ],
    )(
        near_source.T, pair, owner, swapped, placed, passed, packed, terms, eval_kernels, totals,
        table, low_table, signs, down_inverse, bead_counts.reshape(1, leaves),
        decay_rate.reshape(1, half), stress.reshape(half // 2, LANES),
    )
    return potential.reshape(-1), new_stress.reshape(-1)


def solution(mesh):
    return jax.shard_map(
        body,
        mesh=mesh,
        in_specs=(
            P(None, ("groups", "wide", "narrow")),
            P(("groups", "wide", "narrow")),
            P(("groups", "wide", "narrow", "pair")),
            P(("groups", "wide", "narrow", "pair")),
            P(("groups", "wide", "narrow")),
            P(("groups", "wide", "narrow")),
            P(("groups", "wide", "narrow")),
            P(("groups", "wide", "narrow"), None),
            P(("groups", "wide", "narrow"), None),
            P(("groups", "wide", "narrow"), None),
            P(("groups", "wide", "narrow")),
            P(("groups", "wide", "narrow"), None),
            P(),
            P(),
            P(None, None, "pair"),
        ),
        out_specs=(
            P(("groups", "wide", "narrow", "pair")),
            P(("groups", "wide", "narrow", "pair")),
        ),
        check_vma=False,
    )
```

```python
import functools

import jax
import jax.numpy as jnp
import ml_dtypes
import numpy as np
from jax import lax
from jax.experimental import pallas as pl
from jax.experimental.pallas import tpu as pltpu
from jax.sharding import PartitionSpec as P

PGRID = 12
G = 1728
MAXL = 10
BCAP = 64
Q = 152
QPAD = 160
LANES = 128
BINS = 864
TILES = 7
ROWS = 32
softening = 0.04
surface_reach = 1.25
CELLS = [
    (i, j, k)
    for i in range(6)
    for j in range(6)
    for k in range(6)
    if 0 in (i, j, k) or 5 in (i, j, k)
]
PARTS = ("wide", "narrow")


def transform_table():
    cells = np.array(CELLS)
    bins = np.arange(BINS)
    freq = np.stack([bins // 144, bins // 12 % 12, bins % 12])
    angle = (cells @ freq % PGRID) * (2.0 * np.pi / PGRID)
    table = np.zeros((QPAD, 2 * TILES * LANES))
    table[:Q, :BINS] = np.cos(angle)
    table[:Q, TILES * LANES : TILES * LANES + BINS] = -np.sin(angle)
    table[np.abs(table) < 1e-9] = 0.0
    return table.astype(ml_dtypes.bfloat16)


def low_part(high):
    root = np.sqrt(0.75)
    held = float(np.asarray(root).astype(ml_dtypes.bfloat16))
    scale = (root - held) / (held * (held * held - 1.0) * (held * held - 0.25))
    value = high.astype(jnp.float32)
    square = value * value
    return (value * (square - 1.0) * (square - 0.25) * scale).astype(jnp.bfloat16)


def sign_rows():
    rows = np.zeros((8, QPAD), np.float32)
    rows[0, :Q] = 1.0
    rows[1, :Q] = [(-1.0) ** i for i, _, _ in CELLS]
    return rows


def iota(shape, dim):
    return lax.broadcasted_iota(jnp.int32, shape, dim)


def per_leaf(values, count, first=0):
    shape = (count, values.shape[1])
    leaf, lane = first + 2 * iota(shape, 0), iota(shape, 1)
    even = jnp.sum(jnp.where(lane == leaf, values, 0.0), axis=1, keepdims=True)
    odd = jnp.sum(jnp.where(lane == leaf + 1, values, 0.0), axis=1, keepdims=True)
    return jnp.where(iota((count, LANES), 1) < BCAP, even, odd)


def block_transpose(x):
    lane, row = iota(x.shape, 1), iota(x.shape, 0)
    for k in (1, 2, 4):
        row_bit, lane_bit = (row & k) != 0, (lane & k) != 0
        below = pltpu.roll(pltpu.roll(x, 8 - k, 0), k, 1)
        above = pltpu.roll(pltpu.roll(x, k, 0), LANES - k, 1)
        x = jnp.where(row_bit == lane_bit, x, jnp.where(lane_bit, below, above))
    return x


def split(x):
    high = x.astype(jnp.bfloat16)
    return high, (x - high.astype(jnp.float32)).astype(jnp.bfloat16)


def product(a, b, contract):
    dims = (((contract[0],), (contract[1],)), ((), ()))
    (a_high, a_low), (b_high, b_low) = split(a), split(b)

    def dot(x, y):
        return lax.dot_general(x, y, dims, preferred_element_type=jnp.float32)

    return dot(a_high, b_high) + (dot(a_low, b_high) + dot(a_high, b_low))


def axis_squares(offset, width):
    area = width * width
    planes = [surface_reach * 0.5 * (i - 2.5) / 2.5 for i in range(6)]
    return [(plane - offset) * (plane - offset) * area for plane in planes]


def surface_kernels(offsets, width):
    gx, gy, gz = [axis_squares(offset, width) for offset in offsets]
    gz = [g + softening for g in gz]
    last, gxy = None, None
    for q, (i, j, k) in enumerate(CELLS):
        if last != (i, j):
            last, gxy = (i, j), gx[i] + gy[j]
        yield q, lax.rsqrt(gxy + gz[k])


def check_sums(offsets, weights, width, checks):
    offsets = [block_transpose(x) for x in offsets]
    weights, width = block_transpose(weights), block_transpose(width)
    for q, kernel in surface_kernels(offsets, width):
        checks[pl.ds(8 * q, 8), :] = kernel * weights
    check = checks[pl.ds(0, Q, stride=8), :]
    for s in range(1, 8):
        check = check + checks[pl.ds(s, Q, stride=8), :]
    return check


def upward(check, up_inverse):
    density = product(check, up_inverse, (0, 0))
    blocks = check.shape[1] // LANES
    density = density.reshape(2 * blocks, 8, 8, Q)
    total = density[:, 0]
    for g in range(1, 8):
        total = total + density[:, g]
    return total.reshape(16 * blocks, Q)


def store_spectra(density, table_high, table_low, target):
    count = density.shape[0] // 2
    high, low = split(density)
    both = jnp.concatenate([high, low], 0)
    for first in range(0, 2 * TILES, 2):
        columns = pl.ds(first * LANES, 2 * LANES)
        part = jnp.dot(both, table_high[:, columns], preferred_element_type=jnp.float32)
        spectra = part[: 2 * count] + part[2 * count :] + jnp.dot(
            high, table_low[:, columns], preferred_element_type=jnp.float32
        )
        for tile in range(first, first + 2):
            for side in range(2):
                for block in range(count // 16):
                    for h in range(2):
                        row = side * count + block * 16 + h * 8
                        start = (block * 16 + h) * ROWS + 16 * side + 8 * (tile // TILES) + tile % TILES
                        target[pl.ds(start, 8, stride=2 * ROWS), :] = spectra[
                            row : row + 8, (tile - first) * LANES : (tile - first + 1) * LANES
                        ]


def pack_kernel(
    kind_count, offsets, charges, keys, levels, counts, send_boxes, m2l_source, m2l_type, m2l_count,
    out, blocks, placed, sources, kinds,
):
    leaves = keys.shape[1]
    half = leaves // 2
    out[4 * half :, :] = jnp.zeros((8, LANES), jnp.float32)
    width = jnp.left_shift(jnp.ones_like(levels[...]), MAXL - levels[...]).astype(jnp.float32)
    for a in range(3):
        summed = jnp.zeros_like(keys[...])
        for bit in range(MAXL):
            summed = summed + (jnp.right_shift(keys[...], 3 * bit + a) & 1) * (1 << bit)
        out[4 * half + a : 4 * half + a + 1, :leaves] = summed.astype(jnp.float32) + 0.5 * width
    out[4 * half + 3 : 4 * half + 4, :leaves] = width
    for r in range(half):
        out[pl.ds(r, 3, stride=half), :] = offsets[:, r * LANES : (r + 1) * LANES]
    beads = per_leaf(counts[...].astype(jnp.float32), half)
    slot = iota((half, LANES), 1) & (BCAP - 1)
    out[3 * half : 4 * half, :] = jnp.where(slot.astype(jnp.float32) < beads, charges[...], 0.0)

    entry = iota(m2l_type.shape, 1)
    square = (leaves, leaves)
    live = jnp.sum(
        jnp.where(iota(square, 0) == iota(square, 1), m2l_count[...].astype(jnp.float32), 0.0),
        axis=1, keepdims=True,
    )
    kinds[...] = jnp.where(entry.astype(jnp.float32) < live, m2l_type[...], kind_count)
    sources[...] = m2l_source[...] * ROWS

    spread = per_leaf(width, half)
    for ch in range(3):
        center = per_leaf(out[4 * half + ch : 4 * half + ch + 1, :leaves], half)
        placed[ch * half : (ch + 1) * half, :] = center + spread * out[ch * half : (ch + 1) * half, :]
    placed[3 * half :, :] = out[3 * half : 4 * half, :]

    sends = send_boxes.shape[1]
    lane = iota((8, LANES), 1)
    for block in range(sends // 16):
        picked = []
        for c in range(2):
            column = block * 16 + 2 * iota((8, sends), 0) + c
            box = jnp.sum(
                jnp.where(iota((8, sends), 1) == column, send_boxes[...].astype(jnp.float32), 0.0),
                axis=1, keepdims=True,
            ).astype(jnp.int32)
            width_here = jnp.sum(
                jnp.where(iota((8, leaves), 1) == box, width, 0.0), axis=1, keepdims=True
            )
            row_of = jnp.broadcast_to(box >> 1, (8, LANES))
            found = [jnp.zeros((8, LANES), jnp.float32)] * 4
            for r in range(half):
                here = row_of == r
                for ch in range(4):
                    found[ch] = jnp.where(here, out[ch * half + r : ch * half + r + 1, :], found[ch])
            aligned = jnp.broadcast_to((box & 1) == c, (8, LANES))
            found = [jnp.where(aligned, x, pltpu.roll(x, BCAP, 1)) for x in found]
            picked.append(found + [jnp.broadcast_to(width_here, (8, LANES))])
        for ch in range(5):
            blocks[pl.ds(block * 64 + ch, 8, stride=8), :] = jnp.where(
                lane < BCAP, picked[0][ch], picked[1][ch]
            )
        for ch in range(5, 8):
            blocks[pl.ds(block * 64 + ch, 8, stride=8), :] = jnp.zeros((8, LANES), jnp.float32)


def own_kernel(packed, out, checks):
    half = (packed.shape[0] - 8) // 4
    width = per_leaf(packed[4 * half + 3 : 4 * half + 4, :], half)
    for block in range(half // 8):
        rows = [packed[c * half + block * 8 : c * half + block * 8 + 8, :] for c in range(4)]
        out[:, block * LANES : (block + 1) * LANES] = check_sums(
            rows[:3], rows[3], width[block * 8 : block * 8 + 8], checks.at[block]
        )


def surface_kernel(pair_ref, packed, eval_kernels):
    half = (packed.shape[0] - 8) // 4
    rows = half // 2
    pair = pair_ref[0]
    width = block_transpose(
        per_leaf(packed[4 * half + 3 : 4 * half + 4, :], rows, pair * half)
    )
    offsets = [
        block_transpose(packed[pl.ds(pl.multiple_of(c * half + pair * rows, 8), rows), :])
        for c in range(3)
    ]
    for q, kernel in surface_kernels(offsets, width):
        eval_kernels[pl.ds(8 * q, 8), :] = kernel


def spread_kernel(pair_ref, packed, targets):
    half = (packed.shape[0] - 8) // 4
    rows = half // 2
    pair = pair_ref[0]
    width = per_leaf(packed[4 * half + 3 : 4 * half + 4, :], rows, pair * half)
    for ch in range(3):
        center = per_leaf(packed[4 * half + ch : 4 * half + ch + 1, :], rows, pair * half)
        offset = packed[pl.ds(pl.multiple_of(ch * half + pair * rows, 8), rows), :]
        flipped = (center + width * offset).T
        for r in range(rows):
            for h in range(2):
                start = ((2 * r + h) * 3 + ch) * BCAP
                targets[pl.ds(start, BCAP), :] = jnp.broadcast_to(
                    flipped[h * BCAP : (h + 1) * BCAP, r : r + 1], (BCAP, LANES)
                )


def far_kernel(
    sources, kinds, pair_ref, arrived, own_check, up_inverse, signs,
    last_bins, other_last_bins, table, translations, other_translations, totals, low_table,
    spectra, kernels, high_table, density, check, checks, sems,
):
    leaves, entries = sources.shape
    half = leaves // 2
    blocks = arrived.shape[0] // 64
    kind_count = translations.shape[0]
    pair = pair_ref[0]

    table_copy = pltpu.make_async_copy(table, high_table, sems.at[0])
    table_copy.start()
    kernel_copies = []
    for side, bins in enumerate((translations, other_translations)):
        for t in range(TILES - 1):
            kernel_copies.append(pltpu.make_async_copy(
                bins.at[:, :, pl.ds(t * LANES, LANES)],
                kernels.at[pl.ds(0, kind_count), pl.ds(16 * side + 2 * t, 2), :],
                sems.at[1 + len(kernel_copies)],
            ))
        kernel_copies.append(pltpu.make_async_copy(
            (last_bins, other_last_bins)[side],
            kernels.at[pl.ds(0, kind_count), pl.ds(16 * side + 2 * TILES - 2, 2), :],
            sems.at[1 + len(kernel_copies)],
        ))
    for copy in kernel_copies:
        copy.start()
    kernels[kind_count] = jnp.zeros((ROWS, LANES), jnp.float32)

    density[...] = jnp.zeros(density.shape, jnp.float32)
    check[0, :, :] = own_check[:, :LANES]
    check[1, :, :] = own_check[:, LANES:]

    def arrive(block, carry):
        beads = [
            arrived[pl.ds(pl.multiple_of(block * 64, 64) + ch, 8, stride=8), :] for ch in range(5)
        ]
        check[leaves // 16 + block, :, :] = check_sums(beads[:3], beads[3], beads[4], checks)
        return carry

    if blocks == 1:
        arrive(0, 0)
    else:
        lax.fori_loop(0, blocks, arrive, 0)
    count = check.shape[0]
    for first in range(0, count, 3):
        some = range(first, min(first + 3, count))
        density[16 * first : 16 * first + 16 * len(some), :Q] = upward(
            jnp.concatenate([check[n] for n in some], 1), up_inverse[...]
        )
    table_copy.wait()
    low_table[...] = low_part(high_table[...])
    sign = jnp.where(pair == 1, signs[1:2, :], signs[0:1, :])
    other_sign = jnp.where(pair == 1, signs[0:1, :], signs[1:2, :])
    store_spectra(
        jnp.concatenate([density[...] * sign, density[...] * other_sign], 0),
        high_table, low_table, spectra,
    )
    for copy in kernel_copies:
        copy.wait()

    def translate(t, carry):
        leaf = pair * half + t
        sums = [[None] * 4, [None] * 4]
        for entry in range(entries):
            kind = kinds[leaf, entry]
            source = spectra[pl.ds(pl.multiple_of(sources[leaf, entry], ROWS), ROWS), :]
            for side in range(2):
                k_re = kernels[kind, pl.ds(16 * side, 8, stride=2), :]
                k_im = kernels[kind, pl.ds(16 * side + 1, 8, stride=2), :]
                s_re, s_im = source[16 * side : 16 * side + 8], source[16 * side + 8 : 16 * side + 16]
                terms = (k_re * s_re, k_im * s_im, k_re * s_im, k_im * s_re)
                for n, term in enumerate(terms):
                    sums[side][n] = term if sums[side][n] is None else sums[side][n] + term
        start = pl.multiple_of(t * ROWS, ROWS)
        for side in range(2):
            rr, ii, ri, ir = sums[side]
            totals[pl.ds(start + 16 * side, 8), :] = rr - ii
            totals[pl.ds(start + 16 * side + 8, 8), :] = ri + ir
        return carry

    lax.fori_loop(0, half, translate, 0, unroll=4)


def evaluate(pair, totals, table, low_table, signs, down_inverse, eval_kernels, densities):
    half = totals.shape[0] // ROWS
    leaves = 2 * half
    rows = half // 2
    sign = jnp.where(pair == 1, signs[1:2, :], signs[0:1, :])
    other_sign = jnp.where(pair == 1, signs[0:1, :], signs[1:2, :])
    lane = iota((half, LANES), 1)
    sides = []
    for side in range(2):
        columns = []
        for c in range(2):
            for t in range(TILES):
                line = totals[pl.ds(16 * side + c * 8 + t, half, stride=ROWS), :]
                if t == TILES - 1:
                    line = jnp.where(lane < BINS - t * LANES, line, 0.0)
                columns.append(line)
        sides.append(jnp.concatenate(columns, 1))
    high, low = split(jnp.concatenate(sides, 0))
    across = (((1,), (1,)), ((), ()))
    both = lax.dot_general(
        jnp.concatenate([high, low], 0), table[...], across,
        preferred_element_type=jnp.float32,
    )
    check = both[:leaves] + both[leaves:] + lax.dot_general(
        high, low_table[...], across, preferred_element_type=jnp.float32
    )
    check = (check[:half] * sign + check[half:] * other_sign)[:, :Q] * (1.0 / G)

    leaf_of = 2 * (lane & 7) + (lane >> 6)
    spread = jnp.where(iota((half, LANES), 0) == leaf_of, 1.0, 0.0)
    densities[...] = product(product(check, down_inverse[...], (1, 0)), spread, (0, 0))
    parts = [jnp.zeros((rows, LANES), jnp.float32)] * 4
    for q in range(Q):
        term = eval_kernels[8 * q : 8 * q + 8, :] * densities[q : q + 1, :]
        parts[q % 4] = parts[q % 4] + term
    return block_transpose((parts[0] + parts[1]) + (parts[2] + parts[3]))


def near_kernel(
    near_source, pair_ref, owner_ref, swapped, placed, passed, targets, eval_kernels, totals,
    high_table, low_table, signs, down_inverse, counts, decay_rate, stress, potential, new_stress,
    table, merged, sums, densities,
):
    entries, leaves = near_source.shape
    half = leaves // 2
    pair = pair_ref[0]
    low = iota((half, LANES), 1) < BCAP
    far = evaluate(
        pair, totals, high_table, low_table, signs, down_inverse, eval_kernels, densities
    )
    swapped_from = jnp.where(((owner_ref[0] & 1) ^ pair) == 1, 0, 2)
    for n, rows_of in ((swapped_from, swapped), (1, placed), (2 - swapped_from, passed)):
        first = n * (leaves * 8)
        for ch in range(4):
            rows = rows_of[ch * half : (ch + 1) * half, :]
            turned = pltpu.roll(rows, BCAP, 1)
            table[pl.ds(first + ch, half, stride=16), :] = jnp.where(low, rows, turned)
            table[pl.ds(first + 8 + ch, half, stride=16), :] = jnp.where(low, turned, rows)
    low = iota((8, LANES), 1) < BCAP

    def merge(t, carry):
        leaf = pair * half + t
        for n in range(entries // 2):
            left = pl.multiple_of(near_source[2 * n, leaf] * 8, 8)
            right = pl.multiple_of(near_source[2 * n + 1, leaf] * 8, 8)
            start = pl.multiple_of((t * (entries // 2) + n) * 8, 8)
            merged[pl.ds(start, 8), :] = jnp.where(
                low, table[pl.ds(left, 8), :], table[pl.ds(right, 8), :]
            )
        return carry

    lax.fori_loop(0, half, merge, 0, unroll=4)

    def one_leaf(t, carry):
        start = pl.multiple_of(t * 3 * BCAP, 8)
        tx, ty, tz = [targets[pl.ds(start + ch * BCAP, BCAP), :] for ch in range(3)]
        total = jnp.zeros((BCAP, LANES), jnp.float32)
        for n in range(entries // 2):
            first = pl.multiple_of((t * (entries // 2) + n) * 8, 8)
            sx, sy, sz, weight = [merged[pl.ds(first + ch, 1), :] for ch in range(4)]
            gx, gy, gz = tx - sx, ty - sy, tz - sz
            squared = gx * gx + gy * gy + (gz * gz + softening)
            total = total + lax.rsqrt(squared) * weight
        sums[pl.ds(pl.multiple_of(t * BCAP, 8), BCAP), :] = total
        return carry

    lax.fori_loop(0, half, one_leaf, 0, unroll=4)
    rows = half // 2
    for r in range(rows):
        block = sums[r * LANES : (r + 1) * LANES, :].T
        potential[r : r + 1, :] = jnp.sum(block, axis=0, keepdims=True)
    combined = potential[...] + far
    beads = per_leaf(counts[...].astype(jnp.float32), rows, pair * half)
    slot = iota((rows, LANES), 1) & (BCAP - 1)
    occupied = slot.astype(jnp.float32) < beads
    decay = per_leaf(decay_rate[...], rows)
    potential[...] = jnp.where(occupied, combined, 0.0)
    new_stress[...] = jnp.where(occupied, decay * stress[...] + combined, 0.0)


VMEM = pl.BlockSpec(memory_space=pltpu.VMEM)
SMEM = pl.BlockSpec(memory_space=pltpu.SMEM)
ANY = pl.BlockSpec(memory_space=pl.ANY)
MIB = 1024 * 1024


def call(kernel, outs, in_specs, scratch=(), limit=40, grid=(), flops=0, bytes_accessed=0):
    return pl.pallas_call(
        kernel,
        out_shape=outs,
        grid=grid,
        in_specs=in_specs,
        out_specs=jax.tree.map(lambda _: VMEM, outs),
        scratch_shapes=list(scratch),
        compiler_params=pltpu.CompilerParams(vmem_limit_bytes=limit * MIB),
        cost_estimate=pl.CostEstimate(
            flops=flops, bytes_accessed=bytes_accessed, transcendentals=0
        ),
    )


def body(
    offsets,
    charges,
    stress,
    decay_rate,
    morton_keys,
    levels,
    bead_counts,
    send_boxes,
    m2l_source,
    m2l_type,
    m2l_count,
    near_source,
    up_inverse,
    down_inverse,
    translations,
):
    f32 = jnp.float32
    leaves = morton_keys.shape[0]
    half = leaves // 2
    parts = lax.axis_size("wide") * lax.axis_size("narrow")
    table = jnp.asarray(transform_table())
    signs = jnp.asarray(sign_rows())
    pair = lax.axis_index("pair").reshape(1)
    owner = (
        lax.axis_index("wide") * lax.axis_size("narrow") + lax.axis_index("narrow")
    ).reshape(1)
    kind_count = translations.shape[0]

    other_translations = lax.ppermute(translations, "pair", [(0, 1), (1, 0)])
    packed, blocks, placed, sources, kinds = call(
        functools.partial(pack_kernel, kind_count),
        [
            jax.ShapeDtypeStruct((4 * half + 8, LANES), f32),
            jax.ShapeDtypeStruct((8 * parts, LANES), f32),
            jax.ShapeDtypeStruct((4 * half, LANES), f32),
            jax.ShapeDtypeStruct(m2l_source.shape, jnp.int32),
            jax.ShapeDtypeStruct(m2l_type.shape, jnp.int32),
        ],
        [VMEM] * 9,
        limit=62,
    )(
        offsets, charges.reshape(half, LANES), morton_keys.reshape(1, leaves),
        levels.reshape(1, leaves), bead_counts.reshape(1, leaves), send_boxes,
        m2l_source, m2l_type, m2l_count.reshape(1, leaves),
    )
    arrived = lax.all_to_all(
        blocks.reshape(parts, 8, LANES), PARTS, split_axis=0, concat_axis=0, tiled=True
    ).reshape(8 * parts, LANES)
    swaps = [(2 * d, 2 * (d ^ 1)) for d in range(parts)]
    for d in range(1, parts - 1, 2):
        swaps += [(2 * d + 1, 2 * d + 3), (2 * d + 3, 2 * d + 1)]
    swapped = lax.ppermute(placed, PARTS + ("pair",), swaps)
    own_check = call(
        own_kernel,
        jax.ShapeDtypeStruct((Q, leaves // 16 * LANES), f32),
        [VMEM],
        [pltpu.VMEM((leaves // 16, Q * 8, LANES), f32)],
        flops=4 * 10**10,
    )(packed)
    eval_kernels = call(
        surface_kernel, jax.ShapeDtypeStruct((Q * 8, LANES), f32), [SMEM, VMEM], flops=10**9
    )(pair, packed)
    targets = call(
        spread_kernel, jax.ShapeDtypeStruct((half * 3 * BCAP, LANES), f32), [SMEM, VMEM],
        flops=10**9,
    )(pair, packed)
    passed = lax.ppermute(swapped, "pair", [(0, 1), (1, 0)])

    last = pl.BlockSpec((kind_count, 2, LANES), lambda i: (0, 0, TILES - 1))
    totals, low_table = call(
        far_kernel,
        [
            jax.ShapeDtypeStruct((half * ROWS, LANES), f32),
            jax.ShapeDtypeStruct(table.shape, table.dtype),
        ],
        [SMEM] * 3 + [VMEM] * 4 + [last] * 2 + [ANY] * 3,
        [
            pltpu.VMEM(((leaves + 2 * parts) * ROWS, LANES), f32),
            pltpu.VMEM((kind_count + 1, ROWS, LANES), f32),
            pltpu.VMEM(table.shape, jnp.bfloat16),
            pltpu.VMEM((leaves + 2 * parts, QPAD), f32),
            pltpu.VMEM(((leaves + 2 * parts) // 16, Q, LANES), f32),
            pltpu.VMEM((Q * 8, LANES), f32),
            pltpu.SemaphoreType.DMA((2 * TILES + 1,)),
        ],
        grid=(1,),
        flops=10**10,
        bytes_accessed=4 * 10**6,
    )(
        sources, kinds, pair, arrived, own_check, up_inverse, signs, translations,
        other_translations, table, translations, other_translations,
    )

    out = jax.ShapeDtypeStruct((half // 2, LANES), f32)
    potential, new_stress = call(
        near_kernel,
        [out, out],
        [SMEM] * 3 + [VMEM] * 13,
        [
            pltpu.VMEM((3 * leaves * 8, LANES), f32),
            pltpu.VMEM((half * near_source.shape[1] // 2 * 8, LANES), f32),
            pltpu.VMEM((half * BCAP, LANES), f32),
            pltpu.VMEM((Q, LANES), f32),
        ],
    )(
        near_source.T, pair, owner, swapped, placed, passed, targets, eval_kernels, totals,
        table, low_table, signs, down_inverse, bead_counts.reshape(1, leaves),
        decay_rate.reshape(1, half), stress.reshape(half // 2, LANES),
    )
    return potential.reshape(-1), new_stress.reshape(-1)


def solution(mesh):
    return jax.shard_map(
        body,
        mesh=mesh,
        in_specs=(
            P(None, ("groups", "wide", "narrow")),
            P(("groups", "wide", "narrow")),
            P(("groups", "wide", "narrow", "pair")),
            P(("groups", "wide", "narrow", "pair")),
            P(("groups", "wide", "narrow")),
            P(("groups", "wide", "narrow")),
            P(("groups", "wide", "narrow")),
            P(("groups", "wide", "narrow"), None),
            P(("groups", "wide", "narrow"), None),
            P(("groups", "wide", "narrow"), None),
            P(("groups", "wide", "narrow")),
            P(("groups", "wide", "narrow"), None),
            P(),
            P(),
            P(None, None, "pair"),
        ),
        out_specs=(
            P(("groups", "wide", "narrow", "pair")),
            P(("groups", "wide", "narrow", "pair")),
        ),
        check_vma=False,
    )
```

```python
import functools

import jax
import jax.numpy as jnp
import ml_dtypes
import numpy as np
from jax import lax
from jax.experimental import pallas as pl
from jax.experimental.pallas import tpu as pltpu
from jax.sharding import PartitionSpec as P

PGRID = 12
G = 1728
MAXL = 10
BCAP = 64
Q = 152
QPAD = 160
LANES = 128
BINS = 864
TILES = 7
ROWS = 32
softening = 0.04
surface_reach = 1.25
CELLS = [
    (i, j, k)
    for i in range(6)
    for j in range(6)
    for k in range(6)
    if 0 in (i, j, k) or 5 in (i, j, k)
]
PARTS = ("wide", "narrow")


def transform_table():
    cells = np.array(CELLS)
    bins = np.arange(BINS)
    freq = np.stack([bins // 144, bins // 12 % 12, bins % 12])
    angle = (cells @ freq % PGRID) * (2.0 * np.pi / PGRID)
    table = np.zeros((QPAD, 2 * TILES * LANES))
    table[:Q, :BINS] = np.cos(angle)
    table[:Q, TILES * LANES : TILES * LANES + BINS] = -np.sin(angle)
    table[np.abs(table) < 1e-9] = 0.0
    return table.astype(ml_dtypes.bfloat16)


def low_part(high):
    root = np.sqrt(0.75)
    held = float(np.asarray(root).astype(ml_dtypes.bfloat16))
    scale = (root - held) / (held * (held * held - 1.0) * (held * held - 0.25))
    value = high.astype(jnp.float32)
    square = value * value
    return (value * (square - 1.0) * (square - 0.25) * scale).astype(jnp.bfloat16)


def sign_rows():
    rows = np.zeros((8, QPAD), np.float32)
    rows[0, :Q] = 1.0
    rows[1, :Q] = [(-1.0) ** i for i, _, _ in CELLS]
    return rows


def iota(shape, dim):
    return lax.broadcasted_iota(jnp.int32, shape, dim)


def per_leaf(values, count, first=0):
    shape = (count, values.shape[1])
    leaf, lane = first + 2 * iota(shape, 0), iota(shape, 1)
    even = jnp.sum(jnp.where(lane == leaf, values, 0.0), axis=1, keepdims=True)
    odd = jnp.sum(jnp.where(lane == leaf + 1, values, 0.0), axis=1, keepdims=True)
    return jnp.where(iota((count, LANES), 1) < BCAP, even, odd)


def block_transpose(x):
    lane, row = iota(x.shape, 1), iota(x.shape, 0)
    for k in (1, 2, 4):
        row_bit, lane_bit = (row & k) != 0, (lane & k) != 0
        below = pltpu.roll(pltpu.roll(x, 8 - k, 0), k, 1)
        above = pltpu.roll(pltpu.roll(x, k, 0), LANES - k, 1)
        x = jnp.where(row_bit == lane_bit, x, jnp.where(lane_bit, below, above))
    return x


def split(x):
    high = x.astype(jnp.bfloat16)
    return high, (x - high.astype(jnp.float32)).astype(jnp.bfloat16)


def product(a, b, contract):
    dims = (((contract[0],), (contract[1],)), ((), ()))
    (a_high, a_low), (b_high, b_low) = split(a), split(b)

    def dot(x, y):
        return lax.dot_general(x, y, dims, preferred_element_type=jnp.float32)

    return dot(a_high, b_high) + (dot(a_low, b_high) + dot(a_high, b_low))


def axis_squares(offset, width):
    area = width * width
    planes = [surface_reach * 0.5 * (i - 2.5) / 2.5 for i in range(6)]
    return [(plane - offset) * (plane - offset) * area for plane in planes]


def surface_kernels(offsets, width):
    gx, gy, gz = [axis_squares(offset, width) for offset in offsets]
    gz = [g + softening for g in gz]
    last, gxy = None, None
    for q, (i, j, k) in enumerate(CELLS):
        if last != (i, j):
            last, gxy = (i, j), gx[i] + gy[j]
        yield q, lax.rsqrt(gxy + gz[k])


def check_sums(offsets, weights, width, checks):
    offsets = [block_transpose(x) for x in offsets]
    weights, width = block_transpose(weights), block_transpose(width)
    for q, kernel in surface_kernels(offsets, width):
        checks[pl.ds(8 * q, 8), :] = kernel * weights
    check = checks[pl.ds(0, Q, stride=8), :]
    for s in range(1, 8):
        check = check + checks[pl.ds(s, Q, stride=8), :]
    return check


def upward(check, up_inverse):
    density = product(check, up_inverse, (0, 0))
    blocks = check.shape[1] // LANES
    density = density.reshape(2 * blocks, 8, 8, Q)
    total = density[:, 0]
    for g in range(1, 8):
        total = total + density[:, g]
    return total.reshape(16 * blocks, Q)


def store_spectra(density, table_high, table_low, target):
    count = density.shape[0] // 2
    high, low = split(density)
    both = jnp.concatenate([high, low], 0)
    for first in range(0, 2 * TILES, 2):
        columns = pl.ds(first * LANES, 2 * LANES)
        part = jnp.dot(both, table_high[:, columns], preferred_element_type=jnp.float32)
        spectra = part[: 2 * count] + part[2 * count :] + jnp.dot(
            high, table_low[:, columns], preferred_element_type=jnp.float32
        )
        for tile in range(first, first + 2):
            for side in range(2):
                for block in range(count // 16):
                    for h in range(2):
                        row = side * count + block * 16 + h * 8
                        start = (block * 16 + h) * ROWS + 16 * side + 8 * (tile // TILES) + tile % TILES
                        target[pl.ds(start, 8, stride=2 * ROWS), :] = spectra[
                            row : row + 8, (tile - first) * LANES : (tile - first + 1) * LANES
                        ]


def pack_kernel(
    kind_count, offsets, charges, keys, levels, counts, send_boxes, m2l_source, m2l_type, m2l_count,
    out, blocks, placed, sources, kinds,
):
    leaves = keys.shape[1]
    half = leaves // 2
    out[4 * half :, :] = jnp.zeros((8, LANES), jnp.float32)
    width = jnp.left_shift(jnp.ones_like(levels[...]), MAXL - levels[...]).astype(jnp.float32)
    for a in range(3):
        summed = jnp.zeros_like(keys[...])
        for bit in range(MAXL):
            summed = summed + (jnp.right_shift(keys[...], 3 * bit + a) & 1) * (1 << bit)
        out[4 * half + a : 4 * half + a + 1, :leaves] = summed.astype(jnp.float32) + 0.5 * width
    out[4 * half + 3 : 4 * half + 4, :leaves] = width
    for r in range(half):
        out[pl.ds(r, 3, stride=half), :] = offsets[:, r * LANES : (r + 1) * LANES]
    beads = per_leaf(counts[...].astype(jnp.float32), half)
    slot = iota((half, LANES), 1) & (BCAP - 1)
    out[3 * half : 4 * half, :] = jnp.where(slot.astype(jnp.float32) < beads, charges[...], 0.0)

    entry = iota(m2l_type.shape, 1)
    square = (leaves, leaves)
    live = jnp.sum(
        jnp.where(iota(square, 0) == iota(square, 1), m2l_count[...].astype(jnp.float32), 0.0),
        axis=1, keepdims=True,
    )
    kinds[...] = jnp.where(entry.astype(jnp.float32) < live, m2l_type[...], kind_count)
    sources[...] = m2l_source[...] * ROWS

    spread = per_leaf(width, half)
    for ch in range(3):
        center = per_leaf(out[4 * half + ch : 4 * half + ch + 1, :leaves], half)
        placed[ch * half : (ch + 1) * half, :] = center + spread * out[ch * half : (ch + 1) * half, :]
    placed[3 * half :, :] = out[3 * half : 4 * half, :]

    sends = send_boxes.shape[1]
    lane = iota((8, LANES), 1)
    for block in range(sends // 16):
        picked = []
        for c in range(2):
            column = block * 16 + 2 * iota((8, sends), 0) + c
            box = jnp.sum(
                jnp.where(iota((8, sends), 1) == column, send_boxes[...].astype(jnp.float32), 0.0),
                axis=1, keepdims=True,
            ).astype(jnp.int32)
            width_here = jnp.sum(
                jnp.where(iota((8, leaves), 1) == box, width, 0.0), axis=1, keepdims=True
            )
            row_of = jnp.broadcast_to(box >> 1, (8, LANES))
            found = [jnp.zeros((8, LANES), jnp.float32)] * 4
            for r in range(half):
                here = row_of == r
                for ch in range(4):
                    found[ch] = jnp.where(here, out[ch * half + r : ch * half + r + 1, :], found[ch])
            aligned = jnp.broadcast_to((box & 1) == c, (8, LANES))
            found = [jnp.where(aligned, x, pltpu.roll(x, BCAP, 1)) for x in found]
            picked.append(found + [jnp.broadcast_to(width_here, (8, LANES))])
        for ch in range(5):
            blocks[pl.ds(block * 64 + ch, 8, stride=8), :] = jnp.where(
                lane < BCAP, picked[0][ch], picked[1][ch]
            )
        for ch in range(5, 8):
            blocks[pl.ds(block * 64 + ch, 8, stride=8), :] = jnp.zeros((8, LANES), jnp.float32)


def own_kernel(packed, out, checks):
    half = (packed.shape[0] - 8) // 4
    width = per_leaf(packed[4 * half + 3 : 4 * half + 4, :], half)
    for block in range(half // 8):
        rows = [packed[c * half + block * 8 : c * half + block * 8 + 8, :] for c in range(4)]
        out[:, block * LANES : (block + 1) * LANES] = check_sums(
            rows[:3], rows[3], width[block * 8 : block * 8 + 8], checks.at[block]
        )


def far_kernel(
    sources, kinds, pair_ref, arrived, own_check, up_inverse, signs,
    last_bins, other_last_bins, table, translations, other_translations, totals, low_table,
    spectra, kernels, high_table, density, check, checks, sems,
):
    leaves, entries = sources.shape
    half = leaves // 2
    blocks = arrived.shape[0] // 64
    kind_count = translations.shape[0]
    pair = pair_ref[0]

    table_copy = pltpu.make_async_copy(table, high_table, sems.at[0])
    table_copy.start()
    kernel_copies = []
    for side, bins in enumerate((translations, other_translations)):
        for t in range(TILES - 1):
            kernel_copies.append(pltpu.make_async_copy(
                bins.at[:, :, pl.ds(t * LANES, LANES)],
                kernels.at[pl.ds(0, kind_count), pl.ds(16 * side + 2 * t, 2), :],
                sems.at[1 + len(kernel_copies)],
            ))
        kernel_copies.append(pltpu.make_async_copy(
            (last_bins, other_last_bins)[side],
            kernels.at[pl.ds(0, kind_count), pl.ds(16 * side + 2 * TILES - 2, 2), :],
            sems.at[1 + len(kernel_copies)],
        ))
    for copy in kernel_copies:
        copy.start()
    kernels[kind_count] = jnp.zeros((ROWS, LANES), jnp.float32)

    density[...] = jnp.zeros(density.shape, jnp.float32)
    check[0, :, :] = own_check[:, :LANES]
    check[1, :, :] = own_check[:, LANES:]

    def arrive(block, carry):
        beads = [
            arrived[pl.ds(pl.multiple_of(block * 64, 64) + ch, 8, stride=8), :] for ch in range(5)
        ]
        check[leaves // 16 + block, :, :] = check_sums(beads[:3], beads[3], beads[4], checks)
        return carry

    if blocks == 1:
        arrive(0, 0)
    else:
        lax.fori_loop(0, blocks, arrive, 0)
    count = check.shape[0]
    for first in range(0, count, 3):
        some = range(first, min(first + 3, count))
        density[16 * first : 16 * first + 16 * len(some), :Q] = upward(
            jnp.concatenate([check[n] for n in some], 1), up_inverse[...]
        )
    table_copy.wait()
    low_table[...] = low_part(high_table[...])
    sign = jnp.where(pair == 1, signs[1:2, :], signs[0:1, :])
    other_sign = jnp.where(pair == 1, signs[0:1, :], signs[1:2, :])
    store_spectra(
        jnp.concatenate([density[...] * sign, density[...] * other_sign], 0),
        high_table, low_table, spectra,
    )
    for copy in kernel_copies:
        copy.wait()

    def translate(t, carry):
        leaf = pair * half + t
        sums = [[None] * 4, [None] * 4]
        for entry in range(entries):
            kind = kinds[leaf, entry]
            start = pl.multiple_of(sources[leaf, entry], ROWS)
            for side in range(2):
                k_re = kernels[kind, pl.ds(16 * side, 8, stride=2), :]
                k_im = kernels[kind, pl.ds(16 * side + 1, 8, stride=2), :]
                s_re = spectra[pl.ds(start + 16 * side, 8), :]
                s_im = spectra[pl.ds(start + 16 * side + 8, 8), :]
                terms = (k_re * s_re, k_im * s_im, k_re * s_im, k_im * s_re)
                for n, term in enumerate(terms):
                    sums[side][n] = term if sums[side][n] is None else sums[side][n] + term
        start = pl.multiple_of(t * ROWS, ROWS)
        for side in range(2):
            rr, ii, ri, ir = sums[side]
            totals[pl.ds(start + 16 * side, 8), :] = rr - ii
            totals[pl.ds(start + 16 * side + 8, 8), :] = ri + ir
        return carry

    lax.fori_loop(0, half, translate, 0, unroll=4)


def evaluate(
    pair, packed, totals, table, low_table, signs, down_inverse, eval_kernels, densities
):
    half = (packed.shape[0] - 8) // 4
    leaves = 2 * half
    rows = half // 2
    width = block_transpose(
        per_leaf(packed[4 * half + 3 : 4 * half + 4, :], rows, pair * half)
    )
    offsets = [
        block_transpose(packed[pl.ds(pl.multiple_of(c * half + pair * rows, 8), rows), :])
        for c in range(3)
    ]
    for q, kernel in surface_kernels(offsets, width):
        eval_kernels[pl.ds(8 * q, 8), :] = kernel
    sign = jnp.where(pair == 1, signs[1:2, :], signs[0:1, :])
    other_sign = jnp.where(pair == 1, signs[0:1, :], signs[1:2, :])
    lane = iota((half, LANES), 1)
    sides = []
    for side in range(2):
        columns = []
        for c in range(2):
            for t in range(TILES):
                line = totals[pl.ds(16 * side + c * 8 + t, half, stride=ROWS), :]
                if t == TILES - 1:
                    line = jnp.where(lane < BINS - t * LANES, line, 0.0)
                columns.append(line)
        sides.append(jnp.concatenate(columns, 1))
    high, low = split(jnp.concatenate(sides, 0))
    across = (((1,), (1,)), ((), ()))
    both = lax.dot_general(
        jnp.concatenate([high, low], 0), table[...], across,
        preferred_element_type=jnp.float32,
    )
    check = both[:leaves] + both[leaves:] + lax.dot_general(
        high, low_table[...], across, preferred_element_type=jnp.float32
    )
    check = (check[:half] * sign + check[half:] * other_sign)[:, :Q] * (1.0 / G)

    leaf_of = 2 * (lane & 7) + (lane >> 6)
    spread = jnp.where(iota((half, LANES), 0) == leaf_of, 1.0, 0.0)
    densities[...] = product(product(check, down_inverse[...], (1, 0)), spread, (0, 0))
    parts = [jnp.zeros((rows, LANES), jnp.float32)] * 4
    for q in range(Q):
        term = eval_kernels[8 * q : 8 * q + 8, :] * densities[q : q + 1, :]
        parts[q % 4] = parts[q % 4] + term
    return block_transpose((parts[0] + parts[1]) + (parts[2] + parts[3]))


def evaluate_kernel(
    pair_ref, packed, placed, totals, high_table, low_table, signs, down_inverse, far, targets,
    eval_kernels, densities,
):
    pair = pair_ref[0]
    half = totals.shape[0] // ROWS
    rows = half // 2
    for ch in range(3):
        mine = placed[pl.ds(pl.multiple_of(ch * half + pair * rows, 8), rows), :]
        flipped = mine.T
        for r in range(rows):
            for h in range(2):
                start = ((2 * r + h) * 3 + ch) * BCAP
                targets[pl.ds(start, BCAP), :] = jnp.broadcast_to(
                    flipped[h * BCAP : (h + 1) * BCAP, r : r + 1], (BCAP, LANES)
                )
    far[...] = evaluate(
        pair, packed, totals, high_table, low_table, signs, down_inverse, eval_kernels, densities
    )


def near_kernel(
    near_source, pair_ref, owner_ref, swapped, placed, passed, targets, far, counts, decay_rate,
    stress, potential, new_stress, table, merged, sums,
):
    entries, leaves = near_source.shape
    half = leaves // 2
    pair = pair_ref[0]
    low = iota((half, LANES), 1) < BCAP
    swapped_from = jnp.where(((owner_ref[0] & 1) ^ pair) == 1, 0, 2)
    for n, rows_of in ((swapped_from, swapped), (1, placed), (2 - swapped_from, passed)):
        first = n * (leaves * 8)
        for ch in range(4):
            rows = rows_of[ch * half : (ch + 1) * half, :]
            turned = pltpu.roll(rows, BCAP, 1)
            table[pl.ds(first + ch, half, stride=16), :] = jnp.where(low, rows, turned)
            table[pl.ds(first + 8 + ch, half, stride=16), :] = jnp.where(low, turned, rows)
    low = iota((8, LANES), 1) < BCAP

    def merge(t, carry):
        leaf = pair * half + t
        for n in range(entries // 2):
            left = pl.multiple_of(near_source[2 * n, leaf] * 8, 8)
            right = pl.multiple_of(near_source[2 * n + 1, leaf] * 8, 8)
            start = pl.multiple_of((t * (entries // 2) + n) * 8, 8)
            merged[pl.ds(start, 8), :] = jnp.where(
                low, table[pl.ds(left, 8), :], table[pl.ds(right, 8), :]
            )
        return carry

    lax.fori_loop(0, half, merge, 0, unroll=4)

    def one_leaf(t, carry):
        start = pl.multiple_of(t * 3 * BCAP, 8)
        tx, ty, tz = [targets[pl.ds(start + ch * BCAP, BCAP), :] for ch in range(3)]
        total = jnp.zeros((BCAP, LANES), jnp.float32)
        for n in range(entries // 2):
            first = pl.multiple_of((t * (entries // 2) + n) * 8, 8)
            sx, sy, sz, weight = [merged[pl.ds(first + ch, 1), :] for ch in range(4)]
            gx, gy, gz = tx - sx, ty - sy, tz - sz
            squared = gx * gx + gy * gy + (gz * gz + softening)
            total = total + lax.rsqrt(squared) * weight
        sums[pl.ds(pl.multiple_of(t * BCAP, 8), BCAP), :] = total
        return carry

    lax.fori_loop(0, half, one_leaf, 0, unroll=4)
    rows = half // 2
    for r in range(rows):
        block = sums[r * LANES : (r + 1) * LANES, :].T
        potential[r : r + 1, :] = jnp.sum(block, axis=0, keepdims=True)
    combined = potential[...] + far[...]
    beads = per_leaf(counts[...].astype(jnp.float32), rows, pair * half)
    slot = iota((rows, LANES), 1) & (BCAP - 1)
    occupied = slot.astype(jnp.float32) < beads
    decay = per_leaf(decay_rate[...], rows)
    potential[...] = jnp.where(occupied, combined, 0.0)
    new_stress[...] = jnp.where(occupied, decay * stress[...] + combined, 0.0)


VMEM = pl.BlockSpec(memory_space=pltpu.VMEM)
SMEM = pl.BlockSpec(memory_space=pltpu.SMEM)
ANY = pl.BlockSpec(memory_space=pl.ANY)
MIB = 1024 * 1024


def call(kernel, outs, in_specs, scratch=(), limit=40, grid=(), flops=0, bytes_accessed=0):
    return pl.pallas_call(
        kernel,
        out_shape=outs,
        grid=grid,
        in_specs=in_specs,
        out_specs=jax.tree.map(lambda _: VMEM, outs),
        scratch_shapes=list(scratch),
        compiler_params=pltpu.CompilerParams(vmem_limit_bytes=limit * MIB),
        cost_estimate=pl.CostEstimate(
            flops=flops, bytes_accessed=bytes_accessed, transcendentals=0
        ),
    )


def body(
    offsets,
    charges,
    stress,
    decay_rate,
    morton_keys,
    levels,
    bead_counts,
    send_boxes,
    m2l_source,
    m2l_type,
    m2l_count,
    near_source,
    up_inverse,
    down_inverse,
    translations,
):
    f32 = jnp.float32
    leaves = morton_keys.shape[0]
    half = leaves // 2
    parts = lax.axis_size("wide") * lax.axis_size("narrow")
    table = jnp.asarray(transform_table())
    signs = jnp.asarray(sign_rows())
    pair = lax.axis_index("pair").reshape(1)
    owner = (
        lax.axis_index("wide") * lax.axis_size("narrow") + lax.axis_index("narrow")
    ).reshape(1)
    kind_count = translations.shape[0]

    other_translations = lax.ppermute(translations, "pair", [(0, 1), (1, 0)])
    packed, blocks, placed, sources, kinds = call(
        functools.partial(pack_kernel, kind_count),
        [
            jax.ShapeDtypeStruct((4 * half + 8, LANES), f32),
            jax.ShapeDtypeStruct((8 * parts, LANES), f32),
            jax.ShapeDtypeStruct((4 * half, LANES), f32),
            jax.ShapeDtypeStruct(m2l_source.shape, jnp.int32),
            jax.ShapeDtypeStruct(m2l_type.shape, jnp.int32),
        ],
        [VMEM] * 9,
        limit=62,
    )(
        offsets, charges.reshape(half, LANES), morton_keys.reshape(1, leaves),
        levels.reshape(1, leaves), bead_counts.reshape(1, leaves), send_boxes,
        m2l_source, m2l_type, m2l_count.reshape(1, leaves),
    )
    arrived = lax.all_to_all(
        blocks.reshape(parts, 8, LANES), PARTS, split_axis=0, concat_axis=0, tiled=True
    ).reshape(8 * parts, LANES)
    swaps = [(2 * d, 2 * (d ^ 1)) for d in range(parts)]
    for d in range(1, parts - 1, 2):
        swaps += [(2 * d + 1, 2 * d + 3), (2 * d + 3, 2 * d + 1)]
    swapped = lax.ppermute(placed, PARTS + ("pair",), swaps)
    own_check = call(
        own_kernel,
        jax.ShapeDtypeStruct((Q, leaves // 16 * LANES), f32),
        [VMEM],
        [pltpu.VMEM((leaves // 16, Q * 8, LANES), f32)],
        flops=4 * 10**10,
    )(packed)
    passed = lax.ppermute(swapped, "pair", [(0, 1), (1, 0)])

    last = pl.BlockSpec((kind_count, 2, LANES), lambda i: (0, 0, TILES - 1))
    totals, low_table = call(
        far_kernel,
        [
            jax.ShapeDtypeStruct((half * ROWS, LANES), f32),
            jax.ShapeDtypeStruct(table.shape, table.dtype),
        ],
        [SMEM] * 3 + [VMEM] * 4 + [last] * 2 + [ANY] * 3,
        [
            pltpu.VMEM(((leaves + 2 * parts) * ROWS, LANES), f32),
            pltpu.VMEM((kind_count + 1, ROWS, LANES), f32),
            pltpu.VMEM(table.shape, jnp.bfloat16),
            pltpu.VMEM((leaves + 2 * parts, QPAD), f32),
            pltpu.VMEM(((leaves + 2 * parts) // 16, Q, LANES), f32),
            pltpu.VMEM((Q * 8, LANES), f32),
            pltpu.SemaphoreType.DMA((2 * TILES + 1,)),
        ],
        grid=(1,),
        flops=10**10,
        bytes_accessed=4 * 10**6,
    )(
        sources, kinds, pair, arrived, own_check, up_inverse, signs, translations,
        other_translations, table, translations, other_translations,
    )

    out = jax.ShapeDtypeStruct((half // 2, LANES), f32)
    far, targets = call(
        evaluate_kernel,
        [out, jax.ShapeDtypeStruct((half * 3 * BCAP, LANES), f32)],
        [SMEM] + [VMEM] * 7,
        [pltpu.VMEM((Q * 8, LANES), f32), pltpu.VMEM((Q, LANES), f32)],
        flops=10**10,
    )(pair, packed, placed, totals, table, low_table, signs, down_inverse)
    potential, new_stress = call(
        near_kernel,
        [out, out],
        [SMEM] * 3 + [VMEM] * 8,
        [
            pltpu.VMEM((3 * leaves * 8, LANES), f32),
            pltpu.VMEM((half * near_source.shape[1] // 2 * 8, LANES), f32),
            pltpu.VMEM((half * BCAP, LANES), f32),
        ],
    )(
        near_source.T, pair, owner, swapped, placed, passed, targets, far,
        bead_counts.reshape(1, leaves), decay_rate.reshape(1, half),
        stress.reshape(half // 2, LANES),
    )
    return potential.reshape(-1), new_stress.reshape(-1)


def solution(mesh):
    return jax.shard_map(
        body,
        mesh=mesh,
        in_specs=(
            P(None, ("groups", "wide", "narrow")),
            P(("groups", "wide", "narrow")),
            P(("groups", "wide", "narrow", "pair")),
            P(("groups", "wide", "narrow", "pair")),
            P(("groups", "wide", "narrow")),
            P(("groups", "wide", "narrow")),
            P(("groups", "wide", "narrow")),
            P(("groups", "wide", "narrow"), None),
            P(("groups", "wide", "narrow"), None),
            P(("groups", "wide", "narrow"), None),
            P(("groups", "wide", "narrow")),
            P(("groups", "wide", "narrow"), None),
            P(),
            P(),
            P(None, None, "pair"),
        ),
        out_specs=(
            P(("groups", "wide", "narrow", "pair")),
            P(("groups", "wide", "narrow", "pair")),
        ),
        check_vma=False,
    )
```

```python
import functools

import jax
import jax.numpy as jnp
import ml_dtypes
import numpy as np
from jax import lax
from jax.experimental import pallas as pl
from jax.experimental.pallas import tpu as pltpu
from jax.sharding import PartitionSpec as P

PGRID = 12
G = 1728
MAXL = 10
BCAP = 64
Q = 152
QPAD = 160
LANES = 128
BINS = 864
TILES = 7
ROWS = 32
softening = 0.04
surface_reach = 1.25
CELLS = [
    (i, j, k)
    for i in range(6)
    for j in range(6)
    for k in range(6)
    if 0 in (i, j, k) or 5 in (i, j, k)
]
PARTS = ("wide", "narrow")


def transform_table():
    cells = np.array(CELLS)
    bins = np.arange(BINS)
    freq = np.stack([bins // 144, bins // 12 % 12, bins % 12])
    angle = (cells @ freq % PGRID) * (2.0 * np.pi / PGRID)
    table = np.zeros((QPAD, 2 * TILES * LANES))
    table[:Q, :BINS] = np.cos(angle)
    table[:Q, TILES * LANES : TILES * LANES + BINS] = -np.sin(angle)
    table[np.abs(table) < 1e-9] = 0.0
    return table.astype(ml_dtypes.bfloat16)


def low_part(high):
    root = np.sqrt(0.75)
    held = float(np.asarray(root).astype(ml_dtypes.bfloat16))
    scale = (root - held) / (held * (held * held - 1.0) * (held * held - 0.25))
    value = high.astype(jnp.float32)
    square = value * value
    return (value * (square - 1.0) * (square - 0.25) * scale).astype(jnp.bfloat16)


def sign_rows():
    rows = np.zeros((8, QPAD), np.float32)
    rows[0, :Q] = 1.0
    rows[1, :Q] = [(-1.0) ** i for i, _, _ in CELLS]
    return rows


def iota(shape, dim):
    return lax.broadcasted_iota(jnp.int32, shape, dim)


def per_leaf(values, count, first=0):
    shape = (count, values.shape[1])
    leaf, lane = first + 2 * iota(shape, 0), iota(shape, 1)
    even = jnp.sum(jnp.where(lane == leaf, values, 0.0), axis=1, keepdims=True)
    odd = jnp.sum(jnp.where(lane == leaf + 1, values, 0.0), axis=1, keepdims=True)
    return jnp.where(iota((count, LANES), 1) < BCAP, even, odd)


def block_transpose(x):
    lane, row = iota(x.shape, 1), iota(x.shape, 0)
    for k in (1, 2, 4):
        row_bit, lane_bit = (row & k) != 0, (lane & k) != 0
        below = pltpu.roll(pltpu.roll(x, 8 - k, 0), k, 1)
        above = pltpu.roll(pltpu.roll(x, k, 0), LANES - k, 1)
        x = jnp.where(row_bit == lane_bit, x, jnp.where(lane_bit, below, above))
    return x


def split(x):
    high = x.astype(jnp.bfloat16)
    return high, (x - high.astype(jnp.float32)).astype(jnp.bfloat16)


def product(a, b, contract):
    dims = (((contract[0],), (contract[1],)), ((), ()))
    (a_high, a_low), (b_high, b_low) = split(a), split(b)

    def dot(x, y):
        return lax.dot_general(x, y, dims, preferred_element_type=jnp.float32)

    return dot(a_high, b_high) + (dot(a_low, b_high) + dot(a_high, b_low))


def axis_squares(offset, width):
    area = width * width
    planes = [surface_reach * 0.5 * (i - 2.5) / 2.5 for i in range(6)]
    return [(plane - offset) * (plane - offset) * area for plane in planes]


def surface_kernels(offsets, width):
    gx, gy, gz = [axis_squares(offset, width) for offset in offsets]
    gz = [g + softening for g in gz]
    last, gxy = None, None
    for q, (i, j, k) in enumerate(CELLS):
        if last != (i, j):
            last, gxy = (i, j), gx[i] + gy[j]
        yield q, lax.rsqrt(gxy + gz[k])


def check_sums(offsets, weights, width, checks):
    offsets = [block_transpose(x) for x in offsets]
    weights, width = block_transpose(weights), block_transpose(width)
    for q, kernel in surface_kernels(offsets, width):
        checks[pl.ds(8 * q, 8), :] = kernel * weights
    check = checks[pl.ds(0, Q, stride=8), :]
    for s in range(1, 8):
        check = check + checks[pl.ds(s, Q, stride=8), :]
    return check


def upward(check, up_inverse):
    density = product(check, up_inverse, (0, 0))
    blocks = check.shape[1] // LANES
    density = density.reshape(2 * blocks, 8, 8, Q)
    total = density[:, 0]
    for g in range(1, 8):
        total = total + density[:, g]
    return total.reshape(16 * blocks, Q)


def store_spectra(density, table_high, table_low, target):
    count = density.shape[0] // 2
    high, low = split(density)
    both = jnp.concatenate([high, low], 0)
    for first in range(0, 2 * TILES, 2):
        columns = pl.ds(first * LANES, 2 * LANES)
        part = jnp.dot(both, table_high[:, columns], preferred_element_type=jnp.float32)
        spectra = part[: 2 * count] + part[2 * count :] + jnp.dot(
            high, table_low[:, columns], preferred_element_type=jnp.float32
        )
        for tile in range(first, first + 2):
            for side in range(2):
                for block in range(count // 16):
                    for h in range(2):
                        row = side * count + block * 16 + h * 8
                        start = (block * 16 + h) * ROWS + 16 * side + 8 * (tile // TILES) + tile % TILES
                        target[pl.ds(start, 8, stride=2 * ROWS), :] = spectra[
                            row : row + 8, (tile - first) * LANES : (tile - first + 1) * LANES
                        ]


def pack_kernel(
    kind_count, offsets, charges, keys, levels, counts, send_boxes, m2l_source, m2l_type, m2l_count,
    out, blocks, placed, sources, kinds,
):
    leaves = keys.shape[1]
    half = leaves // 2
    out[4 * half :, :] = jnp.zeros((8, LANES), jnp.float32)
    width = jnp.left_shift(jnp.ones_like(levels[...]), MAXL - levels[...]).astype(jnp.float32)
    for a in range(3):
        summed = jnp.zeros_like(keys[...])
        for bit in range(MAXL):
            summed = summed + (jnp.right_shift(keys[...], 3 * bit + a) & 1) * (1 << bit)
        out[4 * half + a : 4 * half + a + 1, :leaves] = summed.astype(jnp.float32) + 0.5 * width
    out[4 * half + 3 : 4 * half + 4, :leaves] = width
    for r in range(half):
        out[pl.ds(r, 3, stride=half), :] = offsets[:, r * LANES : (r + 1) * LANES]
    beads = per_leaf(counts[...].astype(jnp.float32), half)
    slot = iota((half, LANES), 1) & (BCAP - 1)
    out[3 * half : 4 * half, :] = jnp.where(slot.astype(jnp.float32) < beads, charges[...], 0.0)

    entry = iota(m2l_type.shape, 1)
    square = (leaves, leaves)
    live = jnp.sum(
        jnp.where(iota(square, 0) == iota(square, 1), m2l_count[...].astype(jnp.float32), 0.0),
        axis=1, keepdims=True,
    )
    kinds[...] = jnp.where(entry.astype(jnp.float32) < live, m2l_type[...], kind_count)
    sources[...] = m2l_source[...] * ROWS

    spread = per_leaf(width, half)
    for ch in range(3):
        center = per_leaf(out[4 * half + ch : 4 * half + ch + 1, :leaves], half)
        placed[ch * half : (ch + 1) * half, :] = center + spread * out[ch * half : (ch + 1) * half, :]
    placed[3 * half :, :] = out[3 * half : 4 * half, :]

    sends = send_boxes.shape[1]
    lane = iota((8, LANES), 1)
    for block in range(sends // 16):
        picked = []
        for c in range(2):
            column = block * 16 + 2 * iota((8, sends), 0) + c
            box = jnp.sum(
                jnp.where(iota((8, sends), 1) == column, send_boxes[...].astype(jnp.float32), 0.0),
                axis=1, keepdims=True,
            ).astype(jnp.int32)
            width_here = jnp.sum(
                jnp.where(iota((8, leaves), 1) == box, width, 0.0), axis=1, keepdims=True
            )
            row_of = jnp.broadcast_to(box >> 1, (8, LANES))
            found = [jnp.zeros((8, LANES), jnp.float32)] * 4
            for r in range(half):
                here = row_of == r
                for ch in range(4):
                    found[ch] = jnp.where(here, out[ch * half + r : ch * half + r + 1, :], found[ch])
            aligned = jnp.broadcast_to((box & 1) == c, (8, LANES))
            found = [jnp.where(aligned, x, pltpu.roll(x, BCAP, 1)) for x in found]
            picked.append(found + [jnp.broadcast_to(width_here, (8, LANES))])
        for ch in range(5):
            blocks[pl.ds(block * 64 + ch, 8, stride=8), :] = jnp.where(
                lane < BCAP, picked[0][ch], picked[1][ch]
            )
        for ch in range(5, 8):
            blocks[pl.ds(block * 64 + ch, 8, stride=8), :] = jnp.zeros((8, LANES), jnp.float32)


def own_kernel(packed, out, checks):
    half = (packed.shape[0] - 8) // 4
    width = per_leaf(packed[4 * half + 3 : 4 * half + 4, :], half)
    for block in range(half // 8):
        rows = [packed[c * half + block * 8 : c * half + block * 8 + 8, :] for c in range(4)]
        out[:, block * LANES : (block + 1) * LANES] = check_sums(
            rows[:3], rows[3], width[block * 8 : block * 8 + 8], checks.at[block]
        )


def far_kernel(
    sources, kinds, pair_ref, arrived, own_check, up_inverse, signs,
    last_bins, other_last_bins, table, translations, other_translations, totals, low_table,
    spectra, kernels, high_table, density, check, checks, sems,
):
    leaves, entries = sources.shape
    half = leaves // 2
    blocks = arrived.shape[0] // 64
    kind_count = translations.shape[0]
    pair = pair_ref[0]

    table_copy = pltpu.make_async_copy(table, high_table, sems.at[0])
    table_copy.start()
    kernel_copies = []
    for side, bins in enumerate((translations, other_translations)):
        for t in range(TILES - 1):
            kernel_copies.append(pltpu.make_async_copy(
                bins.at[:, :, pl.ds(t * LANES, LANES)],
                kernels.at[pl.ds(0, kind_count), pl.ds(16 * side + 2 * t, 2), :],
                sems.at[1 + len(kernel_copies)],
            ))
        kernel_copies.append(pltpu.make_async_copy(
            (last_bins, other_last_bins)[side],
            kernels.at[pl.ds(0, kind_count), pl.ds(16 * side + 2 * TILES - 2, 2), :],
            sems.at[1 + len(kernel_copies)],
        ))
    for copy in kernel_copies:
        copy.start()
    kernels[kind_count] = jnp.zeros((ROWS, LANES), jnp.float32)

    density[...] = jnp.zeros(density.shape, jnp.float32)
    check[0, :, :] = own_check[:, :LANES]
    check[1, :, :] = own_check[:, LANES:]

    def arrive(block, carry):
        beads = [
            arrived[pl.ds(pl.multiple_of(block * 64, 64) + ch, 8, stride=8), :] for ch in range(5)
        ]
        check[leaves // 16 + block, :, :] = check_sums(beads[:3], beads[3], beads[4], checks)
        return carry

    if blocks == 1:
        arrive(0, 0)
    else:
        lax.fori_loop(0, blocks, arrive, 0)
    count = check.shape[0]
    for first in range(0, count, 3):
        some = range(first, min(first + 3, count))
        density[16 * first : 16 * first + 16 * len(some), :Q] = upward(
            jnp.concatenate([check[n] for n in some], 1), up_inverse[...]
        )
    table_copy.wait()
    low_table[...] = low_part(high_table[...])
    sign = jnp.where(pair == 1, signs[1:2, :], signs[0:1, :])
    other_sign = jnp.where(pair == 1, signs[0:1, :], signs[1:2, :])
    store_spectra(
        jnp.concatenate([density[...] * sign, density[...] * other_sign], 0),
        high_table, low_table, spectra,
    )
    for copy in kernel_copies:
        copy.wait()

    def translate(t, carry):
        leaf = pair * half + t
        sums = [[None] * 4, [None] * 4]
        for entry in range(entries):
            kind = kinds[leaf, entry]
            start = pl.multiple_of(sources[leaf, entry], ROWS)
            for side in range(2):
                k_re = kernels[kind, pl.ds(16 * side, 8, stride=2), :]
                k_im = kernels[kind, pl.ds(16 * side + 1, 8, stride=2), :]
                s_re = spectra[pl.ds(start + 16 * side, 8), :]
                s_im = spectra[pl.ds(start + 16 * side + 8, 8), :]
                terms = (k_re * s_re, k_im * s_im, k_re * s_im, k_im * s_re)
                for n, term in enumerate(terms):
                    sums[side][n] = term if sums[side][n] is None else sums[side][n] + term
        start = pl.multiple_of(t * ROWS, ROWS)
        for side in range(2):
            rr, ii, ri, ir = sums[side]
            totals[pl.ds(start + 16 * side, 8), :] = rr - ii
            totals[pl.ds(start + 16 * side + 8, 8), :] = ri + ir
        return carry

    lax.fori_loop(0, half, translate, 0, unroll=4)


def evaluate(
    pair, packed, totals, table, low_table, signs, down_inverse, eval_kernels, densities
):
    half = (packed.shape[0] - 8) // 4
    leaves = 2 * half
    rows = half // 2
    width = block_transpose(
        per_leaf(packed[4 * half + 3 : 4 * half + 4, :], rows, pair * half)
    )
    offsets = [
        block_transpose(packed[pl.ds(pl.multiple_of(c * half + pair * rows, 8), rows), :])
        for c in range(3)
    ]
    for q, kernel in surface_kernels(offsets, width):
        eval_kernels[pl.ds(8 * q, 8), :] = kernel
    sign = jnp.where(pair == 1, signs[1:2, :], signs[0:1, :])
    other_sign = jnp.where(pair == 1, signs[0:1, :], signs[1:2, :])
    lane = iota((half, LANES), 1)
    sides = []
    for side in range(2):
        columns = []
        for c in range(2):
            for t in range(TILES):
                line = totals[pl.ds(16 * side + c * 8 + t, half, stride=ROWS), :]
                if t == TILES - 1:
                    line = jnp.where(lane < BINS - t * LANES, line, 0.0)
                columns.append(line)
        sides.append(jnp.concatenate(columns, 1))
    high, low = split(jnp.concatenate(sides, 0))
    across = (((1,), (1,)), ((), ()))
    both = lax.dot_general(
        jnp.concatenate([high, low], 0), table[...], across,
        preferred_element_type=jnp.float32,
    )
    check = both[:leaves] + both[leaves:] + lax.dot_general(
        high, low_table[...], across, preferred_element_type=jnp.float32
    )
    check = (check[:half] * sign + check[half:] * other_sign)[:, :Q] * (1.0 / G)

    leaf_of = 2 * (lane & 7) + (lane >> 6)
    spread = jnp.where(iota((half, LANES), 0) == leaf_of, 1.0, 0.0)
    densities[...] = product(product(check, down_inverse[...], (1, 0)), spread, (0, 0))
    parts = [jnp.zeros((rows, LANES), jnp.float32)] * 4
    for q in range(Q):
        term = eval_kernels[8 * q : 8 * q + 8, :] * densities[q : q + 1, :]
        parts[q % 4] = parts[q % 4] + term
    return block_transpose((parts[0] + parts[1]) + (parts[2] + parts[3]))


def relay_kernel(beads, totals, out):
    out[...] = beads[...]


def evaluate_kernel(
    pair_ref, packed, placed, totals, high_table, low_table, signs, down_inverse, far, targets,
    eval_kernels, densities,
):
    pair = pair_ref[0]
    half = totals.shape[0] // ROWS
    rows = half // 2
    for ch in range(3):
        mine = placed[pl.ds(pl.multiple_of(ch * half + pair * rows, 8), rows), :]
        flipped = mine.T
        for r in range(rows):
            for h in range(2):
                start = ((2 * r + h) * 3 + ch) * BCAP
                targets[pl.ds(start, BCAP), :] = jnp.broadcast_to(
                    flipped[h * BCAP : (h + 1) * BCAP, r : r + 1], (BCAP, LANES)
                )
    far[...] = evaluate(
        pair, packed, totals, high_table, low_table, signs, down_inverse, eval_kernels, densities
    )


def near_kernel(
    near_source, pair_ref, owner_ref, swapped, placed, passed, targets, far, counts, decay_rate,
    stress, potential, new_stress, table, merged, sums,
):
    entries, leaves = near_source.shape
    half = leaves // 2
    pair = pair_ref[0]
    low = iota((half, LANES), 1) < BCAP
    swapped_from = jnp.where(((owner_ref[0] & 1) ^ pair) == 1, 0, 2)
    for n, rows_of in ((swapped_from, swapped), (1, placed), (2 - swapped_from, passed)):
        first = n * (leaves * 8)
        for ch in range(4):
            rows = rows_of[ch * half : (ch + 1) * half, :]
            turned = pltpu.roll(rows, BCAP, 1)
            table[pl.ds(first + ch, half, stride=16), :] = jnp.where(low, rows, turned)
            table[pl.ds(first + 8 + ch, half, stride=16), :] = jnp.where(low, turned, rows)
    low = iota((8, LANES), 1) < BCAP

    def merge(t, carry):
        leaf = pair * half + t
        for n in range(entries // 2):
            left = pl.multiple_of(near_source[2 * n, leaf] * 8, 8)
            right = pl.multiple_of(near_source[2 * n + 1, leaf] * 8, 8)
            start = pl.multiple_of((t * (entries // 2) + n) * 8, 8)
            merged[pl.ds(start, 8), :] = jnp.where(
                low, table[pl.ds(left, 8), :], table[pl.ds(right, 8), :]
            )
        return carry

    lax.fori_loop(0, half, merge, 0, unroll=4)

    def one_leaf(t, carry):
        start = pl.multiple_of(t * 3 * BCAP, 8)
        tx, ty, tz = [targets[pl.ds(start + ch * BCAP, BCAP), :] for ch in range(3)]
        total = jnp.zeros((BCAP, LANES), jnp.float32)
        for n in range(entries // 2):
            first = pl.multiple_of((t * (entries // 2) + n) * 8, 8)
            sx, sy, sz, weight = [merged[pl.ds(first + ch, 1), :] for ch in range(4)]
            gx, gy, gz = tx - sx, ty - sy, tz - sz
            squared = gx * gx + gy * gy + (gz * gz + softening)
            total = total + lax.rsqrt(squared) * weight
        sums[pl.ds(pl.multiple_of(t * BCAP, 8), BCAP), :] = total
        return carry

    lax.fori_loop(0, half, one_leaf, 0, unroll=4)
    rows = half // 2
    for r in range(rows):
        block = sums[r * LANES : (r + 1) * LANES, :].T
        potential[r : r + 1, :] = jnp.sum(block, axis=0, keepdims=True)
    combined = potential[...] + far[...]
    beads = per_leaf(counts[...].astype(jnp.float32), rows, pair * half)
    slot = iota((rows, LANES), 1) & (BCAP - 1)
    occupied = slot.astype(jnp.float32) < beads
    decay = per_leaf(decay_rate[...], rows)
    potential[...] = jnp.where(occupied, combined, 0.0)
    new_stress[...] = jnp.where(occupied, decay * stress[...] + combined, 0.0)


VMEM = pl.BlockSpec(memory_space=pltpu.VMEM)
SMEM = pl.BlockSpec(memory_space=pltpu.SMEM)
ANY = pl.BlockSpec(memory_space=pl.ANY)
MIB = 1024 * 1024


def call(kernel, outs, in_specs, scratch=(), limit=40, grid=(), flops=0, bytes_accessed=0):
    return pl.pallas_call(
        kernel,
        out_shape=outs,
        grid=grid,
        in_specs=in_specs,
        out_specs=jax.tree.map(lambda _: VMEM, outs),
        scratch_shapes=list(scratch),
        compiler_params=pltpu.CompilerParams(vmem_limit_bytes=limit * MIB),
        cost_estimate=pl.CostEstimate(
            flops=flops, bytes_accessed=bytes_accessed, transcendentals=0
        ),
    )


def body(
    offsets,
    charges,
    stress,
    decay_rate,
    morton_keys,
    levels,
    bead_counts,
    send_boxes,
    m2l_source,
    m2l_type,
    m2l_count,
    near_source,
    up_inverse,
    down_inverse,
    translations,
):
    f32 = jnp.float32
    leaves = morton_keys.shape[0]
    half = leaves // 2
    parts = lax.axis_size("wide") * lax.axis_size("narrow")
    table = jnp.asarray(transform_table())
    signs = jnp.asarray(sign_rows())
    pair = lax.axis_index("pair").reshape(1)
    owner = (
        lax.axis_index("wide") * lax.axis_size("narrow") + lax.axis_index("narrow")
    ).reshape(1)
    kind_count = translations.shape[0]

    other_translations = lax.ppermute(translations, "pair", [(0, 1), (1, 0)])
    packed, blocks, placed, sources, kinds = call(
        functools.partial(pack_kernel, kind_count),
        [
            jax.ShapeDtypeStruct((4 * half + 8, LANES), f32),
            jax.ShapeDtypeStruct((8 * parts, LANES), f32),
            jax.ShapeDtypeStruct((4 * half, LANES), f32),
            jax.ShapeDtypeStruct(m2l_source.shape, jnp.int32),
            jax.ShapeDtypeStruct(m2l_type.shape, jnp.int32),
        ],
        [VMEM] * 9,
        limit=62,
    )(
        offsets, charges.reshape(half, LANES), morton_keys.reshape(1, leaves),
        levels.reshape(1, leaves), bead_counts.reshape(1, leaves), send_boxes,
        m2l_source, m2l_type, m2l_count.reshape(1, leaves),
    )
    arrived = lax.all_to_all(
        blocks.reshape(parts, 8, LANES), PARTS, split_axis=0, concat_axis=0, tiled=True
    ).reshape(8 * parts, LANES)
    swaps = [(2 * d, 2 * (d ^ 1)) for d in range(parts)]
    for d in range(1, parts - 1, 2):
        swaps += [(2 * d + 1, 2 * d + 3), (2 * d + 3, 2 * d + 1)]
    swapped = lax.ppermute(placed, PARTS + ("pair",), swaps)
    own_check = call(
        own_kernel,
        jax.ShapeDtypeStruct((Q, leaves // 16 * LANES), f32),
        [VMEM],
        [pltpu.VMEM((leaves // 16, Q * 8, LANES), f32)],
        flops=4 * 10**10,
    )(packed)

    last = pl.BlockSpec((kind_count, 2, LANES), lambda i: (0, 0, TILES - 1))
    totals, low_table = call(
        far_kernel,
        [
            jax.ShapeDtypeStruct((half * ROWS, LANES), f32),
            jax.ShapeDtypeStruct(table.shape, table.dtype),
        ],
        [SMEM] * 3 + [VMEM] * 4 + [last] * 2 + [ANY] * 3,
        [
            pltpu.VMEM(((leaves + 2 * parts) * ROWS, LANES), f32),
            pltpu.VMEM((kind_count + 1, ROWS, LANES), f32),
            pltpu.VMEM(table.shape, jnp.bfloat16),
            pltpu.VMEM((leaves + 2 * parts, QPAD), f32),
            pltpu.VMEM(((leaves + 2 * parts) // 16, Q, LANES), f32),
            pltpu.VMEM((Q * 8, LANES), f32),
            pltpu.SemaphoreType.DMA((2 * TILES + 1,)),
        ],
        grid=(1,),
        flops=10**10,
        bytes_accessed=4 * 10**6,
    )(
        sources, kinds, pair, arrived, own_check, up_inverse, signs, translations,
        other_translations, table, translations, other_translations,
    )

    relayed = call(
        relay_kernel, jax.ShapeDtypeStruct(swapped.shape, f32), [VMEM, ANY]
    )(swapped, totals)
    passed = lax.ppermute(relayed, "pair", [(0, 1), (1, 0)])

    out = jax.ShapeDtypeStruct((half // 2, LANES), f32)
    far, targets = call(
        evaluate_kernel,
        [out, jax.ShapeDtypeStruct((half * 3 * BCAP, LANES), f32)],
        [SMEM] + [VMEM] * 7,
        [pltpu.VMEM((Q * 8, LANES), f32), pltpu.VMEM((Q, LANES), f32)],
        flops=10**10,
    )(pair, packed, placed, totals, table, low_table, signs, down_inverse)
    potential, new_stress = call(
        near_kernel,
        [out, out],
        [SMEM] * 3 + [VMEM] * 8,
        [
            pltpu.VMEM((3 * leaves * 8, LANES), f32),
            pltpu.VMEM((half * near_source.shape[1] // 2 * 8, LANES), f32),
            pltpu.VMEM((half * BCAP, LANES), f32),
        ],
    )(
        near_source.T, pair, owner, swapped, placed, passed, targets, far,
        bead_counts.reshape(1, leaves), decay_rate.reshape(1, half),
        stress.reshape(half // 2, LANES),
    )
    return potential.reshape(-1), new_stress.reshape(-1)


def solution(mesh):
    return jax.shard_map(
        body,
        mesh=mesh,
        in_specs=(
            P(None, ("groups", "wide", "narrow")),
            P(("groups", "wide", "narrow")),
            P(("groups", "wide", "narrow", "pair")),
            P(("groups", "wide", "narrow", "pair")),
            P(("groups", "wide", "narrow")),
            P(("groups", "wide", "narrow")),
            P(("groups", "wide", "narrow")),
            P(("groups", "wide", "narrow"), None),
            P(("groups", "wide", "narrow"), None),
            P(("groups", "wide", "narrow"), None),
            P(("groups", "wide", "narrow")),
            P(("groups", "wide", "narrow"), None),
            P(),
            P(),
            P(None, None, "pair"),
        ),
        out_specs=(
            P(("groups", "wide", "narrow", "pair")),
            P(("groups", "wide", "narrow", "pair")),
        ),
        check_vma=False,
    )
```

```python
import functools

import jax
import jax.numpy as jnp
import ml_dtypes
import numpy as np
from jax import lax
from jax.experimental import pallas as pl
from jax.experimental.pallas import tpu as pltpu
from jax.sharding import PartitionSpec as P

PGRID = 12
G = 1728
MAXL = 10
BCAP = 64
Q = 152
QPAD = 160
LANES = 128
BINS = 864
TILES = 7
ROWS = 32
softening = 0.04
surface_reach = 1.25
CELLS = [
    (i, j, k)
    for i in range(6)
    for j in range(6)
    for k in range(6)
    if 0 in (i, j, k) or 5 in (i, j, k)
]
PARTS = ("wide", "narrow")


def transform_table():
    cells = np.array(CELLS)
    bins = np.arange(BINS)
    freq = np.stack([bins // 144, bins // 12 % 12, bins % 12])
    angle = (cells @ freq % PGRID) * (2.0 * np.pi / PGRID)
    table = np.zeros((QPAD, 2 * TILES * LANES))
    table[:Q, :BINS] = np.cos(angle)
    table[:Q, TILES * LANES : TILES * LANES + BINS] = -np.sin(angle)
    table[np.abs(table) < 1e-9] = 0.0
    return table.astype(ml_dtypes.bfloat16)


def low_part(high):
    root = np.sqrt(0.75)
    held = float(np.asarray(root).astype(ml_dtypes.bfloat16))
    scale = (root - held) / (held * (held * held - 1.0) * (held * held - 0.25))
    value = high.astype(jnp.float32)
    square = value * value
    return (value * (square - 1.0) * (square - 0.25) * scale).astype(jnp.bfloat16)


def sign_rows():
    rows = np.zeros((8, QPAD), np.float32)
    rows[0, :Q] = 1.0
    rows[1, :Q] = [(-1.0) ** i for i, _, _ in CELLS]
    return rows


def iota(shape, dim):
    return lax.broadcasted_iota(jnp.int32, shape, dim)


def per_leaf(values, count, first=0):
    shape = (count, values.shape[1])
    leaf, lane = first + 2 * iota(shape, 0), iota(shape, 1)
    even = jnp.sum(jnp.where(lane == leaf, values, 0.0), axis=1, keepdims=True)
    odd = jnp.sum(jnp.where(lane == leaf + 1, values, 0.0), axis=1, keepdims=True)
    return jnp.where(iota((count, LANES), 1) < BCAP, even, odd)


def block_transpose(x):
    lane, row = iota(x.shape, 1), iota(x.shape, 0)
    for k in (1, 2, 4):
        row_bit, lane_bit = (row & k) != 0, (lane & k) != 0
        below = pltpu.roll(pltpu.roll(x, 8 - k, 0), k, 1)
        above = pltpu.roll(pltpu.roll(x, k, 0), LANES - k, 1)
        x = jnp.where(row_bit == lane_bit, x, jnp.where(lane_bit, below, above))
    return x


def split(x):
    high = x.astype(jnp.bfloat16)
    return high, (x - high.astype(jnp.float32)).astype(jnp.bfloat16)


def thirds(x):
    high = x.astype(jnp.bfloat16).astype(jnp.float32)
    rest = x - high
    middle = rest.astype(jnp.bfloat16).astype(jnp.float32)
    return high, middle, rest - middle


def product(a, b, contract):
    dims = (((contract[0],), (contract[1],)), ((), ()))
    (a_high, a_low), (b_high, b_low) = split(a), split(b)

    def dot(x, y):
        return lax.dot_general(x, y, dims, preferred_element_type=jnp.float32)

    return dot(a_high, b_high) + (dot(a_low, b_high) + dot(a_high, b_low))


def axis_squares(offset, width):
    area = width * width
    planes = [surface_reach * 0.5 * (i - 2.5) / 2.5 for i in range(6)]
    return [(plane - offset) * (plane - offset) * area for plane in planes]


def surface_kernels(offsets, width):
    gx, gy, gz = [axis_squares(offset, width) for offset in offsets]
    gz = [g + softening for g in gz]
    last, gxy = None, None
    for q, (i, j, k) in enumerate(CELLS):
        if last != (i, j):
            last, gxy = (i, j), gx[i] + gy[j]
        yield q, lax.rsqrt(gxy + gz[k])


def check_sums(offsets, weights, width, checks):
    offsets = [block_transpose(x) for x in offsets]
    weights, width = block_transpose(weights), block_transpose(width)
    for q, kernel in surface_kernels(offsets, width):
        checks[pl.ds(8 * q, 8), :] = kernel * weights
    check = checks[pl.ds(0, Q, stride=8), :]
    for s in range(1, 8):
        check = check + checks[pl.ds(s, Q, stride=8), :]
    return check


def upward(check, up_inverse):
    density = product(check, up_inverse, (0, 0))
    blocks = check.shape[1] // LANES
    density = density.reshape(2 * blocks, 8, 8, Q)
    total = density[:, 0]
    for g in range(1, 8):
        total = total + density[:, g]
    return total.reshape(16 * blocks, Q)


def store_spectra(density, table_high, table_low, target):
    count = density.shape[0] // 2
    high, low = split(density)
    both = jnp.concatenate([high, low], 0)
    for first in range(0, 2 * TILES, 2):
        columns = pl.ds(first * LANES, 2 * LANES)
        part = jnp.dot(both, table_high[:, columns], preferred_element_type=jnp.float32)
        spectra = part[: 2 * count] + part[2 * count :] + jnp.dot(
            high, table_low[:, columns], preferred_element_type=jnp.float32
        )
        for tile in range(first, first + 2):
            for side in range(2):
                for block in range(count // 16):
                    for h in range(2):
                        row = side * count + block * 16 + h * 8
                        start = (block * 16 + h) * ROWS + 16 * side + 8 * (tile // TILES) + tile % TILES
                        target[pl.ds(start, 8, stride=2 * ROWS), :] = spectra[
                            row : row + 8, (tile - first) * LANES : (tile - first + 1) * LANES
                        ]


def pack_kernel(
    kind_count, offsets, charges, keys, levels, counts, send_boxes, m2l_source, m2l_type, m2l_count,
    out, blocks, placed, sources, kinds,
):
    leaves = keys.shape[1]
    half = leaves // 2
    out[4 * half :, :] = jnp.zeros((8, LANES), jnp.float32)
    width = jnp.left_shift(jnp.ones_like(levels[...]), MAXL - levels[...]).astype(jnp.float32)
    for a in range(3):
        summed = jnp.zeros_like(keys[...])
        for bit in range(MAXL):
            summed = summed + (jnp.right_shift(keys[...], 3 * bit + a) & 1) * (1 << bit)
        out[4 * half + a : 4 * half + a + 1, :leaves] = summed.astype(jnp.float32) + 0.5 * width
    out[4 * half + 3 : 4 * half + 4, :leaves] = width
    for r in range(half):
        out[pl.ds(r, 3, stride=half), :] = offsets[:, r * LANES : (r + 1) * LANES]
    beads = per_leaf(counts[...].astype(jnp.float32), half)
    slot = iota((half, LANES), 1) & (BCAP - 1)
    out[3 * half : 4 * half, :] = jnp.where(slot.astype(jnp.float32) < beads, charges[...], 0.0)

    entry = iota(m2l_type.shape, 1)
    square = (leaves, leaves)
    live = jnp.sum(
        jnp.where(iota(square, 0) == iota(square, 1), m2l_count[...].astype(jnp.float32), 0.0),
        axis=1, keepdims=True,
    )
    kinds[...] = jnp.where(entry.astype(jnp.float32) < live, m2l_type[...], kind_count)
    sources[...] = m2l_source[...] * ROWS

    spread = per_leaf(width, half)
    for ch in range(3):
        center = per_leaf(out[4 * half + ch : 4 * half + ch + 1, :leaves], half)
        placed[ch * half : (ch + 1) * half, :] = center + spread * out[ch * half : (ch + 1) * half, :]
    placed[3 * half :, :] = out[3 * half : 4 * half, :]

    sends = send_boxes.shape[1]
    lane = iota((8, LANES), 1)
    for block in range(sends // 16):
        picked = []
        for c in range(2):
            column = block * 16 + 2 * iota((8, sends), 0) + c
            box = jnp.sum(
                jnp.where(iota((8, sends), 1) == column, send_boxes[...].astype(jnp.float32), 0.0),
                axis=1, keepdims=True,
            ).astype(jnp.int32)
            width_here = jnp.sum(
                jnp.where(iota((8, leaves), 1) == box, width, 0.0), axis=1, keepdims=True
            )
            row_of = jnp.broadcast_to(box >> 1, (8, LANES))
            found = [jnp.zeros((8, LANES), jnp.float32)] * 4
            for r in range(half):
                here = row_of == r
                for ch in range(4):
                    found[ch] = jnp.where(here, out[ch * half + r : ch * half + r + 1, :], found[ch])
            aligned = jnp.broadcast_to((box & 1) == c, (8, LANES))
            found = [jnp.where(aligned, x, pltpu.roll(x, BCAP, 1)) for x in found]
            picked.append(found + [jnp.broadcast_to(width_here, (8, LANES))])
        for ch in range(5):
            blocks[pl.ds(block * 64 + ch, 8, stride=8), :] = jnp.where(
                lane < BCAP, picked[0][ch], picked[1][ch]
            )
        for ch in range(5, 8):
            blocks[pl.ds(block * 64 + ch, 8, stride=8), :] = jnp.zeros((8, LANES), jnp.float32)


def own_kernel(packed, out, checks):
    half = (packed.shape[0] - 8) // 4
    width = per_leaf(packed[4 * half + 3 : 4 * half + 4, :], half)
    for block in range(half // 8):
        rows = [packed[c * half + block * 8 : c * half + block * 8 + 8, :] for c in range(4)]
        out[:, block * LANES : (block + 1) * LANES] = check_sums(
            rows[:3], rows[3], width[block * 8 : block * 8 + 8], checks.at[block]
        )


def far_kernel(
    sources, kinds, pair_ref, arrived, own_check, up_inverse, signs,
    last_bins, other_last_bins, table, translations, other_translations, totals, low_table,
    spectra, kernels, high_table, density, check, checks, sems,
):
    leaves, entries = sources.shape
    half = leaves // 2
    blocks = arrived.shape[0] // 64
    kind_count = translations.shape[0]
    pair = pair_ref[0]

    table_copy = pltpu.make_async_copy(table, high_table, sems.at[0])
    table_copy.start()
    kernel_copies = []
    for side, bins in enumerate((translations, other_translations)):
        for t in range(TILES - 1):
            kernel_copies.append(pltpu.make_async_copy(
                bins.at[:, :, pl.ds(t * LANES, LANES)],
                kernels.at[pl.ds(0, kind_count), pl.ds(16 * side + 2 * t, 2), :],
                sems.at[1 + len(kernel_copies)],
            ))
        kernel_copies.append(pltpu.make_async_copy(
            (last_bins, other_last_bins)[side],
            kernels.at[pl.ds(0, kind_count), pl.ds(16 * side + 2 * TILES - 2, 2), :],
            sems.at[1 + len(kernel_copies)],
        ))
    for copy in kernel_copies:
        copy.start()
    kernels[kind_count] = jnp.zeros((ROWS, LANES), jnp.float32)

    density[...] = jnp.zeros(density.shape, jnp.float32)
    check[0, :, :] = own_check[:, :LANES]
    check[1, :, :] = own_check[:, LANES:]

    def arrive(block, carry):
        beads = [
            arrived[pl.ds(pl.multiple_of(block * 64, 64) + ch, 8, stride=8), :] for ch in range(5)
        ]
        check[leaves // 16 + block, :, :] = check_sums(beads[:3], beads[3], beads[4], checks)
        return carry

    if blocks == 1:
        arrive(0, 0)
    else:
        lax.fori_loop(0, blocks, arrive, 0)
    count = check.shape[0]
    for first in range(0, count, 3):
        some = range(first, min(first + 3, count))
        density[16 * first : 16 * first + 16 * len(some), :Q] = upward(
            jnp.concatenate([check[n] for n in some], 1), up_inverse[...]
        )
    table_copy.wait()
    low_table[...] = low_part(high_table[...])
    sign = jnp.where(pair == 1, signs[1:2, :], signs[0:1, :])
    other_sign = jnp.where(pair == 1, signs[0:1, :], signs[1:2, :])
    store_spectra(
        jnp.concatenate([density[...] * sign, density[...] * other_sign], 0),
        high_table, low_table, spectra,
    )
    for copy in kernel_copies:
        copy.wait()

    def translate(t, carry):
        leaf = pair * half + t
        sums = [[None] * 4, [None] * 4]
        for entry in range(entries):
            kind = kinds[leaf, entry]
            start = pl.multiple_of(sources[leaf, entry], ROWS)
            for side in range(2):
                k_re = kernels[kind, pl.ds(16 * side, 8, stride=2), :]
                k_im = kernels[kind, pl.ds(16 * side + 1, 8, stride=2), :]
                s_re = spectra[pl.ds(start + 16 * side, 8), :]
                s_im = spectra[pl.ds(start + 16 * side + 8, 8), :]
                terms = (k_re * s_re, k_im * s_im, k_re * s_im, k_im * s_re)
                for n, term in enumerate(terms):
                    sums[side][n] = term if sums[side][n] is None else sums[side][n] + term
        start = pl.multiple_of(t * ROWS, ROWS)
        for side in range(2):
            rr, ii, ri, ir = sums[side]
            totals[pl.ds(start + 16 * side, 8), :] = rr - ii
            totals[pl.ds(start + 16 * side + 8, 8), :] = ri + ir
        return carry

    lax.fori_loop(0, half, translate, 0, unroll=8)


def evaluate(
    pair, packed, totals, table, low_table, signs, down_inverse, eval_kernels, densities
):
    half = (packed.shape[0] - 8) // 4
    leaves = 2 * half
    rows = half // 2
    width = block_transpose(
        per_leaf(packed[4 * half + 3 : 4 * half + 4, :], rows, pair * half)
    )
    offsets = [
        block_transpose(packed[pl.ds(pl.multiple_of(c * half + pair * rows, 8), rows), :])
        for c in range(3)
    ]
    for q, kernel in surface_kernels(offsets, width):
        eval_kernels[pl.ds(8 * q, 8), :] = kernel
    sign = jnp.where(pair == 1, signs[1:2, :], signs[0:1, :])
    other_sign = jnp.where(pair == 1, signs[0:1, :], signs[1:2, :])
    lane = iota((half, LANES), 1)
    sides = []
    for side in range(2):
        columns = []
        for c in range(2):
            for t in range(TILES):
                line = totals[pl.ds(16 * side + c * 8 + t, half, stride=ROWS), :]
                if t == TILES - 1:
                    line = jnp.where(lane < BINS - t * LANES, line, 0.0)
                columns.append(line)
        sides.append(jnp.concatenate(columns, 1))
    high, low = split(jnp.concatenate(sides, 0))
    across = (((1,), (1,)), ((), ()))
    both = lax.dot_general(
        jnp.concatenate([high, low], 0), table[...], across,
        preferred_element_type=jnp.float32,
    )
    check = both[:leaves] + both[leaves:] + lax.dot_general(
        high, low_table[...], across, preferred_element_type=jnp.float32
    )
    check = (check[:half] * sign + check[half:] * other_sign)[:, :Q] * (1.0 / G)

    leaf_of = 2 * (lane & 7) + (lane >> 6)
    spread = jnp.where(iota((half, LANES), 0) == leaf_of, 1.0, 0.0)
    densities[...] = product(product(check, down_inverse[...], (1, 0)), spread, (0, 0))
    parts = [jnp.zeros((rows, LANES), jnp.float32)] * 4
    for q in range(Q):
        term = eval_kernels[8 * q : 8 * q + 8, :] * densities[q : q + 1, :]
        parts[q % 4] = parts[q % 4] + term
    return block_transpose((parts[0] + parts[1]) + (parts[2] + parts[3]))


def target_terms(pair, packed, stacked, terms):
    half = (packed.shape[0] - 8) // 4
    rows = half // 2
    width = per_leaf(packed[4 * half + 3 : 4 * half + 4, :], rows, pair * half)
    places = [
        width * packed[pl.ds(pl.multiple_of(c * half + pair * rows, 8), rows), :] for c in range(3)
    ]
    norm = places[0] * places[0] + places[1] * places[1] + (places[2] * places[2] + softening)
    pieces = [thirds(-2.0 * x) for x in places]
    norms = thirds(norm)
    one, zero = jnp.ones((rows, LANES), jnp.float32), jnp.zeros((rows, LANES), jnp.float32)
    for third in range(3):
        x, y, z = [piece[third] for piece in pieces]
        unit = one if third == 0 else zero
        first = [x, y, z, unit, norms[third]]
        second = [x, y, z, unit] if third < 2 else [zero] * 4
        last = [x, y, z, unit] if third < 1 else [zero] * 4
        for row, values in enumerate(first + second + last + [zero] * 3):
            stacked[pl.ds(16 * third + row, rows, stride=48), :] = values
    for r in range(rows):
        terms[r * LANES : (r + 1) * LANES, :] = (
            stacked[48 * r : 48 * (r + 1), :].T.astype(jnp.bfloat16)
        )


def near_kernel(
    near_source, pair_ref, owner_ref, swapped, placed, passed, packed, totals, high_table, low_table,
    signs, down_inverse, counts, decay_rate, stress, potential, new_stress,
    table, merged, centers, factors, stacked, terms, sums, eval_kernels, densities,
):
    entries, leaves = near_source.shape
    half = leaves // 2
    rows = half // 2
    pair = pair_ref[0]
    low = iota((half, LANES), 1) < BCAP
    target_terms(pair, packed, stacked, terms)
    far = evaluate(
        pair, packed, totals, high_table, low_table, signs, down_inverse, eval_kernels, densities
    )
    swapped_from = jnp.where(((owner_ref[0] & 1) ^ pair) == 1, 0, 2)
    for n, rows_of in ((swapped_from, swapped), (1, placed), (2 - swapped_from, passed)):
        first = n * (leaves * 8)
        for ch in range(4):
            beads = rows_of[ch * half : (ch + 1) * half, :]
            turned = pltpu.roll(beads, BCAP, 1)
            table[pl.ds(first + ch, half, stride=16), :] = jnp.where(low, beads, turned)
            table[pl.ds(first + 8 + ch, half, stride=16), :] = jnp.where(low, turned, beads)
    low = iota((rows, LANES), 1) < BCAP
    for ch in range(3):
        center = per_leaf(packed[4 * half + ch : 4 * half + ch + 1, :], rows, pair * half)
        turned = pltpu.roll(center, BCAP, 1)
        centers[pl.ds(ch, rows, stride=16), :] = jnp.where(low, center, turned)
        centers[pl.ds(8 + ch, rows, stride=16), :] = jnp.where(low, turned, center)
    pairs = entries // 2
    one, zero = jnp.ones((pairs, LANES), jnp.float32), jnp.zeros((pairs, LANES), jnp.float32)

    def prepare(t, carry):
        leaf = pair * half + t
        start = pl.multiple_of(t * pairs * 8, 8)
        for n in range(pairs):
            left = pl.multiple_of(near_source[2 * n, leaf] * 8, 8)
            right = pl.multiple_of(near_source[2 * n + 1, leaf] * 8, 8)
            merged[pl.ds(start + n * 8, 8), :] = jnp.where(
                low, table[pl.ds(left, 8), :], table[pl.ds(right, 8), :]
            )
        place = pl.multiple_of(t * 8, 8)
        x, y, z = [
            merged[pl.ds(start + ch, pairs, stride=8), :] - centers[pl.ds(place + ch, 1), :]
            for ch in range(3)
        ]
        pieces = [thirds(v) for v in (x, y, z, x * x + y * y + z * z)]
        lines = [piece[0] for piece in pieces] + [one]
        lines += [piece[1] for piece in pieces] + [piece[2] for piece in pieces] + [zero] * 3
        start = pl.multiple_of(t * pairs * 16, 16)
        for row, values in enumerate(lines):
            factors[pl.ds(start + row, pairs, stride=16), :] = values
        return carry

    lax.fori_loop(0, half, prepare, 0, unroll=8)

    def one_leaf(t, carry):
        mine = terms[pl.ds(pl.multiple_of(t * BCAP, BCAP), BCAP), :]
        total = jnp.zeros((BCAP, LANES), jnp.float32)
        for n in range(0, pairs, 2):
            start = pl.multiple_of((t * pairs + n) * 16, 16)
            both = jnp.concatenate(
                [factors[pl.ds(start, 16), :], factors[pl.ds(start + 16, 16), :]], 1
            ).astype(jnp.bfloat16)
            squared = jnp.dot(
                mine, jnp.concatenate([both] * 3, 0), preferred_element_type=jnp.float32
            )
            for side in range(2):
                weight = merged[pl.ds((t * pairs + n + side) * 8 + 3, 1), :]
                total = total + lax.rsqrt(squared[:, side * LANES : (side + 1) * LANES]) * weight
        sums[pl.ds(pl.multiple_of(t * BCAP, 8), BCAP), :] = total
        return carry

    lax.fori_loop(0, half, one_leaf, 0, unroll=4)
    for r in range(rows):
        block = sums[r * LANES : (r + 1) * LANES, :].T
        potential[r : r + 1, :] = jnp.sum(block, axis=0, keepdims=True)
    combined = potential[...] + far
    beads = per_leaf(counts[...].astype(jnp.float32), rows, pair * half)
    slot = iota((rows, LANES), 1) & (BCAP - 1)
    occupied = slot.astype(jnp.float32) < beads
    decay = per_leaf(decay_rate[...], rows)
    potential[...] = jnp.where(occupied, combined, 0.0)
    new_stress[...] = jnp.where(occupied, decay * stress[...] + combined, 0.0)


VMEM = pl.BlockSpec(memory_space=pltpu.VMEM)
SMEM = pl.BlockSpec(memory_space=pltpu.SMEM)
ANY = pl.BlockSpec(memory_space=pl.ANY)
MIB = 1024 * 1024


def call(kernel, outs, in_specs, scratch=(), limit=40, grid=(), flops=0, bytes_accessed=0):
    return pl.pallas_call(
        kernel,
        out_shape=outs,
        grid=grid,
        in_specs=in_specs,
        out_specs=jax.tree.map(lambda _: VMEM, outs),
        scratch_shapes=list(scratch),
        compiler_params=pltpu.CompilerParams(vmem_limit_bytes=limit * MIB),
        cost_estimate=pl.CostEstimate(
            flops=flops, bytes_accessed=bytes_accessed, transcendentals=0
        ),
    )


def body(
    offsets,
    charges,
    stress,
    decay_rate,
    morton_keys,
    levels,
    bead_counts,
    send_boxes,
    m2l_source,
    m2l_type,
    m2l_count,
    near_source,
    up_inverse,
    down_inverse,
    translations,
):
    f32 = jnp.float32
    leaves = morton_keys.shape[0]
    half = leaves // 2
    parts = lax.axis_size("wide") * lax.axis_size("narrow")
    table = jnp.asarray(transform_table())
    signs = jnp.asarray(sign_rows())
    pair = lax.axis_index("pair").reshape(1)
    owner = (
        lax.axis_index("wide") * lax.axis_size("narrow") + lax.axis_index("narrow")
    ).reshape(1)
    kind_count = translations.shape[0]

    other_translations = lax.ppermute(translations, "pair", [(0, 1), (1, 0)])
    packed, blocks, placed, sources, kinds = call(
        functools.partial(pack_kernel, kind_count),
        [
            jax.ShapeDtypeStruct((4 * half + 8, LANES), f32),
            jax.ShapeDtypeStruct((8 * parts, LANES), f32),
            jax.ShapeDtypeStruct((4 * half, LANES), f32),
            jax.ShapeDtypeStruct(m2l_source.shape, jnp.int32),
            jax.ShapeDtypeStruct(m2l_type.shape, jnp.int32),
        ],
        [VMEM] * 9,
        limit=62,
    )(
        offsets, charges.reshape(half, LANES), morton_keys.reshape(1, leaves),
        levels.reshape(1, leaves), bead_counts.reshape(1, leaves), send_boxes,
        m2l_source, m2l_type, m2l_count.reshape(1, leaves),
    )
    arrived = lax.all_to_all(
        blocks.reshape(parts, 8, LANES), PARTS, split_axis=0, concat_axis=0, tiled=True
    ).reshape(8 * parts, LANES)
    swaps = [(2 * d, 2 * (d ^ 1)) for d in range(parts)]
    for d in range(1, parts - 1, 2):
        swaps += [(2 * d + 1, 2 * d + 3), (2 * d + 3, 2 * d + 1)]
    swapped = lax.ppermute(placed, PARTS + ("pair",), swaps)
    own_check = call(
        own_kernel,
        jax.ShapeDtypeStruct((Q, leaves // 16 * LANES), f32),
        [VMEM],
        [pltpu.VMEM((leaves // 16, Q * 8, LANES), f32)],
        flops=4 * 10**10,
    )(packed)
    passed = lax.ppermute(swapped, "pair", [(0, 1), (1, 0)])

    last = pl.BlockSpec((kind_count, 2, LANES), lambda i: (0, 0, TILES - 1))
    totals, low_table = call(
        far_kernel,
        [
            jax.ShapeDtypeStruct((half * ROWS, LANES), f32),
            jax.ShapeDtypeStruct(table.shape, table.dtype),
        ],
        [SMEM] * 3 + [VMEM] * 4 + [last] * 2 + [ANY] * 3,
        [
            pltpu.VMEM(((leaves + 2 * parts) * ROWS, LANES), f32),
            pltpu.VMEM((kind_count + 1, ROWS, LANES), f32),
            pltpu.VMEM(table.shape, jnp.bfloat16),
            pltpu.VMEM((leaves + 2 * parts, QPAD), f32),
            pltpu.VMEM(((leaves + 2 * parts) // 16, Q, LANES), f32),
            pltpu.VMEM((Q * 8, LANES), f32),
            pltpu.SemaphoreType.DMA((2 * TILES + 1,)),
        ],
        grid=(1,),
        flops=10**10,
        bytes_accessed=4 * 10**6,
    )(
        sources, kinds, pair, arrived, own_check, up_inverse, signs, translations,
        other_translations, table, translations, other_translations,
    )

    out = jax.ShapeDtypeStruct((half // 2, LANES), f32)
    potential, new_stress = call(
        near_kernel,
        [out, out],
        [SMEM] * 3 + [VMEM] * 12,
        [
            pltpu.VMEM((3 * leaves * 8, LANES), f32),
            pltpu.VMEM((half * near_source.shape[1] // 2 * 8, LANES), f32),
            pltpu.VMEM((half * 8, LANES), f32),
            pltpu.VMEM((half * near_source.shape[1] // 2 * 16, LANES), f32),
            pltpu.VMEM((half // 2 * 48, LANES), f32),
            pltpu.VMEM((half * BCAP, 48), jnp.bfloat16),
            pltpu.VMEM((half * BCAP, LANES), f32),
            pltpu.VMEM((Q * 8, LANES), f32),
            pltpu.VMEM((Q, LANES), f32),
        ],
    )(
        near_source.T, pair, owner, swapped, placed, passed, packed, totals, table, low_table, signs,
        down_inverse, bead_counts.reshape(1, leaves), decay_rate.reshape(1, half),
        stress.reshape(half // 2, LANES),
    )
    return potential.reshape(-1), new_stress.reshape(-1)


def solution(mesh):
    return jax.shard_map(
        body,
        mesh=mesh,
        in_specs=(
            P(None, ("groups", "wide", "narrow")),
            P(("groups", "wide", "narrow")),
            P(("groups", "wide", "narrow", "pair")),
            P(("groups", "wide", "narrow", "pair")),
            P(("groups", "wide", "narrow")),
            P(("groups", "wide", "narrow")),
            P(("groups", "wide", "narrow")),
            P(("groups", "wide", "narrow"), None),
            P(("groups", "wide", "narrow"), None),
            P(("groups", "wide", "narrow"), None),
            P(("groups", "wide", "narrow")),
            P(("groups", "wide", "narrow"), None),
            P(),
            P(),
            P(None, None, "pair"),
        ),
        out_specs=(
            P(("groups", "wide", "narrow", "pair")),
            P(("groups", "wide", "narrow", "pair")),
        ),
        check_vma=False,
    )
```

```python
import functools

import jax
import jax.numpy as jnp
import ml_dtypes
import numpy as np
from jax import lax
from jax.experimental import pallas as pl
from jax.experimental.pallas import tpu as pltpu
from jax.sharding import PartitionSpec as P

PGRID = 12
G = 1728
MAXL = 10
BCAP = 64
Q = 152
QPAD = 160
LANES = 128
BINS = 864
TILES = 7
ROWS = 32
softening = 0.04
surface_reach = 1.25
CELLS = [
    (i, j, k)
    for i in range(6)
    for j in range(6)
    for k in range(6)
    if 0 in (i, j, k) or 5 in (i, j, k)
]
PARTS = ("wide", "narrow")


def transform_table():
    cells = np.array(CELLS)
    bins = np.arange(BINS)
    freq = np.stack([bins // 144, bins // 12 % 12, bins % 12])
    angle = (cells @ freq % PGRID) * (2.0 * np.pi / PGRID)
    table = np.zeros((QPAD, 2 * TILES * LANES))
    table[:Q, :BINS] = np.cos(angle)
    table[:Q, TILES * LANES : TILES * LANES + BINS] = -np.sin(angle)
    table[np.abs(table) < 1e-9] = 0.0
    return table.astype(ml_dtypes.bfloat16)


def low_part(high):
    root = np.sqrt(0.75)
    held = float(np.asarray(root).astype(ml_dtypes.bfloat16))
    scale = (root - held) / (held * (held * held - 1.0) * (held * held - 0.25))
    value = high.astype(jnp.float32)
    square = value * value
    return (value * (square - 1.0) * (square - 0.25) * scale).astype(jnp.bfloat16)


def sign_rows():
    rows = np.zeros((8, QPAD), np.float32)
    rows[0, :Q] = 1.0
    rows[1, :Q] = [(-1.0) ** i for i, _, _ in CELLS]
    return rows


def iota(shape, dim):
    return lax.broadcasted_iota(jnp.int32, shape, dim)


def per_leaf(values, count, first=0):
    shape = (count, values.shape[1])
    leaf, lane = first + 2 * iota(shape, 0), iota(shape, 1)
    even = jnp.sum(jnp.where(lane == leaf, values, 0.0), axis=1, keepdims=True)
    odd = jnp.sum(jnp.where(lane == leaf + 1, values, 0.0), axis=1, keepdims=True)
    return jnp.where(iota((count, LANES), 1) < BCAP, even, odd)


def block_transpose(x):
    lane, row = iota(x.shape, 1), iota(x.shape, 0)
    for k in (1, 2, 4):
        row_bit, lane_bit = (row & k) != 0, (lane & k) != 0
        below = pltpu.roll(pltpu.roll(x, 8 - k, 0), k, 1)
        above = pltpu.roll(pltpu.roll(x, k, 0), LANES - k, 1)
        x = jnp.where(row_bit == lane_bit, x, jnp.where(lane_bit, below, above))
    return x


def split(x):
    high = x.astype(jnp.bfloat16)
    return high, (x - high.astype(jnp.float32)).astype(jnp.bfloat16)


def thirds(x):
    high = x.astype(jnp.bfloat16).astype(jnp.float32)
    rest = x - high
    middle = rest.astype(jnp.bfloat16).astype(jnp.float32)
    return high, middle, rest - middle


def product(a, b, contract):
    dims = (((contract[0],), (contract[1],)), ((), ()))
    (a_high, a_low), (b_high, b_low) = split(a), split(b)

    def dot(x, y):
        return lax.dot_general(x, y, dims, preferred_element_type=jnp.float32)

    return dot(a_high, b_high) + (dot(a_low, b_high) + dot(a_high, b_low))


def axis_squares(offset, width):
    area = width * width
    planes = [surface_reach * 0.5 * (i - 2.5) / 2.5 for i in range(6)]
    return [(plane - offset) * (plane - offset) * area for plane in planes]


def surface_kernels(offsets, width):
    gx, gy, gz = [axis_squares(offset, width) for offset in offsets]
    gz = [g + softening for g in gz]
    last, gxy = None, None
    for q, (i, j, k) in enumerate(CELLS):
        if last != (i, j):
            last, gxy = (i, j), gx[i] + gy[j]
        yield q, lax.rsqrt(gxy + gz[k])


def check_sums(offsets, weights, width, checks):
    offsets = [block_transpose(x) for x in offsets]
    weights, width = block_transpose(weights), block_transpose(width)
    for q, kernel in surface_kernels(offsets, width):
        checks[pl.ds(8 * q, 8), :] = kernel * weights
    check = checks[pl.ds(0, Q, stride=8), :]
    for s in range(1, 8):
        check = check + checks[pl.ds(s, Q, stride=8), :]
    return check


def upward(check, up_inverse):
    density = product(check, up_inverse, (0, 0))
    blocks = check.shape[1] // LANES
    density = density.reshape(2 * blocks, 8, 8, Q)
    total = density[:, 0]
    for g in range(1, 8):
        total = total + density[:, g]
    return total.reshape(16 * blocks, Q)


def store_spectra(density, table_high, table_low, target):
    count = density.shape[0] // 2
    high, low = split(density)
    both = jnp.concatenate([high, low], 0)
    for first in range(0, 2 * TILES, 2):
        columns = pl.ds(first * LANES, 2 * LANES)
        part = jnp.dot(both, table_high[:, columns], preferred_element_type=jnp.float32)
        spectra = part[: 2 * count] + part[2 * count :] + jnp.dot(
            high, table_low[:, columns], preferred_element_type=jnp.float32
        )
        for tile in range(first, first + 2):
            for side in range(2):
                for block in range(count // 16):
                    for h in range(2):
                        row = side * count + block * 16 + h * 8
                        start = (block * 16 + h) * ROWS + 16 * side + 8 * (tile // TILES) + tile % TILES
                        target[pl.ds(start, 8, stride=2 * ROWS), :] = spectra[
                            row : row + 8, (tile - first) * LANES : (tile - first + 1) * LANES
                        ]


def pack_kernel(
    kind_count, offsets, charges, keys, levels, counts, send_boxes, m2l_source, m2l_type, m2l_count,
    out, blocks, placed, sources, kinds,
):
    leaves = keys.shape[1]
    half = leaves // 2
    out[4 * half :, :] = jnp.zeros((8, LANES), jnp.float32)
    width = jnp.left_shift(jnp.ones_like(levels[...]), MAXL - levels[...]).astype(jnp.float32)
    for a in range(3):
        summed = jnp.zeros_like(keys[...])
        for bit in range(MAXL):
            summed = summed + (jnp.right_shift(keys[...], 3 * bit + a) & 1) * (1 << bit)
        out[4 * half + a : 4 * half + a + 1, :leaves] = summed.astype(jnp.float32) + 0.5 * width
    out[4 * half + 3 : 4 * half + 4, :leaves] = width
    for r in range(half):
        out[pl.ds(r, 3, stride=half), :] = offsets[:, r * LANES : (r + 1) * LANES]
    beads = per_leaf(counts[...].astype(jnp.float32), half)
    slot = iota((half, LANES), 1) & (BCAP - 1)
    out[3 * half : 4 * half, :] = jnp.where(slot.astype(jnp.float32) < beads, charges[...], 0.0)

    entry = iota(m2l_type.shape, 1)
    square = (leaves, leaves)
    live = jnp.sum(
        jnp.where(iota(square, 0) == iota(square, 1), m2l_count[...].astype(jnp.float32), 0.0),
        axis=1, keepdims=True,
    )
    kinds[...] = jnp.where(entry.astype(jnp.float32) < live, m2l_type[...], kind_count)
    sources[...] = m2l_source[...] * ROWS

    spread = per_leaf(width, half)
    for ch in range(3):
        center = per_leaf(out[4 * half + ch : 4 * half + ch + 1, :leaves], half)
        placed[ch * half : (ch + 1) * half, :] = center + spread * out[ch * half : (ch + 1) * half, :]
    placed[3 * half :, :] = out[3 * half : 4 * half, :]

    sends = send_boxes.shape[1]
    lane = iota((8, LANES), 1)
    for block in range(sends // 16):
        picked = []
        for c in range(2):
            column = block * 16 + 2 * iota((8, sends), 0) + c
            box = jnp.sum(
                jnp.where(iota((8, sends), 1) == column, send_boxes[...].astype(jnp.float32), 0.0),
                axis=1, keepdims=True,
            ).astype(jnp.int32)
            width_here = jnp.sum(
                jnp.where(iota((8, leaves), 1) == box, width, 0.0), axis=1, keepdims=True
            )
            row_of = jnp.broadcast_to(box >> 1, (8, LANES))
            found = [jnp.zeros((8, LANES), jnp.float32)] * 4
            for r in range(half):
                here = row_of == r
                for ch in range(4):
                    found[ch] = jnp.where(here, out[ch * half + r : ch * half + r + 1, :], found[ch])
            aligned = jnp.broadcast_to((box & 1) == c, (8, LANES))
            found = [jnp.where(aligned, x, pltpu.roll(x, BCAP, 1)) for x in found]
            picked.append(found + [jnp.broadcast_to(width_here, (8, LANES))])
        for ch in range(5):
            blocks[pl.ds(block * 64 + ch, 8, stride=8), :] = jnp.where(
                lane < BCAP, picked[0][ch], picked[1][ch]
            )
        for ch in range(5, 8):
            blocks[pl.ds(block * 64 + ch, 8, stride=8), :] = jnp.zeros((8, LANES), jnp.float32)


def own_kernel(packed, out, checks):
    half = (packed.shape[0] - 8) // 4
    width = per_leaf(packed[4 * half + 3 : 4 * half + 4, :], half)
    for block in range(half // 8):
        rows = [packed[c * half + block * 8 : c * half + block * 8 + 8, :] for c in range(4)]
        out[:, block * LANES : (block + 1) * LANES] = check_sums(
            rows[:3], rows[3], width[block * 8 : block * 8 + 8], checks.at[block]
        )


def far_kernel(
    sources, kinds, pair_ref, arrived, own_check, up_inverse, signs,
    last_bins, other_last_bins, table, translations, other_translations, totals, low_table,
    spectra, kernels, high_table, density, check, checks, sems,
):
    leaves, entries = sources.shape
    half = leaves // 2
    blocks = arrived.shape[0] // 64
    kind_count = translations.shape[0]
    pair = pair_ref[0]

    table_copy = pltpu.make_async_copy(table, high_table, sems.at[0])
    table_copy.start()
    kernel_copies = []
    for side, bins in enumerate((translations, other_translations)):
        for t in range(TILES - 1):
            kernel_copies.append(pltpu.make_async_copy(
                bins.at[:, :, pl.ds(t * LANES, LANES)],
                kernels.at[pl.ds(0, kind_count), pl.ds(16 * side + 2 * t, 2), :],
                sems.at[1 + len(kernel_copies)],
            ))
        kernel_copies.append(pltpu.make_async_copy(
            (last_bins, other_last_bins)[side],
            kernels.at[pl.ds(0, kind_count), pl.ds(16 * side + 2 * TILES - 2, 2), :],
            sems.at[1 + len(kernel_copies)],
        ))
    for copy in kernel_copies:
        copy.start()
    kernels[kind_count] = jnp.zeros((ROWS, LANES), jnp.float32)

    density[...] = jnp.zeros(density.shape, jnp.float32)
    check[0, :, :] = own_check[:, :LANES]
    check[1, :, :] = own_check[:, LANES:]

    def arrive(block, carry):
        beads = [
            arrived[pl.ds(pl.multiple_of(block * 64, 64) + ch, 8, stride=8), :] for ch in range(5)
        ]
        check[leaves // 16 + block, :, :] = check_sums(beads[:3], beads[3], beads[4], checks)
        return carry

    if blocks == 1:
        arrive(0, 0)
    else:
        lax.fori_loop(0, blocks, arrive, 0)
    count = check.shape[0]
    for first in range(0, count, 3):
        some = range(first, min(first + 3, count))
        density[16 * first : 16 * first + 16 * len(some), :Q] = upward(
            jnp.concatenate([check[n] for n in some], 1), up_inverse[...]
        )
    table_copy.wait()
    low_table[...] = low_part(high_table[...])
    sign = jnp.where(pair == 1, signs[1:2, :], signs[0:1, :])
    other_sign = jnp.where(pair == 1, signs[0:1, :], signs[1:2, :])
    store_spectra(
        jnp.concatenate([density[...] * sign, density[...] * other_sign], 0),
        high_table, low_table, spectra,
    )
    for copy in kernel_copies:
        copy.wait()

    def translate(t, carry):
        leaf = pair * half + t
        sums = [[None] * 4, [None] * 4]
        for entry in range(entries):
            kind = kinds[leaf, entry]
            start = pl.multiple_of(sources[leaf, entry], ROWS)
            for side in range(2):
                k_re = kernels[kind, pl.ds(16 * side, 8, stride=2), :]
                k_im = kernels[kind, pl.ds(16 * side + 1, 8, stride=2), :]
                s_re = spectra[pl.ds(start + 16 * side, 8), :]
                s_im = spectra[pl.ds(start + 16 * side + 8, 8), :]
                terms = (k_re * s_re, k_im * s_im, k_re * s_im, k_im * s_re)
                for n, term in enumerate(terms):
                    sums[side][n] = term if sums[side][n] is None else sums[side][n] + term
        start = pl.multiple_of(t * ROWS, ROWS)
        for side in range(2):
            rr, ii, ri, ir = sums[side]
            totals[pl.ds(start + 16 * side, 8), :] = rr - ii
            totals[pl.ds(start + 16 * side + 8, 8), :] = ri + ir
        return carry

    lax.fori_loop(0, half, translate, 0, unroll=4)


def evaluate(
    pair, packed, totals, table, low_table, signs, down_inverse, eval_kernels, densities
):
    half = (packed.shape[0] - 8) // 4
    leaves = 2 * half
    rows = half // 2
    width = block_transpose(
        per_leaf(packed[4 * half + 3 : 4 * half + 4, :], rows, pair * half)
    )
    offsets = [
        block_transpose(packed[pl.ds(pl.multiple_of(c * half + pair * rows, 8), rows), :])
        for c in range(3)
    ]
    for q, kernel in surface_kernels(offsets, width):
        eval_kernels[pl.ds(8 * q, 8), :] = kernel
    sign = jnp.where(pair == 1, signs[1:2, :], signs[0:1, :])
    other_sign = jnp.where(pair == 1, signs[0:1, :], signs[1:2, :])
    lane = iota((half, LANES), 1)
    sides = []
    for side in range(2):
        columns = []
        for c in range(2):
            for t in range(TILES):
                line = totals[pl.ds(16 * side + c * 8 + t, half, stride=ROWS), :]
                if t == TILES - 1:
                    line = jnp.where(lane < BINS - t * LANES, line, 0.0)
                columns.append(line)
        sides.append(jnp.concatenate(columns, 1))
    high, low = split(jnp.concatenate(sides, 0))
    across = (((1,), (1,)), ((), ()))
    both = lax.dot_general(
        jnp.concatenate([high, low], 0), table[...], across,
        preferred_element_type=jnp.float32,
    )
    check = both[:leaves] + both[leaves:] + lax.dot_general(
        high, low_table[...], across, preferred_element_type=jnp.float32
    )
    check = (check[:half] * sign + check[half:] * other_sign)[:, :Q] * (1.0 / G)

    leaf_of = 2 * (lane & 7) + (lane >> 6)
    spread = jnp.where(iota((half, LANES), 0) == leaf_of, 1.0, 0.0)
    densities[...] = product(product(check, down_inverse[...], (1, 0)), spread, (0, 0))
    parts = [jnp.zeros((rows, LANES), jnp.float32)] * 4
    for q in range(Q):
        term = eval_kernels[8 * q : 8 * q + 8, :] * densities[q : q + 1, :]
        parts[q % 4] = parts[q % 4] + term
    return block_transpose((parts[0] + parts[1]) + (parts[2] + parts[3]))


def target_terms(pair, packed, stacked, terms):
    half = (packed.shape[0] - 8) // 4
    rows = half // 2
    width = per_leaf(packed[4 * half + 3 : 4 * half + 4, :], rows, pair * half)
    places = [
        width * packed[pl.ds(pl.multiple_of(c * half + pair * rows, 8), rows), :] for c in range(3)
    ]
    norm = places[0] * places[0] + places[1] * places[1] + (places[2] * places[2] + softening)
    pieces = [thirds(-2.0 * x) for x in places]
    norms = thirds(norm)
    one, zero = jnp.ones((rows, LANES), jnp.float32), jnp.zeros((rows, LANES), jnp.float32)
    for third in range(3):
        x, y, z = [piece[third] for piece in pieces]
        unit = one if third == 0 else zero
        first = [x, y, z, unit, norms[third]]
        second = [x, y, z, unit] if third < 2 else [zero] * 4
        last = [x, y, z, unit] if third < 1 else [zero] * 4
        for row, values in enumerate(first + second + last + [zero] * 3):
            stacked[pl.ds(16 * third + row, rows, stride=48), :] = values
    for r in range(rows):
        terms[r * LANES : (r + 1) * LANES, :] = (
            stacked[48 * r : 48 * (r + 1), :].T.astype(jnp.bfloat16)
        )


def near_kernel(
    near_source, pair_ref, owner_ref, swapped, placed, passed, packed, totals, high_table, low_table,
    signs, down_inverse, counts, decay_rate, stress, potential, new_stress,
    table, merged, centers, factors, stacked, terms, sums, eval_kernels, densities,
):
    entries, leaves = near_source.shape
    half = leaves // 2
    rows = half // 2
    pair = pair_ref[0]
    low = iota((half, LANES), 1) < BCAP
    target_terms(pair, packed, stacked, terms)
    far = evaluate(
        pair, packed, totals, high_table, low_table, signs, down_inverse, eval_kernels, densities
    )
    swapped_from = jnp.where(((owner_ref[0] & 1) ^ pair) == 1, 0, 2)
    for n, rows_of in ((swapped_from, swapped), (1, placed), (2 - swapped_from, passed)):
        first = n * (leaves * 8)
        for ch in range(4):
            beads = rows_of[ch * half : (ch + 1) * half, :]
            turned = pltpu.roll(beads, BCAP, 1)
            table[pl.ds(first + ch, half, stride=16), :] = jnp.where(low, beads, turned)
            table[pl.ds(first + 8 + ch, half, stride=16), :] = jnp.where(low, turned, beads)
    low = iota((rows, LANES), 1) < BCAP
    for ch in range(3):
        center = per_leaf(packed[4 * half + ch : 4 * half + ch + 1, :], rows, pair * half)
        turned = pltpu.roll(center, BCAP, 1)
        centers[pl.ds(ch, rows, stride=16), :] = jnp.where(low, center, turned)
        centers[pl.ds(8 + ch, rows, stride=16), :] = jnp.where(low, turned, center)
    pairs = entries // 2
    one, zero = jnp.ones((pairs, LANES), jnp.float32), jnp.zeros((pairs, LANES), jnp.float32)

    def prepare(t):
        leaf = pair * half + t
        start = t * pairs * 8
        for n in range(pairs):
            left = pl.multiple_of(near_source[2 * n, leaf] * 8, 8)
            right = pl.multiple_of(near_source[2 * n + 1, leaf] * 8, 8)
            merged[pl.ds(start + n * 8, 8), :] = jnp.where(
                low, table[pl.ds(left, 8), :], table[pl.ds(right, 8), :]
            )
        place = t * 8
        x, y, z = [
            merged[pl.ds(start + ch, pairs, stride=8), :] - centers[pl.ds(place + ch, 1), :]
            for ch in range(3)
        ]
        pieces = [thirds(v) for v in (x, y, z, x * x + y * y + z * z)]
        lines = [piece[0] for piece in pieces] + [one]
        lines += [piece[1] for piece in pieces] + [piece[2] for piece in pieces] + [zero] * 3
        start = t * pairs * 16
        for row, values in enumerate(lines):
            factors[pl.ds(start + row, pairs, stride=16), :] = values

    for t in range(half):
        prepare(t)

    def one_leaf(t, carry):
        mine = terms[pl.ds(pl.multiple_of(t * BCAP, BCAP), BCAP), :]
        total = jnp.zeros((BCAP, LANES), jnp.float32)
        for n in range(0, pairs, 2):
            start = pl.multiple_of((t * pairs + n) * 16, 16)
            both = jnp.concatenate(
                [factors[pl.ds(start, 16), :], factors[pl.ds(start + 16, 16), :]], 1
            ).astype(jnp.bfloat16)
            squared = jnp.dot(
                mine, jnp.concatenate([both] * 3, 0), preferred_element_type=jnp.float32
            )
            for side in range(2):
                weight = merged[pl.ds((t * pairs + n + side) * 8 + 3, 1), :]
                total = total + lax.rsqrt(squared[:, side * LANES : (side + 1) * LANES]) * weight
        sums[pl.ds(pl.multiple_of(t * BCAP, 8), BCAP), :] = total
        return carry

    lax.fori_loop(0, half, one_leaf, 0, unroll=4)
    for r in range(rows):
        block = sums[r * LANES : (r + 1) * LANES, :].T
        potential[r : r + 1, :] = jnp.sum(block, axis=0, keepdims=True)
    combined = potential[...] + far
    beads = per_leaf(counts[...].astype(jnp.float32), rows, pair * half)
    slot = iota((rows, LANES), 1) & (BCAP - 1)
    occupied = slot.astype(jnp.float32) < beads
    decay = per_leaf(decay_rate[...], rows)
    potential[...] = jnp.where(occupied, combined, 0.0)
    new_stress[...] = jnp.where(occupied, decay * stress[...] + combined, 0.0)


VMEM = pl.BlockSpec(memory_space=pltpu.VMEM)
SMEM = pl.BlockSpec(memory_space=pltpu.SMEM)
ANY = pl.BlockSpec(memory_space=pl.ANY)
MIB = 1024 * 1024


def call(kernel, outs, in_specs, scratch=(), limit=40, grid=(), flops=0, bytes_accessed=0):
    return pl.pallas_call(
        kernel,
        out_shape=outs,
        grid=grid,
        in_specs=in_specs,
        out_specs=jax.tree.map(lambda _: VMEM, outs),
        scratch_shapes=list(scratch),
        compiler_params=pltpu.CompilerParams(vmem_limit_bytes=limit * MIB),
        cost_estimate=pl.CostEstimate(
            flops=flops, bytes_accessed=bytes_accessed, transcendentals=0
        ),
    )


def body(
    offsets,
    charges,
    stress,
    decay_rate,
    morton_keys,
    levels,
    bead_counts,
    send_boxes,
    m2l_source,
    m2l_type,
    m2l_count,
    near_source,
    up_inverse,
    down_inverse,
    translations,
):
    f32 = jnp.float32
    leaves = morton_keys.shape[0]
    half = leaves // 2
    parts = lax.axis_size("wide") * lax.axis_size("narrow")
    table = jnp.asarray(transform_table())
    signs = jnp.asarray(sign_rows())
    pair = lax.axis_index("pair").reshape(1)
    owner = (
        lax.axis_index("wide") * lax.axis_size("narrow") + lax.axis_index("narrow")
    ).reshape(1)
    kind_count = translations.shape[0]

    other_translations = lax.ppermute(translations, "pair", [(0, 1), (1, 0)])
    packed, blocks, placed, sources, kinds = call(
        functools.partial(pack_kernel, kind_count),
        [
            jax.ShapeDtypeStruct((4 * half + 8, LANES), f32),
            jax.ShapeDtypeStruct((8 * parts, LANES), f32),
            jax.ShapeDtypeStruct((4 * half, LANES), f32),
            jax.ShapeDtypeStruct(m2l_source.shape, jnp.int32),
            jax.ShapeDtypeStruct(m2l_type.shape, jnp.int32),
        ],
        [VMEM] * 9,
        limit=62,
    )(
        offsets, charges.reshape(half, LANES), morton_keys.reshape(1, leaves),
        levels.reshape(1, leaves), bead_counts.reshape(1, leaves), send_boxes,
        m2l_source, m2l_type, m2l_count.reshape(1, leaves),
    )
    arrived = lax.all_to_all(
        blocks.reshape(parts, 8, LANES), PARTS, split_axis=0, concat_axis=0, tiled=True
    ).reshape(8 * parts, LANES)
    swaps = [(2 * d, 2 * (d ^ 1)) for d in range(parts)]
    for d in range(1, parts - 1, 2):
        swaps += [(2 * d + 1, 2 * d + 3), (2 * d + 3, 2 * d + 1)]
    swapped = lax.ppermute(placed, PARTS + ("pair",), swaps)
    own_check = call(
        own_kernel,
        jax.ShapeDtypeStruct((Q, leaves // 16 * LANES), f32),
        [VMEM],
        [pltpu.VMEM((leaves // 16, Q * 8, LANES), f32)],
        flops=4 * 10**10,
    )(packed)
    passed = lax.ppermute(swapped, "pair", [(0, 1), (1, 0)])

    last = pl.BlockSpec((kind_count, 2, LANES), lambda i: (0, 0, TILES - 1))
    totals, low_table = call(
        far_kernel,
        [
            jax.ShapeDtypeStruct((half * ROWS, LANES), f32),
            jax.ShapeDtypeStruct(table.shape, table.dtype),
        ],
        [SMEM] * 3 + [VMEM] * 4 + [last] * 2 + [ANY] * 3,
        [
            pltpu.VMEM(((leaves + 2 * parts) * ROWS, LANES), f32),
            pltpu.VMEM((kind_count + 1, ROWS, LANES), f32),
            pltpu.VMEM(table.shape, jnp.bfloat16),
            pltpu.VMEM((leaves + 2 * parts, QPAD), f32),
            pltpu.VMEM(((leaves + 2 * parts) // 16, Q, LANES), f32),
            pltpu.VMEM((Q * 8, LANES), f32),
            pltpu.SemaphoreType.DMA((2 * TILES + 1,)),
        ],
        grid=(1,),
        flops=10**10,
        bytes_accessed=4 * 10**6,
    )(
        sources, kinds, pair, arrived, own_check, up_inverse, signs, translations,
        other_translations, table, translations, other_translations,
    )

    out = jax.ShapeDtypeStruct((half // 2, LANES), f32)
    potential, new_stress = call(
        near_kernel,
        [out, out],
        [SMEM] * 3 + [VMEM] * 12,
        [
            pltpu.VMEM((3 * leaves * 8, LANES), f32),
            pltpu.VMEM((half * near_source.shape[1] // 2 * 8, LANES), f32),
            pltpu.VMEM((half * 8, LANES), f32),
            pltpu.VMEM((half * near_source.shape[1] // 2 * 16, LANES), f32),
            pltpu.VMEM((half // 2 * 48, LANES), f32),
            pltpu.VMEM((half * BCAP, 48), jnp.bfloat16),
            pltpu.VMEM((half * BCAP, LANES), f32),
            pltpu.VMEM((Q * 8, LANES), f32),
            pltpu.VMEM((Q, LANES), f32),
        ],
    )(
        near_source.T, pair, owner, swapped, placed, passed, packed, totals, table, low_table, signs,
        down_inverse, bead_counts.reshape(1, leaves), decay_rate.reshape(1, half),
        stress.reshape(half // 2, LANES),
    )
    return potential.reshape(-1), new_stress.reshape(-1)


def solution(mesh):
    return jax.shard_map(
        body,
        mesh=mesh,
        in_specs=(
            P(None, ("groups", "wide", "narrow")),
            P(("groups", "wide", "narrow")),
            P(("groups", "wide", "narrow", "pair")),
            P(("groups", "wide", "narrow", "pair")),
            P(("groups", "wide", "narrow")),
            P(("groups", "wide", "narrow")),
            P(("groups", "wide", "narrow")),
            P(("groups", "wide", "narrow"), None),
            P(("groups", "wide", "narrow"), None),
            P(("groups", "wide", "narrow"), None),
            P(("groups", "wide", "narrow")),
            P(("groups", "wide", "narrow"), None),
            P(),
            P(),
            P(None, None, "pair"),
        ),
        out_specs=(
            P(("groups", "wide", "narrow", "pair")),
            P(("groups", "wide", "narrow", "pair")),
        ),
        check_vma=False,
    )
```

```python
import functools

import jax
import jax.numpy as jnp
import ml_dtypes
import numpy as np
from jax import lax
from jax.experimental import pallas as pl
from jax.experimental.pallas import tpu as pltpu
from jax.sharding import PartitionSpec as P

PGRID = 12
G = 1728
MAXL = 10
BCAP = 64
Q = 152
QPAD = 160
LANES = 128
BINS = 864
TILES = 7
ROWS = 32
softening = 0.04
surface_reach = 1.25
CELLS = [
    (i, j, k)
    for i in range(6)
    for j in range(6)
    for k in range(6)
    if 0 in (i, j, k) or 5 in (i, j, k)
]
PARTS = ("wide", "narrow")


def transform_table():
    cells = np.array(CELLS)
    bins = np.arange(BINS)
    freq = np.stack([bins // 144, bins // 12 % 12, bins % 12])
    angle = (cells @ freq % PGRID) * (2.0 * np.pi / PGRID)
    table = np.zeros((QPAD, 2 * TILES * LANES))
    table[:Q, :BINS] = np.cos(angle)
    table[:Q, TILES * LANES : TILES * LANES + BINS] = -np.sin(angle)
    table[np.abs(table) < 1e-9] = 0.0
    return table.astype(ml_dtypes.bfloat16)


def low_part(high):
    root = np.sqrt(0.75)
    held = float(np.asarray(root).astype(ml_dtypes.bfloat16))
    scale = (root - held) / (held * (held * held - 1.0) * (held * held - 0.25))
    value = high.astype(jnp.float32)
    square = value * value
    return (value * (square - 1.0) * (square - 0.25) * scale).astype(jnp.bfloat16)


def sign_rows():
    rows = np.zeros((8, QPAD), np.float32)
    rows[0, :Q] = 1.0
    rows[1, :Q] = [(-1.0) ** i for i, _, _ in CELLS]
    return rows


def iota(shape, dim):
    return lax.broadcasted_iota(jnp.int32, shape, dim)


def per_leaf(values, count, first=0):
    shape = (count, values.shape[1])
    leaf, lane = first + 2 * iota(shape, 0), iota(shape, 1)
    even = jnp.sum(jnp.where(lane == leaf, values, 0.0), axis=1, keepdims=True)
    odd = jnp.sum(jnp.where(lane == leaf + 1, values, 0.0), axis=1, keepdims=True)
    return jnp.where(iota((count, LANES), 1) < BCAP, even, odd)


def block_transpose(x):
    lane, row = iota(x.shape, 1), iota(x.shape, 0)
    for k in (1, 2, 4):
        row_bit, lane_bit = (row & k) != 0, (lane & k) != 0
        below = pltpu.roll(pltpu.roll(x, 8 - k, 0), k, 1)
        above = pltpu.roll(pltpu.roll(x, k, 0), LANES - k, 1)
        x = jnp.where(row_bit == lane_bit, x, jnp.where(lane_bit, below, above))
    return x


def split(x):
    high = x.astype(jnp.bfloat16)
    return high, (x - high.astype(jnp.float32)).astype(jnp.bfloat16)


def thirds(x):
    high = x.astype(jnp.bfloat16).astype(jnp.float32)
    rest = x - high
    middle = rest.astype(jnp.bfloat16).astype(jnp.float32)
    return high, middle, rest - middle


def product(a, b, contract):
    dims = (((contract[0],), (contract[1],)), ((), ()))
    (a_high, a_low), (b_high, b_low) = split(a), split(b)

    def dot(x, y):
        return lax.dot_general(x, y, dims, preferred_element_type=jnp.float32)

    return dot(a_high, b_high) + (dot(a_low, b_high) + dot(a_high, b_low))


def axis_squares(offset, width):
    area = width * width
    planes = [surface_reach * 0.5 * (i - 2.5) / 2.5 for i in range(6)]
    return [(plane - offset) * (plane - offset) * area for plane in planes]


def surface_kernels(offsets, width):
    gx, gy, gz = [axis_squares(offset, width) for offset in offsets]
    gz = [g + softening for g in gz]
    last, gxy = None, None
    for q, (i, j, k) in enumerate(CELLS):
        if last != (i, j):
            last, gxy = (i, j), gx[i] + gy[j]
        yield q, lax.rsqrt(gxy + gz[k])


def check_sums(offsets, weights, width, checks):
    offsets = [block_transpose(x) for x in offsets]
    weights, width = block_transpose(weights), block_transpose(width)
    for q, kernel in surface_kernels(offsets, width):
        checks[pl.ds(8 * q, 8), :] = kernel * weights
    check = checks[pl.ds(0, Q, stride=8), :]
    for s in range(1, 8):
        check = check + checks[pl.ds(s, Q, stride=8), :]
    return check


def upward(check, up_inverse):
    density = product(check, up_inverse, (0, 0))
    blocks = check.shape[1] // LANES
    density = density.reshape(2 * blocks, 8, 8, Q)
    total = density[:, 0]
    for g in range(1, 8):
        total = total + density[:, g]
    return total.reshape(16 * blocks, Q)


def store_spectra(density, table_high, table_low, target):
    count = density.shape[0] // 2
    high, low = split(density)
    both = jnp.concatenate([high, low], 0)
    for first in range(0, 2 * TILES, 2):
        columns = pl.ds(first * LANES, 2 * LANES)
        part = jnp.dot(both, table_high[:, columns], preferred_element_type=jnp.float32)
        spectra = part[: 2 * count] + part[2 * count :] + jnp.dot(
            high, table_low[:, columns], preferred_element_type=jnp.float32
        )
        for tile in range(first, first + 2):
            for side in range(2):
                for block in range(count // 16):
                    for h in range(2):
                        row = side * count + block * 16 + h * 8
                        start = (block * 16 + h) * ROWS + 16 * side + 8 * (tile // TILES) + tile % TILES
                        target[pl.ds(start, 8, stride=2 * ROWS), :] = spectra[
                            row : row + 8, (tile - first) * LANES : (tile - first + 1) * LANES
                        ]


def pack_kernel(
    kind_count, offsets, charges, keys, levels, counts, send_boxes, m2l_source, m2l_type, m2l_count,
    out, blocks, placed, sources, kinds,
):
    leaves = keys.shape[1]
    half = leaves // 2
    out[4 * half :, :] = jnp.zeros((8, LANES), jnp.float32)
    width = jnp.left_shift(jnp.ones_like(levels[...]), MAXL - levels[...]).astype(jnp.float32)
    for a in range(3):
        summed = jnp.zeros_like(keys[...])
        for bit in range(MAXL):
            summed = summed + (jnp.right_shift(keys[...], 3 * bit + a) & 1) * (1 << bit)
        out[4 * half + a : 4 * half + a + 1, :leaves] = summed.astype(jnp.float32) + 0.5 * width
    out[4 * half + 3 : 4 * half + 4, :leaves] = width
    for r in range(half):
        out[pl.ds(r, 3, stride=half), :] = offsets[:, r * LANES : (r + 1) * LANES]
    beads = per_leaf(counts[...].astype(jnp.float32), half)
    slot = iota((half, LANES), 1) & (BCAP - 1)
    out[3 * half : 4 * half, :] = jnp.where(slot.astype(jnp.float32) < beads, charges[...], 0.0)

    entry = iota(m2l_type.shape, 1)
    square = (leaves, leaves)
    live = jnp.sum(
        jnp.where(iota(square, 0) == iota(square, 1), m2l_count[...].astype(jnp.float32), 0.0),
        axis=1, keepdims=True,
    )
    kinds[...] = jnp.where(entry.astype(jnp.float32) < live, m2l_type[...], kind_count)
    sources[...] = m2l_source[...] * ROWS

    spread = per_leaf(width, half)
    for ch in range(3):
        center = per_leaf(out[4 * half + ch : 4 * half + ch + 1, :leaves], half)
        placed[ch * half : (ch + 1) * half, :] = center + spread * out[ch * half : (ch + 1) * half, :]
    placed[3 * half :, :] = out[3 * half : 4 * half, :]

    sends = send_boxes.shape[1]
    lane = iota((8, LANES), 1)
    for block in range(sends // 16):
        picked = []
        for c in range(2):
            column = block * 16 + 2 * iota((8, sends), 0) + c
            box = jnp.sum(
                jnp.where(iota((8, sends), 1) == column, send_boxes[...].astype(jnp.float32), 0.0),
                axis=1, keepdims=True,
            ).astype(jnp.int32)
            width_here = jnp.sum(
                jnp.where(iota((8, leaves), 1) == box, width, 0.0), axis=1, keepdims=True
            )
            row_of = jnp.broadcast_to(box >> 1, (8, LANES))
            found = [jnp.zeros((8, LANES), jnp.float32)] * 4
            for r in range(half):
                here = row_of == r
                for ch in range(4):
                    found[ch] = jnp.where(here, out[ch * half + r : ch * half + r + 1, :], found[ch])
            aligned = jnp.broadcast_to((box & 1) == c, (8, LANES))
            found = [jnp.where(aligned, x, pltpu.roll(x, BCAP, 1)) for x in found]
            picked.append(found + [jnp.broadcast_to(width_here, (8, LANES))])
        for ch in range(5):
            blocks[pl.ds(block * 64 + ch, 8, stride=8), :] = jnp.where(
                lane < BCAP, picked[0][ch], picked[1][ch]
            )
        for ch in range(5, 8):
            blocks[pl.ds(block * 64 + ch, 8, stride=8), :] = jnp.zeros((8, LANES), jnp.float32)


def own_kernel(packed, out, checks):
    half = (packed.shape[0] - 8) // 4
    width = per_leaf(packed[4 * half + 3 : 4 * half + 4, :], half)
    for block in range(half // 8):
        rows = [packed[c * half + block * 8 : c * half + block * 8 + 8, :] for c in range(4)]
        out[:, block * LANES : (block + 1) * LANES] = check_sums(
            rows[:3], rows[3], width[block * 8 : block * 8 + 8], checks.at[block]
        )


def far_kernel(
    sources, kinds, pair_ref, arrived, own_check, up_inverse, signs,
    last_bins, other_last_bins, table, translations, other_translations, totals, low_table,
    spectra, kernels, high_table, density, check, checks, sems,
):
    leaves, entries = sources.shape
    half = leaves // 2
    blocks = arrived.shape[0] // 64
    kind_count = translations.shape[0]
    pair = pair_ref[0]

    table_copy = pltpu.make_async_copy(table, high_table, sems.at[0])
    table_copy.start()
    kernel_copies = []
    for side, bins in enumerate((translations, other_translations)):
        for t in range(TILES - 1):
            kernel_copies.append(pltpu.make_async_copy(
                bins.at[:, :, pl.ds(t * LANES, LANES)],
                kernels.at[pl.ds(0, kind_count), pl.ds(16 * side + 2 * t, 2), :],
                sems.at[1 + len(kernel_copies)],
            ))
        kernel_copies.append(pltpu.make_async_copy(
            (last_bins, other_last_bins)[side],
            kernels.at[pl.ds(0, kind_count), pl.ds(16 * side + 2 * TILES - 2, 2), :],
            sems.at[1 + len(kernel_copies)],
        ))
    for copy in kernel_copies:
        copy.start()
    kernels[kind_count] = jnp.zeros((ROWS, LANES), jnp.float32)

    density[...] = jnp.zeros(density.shape, jnp.float32)
    check[0, :, :] = own_check[:, :LANES]
    check[1, :, :] = own_check[:, LANES:]

    def arrive(block, carry):
        beads = [
            arrived[pl.ds(pl.multiple_of(block * 64, 64) + ch, 8, stride=8), :] for ch in range(5)
        ]
        check[leaves // 16 + block, :, :] = check_sums(beads[:3], beads[3], beads[4], checks)
        return carry

    if blocks == 1:
        arrive(0, 0)
    else:
        lax.fori_loop(0, blocks, arrive, 0)
    count = check.shape[0]
    for first in range(0, count, 3):
        some = range(first, min(first + 3, count))
        density[16 * first : 16 * first + 16 * len(some), :Q] = upward(
            jnp.concatenate([check[n] for n in some], 1), up_inverse[...]
        )
    table_copy.wait()
    low_table[...] = low_part(high_table[...])
    sign = jnp.where(pair == 1, signs[1:2, :], signs[0:1, :])
    other_sign = jnp.where(pair == 1, signs[0:1, :], signs[1:2, :])
    store_spectra(
        jnp.concatenate([density[...] * sign, density[...] * other_sign], 0),
        high_table, low_table, spectra,
    )
    for copy in kernel_copies:
        copy.wait()

    def translate(t, carry):
        leaf = pair * half + t
        sums = [[None] * 4, [None] * 4]
        for entry in range(entries):
            kind = kinds[leaf, entry]
            start = pl.multiple_of(sources[leaf, entry], ROWS)
            for side in range(2):
                k_re = kernels[kind, pl.ds(16 * side, 8, stride=2), :]
                k_im = kernels[kind, pl.ds(16 * side + 1, 8, stride=2), :]
                s_re = spectra[pl.ds(start + 16 * side, 8), :]
                s_im = spectra[pl.ds(start + 16 * side + 8, 8), :]
                terms = (k_re * s_re, k_im * s_im, k_re * s_im, k_im * s_re)
                for n, term in enumerate(terms):
                    sums[side][n] = term if sums[side][n] is None else sums[side][n] + term
        start = pl.multiple_of(t * ROWS, ROWS)
        for side in range(2):
            rr, ii, ri, ir = sums[side]
            totals[pl.ds(start + 16 * side, 8), :] = rr - ii
            totals[pl.ds(start + 16 * side + 8, 8), :] = ri + ir
        return carry

    lax.fori_loop(0, half, translate, 0, unroll=4)


def evaluate(
    pair, packed, totals, table, low_table, signs, down_inverse, eval_kernels, densities
):
    half = (packed.shape[0] - 8) // 4
    leaves = 2 * half
    rows = half // 2
    width = block_transpose(
        per_leaf(packed[4 * half + 3 : 4 * half + 4, :], rows, pair * half)
    )
    offsets = [
        block_transpose(packed[pl.ds(pl.multiple_of(c * half + pair * rows, 8), rows), :])
        for c in range(3)
    ]
    for q, kernel in surface_kernels(offsets, width):
        eval_kernels[pl.ds(8 * q, 8), :] = kernel
    sign = jnp.where(pair == 1, signs[1:2, :], signs[0:1, :])
    other_sign = jnp.where(pair == 1, signs[0:1, :], signs[1:2, :])
    lane = iota((half, LANES), 1)
    sides = []
    for side in range(2):
        columns = []
        for c in range(2):
            for t in range(TILES):
                line = totals[pl.ds(16 * side + c * 8 + t, half, stride=ROWS), :]
                if t == TILES - 1:
                    line = jnp.where(lane < BINS - t * LANES, line, 0.0)
                columns.append(line)
        sides.append(jnp.concatenate(columns, 1))
    high, low = split(jnp.concatenate(sides, 0))
    across = (((1,), (1,)), ((), ()))
    both = lax.dot_general(
        jnp.concatenate([high, low], 0), table[...], across,
        preferred_element_type=jnp.float32,
    )
    check = both[:leaves] + both[leaves:] + lax.dot_general(
        high, low_table[...], across, preferred_element_type=jnp.float32
    )
    check = (check[:half] * sign + check[half:] * other_sign)[:, :Q] * (1.0 / G)

    leaf_of = 2 * (lane & 7) + (lane >> 6)
    spread = jnp.where(iota((half, LANES), 0) == leaf_of, 1.0, 0.0)
    densities[...] = product(product(check, down_inverse[...], (1, 0)), spread, (0, 0))
    parts = [jnp.zeros((rows, LANES), jnp.float32)] * 4
    for q in range(Q):
        term = eval_kernels[8 * q : 8 * q + 8, :] * densities[q : q + 1, :]
        parts[q % 4] = parts[q % 4] + term
    return block_transpose((parts[0] + parts[1]) + (parts[2] + parts[3]))


def target_terms(pair, packed, stacked, terms):
    half = (packed.shape[0] - 8) // 4
    rows = half // 2
    width = per_leaf(packed[4 * half + 3 : 4 * half + 4, :], rows, pair * half)
    places = [
        width * packed[pl.ds(pl.multiple_of(c * half + pair * rows, 8), rows), :] for c in range(3)
    ]
    norm = places[0] * places[0] + places[1] * places[1] + (places[2] * places[2] + softening)
    pieces = [thirds(-2.0 * x) for x in places]
    norms = thirds(norm)
    one, zero = jnp.ones((rows, LANES), jnp.float32), jnp.zeros((rows, LANES), jnp.float32)
    for third in range(3):
        x, y, z = [piece[third] for piece in pieces]
        unit = one if third == 0 else zero
        first = [x, y, z, unit, norms[third]]
        second = [x, y, z, unit] if third < 2 else [zero] * 4
        last = [x, y, z, unit] if third < 1 else [zero] * 4
        for row, values in enumerate(first + second + last + [zero] * 3):
            stacked[pl.ds(16 * third + row, rows, stride=48), :] = values
    for r in range(rows):
        terms[r * LANES : (r + 1) * LANES, :] = (
            stacked[48 * r : 48 * (r + 1), :].T.astype(jnp.bfloat16)
        )


def near_kernel(
    near_source, pair_ref, owner_ref, swapped, placed, passed, packed, totals, high_table, low_table,
    signs, down_inverse, counts, decay_rate, stress, potential, new_stress,
    table, merged, centers, factors, stacked, terms, eval_kernels, densities,
):
    entries, leaves = near_source.shape
    half = leaves // 2
    rows = half // 2
    pair = pair_ref[0]
    low = iota((half, LANES), 1) < BCAP
    target_terms(pair, packed, stacked, terms)
    far = evaluate(
        pair, packed, totals, high_table, low_table, signs, down_inverse, eval_kernels, densities
    )
    swapped_from = jnp.where(((owner_ref[0] & 1) ^ pair) == 1, 0, 2)
    for n, rows_of in ((swapped_from, swapped), (1, placed), (2 - swapped_from, passed)):
        first = n * (leaves * 8)
        for ch in range(4):
            beads = rows_of[ch * half : (ch + 1) * half, :]
            turned = pltpu.roll(beads, BCAP, 1)
            table[pl.ds(first + ch, half, stride=16), :] = jnp.where(low, beads, turned)
            table[pl.ds(first + 8 + ch, half, stride=16), :] = jnp.where(low, turned, beads)
    low = iota((rows, LANES), 1) < BCAP
    for ch in range(3):
        center = per_leaf(packed[4 * half + ch : 4 * half + ch + 1, :], rows, pair * half)
        turned = pltpu.roll(center, BCAP, 1)
        centers[pl.ds(ch, rows, stride=16), :] = jnp.where(low, center, turned)
        centers[pl.ds(8 + ch, rows, stride=16), :] = jnp.where(low, turned, center)
    pairs = entries // 2
    one, zero = jnp.ones((pairs, LANES), jnp.float32), jnp.zeros((pairs, LANES), jnp.float32)

    def prepare(t):
        leaf = pair * half + t
        start = t * pairs * 8
        for n in range(pairs):
            left = pl.multiple_of(near_source[2 * n, leaf] * 8, 8)
            right = pl.multiple_of(near_source[2 * n + 1, leaf] * 8, 8)
            merged[pl.ds(start + n * 8, 8), :] = jnp.where(
                low, table[pl.ds(left, 8), :], table[pl.ds(right, 8), :]
            )
        place = t * 8
        x, y, z = [
            merged[pl.ds(start + ch, pairs, stride=8), :] - centers[pl.ds(place + ch, 1), :]
            for ch in range(3)
        ]
        pieces = [thirds(v) for v in (x, y, z, x * x + y * y + z * z)]
        lines = [piece[0] for piece in pieces] + [one]
        lines += [piece[1] for piece in pieces] + [piece[2] for piece in pieces] + [zero] * 3
        start = t * pairs * 16
        for row, values in enumerate(lines):
            factors[pl.ds(start + row, pairs, stride=16), :] = values

    for t in range(half):
        prepare(t)

    def one_leaf(t):
        mine = terms[pl.ds(pl.multiple_of(t * BCAP, BCAP), BCAP), :]
        total = jnp.zeros((BCAP, LANES), jnp.float32)
        for n in range(0, pairs, 2):
            start = pl.multiple_of((t * pairs + n) * 16, 16)
            both = jnp.concatenate(
                [factors[pl.ds(start, 16), :], factors[pl.ds(start + 16, 16), :]], 1
            ).astype(jnp.bfloat16)
            squared = jnp.dot(
                mine, jnp.concatenate([both] * 3, 0), preferred_element_type=jnp.float32
            )
            for side in range(2):
                weight = merged[pl.ds((t * pairs + n + side) * 8 + 3, 1), :]
                total = total + lax.rsqrt(squared[:, side * LANES : (side + 1) * LANES]) * weight
        return total

    def two_leaves(r, carry):
        block = jnp.concatenate([one_leaf(2 * r), one_leaf(2 * r + 1)], 0).T
        potential[pl.ds(r, 1), :] = jnp.sum(block, axis=0, keepdims=True)
        return carry

    lax.fori_loop(0, rows, two_leaves, 0, unroll=2)
    combined = potential[...] + far
    beads = per_leaf(counts[...].astype(jnp.float32), rows, pair * half)
    slot = iota((rows, LANES), 1) & (BCAP - 1)
    occupied = slot.astype(jnp.float32) < beads
    decay = per_leaf(decay_rate[...], rows)
    potential[...] = jnp.where(occupied, combined, 0.0)
    new_stress[...] = jnp.where(occupied, decay * stress[...] + combined, 0.0)


VMEM = pl.BlockSpec(memory_space=pltpu.VMEM)
SMEM = pl.BlockSpec(memory_space=pltpu.SMEM)
ANY = pl.BlockSpec(memory_space=pl.ANY)
MIB = 1024 * 1024


def call(kernel, outs, in_specs, scratch=(), limit=40, grid=(), flops=0, bytes_accessed=0):
    return pl.pallas_call(
        kernel,
        out_shape=outs,
        grid=grid,
        in_specs=in_specs,
        out_specs=jax.tree.map(lambda _: VMEM, outs),
        scratch_shapes=list(scratch),
        compiler_params=pltpu.CompilerParams(vmem_limit_bytes=limit * MIB),
        cost_estimate=pl.CostEstimate(
            flops=flops, bytes_accessed=bytes_accessed, transcendentals=0
        ),
    )


def body(
    offsets,
    charges,
    stress,
    decay_rate,
    morton_keys,
    levels,
    bead_counts,
    send_boxes,
    m2l_source,
    m2l_type,
    m2l_count,
    near_source,
    up_inverse,
    down_inverse,
    translations,
):
    f32 = jnp.float32
    leaves = morton_keys.shape[0]
    half = leaves // 2
    parts = lax.axis_size("wide") * lax.axis_size("narrow")
    table = jnp.asarray(transform_table())
    signs = jnp.asarray(sign_rows())
    pair = lax.axis_index("pair").reshape(1)
    owner = (
        lax.axis_index("wide") * lax.axis_size("narrow") + lax.axis_index("narrow")
    ).reshape(1)
    kind_count = translations.shape[0]

    other_translations = lax.ppermute(translations, "pair", [(0, 1), (1, 0)])
    packed, blocks, placed, sources, kinds = call(
        functools.partial(pack_kernel, kind_count),
        [
            jax.ShapeDtypeStruct((4 * half + 8, LANES), f32),
            jax.ShapeDtypeStruct((8 * parts, LANES), f32),
            jax.ShapeDtypeStruct((4 * half, LANES), f32),
            jax.ShapeDtypeStruct(m2l_source.shape, jnp.int32),
            jax.ShapeDtypeStruct(m2l_type.shape, jnp.int32),
        ],
        [VMEM] * 9,
        limit=62,
    )(
        offsets, charges.reshape(half, LANES), morton_keys.reshape(1, leaves),
        levels.reshape(1, leaves), bead_counts.reshape(1, leaves), send_boxes,
        m2l_source, m2l_type, m2l_count.reshape(1, leaves),
    )
    arrived = lax.all_to_all(
        blocks.reshape(parts, 8, LANES), PARTS, split_axis=0, concat_axis=0, tiled=True
    ).reshape(8 * parts, LANES)
    swaps = [(2 * d, 2 * (d ^ 1)) for d in range(parts)]
    for d in range(1, parts - 1, 2):
        swaps += [(2 * d + 1, 2 * d + 3), (2 * d + 3, 2 * d + 1)]
    swapped = lax.ppermute(placed, PARTS + ("pair",), swaps)
    own_check = call(
        own_kernel,
        jax.ShapeDtypeStruct((Q, leaves // 16 * LANES), f32),
        [VMEM],
        [pltpu.VMEM((leaves // 16, Q * 8, LANES), f32)],
        flops=4 * 10**10,
    )(packed)
    passed = lax.ppermute(swapped, "pair", [(0, 1), (1, 0)])

    last = pl.BlockSpec((kind_count, 2, LANES), lambda i: (0, 0, TILES - 1))
    totals, low_table = call(
        far_kernel,
        [
            jax.ShapeDtypeStruct((half * ROWS, LANES), f32),
            jax.ShapeDtypeStruct(table.shape, table.dtype),
        ],
        [SMEM] * 3 + [VMEM] * 4 + [last] * 2 + [ANY] * 3,
        [
            pltpu.VMEM(((leaves + 2 * parts) * ROWS, LANES), f32),
            pltpu.VMEM((kind_count + 1, ROWS, LANES), f32),
            pltpu.VMEM(table.shape, jnp.bfloat16),
            pltpu.VMEM((leaves + 2 * parts, QPAD), f32),
            pltpu.VMEM(((leaves + 2 * parts) // 16, Q, LANES), f32),
            pltpu.VMEM((Q * 8, LANES), f32),
            pltpu.SemaphoreType.DMA((2 * TILES + 1,)),
        ],
        grid=(1,),
        flops=10**10,
        bytes_accessed=4 * 10**6,
    )(
        sources, kinds, pair, arrived, own_check, up_inverse, signs, translations,
        other_translations, table, translations, other_translations,
    )

    out = jax.ShapeDtypeStruct((half // 2, LANES), f32)
    potential, new_stress = call(
        near_kernel,
        [out, out],
        [SMEM] * 3 + [VMEM] * 12,
        [
            pltpu.VMEM((3 * leaves * 8, LANES), f32),
            pltpu.VMEM((half * near_source.shape[1] // 2 * 8, LANES), f32),
            pltpu.VMEM((half * 8, LANES), f32),
            pltpu.VMEM((half * near_source.shape[1] // 2 * 16, LANES), f32),
            pltpu.VMEM((half // 2 * 48, LANES), f32),
            pltpu.VMEM((half * BCAP, 48), jnp.bfloat16),
            pltpu.VMEM((Q * 8, LANES), f32),
            pltpu.VMEM((Q, LANES), f32),
        ],
    )(
        near_source.T, pair, owner, swapped, placed, passed, packed, totals, table, low_table, signs,
        down_inverse, bead_counts.reshape(1, leaves), decay_rate.reshape(1, half),
        stress.reshape(half // 2, LANES),
    )
    return potential.reshape(-1), new_stress.reshape(-1)


def solution(mesh):
    return jax.shard_map(
        body,
        mesh=mesh,
        in_specs=(
            P(None, ("groups", "wide", "narrow")),
            P(("groups", "wide", "narrow")),
            P(("groups", "wide", "narrow", "pair")),
            P(("groups", "wide", "narrow", "pair")),
            P(("groups", "wide", "narrow")),
            P(("groups", "wide", "narrow")),
            P(("groups", "wide", "narrow")),
            P(("groups", "wide", "narrow"), None),
            P(("groups", "wide", "narrow"), None),
            P(("groups", "wide", "narrow"), None),
            P(("groups", "wide", "narrow")),
            P(("groups", "wide", "narrow"), None),
            P(),
            P(),
            P(None, None, "pair"),
        ),
        out_specs=(
            P(("groups", "wide", "narrow", "pair")),
            P(("groups", "wide", "narrow", "pair")),
        ),
        check_vma=False,
    )
```

```python
import functools

import jax
import jax.numpy as jnp
import ml_dtypes
import numpy as np
from jax import lax
from jax.experimental import pallas as pl
from jax.experimental.pallas import tpu as pltpu
from jax.sharding import PartitionSpec as P

PGRID = 12
G = 1728
MAXL = 10
BCAP = 64
Q = 152
QPAD = 160
LANES = 128
BINS = 864
TILES = 7
ROWS = 32
softening = 0.04
surface_reach = 1.25
CELLS = [
    (i, j, k)
    for i in range(6)
    for j in range(6)
    for k in range(6)
    if 0 in (i, j, k) or 5 in (i, j, k)
]
PARTS = ("wide", "narrow")


def transform_table():
    cells = np.array(CELLS)
    bins = np.arange(BINS)
    freq = np.stack([bins // 144, bins // 12 % 12, bins % 12])
    angle = (cells @ freq % PGRID) * (2.0 * np.pi / PGRID)
    table = np.zeros((QPAD, 2 * TILES * LANES))
    table[:Q, :BINS] = np.cos(angle)
    table[:Q, TILES * LANES : TILES * LANES + BINS] = -np.sin(angle)
    table[np.abs(table) < 1e-9] = 0.0
    return table.astype(ml_dtypes.bfloat16)


def low_part(high):
    root = np.sqrt(0.75)
    held = float(np.asarray(root).astype(ml_dtypes.bfloat16))
    scale = (root - held) / (held * (held * held - 1.0) * (held * held - 0.25))
    value = high.astype(jnp.float32)
    square = value * value
    return (value * (square - 1.0) * (square - 0.25) * scale).astype(jnp.bfloat16)


def sign_rows():
    rows = np.zeros((8, QPAD), np.float32)
    rows[0, :Q] = 1.0
    rows[1, :Q] = [(-1.0) ** i for i, _, _ in CELLS]
    return rows


def iota(shape, dim):
    return lax.broadcasted_iota(jnp.int32, shape, dim)


def per_leaf(values, count, first=0):
    shape = (count, values.shape[1])
    leaf, lane = first + 2 * iota(shape, 0), iota(shape, 1)
    even = jnp.sum(jnp.where(lane == leaf, values, 0.0), axis=1, keepdims=True)
    odd = jnp.sum(jnp.where(lane == leaf + 1, values, 0.0), axis=1, keepdims=True)
    return jnp.where(iota((count, LANES), 1) < BCAP, even, odd)


def block_transpose(x):
    lane, row = iota(x.shape, 1), iota(x.shape, 0)
    for k in (1, 2, 4):
        row_bit, lane_bit = (row & k) != 0, (lane & k) != 0
        below = pltpu.roll(pltpu.roll(x, 8 - k, 0), k, 1)
        above = pltpu.roll(pltpu.roll(x, k, 0), LANES - k, 1)
        x = jnp.where(row_bit == lane_bit, x, jnp.where(lane_bit, below, above))
    return x


def split(x):
    high = x.astype(jnp.bfloat16)
    return high, (x - high.astype(jnp.float32)).astype(jnp.bfloat16)


def thirds(x):
    high = x.astype(jnp.bfloat16).astype(jnp.float32)
    rest = x - high
    middle = rest.astype(jnp.bfloat16).astype(jnp.float32)
    return high, middle, rest - middle


def product(a, b, contract):
    dims = (((contract[0],), (contract[1],)), ((), ()))
    (a_high, a_low), (b_high, b_low) = split(a), split(b)

    def dot(x, y):
        return lax.dot_general(x, y, dims, preferred_element_type=jnp.float32)

    return dot(a_high, b_high) + (dot(a_low, b_high) + dot(a_high, b_low))


def axis_squares(offset, width):
    area = width * width
    planes = [surface_reach * 0.5 * (i - 2.5) / 2.5 for i in range(6)]
    return [(plane - offset) * (plane - offset) * area for plane in planes]


def surface_kernels(offsets, width):
    gx, gy, gz = [axis_squares(offset, width) for offset in offsets]
    gz = [g + softening for g in gz]
    last, gxy = None, None
    for q, (i, j, k) in enumerate(CELLS):
        if last != (i, j):
            last, gxy = (i, j), gx[i] + gy[j]
        yield q, lax.rsqrt(gxy + gz[k])


def check_sums(offsets, weights, width, checks):
    offsets = [block_transpose(x) for x in offsets]
    weights, width = block_transpose(weights), block_transpose(width)
    for q, kernel in surface_kernels(offsets, width):
        checks[pl.ds(8 * q, 8), :] = kernel * weights
    check = checks[pl.ds(0, Q, stride=8), :]
    for s in range(1, 8):
        check = check + checks[pl.ds(s, Q, stride=8), :]
    return check


def upward(check, up_inverse):
    density = product(check, up_inverse, (0, 0))
    blocks = check.shape[1] // LANES
    density = density.reshape(2 * blocks, 8, 8, Q)
    total = density[:, 0]
    for g in range(1, 8):
        total = total + density[:, g]
    return total.reshape(16 * blocks, Q)


def store_spectra(density, table_high, table_low, target):
    count = density.shape[0] // 2
    high, low = split(density)
    both = jnp.concatenate([high, low], 0)
    for first in range(0, 2 * TILES, 2):
        columns = pl.ds(first * LANES, 2 * LANES)
        part = jnp.dot(both, table_high[:, columns], preferred_element_type=jnp.float32)
        spectra = part[: 2 * count] + part[2 * count :] + jnp.dot(
            high, table_low[:, columns], preferred_element_type=jnp.float32
        )
        for tile in range(first, first + 2):
            for side in range(2):
                for block in range(count // 16):
                    for h in range(2):
                        row = side * count + block * 16 + h * 8
                        start = (block * 16 + h) * ROWS + 16 * side + 8 * (tile // TILES) + tile % TILES
                        target[pl.ds(start, 8, stride=2 * ROWS), :] = spectra[
                            row : row + 8, (tile - first) * LANES : (tile - first + 1) * LANES
                        ]


def pack_kernel(
    kind_count, offsets, charges, keys, levels, counts, send_boxes, m2l_source, m2l_type, m2l_count,
    out, blocks, placed, sources, kinds,
):
    leaves = keys.shape[1]
    half = leaves // 2
    out[4 * half :, :] = jnp.zeros((8, LANES), jnp.float32)
    width = jnp.left_shift(jnp.ones_like(levels[...]), MAXL - levels[...]).astype(jnp.float32)
    for a in range(3):
        summed = jnp.zeros_like(keys[...])
        for bit in range(MAXL):
            summed = summed + (jnp.right_shift(keys[...], 3 * bit + a) & 1) * (1 << bit)
        out[4 * half + a : 4 * half + a + 1, :leaves] = summed.astype(jnp.float32) + 0.5 * width
    out[4 * half + 3 : 4 * half + 4, :leaves] = width
    for r in range(half):
        out[pl.ds(r, 3, stride=half), :] = offsets[:, r * LANES : (r + 1) * LANES]
    beads = per_leaf(counts[...].astype(jnp.float32), half)
    slot = iota((half, LANES), 1) & (BCAP - 1)
    out[3 * half : 4 * half, :] = jnp.where(slot.astype(jnp.float32) < beads, charges[...], 0.0)

    entry = iota(m2l_type.shape, 1)
    square = (leaves, leaves)
    live = jnp.sum(
        jnp.where(iota(square, 0) == iota(square, 1), m2l_count[...].astype(jnp.float32), 0.0),
        axis=1, keepdims=True,
    )
    kinds[...] = jnp.where(entry.astype(jnp.float32) < live, m2l_type[...], kind_count)
    sources[...] = m2l_source[...] * ROWS

    spread = per_leaf(width, half)
    for ch in range(3):
        center = per_leaf(out[4 * half + ch : 4 * half + ch + 1, :leaves], half)
        placed[ch * half : (ch + 1) * half, :] = center + spread * out[ch * half : (ch + 1) * half, :]
    placed[3 * half :, :] = out[3 * half : 4 * half, :]

    sends = send_boxes.shape[1]
    lane = iota((8, LANES), 1)
    for block in range(sends // 16):
        picked = []
        for c in range(2):
            column = block * 16 + 2 * iota((8, sends), 0) + c
            box = jnp.sum(
                jnp.where(iota((8, sends), 1) == column, send_boxes[...].astype(jnp.float32), 0.0),
                axis=1, keepdims=True,
            ).astype(jnp.int32)
            width_here = jnp.sum(
                jnp.where(iota((8, leaves), 1) == box, width, 0.0), axis=1, keepdims=True
            )
            row_of = jnp.broadcast_to(box >> 1, (8, LANES))
            found = [jnp.zeros((8, LANES), jnp.float32)] * 4
            for r in range(half):
                here = row_of == r
                for ch in range(4):
                    found[ch] = jnp.where(here, out[ch * half + r : ch * half + r + 1, :], found[ch])
            aligned = jnp.broadcast_to((box & 1) == c, (8, LANES))
            found = [jnp.where(aligned, x, pltpu.roll(x, BCAP, 1)) for x in found]
            picked.append(found + [jnp.broadcast_to(width_here, (8, LANES))])
        for ch in range(5):
            blocks[pl.ds(block * 64 + ch, 8, stride=8), :] = jnp.where(
                lane < BCAP, picked[0][ch], picked[1][ch]
            )
        for ch in range(5, 8):
            blocks[pl.ds(block * 64 + ch, 8, stride=8), :] = jnp.zeros((8, LANES), jnp.float32)


def target_terms(pair, packed, stacked, terms, start):
    half = (packed.shape[0] - 8) // 4
    rows = half // 2
    width = per_leaf(packed[4 * half + 3 : 4 * half + 4, :], rows, pair * half)
    places = [
        width * packed[pl.ds(pl.multiple_of(c * half + pair * rows, 8), rows), :] for c in range(3)
    ]
    norm = places[0] * places[0] + places[1] * places[1] + (places[2] * places[2] + softening)
    pieces = [thirds(-2.0 * x) for x in places]
    norms = thirds(norm)
    one, zero = jnp.ones((rows, LANES), jnp.float32), jnp.zeros((rows, LANES), jnp.float32)
    for third in range(3):
        x, y, z = [piece[third] for piece in pieces]
        unit = one if third == 0 else zero
        first = [x, y, z, unit, norms[third]]
        second = [x, y, z, unit] if third < 2 else [zero] * 4
        last = [x, y, z, unit] if third < 1 else [zero] * 4
        for row, values in enumerate(first + second + last + [zero] * 3):
            stacked[pl.ds(16 * third + row, rows, stride=48), :] = values
    for r in range(rows):
        line = start + r * LANES
        terms[line : line + LANES, :48] = stacked[48 * r : 48 * (r + 1), :].T


def own_kernel(pair_ref, packed, out, checks, stacked):
    half = (packed.shape[0] - 8) // 4
    rows = half // 2
    pair = pair_ref[0]
    width = per_leaf(packed[4 * half + 3 : 4 * half + 4, :], half)
    for block in range(half // 8):
        beads = [packed[c * half + block * 8 : c * half + block * 8 + 8, :] for c in range(4)]
        out[block * Q : (block + 1) * Q, :] = check_sums(
            beads[:3], beads[3], width[block * 8 : block * 8 + 8], checks.at[block]
        )
    width = block_transpose(
        per_leaf(packed[4 * half + 3 : 4 * half + 4, :], rows, pair * half)
    )
    offsets = [
        block_transpose(packed[pl.ds(pl.multiple_of(c * half + pair * rows, 8), rows), :])
        for c in range(3)
    ]
    first = half // 8 * Q
    for q, kernel in surface_kernels(offsets, width):
        out[first + 8 * q : first + 8 * q + 8, :] = kernel
    target_terms(pair, packed, stacked, out, first + 8 * Q)


def far_kernel(
    sources, kinds, pair_ref, arrived, own_check, up_inverse, signs,
    last_bins, other_last_bins, table, translations, other_translations, totals, low_table,
    spectra, kernels, high_table, density, check, checks, sems,
):
    leaves, entries = sources.shape
    half = leaves // 2
    blocks = arrived.shape[0] // 64
    kind_count = translations.shape[0]
    pair = pair_ref[0]

    table_copy = pltpu.make_async_copy(table, high_table, sems.at[0])
    table_copy.start()
    kernel_copies = []
    for side, bins in enumerate((translations, other_translations)):
        for t in range(TILES - 1):
            kernel_copies.append(pltpu.make_async_copy(
                bins.at[:, :, pl.ds(t * LANES, LANES)],
                kernels.at[pl.ds(0, kind_count), pl.ds(16 * side + 2 * t, 2), :],
                sems.at[1 + len(kernel_copies)],
            ))
        kernel_copies.append(pltpu.make_async_copy(
            (last_bins, other_last_bins)[side],
            kernels.at[pl.ds(0, kind_count), pl.ds(16 * side + 2 * TILES - 2, 2), :],
            sems.at[1 + len(kernel_copies)],
        ))
    for copy in kernel_copies:
        copy.start()
    kernels[kind_count] = jnp.zeros((ROWS, LANES), jnp.float32)

    density[...] = jnp.zeros(density.shape, jnp.float32)
    for block in range(leaves // 16):
        check[block, :, :] = own_check[block * Q : (block + 1) * Q, :]

    def arrive(block, carry):
        beads = [
            arrived[pl.ds(pl.multiple_of(block * 64, 64) + ch, 8, stride=8), :] for ch in range(5)
        ]
        check[leaves // 16 + block, :, :] = check_sums(beads[:3], beads[3], beads[4], checks)
        return carry

    if blocks == 1:
        arrive(0, 0)
    else:
        lax.fori_loop(0, blocks, arrive, 0)
    count = check.shape[0]
    for first in range(0, count, 3):
        some = range(first, min(first + 3, count))
        density[16 * first : 16 * first + 16 * len(some), :Q] = upward(
            jnp.concatenate([check[n] for n in some], 1), up_inverse[...]
        )
    table_copy.wait()
    low_table[...] = low_part(high_table[...])
    sign = jnp.where(pair == 1, signs[1:2, :], signs[0:1, :])
    other_sign = jnp.where(pair == 1, signs[0:1, :], signs[1:2, :])
    store_spectra(
        jnp.concatenate([density[...] * sign, density[...] * other_sign], 0),
        high_table, low_table, spectra,
    )
    for copy in kernel_copies:
        copy.wait()

    def translate(t, carry):
        leaf = pair * half + t
        sums = [[None] * 4, [None] * 4]
        for entry in range(entries):
            kind = kinds[leaf, entry]
            start = pl.multiple_of(sources[leaf, entry], ROWS)
            for side in range(2):
                k_re = kernels[kind, pl.ds(16 * side, 8, stride=2), :]
                k_im = kernels[kind, pl.ds(16 * side + 1, 8, stride=2), :]
                s_re = spectra[pl.ds(start + 16 * side, 8), :]
                s_im = spectra[pl.ds(start + 16 * side + 8, 8), :]
                terms = (k_re * s_re, k_im * s_im, k_re * s_im, k_im * s_re)
                for n, term in enumerate(terms):
                    sums[side][n] = term if sums[side][n] is None else sums[side][n] + term
        start = pl.multiple_of(t * ROWS, ROWS)
        for side in range(2):
            rr, ii, ri, ir = sums[side]
            totals[pl.ds(start + 16 * side, 8), :] = rr - ii
            totals[pl.ds(start + 16 * side + 8, 8), :] = ri + ir
        return carry

    lax.fori_loop(0, half, translate, 0, unroll=4)


def evaluate(pair, totals, table, low_table, signs, down_inverse, own, densities):
    half = totals.shape[0] // ROWS
    leaves = 2 * half
    rows = half // 2
    start = half // 8 * Q
    sign = jnp.where(pair == 1, signs[1:2, :], signs[0:1, :])
    other_sign = jnp.where(pair == 1, signs[0:1, :], signs[1:2, :])
    lane = iota((half, LANES), 1)
    sides = []
    for side in range(2):
        columns = []
        for c in range(2):
            for t in range(TILES):
                line = totals[pl.ds(16 * side + c * 8 + t, half, stride=ROWS), :]
                if t == TILES - 1:
                    line = jnp.where(lane < BINS - t * LANES, line, 0.0)
                columns.append(line)
        sides.append(jnp.concatenate(columns, 1))
    high, low = split(jnp.concatenate(sides, 0))
    across = (((1,), (1,)), ((), ()))
    both = lax.dot_general(
        jnp.concatenate([high, low], 0), table[...], across,
        preferred_element_type=jnp.float32,
    )
    check = both[:leaves] + both[leaves:] + lax.dot_general(
        high, low_table[...], across, preferred_element_type=jnp.float32
    )
    check = (check[:half] * sign + check[half:] * other_sign)[:, :Q] * (1.0 / G)

    leaf_of = 2 * (lane & 7) + (lane >> 6)
    spread = jnp.where(iota((half, LANES), 0) == leaf_of, 1.0, 0.0)
    densities[...] = product(product(check, down_inverse[...], (1, 0)), spread, (0, 0))
    parts = [jnp.zeros((rows, LANES), jnp.float32)] * 4
    for q in range(Q):
        term = own[start + 8 * q : start + 8 * q + 8, :] * densities[q : q + 1, :]
        parts[q % 4] = parts[q % 4] + term
    return block_transpose((parts[0] + parts[1]) + (parts[2] + parts[3]))


def near_kernel(
    near_source, pair_ref, owner_ref, swapped, placed, passed, packed, own, totals, high_table,
    low_table, signs, down_inverse, counts, decay_rate, stress, potential, new_stress,
    table, merged, centers, factors, sums, densities,
):
    entries, leaves = near_source.shape
    half = leaves // 2
    rows = half // 2
    pair = pair_ref[0]
    low = iota((half, LANES), 1) < BCAP
    far = evaluate(pair, totals, high_table, low_table, signs, down_inverse, own, densities)
    swapped_from = jnp.where(((owner_ref[0] & 1) ^ pair) == 1, 0, 2)
    for n, rows_of in ((swapped_from, swapped), (1, placed), (2 - swapped_from, passed)):
        first = n * (leaves * 8)
        for ch in range(4):
            beads = rows_of[ch * half : (ch + 1) * half, :]
            turned = pltpu.roll(beads, BCAP, 1)
            table[pl.ds(first + ch, half, stride=16), :] = jnp.where(low, beads, turned)
            table[pl.ds(first + 8 + ch, half, stride=16), :] = jnp.where(low, turned, beads)
    low = iota((rows, LANES), 1) < BCAP
    for ch in range(3):
        center = per_leaf(packed[4 * half + ch : 4 * half + ch + 1, :], rows, pair * half)
        turned = pltpu.roll(center, BCAP, 1)
        centers[pl.ds(ch, rows, stride=16), :] = jnp.where(low, center, turned)
        centers[pl.ds(8 + ch, rows, stride=16), :] = jnp.where(low, turned, center)
    pairs = entries // 2
    one, zero = jnp.ones((pairs, LANES), jnp.float32), jnp.zeros((pairs, LANES), jnp.float32)

    def prepare(t):
        leaf = pair * half + t
        start = t * pairs * 8
        for n in range(pairs):
            left = pl.multiple_of(near_source[2 * n, leaf] * 8, 8)
            right = pl.multiple_of(near_source[2 * n + 1, leaf] * 8, 8)
            merged[pl.ds(start + n * 8, 8), :] = jnp.where(
                low, table[pl.ds(left, 8), :], table[pl.ds(right, 8), :]
            )
        place = t * 8
        x, y, z = [
            merged[pl.ds(start + ch, pairs, stride=8), :] - centers[pl.ds(place + ch, 1), :]
            for ch in range(3)
        ]
        pieces = [thirds(v) for v in (x, y, z, x * x + y * y + z * z)]
        lines = [piece[0] for piece in pieces] + [one]
        lines += [piece[1] for piece in pieces] + [piece[2] for piece in pieces] + [zero] * 3
        start = t * pairs * 16
        for row, values in enumerate(lines):
            factors[pl.ds(start + row, pairs, stride=16), :] = values

    for t in range(half):
        prepare(t)

    def one_leaf(t, carry):
        line = pl.multiple_of(half // 8 * Q + 8 * Q + t * BCAP, 8)
        mine = own[pl.ds(line, BCAP), :48].astype(jnp.bfloat16)
        total = jnp.zeros((BCAP, LANES), jnp.float32)
        for n in range(0, pairs, 2):
            start = pl.multiple_of((t * pairs + n) * 16, 16)
            both = jnp.concatenate(
                [factors[pl.ds(start, 16), :], factors[pl.ds(start + 16, 16), :]], 1
            ).astype(jnp.bfloat16)
            squared = jnp.dot(
                mine, jnp.concatenate([both] * 3, 0), preferred_element_type=jnp.float32
            )
            for side in range(2):
                weight = merged[pl.ds((t * pairs + n + side) * 8 + 3, 1), :]
                total = total + lax.rsqrt(squared[:, side * LANES : (side + 1) * LANES]) * weight
        sums[pl.ds(pl.multiple_of(t * BCAP, 8), BCAP), :] = total
        return carry

    lax.fori_loop(0, half, one_leaf, 0, unroll=4)
    for r in range(rows):
        block = sums[r * LANES : (r + 1) * LANES, :].T
        potential[r : r + 1, :] = jnp.sum(block, axis=0, keepdims=True)
    combined = potential[...] + far
    beads = per_leaf(counts[...].astype(jnp.float32), rows, pair * half)
    slot = iota((rows, LANES), 1) & (BCAP - 1)
    occupied = slot.astype(jnp.float32) < beads
    decay = per_leaf(decay_rate[...], rows)
    potential[...] = jnp.where(occupied, combined, 0.0)
    new_stress[...] = jnp.where(occupied, decay * stress[...] + combined, 0.0)


VMEM = pl.BlockSpec(memory_space=pltpu.VMEM)
SMEM = pl.BlockSpec(memory_space=pltpu.SMEM)
ANY = pl.BlockSpec(memory_space=pl.ANY)
MIB = 1024 * 1024


def call(kernel, outs, in_specs, scratch=(), limit=40, grid=(), flops=0, bytes_accessed=0):
    return pl.pallas_call(
        kernel,
        out_shape=outs,
        grid=grid,
        in_specs=in_specs,
        out_specs=jax.tree.map(lambda _: VMEM, outs),
        scratch_shapes=list(scratch),
        compiler_params=pltpu.CompilerParams(vmem_limit_bytes=limit * MIB),
        cost_estimate=pl.CostEstimate(
            flops=flops, bytes_accessed=bytes_accessed, transcendentals=0
        ),
    )


def body(
    offsets,
    charges,
    stress,
    decay_rate,
    morton_keys,
    levels,
    bead_counts,
    send_boxes,
    m2l_source,
    m2l_type,
    m2l_count,
    near_source,
    up_inverse,
    down_inverse,
    translations,
):
    f32 = jnp.float32
    leaves = morton_keys.shape[0]
    half = leaves // 2
    parts = lax.axis_size("wide") * lax.axis_size("narrow")
    table = jnp.asarray(transform_table())
    signs = jnp.asarray(sign_rows())
    pair = lax.axis_index("pair").reshape(1)
    owner = (
        lax.axis_index("wide") * lax.axis_size("narrow") + lax.axis_index("narrow")
    ).reshape(1)
    kind_count = translations.shape[0]

    other_translations = lax.ppermute(translations, "pair", [(0, 1), (1, 0)])
    packed, blocks, placed, sources, kinds = call(
        functools.partial(pack_kernel, kind_count),
        [
            jax.ShapeDtypeStruct((4 * half + 8, LANES), f32),
            jax.ShapeDtypeStruct((8 * parts, LANES), f32),
            jax.ShapeDtypeStruct((4 * half, LANES), f32),
            jax.ShapeDtypeStruct(m2l_source.shape, jnp.int32),
            jax.ShapeDtypeStruct(m2l_type.shape, jnp.int32),
        ],
        [VMEM] * 9,
        limit=62,
    )(
        offsets, charges.reshape(half, LANES), morton_keys.reshape(1, leaves),
        levels.reshape(1, leaves), bead_counts.reshape(1, leaves), send_boxes,
        m2l_source, m2l_type, m2l_count.reshape(1, leaves),
    )
    arrived = lax.all_to_all(
        blocks.reshape(parts, 8, LANES), PARTS, split_axis=0, concat_axis=0, tiled=True
    ).reshape(8 * parts, LANES)
    swaps = [(2 * d, 2 * (d ^ 1)) for d in range(parts)]
    for d in range(1, parts - 1, 2):
        swaps += [(2 * d + 1, 2 * d + 3), (2 * d + 3, 2 * d + 1)]
    swapped = lax.ppermute(placed, PARTS + ("pair",), swaps)
    own = call(
        own_kernel,
        jax.ShapeDtypeStruct((leaves // 16 * Q + 8 * Q + half * BCAP, LANES), f32),
        [SMEM, VMEM],
        [
            pltpu.VMEM((leaves // 16, Q * 8, LANES), f32),
            pltpu.VMEM((half // 2 * 48, LANES), f32),
        ],
        limit=16,
        flops=4 * 10**10,
    )(pair, packed)
    passed = lax.ppermute(swapped, "pair", [(0, 1), (1, 0)])

    last = pl.BlockSpec((kind_count, 2, LANES), lambda i: (0, 0, TILES - 1))
    totals, low_table = call(
        far_kernel,
        [
            jax.ShapeDtypeStruct((half * ROWS, LANES), f32),
            jax.ShapeDtypeStruct(table.shape, table.dtype),
        ],
        [SMEM] * 3 + [VMEM] * 4 + [last] * 2 + [ANY] * 3,
        [
            pltpu.VMEM(((leaves + 2 * parts) * ROWS, LANES), f32),
            pltpu.VMEM((kind_count + 1, ROWS, LANES), f32),
            pltpu.VMEM(table.shape, jnp.bfloat16),
            pltpu.VMEM((leaves + 2 * parts, QPAD), f32),
            pltpu.VMEM(((leaves + 2 * parts) // 16, Q, LANES), f32),
            pltpu.VMEM((Q * 8, LANES), f32),
            pltpu.SemaphoreType.DMA((2 * TILES + 1,)),
        ],
        limit=24,
        grid=(1,),
        flops=10**10,
        bytes_accessed=4 * 10**6,
    )(
        sources, kinds, pair, arrived, own, up_inverse, signs, translations,
        other_translations, table, translations, other_translations,
    )

    out = jax.ShapeDtypeStruct((half // 2, LANES), f32)
    potential, new_stress = call(
        near_kernel,
        [out, out],
        [SMEM] * 3 + [VMEM] * 13,
        [
            pltpu.VMEM((3 * leaves * 8, LANES), f32),
            pltpu.VMEM((half * near_source.shape[1] // 2 * 8, LANES), f32),
            pltpu.VMEM((half * 8, LANES), f32),
            pltpu.VMEM((half * near_source.shape[1] // 2 * 16, LANES), f32),
            pltpu.VMEM((half * BCAP, LANES), f32),
            pltpu.VMEM((Q, LANES), f32),
        ],
        limit=16,
    )(
        near_source.T, pair, owner, swapped, placed, passed, packed, own, totals, table, low_table,
        signs, down_inverse, bead_counts.reshape(1, leaves), decay_rate.reshape(1, half),
        stress.reshape(half // 2, LANES),
    )
    return potential.reshape(-1), new_stress.reshape(-1)


def solution(mesh):
    return jax.shard_map(
        body,
        mesh=mesh,
        in_specs=(
            P(None, ("groups", "wide", "narrow")),
            P(("groups", "wide", "narrow")),
            P(("groups", "wide", "narrow", "pair")),
            P(("groups", "wide", "narrow", "pair")),
            P(("groups", "wide", "narrow")),
            P(("groups", "wide", "narrow")),
            P(("groups", "wide", "narrow")),
            P(("groups", "wide", "narrow"), None),
            P(("groups", "wide", "narrow"), None),
            P(("groups", "wide", "narrow"), None),
            P(("groups", "wide", "narrow")),
            P(("groups", "wide", "narrow"), None),
            P(),
            P(),
            P(None, None, "pair"),
        ),
        out_specs=(
            P(("groups", "wide", "narrow", "pair")),
            P(("groups", "wide", "narrow", "pair")),
        ),
        check_vma=False,
    )
```

```python
import functools

import jax
import jax.numpy as jnp
import ml_dtypes
import numpy as np
from jax import lax
from jax.experimental import pallas as pl
from jax.experimental.pallas import tpu as pltpu
from jax.sharding import PartitionSpec as P

PGRID = 12
G = 1728
MAXL = 10
BCAP = 64
Q = 152
QPAD = 160
LANES = 128
BINS = 864
TILES = 7
ROWS = 32
softening = 0.04
surface_reach = 1.25
CELLS = [
    (i, j, k)
    for i in range(6)
    for j in range(6)
    for k in range(6)
    if 0 in (i, j, k) or 5 in (i, j, k)
]
PARTS = ("wide", "narrow")


def transform_table():
    cells = np.array(CELLS)
    bins = np.arange(BINS)
    freq = np.stack([bins // 144, bins // 12 % 12, bins % 12])
    angle = (cells @ freq % PGRID) * (2.0 * np.pi / PGRID)
    table = np.zeros((QPAD, 2 * TILES * LANES))
    table[:Q, :BINS] = np.cos(angle)
    table[:Q, TILES * LANES : TILES * LANES + BINS] = -np.sin(angle)
    table[np.abs(table) < 1e-9] = 0.0
    return table.astype(ml_dtypes.bfloat16)


def low_part(high):
    root = np.sqrt(0.75)
    held = float(np.asarray(root).astype(ml_dtypes.bfloat16))
    scale = (root - held) / (held * (held * held - 1.0) * (held * held - 0.25))
    value = high.astype(jnp.float32)
    square = value * value
    return (value * (square - 1.0) * (square - 0.25) * scale).astype(jnp.bfloat16)


def sign_rows():
    rows = np.zeros((8, QPAD), np.float32)
    rows[0, :Q] = 1.0
    rows[1, :Q] = [(-1.0) ** i for i, _, _ in CELLS]
    return rows


def iota(shape, dim):
    return lax.broadcasted_iota(jnp.int32, shape, dim)


def per_leaf(values, count, first=0):
    shape = (count, values.shape[1])
    leaf, lane = first + 2 * iota(shape, 0), iota(shape, 1)
    even = jnp.sum(jnp.where(lane == leaf, values, 0.0), axis=1, keepdims=True)
    odd = jnp.sum(jnp.where(lane == leaf + 1, values, 0.0), axis=1, keepdims=True)
    return jnp.where(iota((count, LANES), 1) < BCAP, even, odd)


def block_transpose(x):
    lane, row = iota(x.shape, 1), iota(x.shape, 0)
    for k in (1, 2, 4):
        row_bit, lane_bit = (row & k) != 0, (lane & k) != 0
        below = pltpu.roll(pltpu.roll(x, 8 - k, 0), k, 1)
        above = pltpu.roll(pltpu.roll(x, k, 0), LANES - k, 1)
        x = jnp.where(row_bit == lane_bit, x, jnp.where(lane_bit, below, above))
    return x


def split(x):
    high = x.astype(jnp.bfloat16)
    return high, (x - high.astype(jnp.float32)).astype(jnp.bfloat16)


def thirds(x):
    high = x.astype(jnp.bfloat16).astype(jnp.float32)
    rest = x - high
    middle = rest.astype(jnp.bfloat16).astype(jnp.float32)
    return high, middle, rest - middle


def product(a, b, contract):
    dims = (((contract[0],), (contract[1],)), ((), ()))
    (a_high, a_low), (b_high, b_low) = split(a), split(b)

    def dot(x, y):
        return lax.dot_general(x, y, dims, preferred_element_type=jnp.float32)

    return dot(a_high, b_high) + (dot(a_low, b_high) + dot(a_high, b_low))


def axis_squares(offset, width):
    area = width * width
    planes = [surface_reach * 0.5 * (i - 2.5) / 2.5 for i in range(6)]
    return [(plane - offset) * (plane - offset) * area for plane in planes]


def surface_kernels(offsets, width):
    gx, gy, gz = [axis_squares(offset, width) for offset in offsets]
    gz = [g + softening for g in gz]
    last, gxy = None, None
    for q, (i, j, k) in enumerate(CELLS):
        if last != (i, j):
            last, gxy = (i, j), gx[i] + gy[j]
        yield q, lax.rsqrt(gxy + gz[k])


def check_sums(offsets, weights, width, checks):
    offsets = [block_transpose(x) for x in offsets]
    weights, width = block_transpose(weights), block_transpose(width)
    for q, kernel in surface_kernels(offsets, width):
        checks[pl.ds(8 * q, 8), :] = kernel * weights
    check = checks[pl.ds(0, Q, stride=8), :]
    for s in range(1, 8):
        check = check + checks[pl.ds(s, Q, stride=8), :]
    return check


def upward(check, up_inverse):
    density = product(check, up_inverse, (0, 0))
    blocks = check.shape[1] // LANES
    density = density.reshape(2 * blocks, 8, 8, Q)
    total = density[:, 0]
    for g in range(1, 8):
        total = total + density[:, g]
    return total.reshape(16 * blocks, Q)


def store_spectra(density, table_high, table_low, target):
    count = density.shape[0] // 2
    high, low = split(density)
    both = jnp.concatenate([high, low], 0)
    for first in range(0, 2 * TILES, 2):
        columns = pl.ds(first * LANES, 2 * LANES)
        part = jnp.dot(both, table_high[:, columns], preferred_element_type=jnp.float32)
        spectra = part[: 2 * count] + part[2 * count :] + jnp.dot(
            high, table_low[:, columns], preferred_element_type=jnp.float32
        )
        for tile in range(first, first + 2):
            for side in range(2):
                for block in range(count // 16):
                    for h in range(2):
                        row = side * count + block * 16 + h * 8
                        start = (block * 16 + h) * ROWS + 16 * side + 8 * (tile // TILES) + tile % TILES
                        target[pl.ds(start, 8, stride=2 * ROWS), :] = spectra[
                            row : row + 8, (tile - first) * LANES : (tile - first + 1) * LANES
                        ]


def pack_kernel(
    kind_count, offsets, charges, keys, levels, counts, send_boxes, m2l_source, m2l_type, m2l_count,
    out, blocks, placed, sources, kinds,
):
    leaves = keys.shape[1]
    half = leaves // 2
    out[4 * half :, :] = jnp.zeros((8, LANES), jnp.float32)
    width = jnp.left_shift(jnp.ones_like(levels[...]), MAXL - levels[...]).astype(jnp.float32)
    for a in range(3):
        summed = jnp.zeros_like(keys[...])
        for bit in range(MAXL):
            summed = summed + (jnp.right_shift(keys[...], 3 * bit + a) & 1) * (1 << bit)
        out[4 * half + a : 4 * half + a + 1, :leaves] = summed.astype(jnp.float32) + 0.5 * width
    out[4 * half + 3 : 4 * half + 4, :leaves] = width
    for r in range(half):
        out[pl.ds(r, 3, stride=half), :] = offsets[:, r * LANES : (r + 1) * LANES]
    beads = per_leaf(counts[...].astype(jnp.float32), half)
    slot = iota((half, LANES), 1) & (BCAP - 1)
    out[3 * half : 4 * half, :] = jnp.where(slot.astype(jnp.float32) < beads, charges[...], 0.0)

    entry = iota(m2l_type.shape, 1)
    square = (leaves, leaves)
    live = jnp.sum(
        jnp.where(iota(square, 0) == iota(square, 1), m2l_count[...].astype(jnp.float32), 0.0),
        axis=1, keepdims=True,
    )
    kinds[...] = jnp.where(entry.astype(jnp.float32) < live, m2l_type[...], kind_count)
    sources[...] = m2l_source[...] * ROWS

    spread = per_leaf(width, half)
    for ch in range(3):
        center = per_leaf(out[4 * half + ch : 4 * half + ch + 1, :leaves], half)
        placed[ch * half : (ch + 1) * half, :] = center + spread * out[ch * half : (ch + 1) * half, :]
    placed[3 * half :, :] = out[3 * half : 4 * half, :]

    sends = send_boxes.shape[1]
    lane = iota((8, LANES), 1)
    for block in range(sends // 16):
        picked = []
        for c in range(2):
            column = block * 16 + 2 * iota((8, sends), 0) + c
            box = jnp.sum(
                jnp.where(iota((8, sends), 1) == column, send_boxes[...].astype(jnp.float32), 0.0),
                axis=1, keepdims=True,
            ).astype(jnp.int32)
            width_here = jnp.sum(
                jnp.where(iota((8, leaves), 1) == box, width, 0.0), axis=1, keepdims=True
            )
            row_of = jnp.broadcast_to(box >> 1, (8, LANES))
            found = [jnp.zeros((8, LANES), jnp.float32)] * 4
            for r in range(half):
                here = row_of == r
                for ch in range(4):
                    found[ch] = jnp.where(here, out[ch * half + r : ch * half + r + 1, :], found[ch])
            aligned = jnp.broadcast_to((box & 1) == c, (8, LANES))
            found = [jnp.where(aligned, x, pltpu.roll(x, BCAP, 1)) for x in found]
            picked.append(found + [jnp.broadcast_to(width_here, (8, LANES))])
        for ch in range(5):
            blocks[pl.ds(block * 64 + ch, 8, stride=8), :] = jnp.where(
                lane < BCAP, picked[0][ch], picked[1][ch]
            )
        for ch in range(5, 8):
            blocks[pl.ds(block * 64 + ch, 8, stride=8), :] = jnp.zeros((8, LANES), jnp.float32)


def target_terms(pair, packed, stacked, terms, start):
    half = (packed.shape[0] - 8) // 4
    rows = half // 2
    width = per_leaf(packed[4 * half + 3 : 4 * half + 4, :], rows, pair * half)
    places = [
        width * packed[pl.ds(pl.multiple_of(c * half + pair * rows, 8), rows), :] for c in range(3)
    ]
    norm = places[0] * places[0] + places[1] * places[1] + (places[2] * places[2] + softening)
    pieces = [thirds(-2.0 * x) for x in places]
    norms = thirds(norm)
    one, zero = jnp.ones((rows, LANES), jnp.float32), jnp.zeros((rows, LANES), jnp.float32)
    for third in range(3):
        x, y, z = [piece[third] for piece in pieces]
        unit = one if third == 0 else zero
        first = [x, y, z, unit, norms[third]]
        second = [x, y, z, unit] if third < 2 else [zero] * 4
        last = [x, y, z, unit] if third < 1 else [zero] * 4
        for row, values in enumerate(first + second + last + [zero] * 3):
            stacked[pl.ds(16 * third + row, rows, stride=48), :] = values
    for r in range(rows):
        line = start + r * LANES
        terms[line : line + LANES, :48] = stacked[48 * r : 48 * (r + 1), :].T


def own_kernel(packed, out, checks, stacked):
    half = (packed.shape[0] - 8) // 4
    rows = half // 2
    pair = lax.axis_index("pair")
    width = per_leaf(packed[4 * half + 3 : 4 * half + 4, :], half)
    for block in range(half // 8):
        beads = [packed[c * half + block * 8 : c * half + block * 8 + 8, :] for c in range(4)]
        out[block * Q : (block + 1) * Q, :] = check_sums(
            beads[:3], beads[3], width[block * 8 : block * 8 + 8], checks.at[block]
        )
    width = block_transpose(
        per_leaf(packed[4 * half + 3 : 4 * half + 4, :], rows, pair * half)
    )
    offsets = [
        block_transpose(packed[pl.ds(pl.multiple_of(c * half + pair * rows, 8), rows), :])
        for c in range(3)
    ]
    first = half // 8 * Q
    for q, kernel in surface_kernels(offsets, width):
        out[first + 8 * q : first + 8 * q + 8, :] = kernel
    target_terms(pair, packed, stacked, out, first + 8 * Q)


def far_kernel(
    sources, kinds, pair_ref, arrived, own_check, up_inverse, signs,
    last_bins, other_last_bins, table, translations, other_translations, totals, low_table,
    spectra, kernels, high_table, density, check, checks, sems,
):
    leaves, entries = sources.shape
    half = leaves // 2
    blocks = arrived.shape[0] // 64
    kind_count = translations.shape[0]
    pair = pair_ref[0]

    table_copy = pltpu.make_async_copy(table, high_table, sems.at[0])
    table_copy.start()
    kernel_copies = []
    for side, bins in enumerate((translations, other_translations)):
        for t in range(TILES - 1):
            kernel_copies.append(pltpu.make_async_copy(
                bins.at[:, :, pl.ds(t * LANES, LANES)],
                kernels.at[pl.ds(0, kind_count), pl.ds(16 * side + 2 * t, 2), :],
                sems.at[1 + len(kernel_copies)],
            ))
        kernel_copies.append(pltpu.make_async_copy(
            (last_bins, other_last_bins)[side],
            kernels.at[pl.ds(0, kind_count), pl.ds(16 * side + 2 * TILES - 2, 2), :],
            sems.at[1 + len(kernel_copies)],
        ))
    for copy in kernel_copies:
        copy.start()
    kernels[kind_count] = jnp.zeros((ROWS, LANES), jnp.float32)

    density[...] = jnp.zeros(density.shape, jnp.float32)
    for block in range(leaves // 16):
        check[block, :, :] = own_check[block * Q : (block + 1) * Q, :]

    def arrive(block, carry):
        beads = [
            arrived[pl.ds(pl.multiple_of(block * 64, 64) + ch, 8, stride=8), :] for ch in range(5)
        ]
        check[leaves // 16 + block, :, :] = check_sums(beads[:3], beads[3], beads[4], checks)
        return carry

    if blocks == 1:
        arrive(0, 0)
    else:
        lax.fori_loop(0, blocks, arrive, 0)
    count = check.shape[0]
    for first in range(0, count, 3):
        some = range(first, min(first + 3, count))
        density[16 * first : 16 * first + 16 * len(some), :Q] = upward(
            jnp.concatenate([check[n] for n in some], 1), up_inverse[...]
        )
    table_copy.wait()
    low_table[...] = low_part(high_table[...])
    sign = jnp.where(pair == 1, signs[1:2, :], signs[0:1, :])
    other_sign = jnp.where(pair == 1, signs[0:1, :], signs[1:2, :])
    store_spectra(
        jnp.concatenate([density[...] * sign, density[...] * other_sign], 0),
        high_table, low_table, spectra,
    )
    for copy in kernel_copies:
        copy.wait()

    def translate(t, carry):
        leaf = pair * half + t
        sums = [[None] * 4, [None] * 4]
        for entry in range(entries):
            kind = kinds[leaf, entry]
            start = pl.multiple_of(sources[leaf, entry], ROWS)
            for side in range(2):
                k_re = kernels[kind, pl.ds(16 * side, 8, stride=2), :]
                k_im = kernels[kind, pl.ds(16 * side + 1, 8, stride=2), :]
                s_re = spectra[pl.ds(start + 16 * side, 8), :]
                s_im = spectra[pl.ds(start + 16 * side + 8, 8), :]
                terms = (k_re * s_re, k_im * s_im, k_re * s_im, k_im * s_re)
                for n, term in enumerate(terms):
                    sums[side][n] = term if sums[side][n] is None else sums[side][n] + term
        start = pl.multiple_of(t * ROWS, ROWS)
        for side in range(2):
            rr, ii, ri, ir = sums[side]
            totals[pl.ds(start + 16 * side, 8), :] = rr - ii
            totals[pl.ds(start + 16 * side + 8, 8), :] = ri + ir
        return carry

    lax.fori_loop(0, half, translate, 0, unroll=4)


def evaluate(pair, totals, table, low_table, signs, down_inverse, own, densities):
    half = totals.shape[0] // ROWS
    leaves = 2 * half
    rows = half // 2
    start = half // 8 * Q
    sign = jnp.where(pair == 1, signs[1:2, :], signs[0:1, :])
    other_sign = jnp.where(pair == 1, signs[0:1, :], signs[1:2, :])
    lane = iota((half, LANES), 1)
    sides = []
    for side in range(2):
        columns = []
        for c in range(2):
            for t in range(TILES):
                line = totals[pl.ds(16 * side + c * 8 + t, half, stride=ROWS), :]
                if t == TILES - 1:
                    line = jnp.where(lane < BINS - t * LANES, line, 0.0)
                columns.append(line)
        sides.append(jnp.concatenate(columns, 1))
    high, low = split(jnp.concatenate(sides, 0))
    across = (((1,), (1,)), ((), ()))
    both = lax.dot_general(
        jnp.concatenate([high, low], 0), table[...], across,
        preferred_element_type=jnp.float32,
    )
    check = both[:leaves] + both[leaves:] + lax.dot_general(
        high, low_table[...], across, preferred_element_type=jnp.float32
    )
    check = (check[:half] * sign + check[half:] * other_sign)[:, :Q] * (1.0 / G)

    leaf_of = 2 * (lane & 7) + (lane >> 6)
    spread = jnp.where(iota((half, LANES), 0) == leaf_of, 1.0, 0.0)
    densities[...] = product(product(check, down_inverse[...], (1, 0)), spread, (0, 0))
    parts = [jnp.zeros((rows, LANES), jnp.float32)] * 4
    for q in range(Q):
        term = own[start + 8 * q : start + 8 * q + 8, :] * densities[q : q + 1, :]
        parts[q % 4] = parts[q % 4] + term
    return block_transpose((parts[0] + parts[1]) + (parts[2] + parts[3]))


def near_kernel(
    near_source, pair_ref, owner_ref, swapped, placed, passed, packed, own, totals, high_table,
    low_table, signs, down_inverse, counts, decay_rate, stress, potential, new_stress,
    table, merged, centers, factors, sums, densities,
):
    entries, leaves = near_source.shape
    half = leaves // 2
    rows = half // 2
    pair = pair_ref[0]
    low = iota((half, LANES), 1) < BCAP
    far = evaluate(pair, totals, high_table, low_table, signs, down_inverse, own, densities)
    swapped_from = jnp.where(((owner_ref[0] & 1) ^ pair) == 1, 0, 2)
    for n, rows_of in ((swapped_from, swapped), (1, placed), (2 - swapped_from, passed)):
        first = n * (leaves * 8)
        for ch in range(4):
            beads = rows_of[ch * half : (ch + 1) * half, :]
            turned = pltpu.roll(beads, BCAP, 1)
            table[pl.ds(first + ch, half, stride=16), :] = jnp.where(low, beads, turned)
            table[pl.ds(first + 8 + ch, half, stride=16), :] = jnp.where(low, turned, beads)
    low = iota((rows, LANES), 1) < BCAP
    for ch in range(3):
        center = per_leaf(packed[4 * half + ch : 4 * half + ch + 1, :], rows, pair * half)
        turned = pltpu.roll(center, BCAP, 1)
        centers[pl.ds(ch, rows, stride=16), :] = jnp.where(low, center, turned)
        centers[pl.ds(8 + ch, rows, stride=16), :] = jnp.where(low, turned, center)
    pairs = entries // 2
    one, zero = jnp.ones((pairs, LANES), jnp.float32), jnp.zeros((pairs, LANES), jnp.float32)

    def prepare(t):
        leaf = pair * half + t
        start = t * pairs * 8
        for n in range(pairs):
            left = pl.multiple_of(near_source[2 * n, leaf] * 8, 8)
            right = pl.multiple_of(near_source[2 * n + 1, leaf] * 8, 8)
            merged[pl.ds(start + n * 8, 8), :] = jnp.where(
                low, table[pl.ds(left, 8), :], table[pl.ds(right, 8), :]
            )
        place = t * 8
        x, y, z = [
            merged[pl.ds(start + ch, pairs, stride=8), :] - centers[pl.ds(place + ch, 1), :]
            for ch in range(3)
        ]
        pieces = [thirds(v) for v in (x, y, z, x * x + y * y + z * z)]
        lines = [piece[0] for piece in pieces] + [one]
        lines += [piece[1] for piece in pieces] + [piece[2] for piece in pieces] + [zero] * 3
        start = t * pairs * 16
        for row, values in enumerate(lines):
            factors[pl.ds(start + row, pairs, stride=16), :] = values

    for t in range(half):
        prepare(t)

    def one_leaf(t, carry):
        line = pl.multiple_of(half // 8 * Q + 8 * Q + t * BCAP, 8)
        mine = own[pl.ds(line, BCAP), :48].astype(jnp.bfloat16)
        total = jnp.zeros((BCAP, LANES), jnp.float32)
        for n in range(0, pairs, 2):
            start = pl.multiple_of((t * pairs + n) * 16, 16)
            both = jnp.concatenate(
                [factors[pl.ds(start, 16), :], factors[pl.ds(start + 16, 16), :]], 1
            ).astype(jnp.bfloat16)
            squared = jnp.dot(
                mine, jnp.concatenate([both] * 3, 0), preferred_element_type=jnp.float32
            )
            for side in range(2):
                weight = merged[pl.ds((t * pairs + n + side) * 8 + 3, 1), :]
                total = total + lax.rsqrt(squared[:, side * LANES : (side + 1) * LANES]) * weight
        sums[pl.ds(pl.multiple_of(t * BCAP, 8), BCAP), :] = total
        return carry

    lax.fori_loop(0, half, one_leaf, 0, unroll=4)
    for r in range(rows):
        block = sums[r * LANES : (r + 1) * LANES, :].T
        potential[r : r + 1, :] = jnp.sum(block, axis=0, keepdims=True)
    combined = potential[...] + far
    beads = per_leaf(counts[...].astype(jnp.float32), rows, pair * half)
    slot = iota((rows, LANES), 1) & (BCAP - 1)
    occupied = slot.astype(jnp.float32) < beads
    decay = per_leaf(decay_rate[...], rows)
    potential[...] = jnp.where(occupied, combined, 0.0)
    new_stress[...] = jnp.where(occupied, decay * stress[...] + combined, 0.0)


VMEM = pl.BlockSpec(memory_space=pltpu.VMEM)
SMEM = pl.BlockSpec(memory_space=pltpu.SMEM)
ANY = pl.BlockSpec(memory_space=pl.ANY)
MIB = 1024 * 1024


def call(kernel, outs, in_specs, scratch=(), limit=40, grid=(), flops=0, bytes_accessed=0):
    return pl.pallas_call(
        kernel,
        out_shape=outs,
        grid=grid,
        in_specs=in_specs,
        out_specs=jax.tree.map(lambda _: VMEM, outs),
        scratch_shapes=list(scratch),
        compiler_params=pltpu.CompilerParams(vmem_limit_bytes=limit * MIB),
        cost_estimate=pl.CostEstimate(
            flops=flops, bytes_accessed=bytes_accessed, transcendentals=0
        ),
    )


def body(
    offsets,
    charges,
    stress,
    decay_rate,
    morton_keys,
    levels,
    bead_counts,
    send_boxes,
    m2l_source,
    m2l_type,
    m2l_count,
    near_source,
    up_inverse,
    down_inverse,
    translations,
):
    f32 = jnp.float32
    leaves = morton_keys.shape[0]
    half = leaves // 2
    parts = lax.axis_size("wide") * lax.axis_size("narrow")
    table = jnp.asarray(transform_table())
    signs = jnp.asarray(sign_rows())
    pair = lax.axis_index("pair").reshape(1)
    owner = (
        lax.axis_index("wide") * lax.axis_size("narrow") + lax.axis_index("narrow")
    ).reshape(1)
    kind_count = translations.shape[0]

    other_translations = lax.ppermute(translations, "pair", [(0, 1), (1, 0)])
    packed, blocks, placed, sources, kinds = call(
        functools.partial(pack_kernel, kind_count),
        [
            jax.ShapeDtypeStruct((4 * half + 8, LANES), f32),
            jax.ShapeDtypeStruct((8 * parts, LANES), f32),
            jax.ShapeDtypeStruct((4 * half, LANES), f32),
            jax.ShapeDtypeStruct(m2l_source.shape, jnp.int32),
            jax.ShapeDtypeStruct(m2l_type.shape, jnp.int32),
        ],
        [VMEM] * 9,
        limit=62,
    )(
        offsets, charges.reshape(half, LANES), morton_keys.reshape(1, leaves),
        levels.reshape(1, leaves), bead_counts.reshape(1, leaves), send_boxes,
        m2l_source, m2l_type, m2l_count.reshape(1, leaves),
    )
    arrived = lax.all_to_all(
        blocks.reshape(parts, 8, LANES), PARTS, split_axis=0, concat_axis=0, tiled=True
    ).reshape(8 * parts, LANES)
    swaps = [(2 * d, 2 * (d ^ 1)) for d in range(parts)]
    for d in range(1, parts - 1, 2):
        swaps += [(2 * d + 1, 2 * d + 3), (2 * d + 3, 2 * d + 1)]
    swapped = lax.ppermute(placed, PARTS + ("pair",), swaps)
    own = call(
        own_kernel,
        jax.ShapeDtypeStruct((leaves // 16 * Q + 8 * Q + half * BCAP, LANES), f32),
        [VMEM],
        [
            pltpu.VMEM((leaves // 16, Q * 8, LANES), f32),
            pltpu.VMEM((half // 2 * 48, LANES), f32),
        ],
        limit=16,
        flops=4 * 10**10,
    )(packed)
    passed = lax.ppermute(swapped, "pair", [(0, 1), (1, 0)])

    last = pl.BlockSpec((kind_count, 2, LANES), lambda i: (0, 0, TILES - 1))
    totals, low_table = call(
        far_kernel,
        [
            jax.ShapeDtypeStruct((half * ROWS, LANES), f32),
            jax.ShapeDtypeStruct(table.shape, table.dtype),
        ],
        [SMEM] * 3 + [VMEM] * 4 + [last] * 2 + [ANY] * 3,
        [
            pltpu.VMEM(((leaves + 2 * parts) * ROWS, LANES), f32),
            pltpu.VMEM((kind_count + 1, ROWS, LANES), f32),
            pltpu.VMEM(table.shape, jnp.bfloat16),
            pltpu.VMEM((leaves + 2 * parts, QPAD), f32),
            pltpu.VMEM(((leaves + 2 * parts) // 16, Q, LANES), f32),
            pltpu.VMEM((Q * 8, LANES), f32),
            pltpu.SemaphoreType.DMA((2 * TILES + 1,)),
        ],
        limit=24,
        grid=(1,),
        flops=10**10,
        bytes_accessed=4 * 10**6,
    )(
        sources, kinds, pair, arrived, own, up_inverse, signs, translations,
        other_translations, table, translations, other_translations,
    )

    out = jax.ShapeDtypeStruct((half // 2, LANES), f32)
    potential, new_stress = call(
        near_kernel,
        [out, out],
        [SMEM] * 3 + [VMEM] * 13,
        [
            pltpu.VMEM((3 * leaves * 8, LANES), f32),
            pltpu.VMEM((half * near_source.shape[1] // 2 * 8, LANES), f32),
            pltpu.VMEM((half * 8, LANES), f32),
            pltpu.VMEM((half * near_source.shape[1] // 2 * 16, LANES), f32),
            pltpu.VMEM((half * BCAP, LANES), f32),
            pltpu.VMEM((Q, LANES), f32),
        ],
        limit=16,
    )(
        near_source.T, pair, owner, swapped, placed, passed, packed, own, totals, table, low_table,
        signs, down_inverse, bead_counts.reshape(1, leaves), decay_rate.reshape(1, half),
        stress.reshape(half // 2, LANES),
    )
    return potential.reshape(-1), new_stress.reshape(-1)


def solution(mesh):
    return jax.shard_map(
        body,
        mesh=mesh,
        in_specs=(
            P(None, ("groups", "wide", "narrow")),
            P(("groups", "wide", "narrow")),
            P(("groups", "wide", "narrow", "pair")),
            P(("groups", "wide", "narrow", "pair")),
            P(("groups", "wide", "narrow")),
            P(("groups", "wide", "narrow")),
            P(("groups", "wide", "narrow")),
            P(("groups", "wide", "narrow"), None),
            P(("groups", "wide", "narrow"), None),
            P(("groups", "wide", "narrow"), None),
            P(("groups", "wide", "narrow")),
            P(("groups", "wide", "narrow"), None),
            P(),
            P(),
            P(None, None, "pair"),
        ),
        out_specs=(
            P(("groups", "wide", "narrow", "pair")),
            P(("groups", "wide", "narrow", "pair")),
        ),
        check_vma=False,
    )
```

```python
import functools

import jax
import jax.numpy as jnp
import ml_dtypes
import numpy as np
from jax import lax
from jax.experimental import pallas as pl
from jax.experimental.pallas import tpu as pltpu
from jax.sharding import PartitionSpec as P

PGRID = 12
G = 1728
MAXL = 10
BCAP = 64
Q = 152
QPAD = 160
LANES = 128
BINS = 864
TILES = 7
ROWS = 32
softening = 0.04
surface_reach = 1.25
CELLS = [
    (i, j, k)
    for i in range(6)
    for j in range(6)
    for k in range(6)
    if 0 in (i, j, k) or 5 in (i, j, k)
]
PARTS = ("wide", "narrow")


def transform_table():
    cells = np.array(CELLS)
    bins = np.arange(BINS)
    freq = np.stack([bins // 144, bins // 12 % 12, bins % 12])
    angle = (cells @ freq % PGRID) * (2.0 * np.pi / PGRID)
    table = np.zeros((QPAD, 2 * TILES * LANES))
    table[:Q, :BINS] = np.cos(angle)
    table[:Q, TILES * LANES : TILES * LANES + BINS] = -np.sin(angle)
    table[np.abs(table) < 1e-9] = 0.0
    return table.astype(ml_dtypes.bfloat16)


def low_part(high):
    root = np.sqrt(0.75)
    held = float(np.asarray(root).astype(ml_dtypes.bfloat16))
    scale = (root - held) / (held * (held * held - 1.0) * (held * held - 0.25))
    value = high.astype(jnp.float32)
    square = value * value
    return (value * (square - 1.0) * (square - 0.25) * scale).astype(jnp.bfloat16)


def sign_rows():
    rows = np.zeros((8, QPAD), np.float32)
    rows[0, :Q] = 1.0
    rows[1, :Q] = [(-1.0) ** i for i, _, _ in CELLS]
    return rows


def iota(shape, dim):
    return lax.broadcasted_iota(jnp.int32, shape, dim)


def per_leaf(values, count, first=0):
    shape = (count, values.shape[1])
    leaf, lane = first + 2 * iota(shape, 0), iota(shape, 1)
    even = jnp.sum(jnp.where(lane == leaf, values, 0.0), axis=1, keepdims=True)
    odd = jnp.sum(jnp.where(lane == leaf + 1, values, 0.0), axis=1, keepdims=True)
    return jnp.where(iota((count, LANES), 1) < BCAP, even, odd)


def block_transpose(x):
    lane, row = iota(x.shape, 1), iota(x.shape, 0)
    for k in (1, 2, 4):
        row_bit, lane_bit = (row & k) != 0, (lane & k) != 0
        below = pltpu.roll(pltpu.roll(x, 8 - k, 0), k, 1)
        above = pltpu.roll(pltpu.roll(x, k, 0), LANES - k, 1)
        x = jnp.where(row_bit == lane_bit, x, jnp.where(lane_bit, below, above))
    return x


def split(x):
    high = x.astype(jnp.bfloat16)
    return high, (x - high.astype(jnp.float32)).astype(jnp.bfloat16)


def thirds(x):
    high = x.astype(jnp.bfloat16).astype(jnp.float32)
    rest = x - high
    middle = rest.astype(jnp.bfloat16).astype(jnp.float32)
    return high, middle, rest - middle


def product(a, b, contract):
    dims = (((contract[0],), (contract[1],)), ((), ()))
    (a_high, a_low), (b_high, b_low) = split(a), split(b)

    def dot(x, y):
        return lax.dot_general(x, y, dims, preferred_element_type=jnp.float32)

    return dot(a_high, b_high) + (dot(a_low, b_high) + dot(a_high, b_low))


def axis_squares(offset, width):
    area = width * width
    planes = [surface_reach * 0.5 * (i - 2.5) / 2.5 for i in range(6)]
    return [(plane - offset) * (plane - offset) * area for plane in planes]


def surface_kernels(offsets, width):
    gx, gy, gz = [axis_squares(offset, width) for offset in offsets]
    gz = [g + softening for g in gz]
    last, gxy = None, None
    for q, (i, j, k) in enumerate(CELLS):
        if last != (i, j):
            last, gxy = (i, j), gx[i] + gy[j]
        yield q, lax.rsqrt(gxy + gz[k])


def check_sums(offsets, weights, width, checks):
    offsets = [block_transpose(x) for x in offsets]
    weights, width = block_transpose(weights), block_transpose(width)
    for q, kernel in surface_kernels(offsets, width):
        checks[pl.ds(8 * q, 8), :] = kernel * weights
    check = checks[pl.ds(0, Q, stride=8), :]
    for s in range(1, 8):
        check = check + checks[pl.ds(s, Q, stride=8), :]
    return check


def upward(check, up_inverse):
    density = product(check, up_inverse, (0, 0))
    blocks = check.shape[1] // LANES
    density = density.reshape(2 * blocks, 8, 8, Q)
    total = density[:, 0]
    for g in range(1, 8):
        total = total + density[:, g]
    return total.reshape(16 * blocks, Q)


def store_spectra(density, table_high, table_low, target):
    count = density.shape[0] // 2
    high, low = split(density)
    both = jnp.concatenate([high, low], 0)
    for first in range(0, 2 * TILES, 2):
        columns = pl.ds(first * LANES, 2 * LANES)
        part = jnp.dot(both, table_high[:, columns], preferred_element_type=jnp.float32)
        spectra = part[: 2 * count] + part[2 * count :] + jnp.dot(
            high, table_low[:, columns], preferred_element_type=jnp.float32
        )
        for tile in range(first, first + 2):
            for side in range(2):
                for block in range(count // 16):
                    for h in range(2):
                        row = side * count + block * 16 + h * 8
                        start = (block * 16 + h) * ROWS + 16 * side + 8 * (tile // TILES) + tile % TILES
                        target[pl.ds(start, 8, stride=2 * ROWS), :] = spectra[
                            row : row + 8, (tile - first) * LANES : (tile - first + 1) * LANES
                        ]


def pack_kernel(
    kind_count, offsets, charges, keys, levels, counts, send_boxes, m2l_source, m2l_type, m2l_count,
    out, blocks, placed, sources, kinds,
):
    leaves = keys.shape[1]
    half = leaves // 2
    out[4 * half :, :] = jnp.zeros((8, LANES), jnp.float32)
    width = jnp.left_shift(jnp.ones_like(levels[...]), MAXL - levels[...]).astype(jnp.float32)
    for a in range(3):
        summed = jnp.zeros_like(keys[...])
        for bit in range(MAXL):
            summed = summed + (jnp.right_shift(keys[...], 3 * bit + a) & 1) * (1 << bit)
        out[4 * half + a : 4 * half + a + 1, :leaves] = summed.astype(jnp.float32) + 0.5 * width
    out[4 * half + 3 : 4 * half + 4, :leaves] = width
    for r in range(half):
        out[pl.ds(r, 3, stride=half), :] = offsets[:, r * LANES : (r + 1) * LANES]
    beads = per_leaf(counts[...].astype(jnp.float32), half)
    slot = iota((half, LANES), 1) & (BCAP - 1)
    out[3 * half : 4 * half, :] = jnp.where(slot.astype(jnp.float32) < beads, charges[...], 0.0)

    entry = iota(m2l_type.shape, 1)
    square = (leaves, leaves)
    live = jnp.sum(
        jnp.where(iota(square, 0) == iota(square, 1), m2l_count[...].astype(jnp.float32), 0.0),
        axis=1, keepdims=True,
    )
    kinds[...] = jnp.where(entry.astype(jnp.float32) < live, m2l_type[...], kind_count)
    sources[...] = m2l_source[...] * ROWS

    spread = per_leaf(width, half)
    for ch in range(3):
        center = per_leaf(out[4 * half + ch : 4 * half + ch + 1, :leaves], half)
        placed[ch * half : (ch + 1) * half, :] = center + spread * out[ch * half : (ch + 1) * half, :]
    placed[3 * half :, :] = out[3 * half : 4 * half, :]

    sends = send_boxes.shape[1]
    lane = iota((8, LANES), 1)
    for block in range(sends // 16):
        picked = []
        for c in range(2):
            column = block * 16 + 2 * iota((8, sends), 0) + c
            box = jnp.sum(
                jnp.where(iota((8, sends), 1) == column, send_boxes[...].astype(jnp.float32), 0.0),
                axis=1, keepdims=True,
            ).astype(jnp.int32)
            width_here = jnp.sum(
                jnp.where(iota((8, leaves), 1) == box, width, 0.0), axis=1, keepdims=True
            )
            row_of = jnp.broadcast_to(box >> 1, (8, LANES))
            found = [jnp.zeros((8, LANES), jnp.float32)] * 4
            for r in range(half):
                here = row_of == r
                for ch in range(4):
                    found[ch] = jnp.where(here, out[ch * half + r : ch * half + r + 1, :], found[ch])
            aligned = jnp.broadcast_to((box & 1) == c, (8, LANES))
            found = [jnp.where(aligned, x, pltpu.roll(x, BCAP, 1)) for x in found]
            picked.append(found + [jnp.broadcast_to(width_here, (8, LANES))])
        for ch in range(5):
            blocks[pl.ds(block * 64 + ch, 8, stride=8), :] = jnp.where(
                lane < BCAP, picked[0][ch], picked[1][ch]
            )
        for ch in range(5, 8):
            blocks[pl.ds(block * 64 + ch, 8, stride=8), :] = jnp.zeros((8, LANES), jnp.float32)


def own_kernel(packed, out, checks):
    half = (packed.shape[0] - 8) // 4
    width = per_leaf(packed[4 * half + 3 : 4 * half + 4, :], half)
    for block in range(half // 8):
        rows = [packed[c * half + block * 8 : c * half + block * 8 + 8, :] for c in range(4)]
        out[:, block * LANES : (block + 1) * LANES] = check_sums(
            rows[:3], rows[3], width[block * 8 : block * 8 + 8], checks.at[block]
        )


def far_kernel(
    sources, kinds, pair_ref, arrived, own_check, up_inverse, signs,
    last_bins, other_last_bins, table, translations, other_translations, totals, low_table,
    spectra, kernels, high_table, density, check, checks, sems,
):
    leaves, entries = sources.shape
    half = leaves // 2
    blocks = arrived.shape[0] // 64
    kind_count = translations.shape[0]
    pair = pair_ref[0]

    table_copy = pltpu.make_async_copy(table, high_table, sems.at[0])
    table_copy.start()
    kernel_copies = []
    for side, bins in enumerate((translations, other_translations)):
        for t in range(TILES - 1):
            kernel_copies.append(pltpu.make_async_copy(
                bins.at[:, :, pl.ds(t * LANES, LANES)],
                kernels.at[pl.ds(0, kind_count), pl.ds(16 * side + 2 * t, 2), :],
                sems.at[1 + len(kernel_copies)],
            ))
        kernel_copies.append(pltpu.make_async_copy(
            (last_bins, other_last_bins)[side],
            kernels.at[pl.ds(0, kind_count), pl.ds(16 * side + 2 * TILES - 2, 2), :],
            sems.at[1 + len(kernel_copies)],
        ))
    for copy in kernel_copies:
        copy.start()
    kernels[kind_count] = jnp.zeros((ROWS, LANES), jnp.float32)

    density[...] = jnp.zeros(density.shape, jnp.float32)
    check[0, :, :] = own_check[:, :LANES]
    check[1, :, :] = own_check[:, LANES:]

    def arrive(block, carry):
        beads = [
            arrived[pl.ds(pl.multiple_of(block * 64, 64) + ch, 8, stride=8), :] for ch in range(5)
        ]
        check[leaves // 16 + block, :, :] = check_sums(beads[:3], beads[3], beads[4], checks)
        return carry

    if blocks == 1:
        arrive(0, 0)
    else:
        lax.fori_loop(0, blocks, arrive, 0)
    count = check.shape[0]
    for first in range(0, count, 3):
        some = range(first, min(first + 3, count))
        density[16 * first : 16 * first + 16 * len(some), :Q] = upward(
            jnp.concatenate([check[n] for n in some], 1), up_inverse[...]
        )
    table_copy.wait()
    low_table[...] = low_part(high_table[...])
    sign = jnp.where(pair == 1, signs[1:2, :], signs[0:1, :])
    other_sign = jnp.where(pair == 1, signs[0:1, :], signs[1:2, :])
    store_spectra(
        jnp.concatenate([density[...] * sign, density[...] * other_sign], 0),
        high_table, low_table, spectra,
    )
    for copy in kernel_copies:
        copy.wait()

    def translate(t, carry):
        leaf = pair * half + t
        sums = [[None] * 4, [None] * 4]
        for entry in range(entries):
            kind = kinds[leaf, entry]
            start = pl.multiple_of(sources[leaf, entry], ROWS)
            for side in range(2):
                k_re = kernels[kind, pl.ds(16 * side, 8, stride=2), :]
                k_im = kernels[kind, pl.ds(16 * side + 1, 8, stride=2), :]
                s_re = spectra[pl.ds(start + 16 * side, 8), :]
                s_im = spectra[pl.ds(start + 16 * side + 8, 8), :]
                terms = (k_re * s_re, k_im * s_im, k_re * s_im, k_im * s_re)
                for n, term in enumerate(terms):
                    sums[side][n] = term if sums[side][n] is None else sums[side][n] + term
        start = pl.multiple_of(t * ROWS, ROWS)
        for side in range(2):
            rr, ii, ri, ir = sums[side]
            totals[pl.ds(start + 16 * side, 8), :] = rr - ii
            totals[pl.ds(start + 16 * side + 8, 8), :] = ri + ir
        return carry

    lax.fori_loop(0, half, translate, 0, unroll=4)


def evaluate(
    pair, packed, totals, table, low_table, signs, down_inverse, eval_kernels, densities
):
    half = (packed.shape[0] - 8) // 4
    leaves = 2 * half
    rows = half // 2
    width = block_transpose(
        per_leaf(packed[4 * half + 3 : 4 * half + 4, :], rows, pair * half)
    )
    offsets = [
        block_transpose(packed[pl.ds(pl.multiple_of(c * half + pair * rows, 8), rows), :])
        for c in range(3)
    ]
    for q, kernel in surface_kernels(offsets, width):
        eval_kernels[pl.ds(8 * q, 8), :] = kernel
    sign = jnp.where(pair == 1, signs[1:2, :], signs[0:1, :])
    other_sign = jnp.where(pair == 1, signs[0:1, :], signs[1:2, :])
    lane = iota((half, LANES), 1)
    sides = []
    for side in range(2):
        columns = []
        for c in range(2):
            for t in range(TILES):
                line = totals[pl.ds(16 * side + c * 8 + t, half, stride=ROWS), :]
                if t == TILES - 1:
                    line = jnp.where(lane < BINS - t * LANES, line, 0.0)
                columns.append(line)
        sides.append(jnp.concatenate(columns, 1))
    high, low = split(jnp.concatenate(sides, 0))
    across = (((1,), (1,)), ((), ()))
    both = lax.dot_general(
        jnp.concatenate([high, low], 0), table[...], across,
        preferred_element_type=jnp.float32,
    )
    check = both[:leaves] + both[leaves:] + lax.dot_general(
        high, low_table[...], across, preferred_element_type=jnp.float32
    )
    check = (check[:half] * sign + check[half:] * other_sign)[:, :Q] * (1.0 / G)

    leaf_of = 2 * (lane & 7) + (lane >> 6)
    spread = jnp.where(iota((half, LANES), 0) == leaf_of, 1.0, 0.0)
    densities[...] = product(product(check, down_inverse[...], (1, 0)), spread, (0, 0))
    parts = [jnp.zeros((rows, LANES), jnp.float32)] * 4
    for q in range(Q):
        term = eval_kernels[8 * q : 8 * q + 8, :] * densities[q : q + 1, :]
        parts[q % 4] = parts[q % 4] + term
    return block_transpose((parts[0] + parts[1]) + (parts[2] + parts[3]))


def target_terms(pair, packed, stacked, terms):
    half = (packed.shape[0] - 8) // 4
    rows = half // 2
    width = per_leaf(packed[4 * half + 3 : 4 * half + 4, :], rows, pair * half)
    places = [
        width * packed[pl.ds(pl.multiple_of(c * half + pair * rows, 8), rows), :] for c in range(3)
    ]
    norm = places[0] * places[0] + places[1] * places[1] + (places[2] * places[2] + softening)
    pieces = [thirds(-2.0 * x) for x in places]
    norms = thirds(norm)
    one, zero = jnp.ones((rows, LANES), jnp.float32), jnp.zeros((rows, LANES), jnp.float32)
    for third in range(3):
        x, y, z = [piece[third] for piece in pieces]
        unit = one if third == 0 else zero
        first = [x, y, z, unit, norms[third]]
        second = [x, y, z, unit] if third < 2 else [zero] * 4
        last = [x, y, z, unit] if third < 1 else [zero] * 4
        for row, values in enumerate(first + second + last + [zero] * 3):
            stacked[pl.ds(16 * third + row, rows, stride=48), :] = values
    for r in range(rows):
        terms[r * LANES : (r + 1) * LANES, :] = (
            stacked[48 * r : 48 * (r + 1), :].T.astype(jnp.bfloat16)
        )


def near_kernel(
    near_source, pair_ref, owner_ref, swapped, placed, passed, packed, totals, high_table, low_table,
    signs, down_inverse, counts, decay_rate, stress, potential, new_stress,
    table, merged, centers, factors, stacked, terms, sums, eval_kernels, densities,
):
    entries, leaves = near_source.shape
    half = leaves // 2
    rows = half // 2
    pair = pair_ref[0]
    low = iota((half, LANES), 1) < BCAP
    target_terms(pair, packed, stacked, terms)
    far = evaluate(
        pair, packed, totals, high_table, low_table, signs, down_inverse, eval_kernels, densities
    )
    swapped_from = jnp.where(((owner_ref[0] & 1) ^ pair) == 1, 0, 2)
    for n, rows_of in ((swapped_from, swapped), (1, placed), (2 - swapped_from, passed)):
        first = n * (leaves * 8)
        for ch in range(4):
            beads = rows_of[ch * half : (ch + 1) * half, :]
            turned = pltpu.roll(beads, BCAP, 1)
            table[pl.ds(first + ch, half, stride=16), :] = jnp.where(low, beads, turned)
            table[pl.ds(first + 8 + ch, half, stride=16), :] = jnp.where(low, turned, beads)
    low = iota((rows, LANES), 1) < BCAP
    for ch in range(3):
        center = per_leaf(packed[4 * half + ch : 4 * half + ch + 1, :], rows, pair * half)
        turned = pltpu.roll(center, BCAP, 1)
        centers[pl.ds(ch, rows, stride=16), :] = jnp.where(low, center, turned)
        centers[pl.ds(8 + ch, rows, stride=16), :] = jnp.where(low, turned, center)
    pairs = entries // 2
    one, zero = jnp.ones((pairs, LANES), jnp.float32), jnp.zeros((pairs, LANES), jnp.float32)

    def prepare(t):
        leaf = pair * half + t
        start = t * pairs * 8
        for n in range(pairs):
            left = pl.multiple_of(near_source[2 * n, leaf] * 8, 8)
            right = pl.multiple_of(near_source[2 * n + 1, leaf] * 8, 8)
            merged[pl.ds(start + n * 8, 8), :] = jnp.where(
                low, table[pl.ds(left, 8), :], table[pl.ds(right, 8), :]
            )
        place = t * 8
        x, y, z = [
            merged[pl.ds(start + ch, pairs, stride=8), :] - centers[pl.ds(place + ch, 1), :]
            for ch in range(3)
        ]
        pieces = [thirds(v) for v in (x, y, z, x * x + y * y + z * z)]
        lines = [piece[0] for piece in pieces] + [one]
        lines += [piece[1] for piece in pieces] + [piece[2] for piece in pieces] + [zero] * 3
        start = t * pairs * 16
        for row, values in enumerate(lines):
            factors[pl.ds(start + row, pairs, stride=16), :] = values

    for t in range(half):
        prepare(t)

    def one_leaf(t, carry):
        mine = terms[pl.ds(pl.multiple_of(t * BCAP, BCAP), BCAP), :]
        total = jnp.zeros((BCAP, LANES), jnp.float32)
        for n in range(0, pairs, 4):
            start = pl.multiple_of((t * pairs + n) * 16, 16)
            some = jnp.concatenate(
                [factors[pl.ds(start + 16 * m, 16), :] for m in range(4)], 1
            ).astype(jnp.bfloat16)
            squared = jnp.dot(
                mine, jnp.concatenate([some] * 3, 0), preferred_element_type=jnp.float32
            )
            for side in range(4):
                weight = merged[pl.ds((t * pairs + n + side) * 8 + 3, 1), :]
                total = total + lax.rsqrt(squared[:, side * LANES : (side + 1) * LANES]) * weight
        sums[pl.ds(pl.multiple_of(t * BCAP, 8), BCAP), :] = total
        return carry

    lax.fori_loop(0, half, one_leaf, 0, unroll=4)
    for r in range(rows):
        block = sums[r * LANES : (r + 1) * LANES, :].T
        potential[r : r + 1, :] = jnp.sum(block, axis=0, keepdims=True)
    combined = potential[...] + far
    beads = per_leaf(counts[...].astype(jnp.float32), rows, pair * half)
    slot = iota((rows, LANES), 1) & (BCAP - 1)
    occupied = slot.astype(jnp.float32) < beads
    decay = per_leaf(decay_rate[...], rows)
    potential[...] = jnp.where(occupied, combined, 0.0)
    new_stress[...] = jnp.where(occupied, decay * stress[...] + combined, 0.0)


VMEM = pl.BlockSpec(memory_space=pltpu.VMEM)
SMEM = pl.BlockSpec(memory_space=pltpu.SMEM)
ANY = pl.BlockSpec(memory_space=pl.ANY)
MIB = 1024 * 1024


def call(kernel, outs, in_specs, scratch=(), limit=40, grid=(), flops=0, bytes_accessed=0):
    return pl.pallas_call(
        kernel,
        out_shape=outs,
        grid=grid,
        in_specs=in_specs,
        out_specs=jax.tree.map(lambda _: VMEM, outs),
        scratch_shapes=list(scratch),
        compiler_params=pltpu.CompilerParams(vmem_limit_bytes=limit * MIB),
        cost_estimate=pl.CostEstimate(
            flops=flops, bytes_accessed=bytes_accessed, transcendentals=0
        ),
    )


def body(
    offsets,
    charges,
    stress,
    decay_rate,
    morton_keys,
    levels,
    bead_counts,
    send_boxes,
    m2l_source,
    m2l_type,
    m2l_count,
    near_source,
    up_inverse,
    down_inverse,
    translations,
):
    f32 = jnp.float32
    leaves = morton_keys.shape[0]
    half = leaves // 2
    parts = lax.axis_size("wide") * lax.axis_size("narrow")
    table = jnp.asarray(transform_table())
    signs = jnp.asarray(sign_rows())
    pair = lax.axis_index("pair").reshape(1)
    owner = (
        lax.axis_index("wide") * lax.axis_size("narrow") + lax.axis_index("narrow")
    ).reshape(1)
    kind_count = translations.shape[0]

    other_translations = lax.ppermute(translations, "pair", [(0, 1), (1, 0)])
    packed, blocks, placed, sources, kinds = call(
        functools.partial(pack_kernel, kind_count),
        [
            jax.ShapeDtypeStruct((4 * half + 8, LANES), f32),
            jax.ShapeDtypeStruct((8 * parts, LANES), f32),
            jax.ShapeDtypeStruct((4 * half, LANES), f32),
            jax.ShapeDtypeStruct(m2l_source.shape, jnp.int32),
            jax.ShapeDtypeStruct(m2l_type.shape, jnp.int32),
        ],
        [VMEM] * 9,
        limit=62,
    )(
        offsets, charges.reshape(half, LANES), morton_keys.reshape(1, leaves),
        levels.reshape(1, leaves), bead_counts.reshape(1, leaves), send_boxes,
        m2l_source, m2l_type, m2l_count.reshape(1, leaves),
    )
    arrived = lax.all_to_all(
        blocks.reshape(parts, 8, LANES), PARTS, split_axis=0, concat_axis=0, tiled=True
    ).reshape(8 * parts, LANES)
    swaps = [(2 * d, 2 * (d ^ 1)) for d in range(parts)]
    for d in range(1, parts - 1, 2):
        swaps += [(2 * d + 1, 2 * d + 3), (2 * d + 3, 2 * d + 1)]
    swapped = lax.ppermute(placed, PARTS + ("pair",), swaps)
    own_check = call(
        own_kernel,
        jax.ShapeDtypeStruct((Q, leaves // 16 * LANES), f32),
        [VMEM],
        [pltpu.VMEM((leaves // 16, Q * 8, LANES), f32)],
        flops=4 * 10**10,
    )(packed)
    passed = lax.ppermute(swapped, "pair", [(0, 1), (1, 0)])

    last = pl.BlockSpec((kind_count, 2, LANES), lambda i: (0, 0, TILES - 1))
    totals, low_table = call(
        far_kernel,
        [
            jax.ShapeDtypeStruct((half * ROWS, LANES), f32),
            jax.ShapeDtypeStruct(table.shape, table.dtype),
        ],
        [SMEM] * 3 + [VMEM] * 4 + [last] * 2 + [ANY] * 3,
        [
            pltpu.VMEM(((leaves + 2 * parts) * ROWS, LANES), f32),
            pltpu.VMEM((kind_count + 1, ROWS, LANES), f32),
            pltpu.VMEM(table.shape, jnp.bfloat16),
            pltpu.VMEM((leaves + 2 * parts, QPAD), f32),
            pltpu.VMEM(((leaves + 2 * parts) // 16, Q, LANES), f32),
            pltpu.VMEM((Q * 8, LANES), f32),
            pltpu.SemaphoreType.DMA((2 * TILES + 1,)),
        ],
        grid=(1,),
        flops=10**10,
        bytes_accessed=4 * 10**6,
    )(
        sources, kinds, pair, arrived, own_check, up_inverse, signs, translations,
        other_translations, table, translations, other_translations,
    )

    out = jax.ShapeDtypeStruct((half // 2, LANES), f32)
    potential, new_stress = call(
        near_kernel,
        [out, out],
        [SMEM] * 3 + [VMEM] * 12,
        [
            pltpu.VMEM((3 * leaves * 8, LANES), f32),
            pltpu.VMEM((half * near_source.shape[1] // 2 * 8, LANES), f32),
            pltpu.VMEM((half * 8, LANES), f32),
            pltpu.VMEM((half * near_source.shape[1] // 2 * 16, LANES), f32),
            pltpu.VMEM((half // 2 * 48, LANES), f32),
            pltpu.VMEM((half * BCAP, 48), jnp.bfloat16),
            pltpu.VMEM((half * BCAP, LANES), f32),
            pltpu.VMEM((Q * 8, LANES), f32),
            pltpu.VMEM((Q, LANES), f32),
        ],
    )(
        near_source.T, pair, owner, swapped, placed, passed, packed, totals, table, low_table, signs,
        down_inverse, bead_counts.reshape(1, leaves), decay_rate.reshape(1, half),
        stress.reshape(half // 2, LANES),
    )
    return potential.reshape(-1), new_stress.reshape(-1)


def solution(mesh):
    return jax.shard_map(
        body,
        mesh=mesh,
        in_specs=(
            P(None, ("groups", "wide", "narrow")),
            P(("groups", "wide", "narrow")),
            P(("groups", "wide", "narrow", "pair")),
            P(("groups", "wide", "narrow", "pair")),
            P(("groups", "wide", "narrow")),
            P(("groups", "wide", "narrow")),
            P(("groups", "wide", "narrow")),
            P(("groups", "wide", "narrow"), None),
            P(("groups", "wide", "narrow"), None),
            P(("groups", "wide", "narrow"), None),
            P(("groups", "wide", "narrow")),
            P(("groups", "wide", "narrow"), None),
            P(),
            P(),
            P(None, None, "pair"),
        ),
        out_specs=(
            P(("groups", "wide", "narrow", "pair")),
            P(("groups", "wide", "narrow", "pair")),
        ),
        check_vma=False,
    )
```
